32 devices in a mesh: dp: 16 (over z, x, core), seq: 2 (over y).
Axes of the slice: x: 2, y: 2, z: 4, core: 2. Of those that a mesh axis runs over, the one named last changes fastest.
Arguments:
- tokens: bfloat16 [32768, 1024], P(('dp', 'seq')), may hold values from -6 to 6
- doc_lengths: int32 [16, 2], P('dp'), may hold values from 256 to 1792, as said below
- variate_ids: int32 [16, 2048], P('dp'), may hold values from 0 to 3
- time_ids: int32 [32768], P(('dp', 'seq')), may hold values from 0 to 511
- in_proj: bfloat16 [1024, 3072], P('dp'), may hold values from -0.1875 to 0.1875
- out_proj: bfloat16 [1024, 1024], P('dp'), may hold values from -1.5 to 1.5
- gate_up: bfloat16 [1024, 8192], P('dp'), may hold values from -0.1875 to 0.1875
- down_proj: bfloat16 [4096, 1024], P('dp'), may hold values from -0.09375 to 0.09375
- attn_gain: bfloat16 [1024], P('dp'), may hold values from 0.5 to 1.5
- ffn_gain: bfloat16 [1024], P('dp'), may hold values from 0.5 to 1.5
- query_gain: float32 [64], replicated, may hold values from 0.5 to 1.5
- key_gain: float32 [64], replicated, may hold values from 0.5 to 1.5
- head_bias: float32 [16, 2], replicated, may hold values from -1 to 1
- cotangent: bfloat16 [32768, 1024], P(('dp', 'seq')), may hold values from -6 to 6
Outputs:
- layer_out: bfloat16 [32768, 1024], P(('dp', 'seq'))
- input_grad: float32 [32768, 1024], P(('dp', 'seq'))
- in_proj_grad: float32 [1024, 3072], P('dp')
- out_proj_grad: float32 [1024, 1024], P('dp')
- gate_up_grad: float32 [1024, 8192], P('dp')
- down_proj_grad: float32 [4096, 1024], P('dp')
- attn_gain_grad: float32 [1024], P('dp')
- ffn_gain_grad: float32 [1024], P('dp')
- query_gain_grad: float32 [64], replicated
- key_gain_grad: float32 [64], replicated
- head_bias_grad: float32 [16, 2], replicated
The draws below stay inside these ranges and needn't reach their ends.
Inputs may be any that keep to these rules, and one draw needn't show every extreme that they name: `doc_lengths`: each pack holds two series, in either order, then padding slots. The longer has 1280 slots or more, the shorter 1024 // 4 to 512, the padding at most 256 slots.
All inputs are finite; a program needn't handle non-finite values.
Results may differ from the reference program's by a relative error of at most 0.018.
Values may be sent and summed in bfloat16 or wider, within the bound.
A program may use at most 320 MiB of HBM per device.

```python
import math
from functools import partial
import jax
import jax.numpy as jnp
from jax import lax

D = 1024
HEADS = 16
HEAD_DIM = 64
FF = 4096
VARIATES = 4
MAX_TIME = 512
PACK = 2048
LOCAL = 1024
PACKS = 16
TOKENS = 32768


def draw_doc_lengths(key, part):
    key = jax.random.fold_in(key, 7)
    pad_key, short_key, order_key, pick_key = jax.random.split(key, 4)
    padding = jax.random.randint(pad_key, (PACKS,), 0, LOCAL // 4 + 1)
    shorter = jax.random.randint(short_key, (PACKS,), LOCAL // 4, LOCAL // 2 + 1)
    chosen = jax.random.randint(pick_key, (), 0, PACKS)
    marked = jnp.arange(PACKS) == chosen
    padding = jnp.where(marked, 0, padding)
    shorter = jnp.where(marked, LOCAL // 4, shorter)
    longer = PACK - padding - shorter
    long_first = jax.random.randint(order_key, (PACKS,), 0, 2) == 1
    first_len = jnp.where(long_first, longer, shorter)
    second_len = jnp.where(long_first, shorter, longer)
    return jnp.stack([first_len, second_len], axis=-1).astype(jnp.int32)


def touch_ends(values, stream_key, least, largest):
    dims = values.shape
    place = [jax.random.randint(jax.random.fold_in(stream_key, axis), (), 0, dims[axis]) for axis in range(len(dims))]
    values = values.at[tuple(place)].set(least)
    longest = dims.index(max(dims))
    place[longest] = (place[longest] + 1) % dims[longest]
    return values.at[tuple(place)].set(largest)


def block_scale(key, shape, pieces, low, largest):
    def one(dim, parts):
        heights = jax.random.uniform(jax.random.fold_in(jax.random.fold_in(key, 6), dim), (parts,), jnp.float32, low / len(pieces), largest / len(pieces))
        return jnp.repeat(jnp.exp(heights), shape[dim] // parts).reshape((-1,) + (1,) * (len(shape) - dim - 1))

    gain = one(*pieces[0])
    for cut in pieces[1:]:
        gain = gain * one(*cut)
    return gain


def bell_draw(stream_key, dims, width, reach, shards=(), held_as=jnp.bfloat16):
    values = width * jax.random.normal(stream_key, dims, jnp.float32)
    if shards:
        values = values * block_scale(stream_key, dims, shards, -0.22, 0.18)
    return jnp.clip(values, -reach, reach).astype(held_as)


def setup_inputs(seed: int = 0) -> dict:
    streams_of = jax.random.split(jax.random.key(seed), 15)
    tokens = bell_draw(streams_of[0], (TOKENS, D), 1.0, 6.0, ((0, 32),))
    doc_lengths = draw_doc_lengths(jax.random.fold_in(streams_of[14], 71), 0)
    variate_ids = touch_ends(jax.random.randint(streams_of[2], (PACKS, PACK), 0, VARIATES), jax.random.fold_in(streams_of[2], 1), 0, VARIATES - 1).astype(jnp.int32)
    time_ids = touch_ends(jax.random.randint(streams_of[3], (TOKENS,), 0, MAX_TIME), jax.random.fold_in(streams_of[3], 1), 0, MAX_TIME - 1).astype(jnp.int32)
    in_proj = bell_draw(streams_of[4], (D, 3 * D), D ** -0.5, 0.1875, ((0, 16),))
    out_proj = bell_draw(streams_of[5], (D, D), (max(D // 64, 4)) ** -0.5, 1.5, ((0, 16),))
    gate_up = bell_draw(streams_of[6], (D, 2 * FF), D ** -0.5, 0.1875, ((0, 16),))
    down_proj = bell_draw(streams_of[7], (FF, D), FF ** -0.5, 0.09375, ((0, 16),))
    attn_gain = jnp.clip(1.0 + 0.1 * jax.random.normal(streams_of[8], (D,), jnp.float32), 0.5, 1.5).astype(jnp.bfloat16)
    ffn_gain = jnp.clip(1.0 + 0.1 * jax.random.normal(streams_of[9], (D,), jnp.float32), 0.5, 1.5).astype(jnp.bfloat16)
    query_gain = jnp.clip(1.0 + 0.1 * jax.random.normal(streams_of[10], (HEAD_DIM,), jnp.float32), 0.5, 1.5)
    key_gain = jnp.clip(1.0 + 0.1 * jax.random.normal(streams_of[11], (HEAD_DIM,), jnp.float32), 0.5, 1.5)
    head_bias = jnp.clip(jax.random.uniform(streams_of[12], (HEADS, 2), jnp.float32, -1.0, 1.0), -1.0, 1.0)
    cotangent = bell_draw(streams_of[13], (TOKENS, D), 1.0, 6.0, ((0, 32),))
    return {"tokens": tokens, "doc_lengths": doc_lengths, "variate_ids": variate_ids, "time_ids": time_ids, "in_proj": in_proj, "out_proj": out_proj, "gate_up": gate_up, "down_proj": down_proj, "attn_gain": attn_gain, "ffn_gain": ffn_gain, "query_gain": query_gain, "key_gain": key_gain, "head_bias": head_bias, "cotangent": cotangent}


EPSILON = 1e-06
ROPE_BASE = 10000.0
NEG_FILL = -1e+30
HIGH = lax.Precision.HIGHEST

@jax.custom_vjp
def low(v):
    return lax.optimization_barrier(v.astype(jnp.bfloat16)).astype(jnp.float32)

@jax.custom_vjp
def low_back(v):
    return v

def low_keep(v):
    return (low(v), None)

def low_pass(kept, grad):
    return (grad,)

def back_keep(v):
    return (v, None)

def back_low(kept, grad):
    return (low(grad),)
low.defvjp(low_keep, low_pass)
low_back.defvjp(back_keep, back_low)

def rms_scale(values, gain_vec):
    return values * lax.rsqrt(lax.optimization_barrier(jnp.mean(values * values, axis=-1, keepdims=True)) + EPSILON) * gain_vec

def rotate_half(values, angles):
    half_dim = values.shape[-1] // 2
    cosine = jnp.cos(angles)
    sine = jnp.sin(angles)
    first = values[..., :half_dim]
    second = values[..., half_dim:]
    return jnp.concatenate([first * cosine - second * sine, second * cosine + first * sine], axis=-1)

def rope_angles(pack_times, half_dim):
    frequency = jnp.exp(jnp.arange(half_dim, dtype=jnp.float32) * (-math.log(ROPE_BASE) / half_dim))
    return pack_times.astype(jnp.float32)[:, None] * frequency[None, :]

def segments_of(lengths, row_count):
    positions = jnp.arange(row_count, dtype=jnp.int32)
    first_end = lengths[0]
    second_end = lengths[0] + lengths[1]
    segment = (positions >= first_end).astype(jnp.int32) + (positions >= second_end).astype(jnp.int32)
    return (segment, positions < second_end)

def attend_head(operands, same_doc, same_var):
    query, key_rows, value_rows, bias_pair = operands
    score_scale = query.shape[-1] ** (-0.5)
    scores = low_back(jnp.dot(query, key_rows.T, precision=HIGH) * score_scale)
    scores = scores + jnp.where(same_var, bias_pair[0], bias_pair[1])
    scores = jnp.where(same_doc, scores, NEG_FILL)
    row_top = lax.optimization_barrier(jnp.max(scores, axis=1, keepdims=True))
    log_total = row_top + jnp.log(lax.optimization_barrier(jnp.sum(jnp.exp(scores - row_top), axis=1, keepdims=True)))
    attn_probs = low(jnp.exp(scores - log_total))
    return jnp.dot(attn_probs, value_rows, precision=HIGH)

def layer_forward(tokens_f, params, segment, variates, angles):
    in_proj, out_proj, gate_up, down_proj, attn_gain, ffn_gain, query_gain, key_gain, head_bias = params
    row_count = tokens_f.shape[0]
    normed = low(rms_scale(tokens_f, attn_gain))
    merged_proj = low_back(jnp.dot(normed, in_proj, precision=HIGH)).reshape(row_count, 3, HEADS, HEAD_DIM)
    turn = angles[:, None, :]
    queries = low(low_back(rotate_half(rms_scale(merged_proj[:, 0], query_gain), turn)))
    key_rows = low(low_back(rotate_half(rms_scale(merged_proj[:, 1], key_gain), turn)))
    value_rows = low(low_back(merged_proj[:, 2]))
    same_doc = segment[:, None] == segment[None, :]
    same_var = variates[:, None] == variates[None, :]
    head_fn = jax.checkpoint(partial(attend_head, same_doc=same_doc, same_var=same_var))
    heads_out = lax.map(head_fn, (queries.transpose(1, 0, 2), key_rows.transpose(1, 0, 2), value_rows.transpose(1, 0, 2), head_bias))
    attended = low(low_back(heads_out.transpose(1, 0, 2).reshape(row_count, HEADS * HEAD_DIM)))
    mixed = low_back(jnp.dot(attended, out_proj, precision=HIGH))
    residual = tokens_f + mixed
    normed_ffn = low(rms_scale(residual, ffn_gain))
    gate_vals = low_back(jnp.dot(normed_ffn, gate_up, precision=HIGH))
    hidden = low(jax.nn.silu(gate_vals[:, :FF]) * gate_vals[:, FF:])
    return residual + low_back(jnp.dot(hidden, down_proj, precision=HIGH))

def reference(tokens, doc_lengths, variate_ids, time_ids, in_proj, out_proj, gate_up, down_proj, attn_gain, ffn_gain, query_gain, key_gain, head_bias, cotangent):
    params = tuple((weight.astype(jnp.float32) for weight in (in_proj, out_proj, gate_up, down_proj, attn_gain, ffn_gain, query_gain, key_gain, head_bias)))
    pack_count = doc_lengths.shape[0]
    pack_tokens_all = tokens.reshape(pack_count, PACK, D)
    pack_cot_all = cotangent.reshape(pack_count, PACK, D)
    pack_times_all = time_ids.reshape(pack_count, PACK)
    zero_grads = jax.tree.map(jnp.zeros_like, params)

    def one_pack(totals, operands):
        pack_tokens, pack_cot, lengths, variates, pack_times = operands
        segment, valid = segments_of(lengths, PACK)
        angles = rope_angles(pack_times, HEAD_DIM // 2)

        def forward(tokens_f, weights):
            return layer_forward(tokens_f, weights, segment, variates, angles)
        result, pull = jax.vjp(forward, pack_tokens.astype(jnp.float32), params)
        seed_grad = pack_cot.astype(jnp.float32) * valid[:, None].astype(jnp.float32)
        token_grad, weight_grads = pull(seed_grad)
        totals = jax.tree.map(jnp.add, totals, weight_grads)
        return (totals, (result.astype(jnp.bfloat16), token_grad))
    totals, (outputs, token_grads) = lax.scan(one_pack, zero_grads, (pack_tokens_all, pack_cot_all, doc_lengths, variate_ids, pack_times_all))
    return (outputs.reshape(TOKENS, D), token_grads.reshape(TOKENS, D), totals[0], totals[1], totals[2], totals[3], totals[4], totals[5], totals[6], totals[7], totals[8])
```

```python
import functools
import math

import jax
import jax.numpy as jnp
from jax import lax
from jax.experimental import pallas as pl
from jax.experimental.pallas import tpu as pltpu
from jax.sharding import PartitionSpec as P

EPSILON = 1e-06
ROPE_BASE = 10000.0
NEG_FILL = -1e30
PAIR = 128
KEY_ROWS = 256
VMEM_BYTES = 48 * 2**20
bf16 = jnp.bfloat16
f32 = jnp.float32
NN = (((1,), (0,)), ((), ()))
NT = (((1,), (1,)), ((), ()))
TN = (((0,), (0,)), ((), ()))


def dot(left, right, dims=NN):
    return lax.dot_general(left, right, dims, preferred_element_type=f32)


def split_two(values):
    high = values.astype(bf16)
    return high, (values - high.astype(f32)).astype(bf16)


def lane_index():
    return lax.broadcasted_iota(jnp.int32, (1, PAIR), 1)


def half_ones(same):
    rows = lax.broadcasted_iota(jnp.int32, (2 * PAIR, PAIR), 0) % PAIR
    cols = lax.broadcasted_iota(jnp.int32, (2 * PAIR, PAIR), 1)
    match = (rows < 64) == (cols < 64)
    return jnp.where(match if same else jnp.logical_not(match), 1.0, 0.0).astype(bf16)


def head_sums(values, ones):
    return dot(jnp.concatenate(split_two(values), axis=1), ones)


def swap_halves(values):
    first = lane_index() % 64 < 32
    return jnp.where(first, pltpu.roll(values, PAIR - 32, 1), pltpu.roll(values, 32, 1))


def qkv_kernel(
    tokens_ref, gain_ref, weight_ref, cos_ref, sin_ref, qgain_ref, kgain_ref,
    q_ref, k_ref, v_ref, raw_ref, normed_ref,
):
    width = tokens_ref.shape[1]
    values = tokens_ref[...].astype(f32)
    inv = lax.rsqrt(jnp.mean(values * values, axis=-1, keepdims=True) + EPSILON)
    normed = (values * inv * gain_ref[...]).astype(bf16)
    normed_ref[...] = normed
    ones = half_ones(True)
    cosine, sine = cos_ref[...], sin_ref[...]
    for part, (out_ref, head_gain, scale) in enumerate(
        ((q_ref, qgain_ref[...], 0.125), (k_ref, kgain_ref[...], 1.0))
    ):
        for chunk in range(width // 256):
            start = part * width + chunk * 256
            raw = dot(normed, weight_ref[:, start : start + 256])
            raw_ref[:, start : start + 256] = raw
            for tile in range(2):
                u = raw[:, tile * PAIR : (tile + 1) * PAIR]
                unit = lax.rsqrt(head_sums(u * u, ones) * (1.0 / 64) + EPSILON)
                u = u * unit * head_gain
                u = u * cosine + swap_halves(u) * sine
                at = chunk * 256 + tile * PAIR
                out_ref[:, at : at + PAIR] = (u * scale).astype(bf16)
    for chunk in range(width // 256):
        start = 2 * width + chunk * 256
        v_ref[:, chunk * 256 : (chunk + 1) * 256] = dot(
            normed, weight_ref[:, start : start + 256]
        ).astype(bf16)


def project(tokens, gain, weight, cosine, sine, qgain, kgain, block=256):
    rows, width = tokens.shape
    by_rows = lambda i: (i, 0)
    whole = lambda i: (0, 0)
    return pl.pallas_call(
        qkv_kernel,
        grid=(rows // block,),
        in_specs=[
            pl.BlockSpec((block, width), by_rows),
            pl.BlockSpec((1, width), whole),
            pl.BlockSpec(weight.shape, whole),
            pl.BlockSpec((block, PAIR), by_rows),
            pl.BlockSpec((block, PAIR), by_rows),
            pl.BlockSpec((1, PAIR), whole),
            pl.BlockSpec((1, PAIR), whole),
        ],
        out_specs=[
            pl.BlockSpec((block, width), by_rows),
            pl.BlockSpec((block, width), by_rows),
            pl.BlockSpec((block, width), by_rows),
            pl.BlockSpec((block, 2 * width), by_rows),
            pl.BlockSpec((block, width), by_rows),
        ],
        out_shape=[
            jax.ShapeDtypeStruct((rows, width), bf16),
            jax.ShapeDtypeStruct((rows, width), bf16),
            jax.ShapeDtypeStruct((rows, width), bf16),
            jax.ShapeDtypeStruct((rows, 2 * width), f32),
            jax.ShapeDtypeStruct((rows, width), bf16),
        ],
        compiler_params=pltpu.CompilerParams(vmem_limit_bytes=VMEM_BYTES),
        cost_estimate=pl.CostEstimate(
            flops=6 * rows * width * width, bytes_accessed=20 * rows * width, transcendentals=0
        ),
    )(tokens, gain, weight, cosine, sine, qgain, kgain)


def merge_kernel(sources, parts, *refs):
    dq_refs = refs[:parts]
    dk_refs = refs[parts : parts + sources]
    dv_refs = refs[parts + sources : parts + 2 * sources]
    raw_ref, cos_ref, sin_ref, qgain_ref, kgain_ref, out_ref, gains_ref = refs[parts + 2 * sources :]
    width = dq_refs[0].shape[1]
    ones = half_ones(True)
    cosine, sine = cos_ref[...], sin_ref[...]

    @pl.when(pl.program_id(0) == 0)
    def _():
        gains_ref[...] = jnp.zeros_like(gains_ref)

    for part, (grad_refs, head_gain) in enumerate(((dq_refs, qgain_ref[...]), (dk_refs, kgain_ref[...]))):
        for tile in range(width // PAIR):
            at = slice(tile * PAIR, (tile + 1) * PAIR)
            grad = grad_refs[0][:, at].astype(f32)
            for ref in grad_refs[1:]:
                grad = grad + ref[:, at].astype(f32)
            grad = grad.astype(bf16).astype(f32)
            grad = grad * cosine - swap_halves(grad) * sine
            there = slice(part * width + tile * PAIR, part * width + (tile + 1) * PAIR)
            raw = raw_ref[:, there]
            unit = lax.rsqrt(head_sums(raw * raw, ones) * (1.0 / 64) + EPSILON)
            hat = raw * unit
            gains_ref[part : part + 1, at] += jnp.sum(grad * hat, axis=0, keepdims=True)
            weighted = grad * head_gain
            inner = head_sums(weighted * hat, ones) * (1.0 / 64)
            out_ref[:, there] = (unit * (weighted - hat * inner)).astype(bf16)
    total = dv_refs[0][...].astype(f32)
    for ref in dv_refs[1:]:
        total = total + ref[...].astype(f32)
    out_ref[:, 2 * width :] = total.astype(bf16)


def merge_grads(dqs, dks, dvs, raw, cosine, sine, qgain, kgain, block=256):
    rows, width = dqs[0].shape
    by_rows = lambda i: (i, 0)
    whole = lambda i: (0, 0)
    grads = list(dqs) + list(dks) + list(dvs)
    return pl.pallas_call(
        functools.partial(merge_kernel, len(dks), len(dqs)),
        grid=(rows // block,),
        in_specs=[pl.BlockSpec((block, width), by_rows)] * len(grads)
        + [
            pl.BlockSpec((block, 2 * width), by_rows),
            pl.BlockSpec((block, PAIR), by_rows),
            pl.BlockSpec((block, PAIR), by_rows),
            pl.BlockSpec((1, PAIR), whole),
            pl.BlockSpec((1, PAIR), whole),
        ],
        out_specs=[pl.BlockSpec((block, 3 * width), by_rows), pl.BlockSpec((8, width), whole)],
        out_shape=[
            jax.ShapeDtypeStruct((rows, 3 * width), bf16),
            jax.ShapeDtypeStruct((8, width), f32),
        ],
        compiler_params=pltpu.CompilerParams(vmem_limit_bytes=VMEM_BYTES),
        cost_estimate=pl.CostEstimate(
            flops=100 * rows * width, bytes_accessed=40 * rows * width, transcendentals=0
        ),
    )(*grads, raw, cosine, sine, qgain, kgain)


def forward_kernel(sources, query_rows, flags, q_ref, aq_ref, coef_ref, *refs):
    keyed = refs[: 3 * sources]
    out_ref, full_ref, query, total = refs[3 * sources :]
    rows = q_ref.shape[0]
    lane = lane_index()
    half = lane < 64
    mine = (half, jnp.logical_not(half))
    both = q_ref[...]
    extra = aq_ref[...]
    for h in range(2):
        query[h] = jnp.where(mine[h], both, extra * coef_ref[0, h : h + 1, :])
        total[h] = jnp.zeros_like(total[h])
    blocks = keyed[0].shape[0] // KEY_ROWS
    for j in range(sources):
        k_ref, v_ref, ak_ref = keyed[3 * j : 3 * j + 3]
        for b in range(blocks):

            @pl.when(flags[j * blocks + b] != 0)
            def _():
                at = slice(b * KEY_ROWS, (b + 1) * KEY_ROWS)
                keys, values, columns = k_ref[at, :], v_ref[at, :], ak_ref[at, :]
                ones = jnp.ones_like(values)
                keys2 = [jnp.where(mine[h], keys, columns) for h in range(2)]
                values2 = [jnp.where(mine[h], values, ones) for h in range(2)]
                for i in range(rows // query_rows):
                    part = slice(i * query_rows, (i + 1) * query_rows)
                    for h in range(2):
                        probs = jnp.exp(dot(query[h, part, :], keys2[h], NT)).astype(bf16)
                        total[h, part, :] += dot(probs, values2[h])

    outs = []
    for h in range(2):
        summed = total[h]
        outs.append(summed / pltpu.roll(summed, 64, 1))
        log_total = jnp.log(jnp.maximum(summed, 1e-30))
        high = log_total.astype(bf16)
        mid, low = split_two(log_total - high.astype(f32))
        base = lane - 64 if h == 0 else lane
        full_ref[:, h * PAIR : (h + 1) * PAIR] = jnp.where(
            base == 11, -high, jnp.where(base == 12, -mid, jnp.where(base == 13, -low, query[h]))
        )
    out_ref[...] = jnp.where(half, outs[0], outs[1]).astype(bf16)


def attend(flags, queries, query_columns, coefficients, keyed):
    rows, width = queries.shape
    pairs = width // PAIR
    key_rows = keyed[0][0].shape[0]
    sources = len(keyed)
    by_pair = lambda p, f: (0, p)
    whole = lambda p, f: (0, 0)
    in_specs = [
        pl.BlockSpec((rows, PAIR), by_pair),
        pl.BlockSpec((rows, PAIR), whole),
        pl.BlockSpec((1, 2, PAIR), lambda p, f: (p, 0, 0)),
    ]
    operands = [queries, query_columns, coefficients]
    for keys, values, columns in keyed:
        in_specs += [
            pl.BlockSpec((key_rows, PAIR), by_pair),
            pl.BlockSpec((key_rows, PAIR), by_pair),
            pl.BlockSpec((key_rows, PAIR), whole),
        ]
        operands += [keys, values, columns]
    return pl.pallas_call(
        functools.partial(forward_kernel, sources, min(512, rows)),
        grid_spec=pltpu.PrefetchScalarGridSpec(
            num_scalar_prefetch=1,
            grid=(pairs,),
            in_specs=in_specs,
            out_specs=[
                pl.BlockSpec((rows, PAIR), by_pair),
                pl.BlockSpec((rows, 2 * PAIR), by_pair),
            ],
            scratch_shapes=[
                pltpu.VMEM((2, rows, PAIR), bf16),
                pltpu.VMEM((2, rows, PAIR), f32),
            ],
        ),
        out_shape=[
            jax.ShapeDtypeStruct((rows, width), bf16),
            jax.ShapeDtypeStruct((rows, 2 * width), bf16),
        ],
        compiler_params=pltpu.CompilerParams(vmem_limit_bytes=VMEM_BYTES),
        cost_estimate=pl.CostEstimate(
            flops=8 * rows * key_rows * sources * width,
            bytes_accessed=12 * rows * width,
            transcendentals=rows * key_rows * sources * 2 * pairs,
        ),
    )(flags, *operands)


def backward_kernel(
    flags, full_ref, grad_ref, out_ref, aq_ref, k_ref, v_ref, ak_ref,
    dq_ref, dk_ref, dv_ref, bias_ref, grads, dq_total,
):
    rows = grad_ref.shape[0]
    lane = lane_index()
    half = lane < 64
    mine = (half, jnp.logical_not(half))
    base = (lane - 64, lane)
    both = grad_ref[...]
    row_total = head_sums(both.astype(f32) * out_ref[...].astype(f32), half_ones(False))
    high, low = split_two(row_total)
    zero = jnp.zeros_like(high)
    for h in range(2):
        extra = jnp.where(base[h] == 0, -high, jnp.where(base[h] == 1, -low, zero))
        grads[h] = jnp.where(mine[h], both, extra)
        dq_total[h] = jnp.zeros_like(dq_total[h])
    for b in range(k_ref.shape[0] // KEY_ROWS):
        at = slice(b * KEY_ROWS, (b + 1) * KEY_ROWS)

        @pl.when(flags[b] != 0)
        def _():
            keys, values, columns = k_ref[at, :], v_ref[at, :], ak_ref[at, :]
            ones = jnp.ones_like(values)
            dks, dvs = [], []
            for h in range(2):
                keys2 = jnp.where(mine[h], keys, columns)
                pick = (base[h] >= 0) & (base[h] < 2)
                values2 = jnp.where(mine[h], values, jnp.where(pick, ones, jnp.zeros_like(ones)))
                full = full_ref[:, h * PAIR : (h + 1) * PAIR]
                probs = jnp.exp(dot(keys2, full, NT))
                score_low = (probs * dot(values2, grads[h], NT)).astype(bf16)
                dks.append(dot(score_low, full))
                dvs.append(dot(probs.astype(bf16), grads[h]))
                dq_total[h] += dot(keys2, score_low, TN)
            dk_ref[at, :] = jnp.where(half, dks[0], dks[1]).astype(dk_ref.dtype)
            dv_ref[at, :] = jnp.where(half, dvs[0], dvs[1]).astype(dv_ref.dtype)

        @pl.when(flags[b] == 0)
        def _():
            dk_ref[at, :] = jnp.zeros((KEY_ROWS, PAIR), dk_ref.dtype)
            dv_ref[at, :] = jnp.zeros((KEY_ROWS, PAIR), dv_ref.dtype)

    dq = [dq_total[h].T for h in range(2)]
    dq_ref[...] = jnp.where(half, dq[0], dq[1]) * 0.125
    variates = aq_ref[...].astype(f32)
    for h in range(2):
        pick = (base[h] >= 0) & (base[h] < 4)
        bias_ref[0, h : h + 1, :] = jnp.sum(
            jnp.where(pick, dq[h] * variates, 0.0), axis=0, keepdims=True
        )


def attend_back(flags, full, grad, out, query_columns, keys, values, key_columns):
    rows, width = grad.shape
    pairs = width // PAIR
    key_rows = keys.shape[0]
    by_pair = lambda p, f: (0, p)
    whole = lambda p, f: (0, 0)
    return pl.pallas_call(
        backward_kernel,
        grid_spec=pltpu.PrefetchScalarGridSpec(
            num_scalar_prefetch=1,
            grid=(pairs,),
            in_specs=[
                pl.BlockSpec((rows, 2 * PAIR), by_pair),
                pl.BlockSpec((rows, PAIR), by_pair),
                pl.BlockSpec((rows, PAIR), by_pair),
                pl.BlockSpec((rows, PAIR), whole),
                pl.BlockSpec((key_rows, PAIR), by_pair),
                pl.BlockSpec((key_rows, PAIR), by_pair),
                pl.BlockSpec((key_rows, PAIR), whole),
            ],
            out_specs=[
                pl.BlockSpec((rows, PAIR), by_pair),
                pl.BlockSpec((key_rows, PAIR), by_pair),
                pl.BlockSpec((key_rows, PAIR), by_pair),
                pl.BlockSpec((1, 2, PAIR), lambda p, f: (p, 0, 0)),
            ],
            scratch_shapes=[
                pltpu.VMEM((2, rows, PAIR), bf16),
                pltpu.VMEM((2, PAIR, rows), f32),
            ],
        ),
        out_shape=[
            jax.ShapeDtypeStruct((rows, width), f32),
            jax.ShapeDtypeStruct((key_rows, width), bf16),
            jax.ShapeDtypeStruct((key_rows, width), bf16),
            jax.ShapeDtypeStruct((pairs, 2, PAIR), f32),
        ],
        compiler_params=pltpu.CompilerParams(vmem_limit_bytes=VMEM_BYTES),
        cost_estimate=pl.CostEstimate(
            flops=20 * rows * key_rows * width,
            bytes_accessed=20 * rows * width,
            transcendentals=rows * key_rows * 2 * pairs,
        ),
    )(flags, full, grad, out, query_columns, keys, values, key_columns)


def slot_columns(segment, variates):
    rows = segment.shape[0]
    same_var = (variates[:, None] == jnp.arange(4, dtype=jnp.int32)[None, :]).astype(f32)
    in_seg = (segment[:, None] == jnp.arange(3, dtype=jnp.int32)[None, :]).astype(f32)
    three = jnp.ones((rows, 3), f32)
    rest = jnp.zeros((rows, 50), f32)
    query = jnp.concatenate([same_var, same_var, (1.0 - in_seg) * NEG_FILL, 0.0 * three, rest], 1)
    key = jnp.concatenate([same_var, same_var, in_seg, three, rest], 1)
    return (
        jnp.concatenate([query, query], 1).astype(bf16),
        jnp.concatenate([key, key], 1).astype(bf16),
    )


def bias_columns(head_bias):
    delta = head_bias[:, 0] - head_bias[:, 1]
    high, low = split_two(delta)
    heads = delta.shape[0]
    row = jnp.concatenate(
        [
            jnp.broadcast_to(high[:, None], (heads, 4)),
            jnp.broadcast_to(low[:, None], (heads, 4)),
            jnp.ones((heads, 3), bf16),
            jnp.zeros((heads, 53), bf16),
        ],
        1,
    )
    return jnp.concatenate([row, row], 1).reshape(heads // 2, 2, PAIR)


def rms_forward(values, gain_vec):
    inv_rms = lax.rsqrt(jnp.mean(values * values, axis=-1, keepdims=True) + EPSILON)
    return (values * inv_rms * gain_vec, inv_rms)


def rms_backward(values, inv_rms, gain_vec, upstream):
    weighted = upstream * gain_vec
    inner_sum = jnp.mean(weighted * values, axis=-1, keepdims=True)
    value_grad = inv_rms * weighted - values * inv_rms * inv_rms * inv_rms * inner_sum
    return (value_grad, upstream * values * inv_rms)


def rows_product(left, right):
    return dot(left, right, TN).astype(bf16)


def shift_by(values, count, step):
    return lax.ppermute(values, "seq", [(i, (i + step) % count) for i in range(count)])


def sum_seq(values, count):
    if count == 2:
        return values.astype(f32) + shift_by(values, count, 1).astype(f32)
    return lax.psum(values.astype(f32), "seq")


def body(
    tokens, doc_lengths, variate_ids, time_ids, in_proj, out_proj, gate_up, down_proj,
    attn_gain, ffn_gain, query_gain, key_gain, head_bias, cotangent,
):
    seq_count = lax.axis_size("seq")
    seq_rank = lax.axis_index("seq")
    local_rows, width = tokens.shape
    pack_rows = local_rows * seq_count
    head_dim = query_gain.shape[0]
    hidden_width = gate_up.shape[1] // 2

    gains = jnp.stack([attn_gain, ffn_gain], axis=1)
    in_wide = jnp.concatenate([in_proj, jnp.pad(gains, ((0, 0), (0, PAIR - 2)))], axis=1)
    gather = lambda w: lax.all_gather(w, "dp", axis=0, tiled=True)
    in_full = gather(in_wide)
    out_full, gate_full, down_full = gather(out_proj), gather(gate_up), gather(down_proj)
    attn_gain_f = in_full[:, 3 * width].astype(f32)[None, :]
    ffn_gain_f = in_full[:, 3 * width + 1].astype(f32)[None, :]

    positions = jnp.arange(pack_rows, dtype=jnp.int32)
    first_end = doc_lengths[0, 0]
    second_end = first_end + doc_lengths[0, 1]
    segment = (positions >= first_end).astype(jnp.int32) + (positions >= second_end).astype(jnp.int32)
    query_columns, key_columns = slot_columns(segment, variate_ids[0])
    coefficients = bias_columns(head_bias)
    start = seq_rank * local_rows
    query_columns = lax.dynamic_slice_in_dim(query_columns, start, local_rows)
    local_segment = lax.dynamic_slice_in_dim(segment, start, local_rows)
    valid_rows = (local_segment < 2).astype(f32)
    source_columns, source_flags = [], []
    for step in range(seq_count):
        begin = ((seq_rank + step) % seq_count) * local_rows
        source_columns.append(lax.dynamic_slice_in_dim(key_columns, begin, local_rows))
        there = lax.dynamic_slice_in_dim(segment, begin, local_rows).reshape(-1, KEY_ROWS)
        source_flags.append(
            ((there[:, 0] <= local_segment[-1]) & (there[:, -1] >= local_segment[0])).astype(jnp.int32)
        )

    half_dim = head_dim // 2
    frequency = jnp.exp(jnp.arange(half_dim, dtype=f32) * (-math.log(ROPE_BASE) / half_dim))
    angles = time_ids.astype(f32)[:, None] * frequency[None, :]
    cosine, sine = jnp.cos(angles), jnp.sin(angles)
    cosine = jnp.concatenate([cosine] * 4, axis=1)
    sine = jnp.concatenate([-sine, sine] * 2, axis=1)
    qgain = jnp.tile(query_gain, 2)[None, :]
    kgain = jnp.tile(key_gain, 2)[None, :]

    queries, keys, values, raw, normed_low = project(
        tokens, attn_gain_f, in_full, cosine, sine, qgain, kgain
    )
    keyed = [(keys, values, source_columns[0])]
    for step in range(1, seq_count):
        keyed.append(
            (
                shift_by(keys, seq_count, -step),
                shift_by(values, seq_count, -step),
                source_columns[step],
            )
        )
    attended, full_query = attend(
        jnp.concatenate(source_flags), queries, query_columns, coefficients, keyed
    )

    inputs_f = tokens.astype(f32)
    residual = inputs_f + dot(attended, out_full)
    normed_ffn, ffn_scale = rms_forward(residual, ffn_gain_f)
    normed_ffn_low = normed_ffn.astype(bf16)
    gate_vals = dot(normed_ffn_low, gate_full)
    gate_part = gate_vals[:, :hidden_width]
    up_part = gate_vals[:, hidden_width:]
    sigmoid_gate = jax.nn.sigmoid(gate_part)
    silu_gate = gate_part * sigmoid_gate
    hidden = (silu_gate * up_part).astype(bf16)
    layer_out = (residual + dot(hidden, down_full)).astype(bf16)

    seed_grad = cotangent.astype(f32) * valid_rows[:, None]
    seed_low = seed_grad.astype(bf16)
    down_grad = rows_product(hidden, seed_low)
    hidden_grad = dot(seed_low, down_full, NT)
    gate_grad_part = hidden_grad * up_part * sigmoid_gate * (1.0 + gate_part * (1.0 - sigmoid_gate))
    up_grad_part = hidden_grad * silu_gate
    gate_vals_grad = jnp.concatenate([gate_grad_part, up_grad_part], axis=1).astype(bf16)
    gate_up_grad = rows_product(normed_ffn_low, gate_vals_grad)
    normed_ffn_grad = dot(gate_vals_grad, gate_full, NT)
    resid_norm_grad, ffn_gain_terms = rms_backward(residual, ffn_scale, ffn_gain_f, normed_ffn_grad)
    residual_grad = seed_grad + resid_norm_grad
    mixed_low = residual_grad.astype(bf16)
    out_proj_grad = rows_product(attended, mixed_low)
    attended_grad = dot(mixed_low, out_full, NT).astype(bf16)

    scatter = lambda g: sum_seq(
        lax.psum_scatter(g, "dp", scatter_dimension=0, tiled=True), seq_count
    )
    dqs, dks, dvs, biases = [], [], [], []
    for step in list(range(1, seq_count)) + [0]:
        there_keys, there_values, there_columns = keyed[step]
        dq, dk, dv, bias = attend_back(
            source_flags[step], full_query, attended_grad, attended, query_columns,
            there_keys, there_values, there_columns,
        )
        dqs.append(dq)
        dks.append(shift_by(dk, seq_count, step) if step else dk)
        dvs.append(shift_by(dv, seq_count, step) if step else dv)
        biases.append(bias)
    merged_grad, head_gain_terms = merge_grads(dqs, dks, dvs, raw, cosine, sine, qgain, kgain)
    in_proj_grad = rows_product(normed_low, merged_grad)
    normed_grad = dot(merged_grad, in_full[:, : 3 * width], NT)
    norm_scale = lax.rsqrt(jnp.mean(inputs_f * inputs_f, axis=-1, keepdims=True) + EPSILON)
    input_norm_grad, attn_gain_terms = rms_backward(inputs_f, norm_scale, attn_gain_f, normed_grad)
    input_grad = residual_grad + input_norm_grad

    same_bias = jnp.sum(sum(biases), axis=-1).reshape(-1)
    heads = same_bias.shape[0]
    head_gains = jnp.sum(head_gain_terms[:2].reshape(2, -1, head_dim), axis=1)
    small = lax.psum(
        jnp.concatenate(
            [
                jnp.sum(attn_gain_terms, axis=0),
                jnp.sum(ffn_gain_terms, axis=0),
                head_gains[0],
                head_gains[1],
                same_bias,
            ]
        ),
        ("dp", "seq"),
    )
    gain_rows = attn_gain.shape[0]
    here = lax.axis_index("dp") * gain_rows
    tail = small[2 * width :]
    same_bias = tail[2 * head_dim : 2 * head_dim + heads]
    return (
        layer_out,
        input_grad,
        scatter(in_proj_grad),
        scatter(out_proj_grad),
        scatter(gate_up_grad),
        scatter(down_grad),
        lax.dynamic_slice_in_dim(small, here, gain_rows),
        lax.dynamic_slice_in_dim(small, width + here, gain_rows),
        tail[:head_dim],
        tail[head_dim : 2 * head_dim],
        jnp.stack([same_bias, -same_bias], axis=1),
    )


def solution(mesh):
    in_specs = (
        P(("dp", "seq"), None),
        P("dp", None),
        P("dp", None),
        P(("dp", "seq")),
        P("dp", None),
        P("dp", None),
        P("dp", None),
        P("dp", None),
        P("dp"),
        P("dp"),
        P(),
        P(),
        P(),
        P(("dp", "seq"), None),
    )
    out_specs = (
        P(("dp", "seq"), None),
        P(("dp", "seq"), None),
        P("dp", None),
        P("dp", None),
        P("dp", None),
        P("dp", None),
        P("dp"),
        P("dp"),
        P(),
        P(),
        P(),
    )
    return jax.shard_map(body, mesh=mesh, in_specs=in_specs, out_specs=out_specs, check_vma=False)
```

```python
import functools
import math

import jax
import jax.numpy as jnp
from jax import lax
from jax.experimental import pallas as pl
from jax.experimental.pallas import tpu as pltpu
from jax.sharding import PartitionSpec as P

EPSILON = 1e-06
ROPE_BASE = 10000.0
NEG_FILL = -1e30
PAIR = 128
CHUNKS = 2
KEY_ROWS = 256
VMEM_BYTES = 48 * 2**20
NO_COST = pl.CostEstimate(flops=1, bytes_accessed=1, transcendentals=0)
bf16 = jnp.bfloat16
f32 = jnp.float32
NN = (((1,), (0,)), ((), ()))
NT = (((1,), (1,)), ((), ()))
TN = (((0,), (0,)), ((), ()))


def dot(left, right, dims=NN):
    return lax.dot_general(left, right, dims, preferred_element_type=f32)


def split_two(values):
    high = values.astype(bf16)
    return high, (values - high.astype(f32)).astype(bf16)


def lane_index():
    return lax.broadcasted_iota(jnp.int32, (1, PAIR), 1)


def half_ones(same):
    rows = lax.broadcasted_iota(jnp.int32, (2 * PAIR, PAIR), 0) % PAIR
    cols = lax.broadcasted_iota(jnp.int32, (2 * PAIR, PAIR), 1)
    match = (rows < 64) == (cols < 64)
    return jnp.where(match if same else jnp.logical_not(match), 1.0, 0.0).astype(bf16)


def head_sums(values, ones):
    return dot(jnp.concatenate(split_two(values), axis=1), ones)


def swap_halves(values):
    first = lane_index() % 64 < 32
    return jnp.where(first, pltpu.roll(values, PAIR - 32, 1), pltpu.roll(values, 32, 1))


def gather_kernel(shard_ref, tokens_ref, times_ref, wide_ref, there_tokens_ref, there_times_ref, arrived, sent, keep):
    place, rank = lax.axis_index("dp"), lax.axis_index("seq")
    z, x, core = place // 4, place // 2 % 2, place % 2
    rows = shard_ref.shape[0]
    lines = 4

    def device(z, x, core, seq):
        return {"dp": z * 4 + x * 2 + core, "seq": seq}

    up, down = device(z + 1, x, core, rank), device(z - 1, x, core, rank)
    over, twin = device(z, 1 - x, core, rank), device(z, x, 1 - core, rank)
    other = device(z, x, core, 1 - rank)
    barrier = pltpu.get_barrier_semaphore()

    def greet(target):
        pl.semaphore_signal(barrier, inc=1, device_id=target, device_id_type=pl.DeviceIdType.MESH)

    for target in (over, twin, other):
        greet(target)
    pl.when(z < lines - 1)(lambda: greet(up))
    pl.when(z > 0)(lambda: greet(down))
    ends = (z == 0).astype(jnp.int32) + (z == lines - 1).astype(jnp.int32)
    pl.semaphore_wait(barrier, 5 - ends)

    def block(z, x, core):
        return z * 4 + x * 2 + core

    def rows_of(which):
        return wide_ref.at[pl.ds(pl.multiple_of(which * rows, rows), rows)]

    def copy(which, path, target, own=False):
        return pltpu.make_async_remote_copy(
            src_ref=shard_ref if own else rows_of(which),
            dst_ref=rows_of(which),
            send_sem=sent.at[path, which],
            recv_sem=arrived.at[which],
            device_id=target,
            device_id_type=pl.DeviceIdType.MESH,
        )

    def swap(source, target, index):
        return pltpu.make_async_remote_copy(
            src_ref=source,
            dst_ref=target,
            send_sem=keep.at[index],
            recv_sem=keep.at[index + 1],
            device_id=other,
            device_id_type=pl.DeviceIdType.MESH,
        )

    me = block(z, x, core)
    pl.when(z < lines - 1)(lambda: copy(me, 0, up, True).start())
    pl.when(z > 0)(lambda: copy(me, 3, down, True).start())
    copy(me, 1, over, True).start()
    copy(me, 2, twin, True).start()
    swaps = [swap(tokens_ref, there_tokens_ref, 0), swap(times_ref, there_times_ref, 2)]
    for each in swaps:
        each.start()
    here = pltpu.make_async_copy(shard_ref, rows_of(me), keep.at[4])
    here.start()

    def pass_over(which):
        copy(which, 2, twin).start()

    for step in range(1, lines):

        @pl.when(z >= step)
        def _():
            which = block(z - step, x, core)
            copy(which, 0, up).wait_recv()
            pl.when(z < lines - 1)(lambda: copy(which, 0, up).start())
            copy(which, 1, over).start()
            pass_over(which)

        @pl.when(z + step < lines)
        def _():
            which = block(z + step, x, core)
            copy(which, 3, down).wait_recv()
            pl.when(z > 0)(lambda: copy(which, 3, down).start())
            copy(which, 1, over).start()
            pass_over(which)

    for line in range(lines):
        which = block(line, 1 - x, core)
        copy(which, 1, over).wait_recv()
        pass_over(which)
    for line in range(lines):
        for side in range(2):
            copy(block(line, side, 1 - core), 2, twin).wait_recv()
    for line in range(lines):
        which = block(line, x, core)
        copy(which, 1, over).wait_send()
        copy(which, 2, twin).wait_send()
        copy(block(line, 1 - x, core), 2, twin).wait_send()
        pl.when((line <= z) & (z < lines - 1))(lambda: copy(which, 0, up).wait_send())
        pl.when((line >= z) & (z > 0))(lambda: copy(which, 3, down).wait_send())
    for each in swaps:
        each.wait()
    here.wait()


def gather_first(shard, tokens, times, places):
    anywhere = pl.BlockSpec(memory_space=pl.ANY)
    return pl.pallas_call(
        gather_kernel,
        in_specs=[anywhere] * 3,
        out_specs=[anywhere] * 3,
        out_shape=[
            jax.ShapeDtypeStruct((shard.shape[0] * places, shard.shape[1]), shard.dtype),
            jax.ShapeDtypeStruct(tokens.shape, tokens.dtype),
            jax.ShapeDtypeStruct(times.shape, times.dtype),
        ],
        scratch_shapes=[
            pltpu.SemaphoreType.DMA((places,)),
            pltpu.SemaphoreType.DMA((4, places)),
            pltpu.SemaphoreType.DMA((5,)),
        ],
        compiler_params=pltpu.CompilerParams(collective_id=0, has_side_effects=True),
        cost_estimate=NO_COST,
    )(shard, tokens, times)


def column_of(part, column, width):
    size = width // CHUNKS
    return (column // size * 3 + part) * size + column % size


def qkv_kernel(
    tokens_ref, gain_ref, weight_ref, cos_ref, sin_ref, qgain_ref, kgain_ref,
    k_ref, v_ref, *own_refs,
):
    width = tokens_ref.shape[1]
    values = tokens_ref[...].astype(f32)
    inv = lax.rsqrt(jnp.mean(values * values, axis=-1, keepdims=True) + EPSILON)
    normed = (values * inv * gain_ref[...]).astype(bf16)
    ones = half_ones(True)
    cosine, sine = cos_ref[...], sin_ref[...]
    turned = [(1, k_ref, kgain_ref[...], 1.0)]
    if own_refs:
        q_ref, raw_ref, normed_ref = own_refs
        normed_ref[...] = normed
        turned.append((0, q_ref, qgain_ref[...], 0.125))
    for part, out_ref, head_gain, scale in turned:
        for chunk in range(width // 256):
            start = column_of(part, chunk * 256, width)
            raw = dot(normed, weight_ref[:, start : start + 256])
            if own_refs:
                raw_ref[:, part * width + chunk * 256 : part * width + (chunk + 1) * 256] = raw
            for tile in range(2):
                u = raw[:, tile * PAIR : (tile + 1) * PAIR]
                unit = lax.rsqrt(head_sums(u * u, ones) * (1.0 / 64) + EPSILON)
                u = u * unit * head_gain
                u = u * cosine + swap_halves(u) * sine
                at = chunk * 256 + tile * PAIR
                out_ref[:, at : at + PAIR] = (u * scale).astype(bf16)
    for chunk in range(width // 256):
        start = column_of(2, chunk * 256, width)
        v_ref[:, chunk * 256 : (chunk + 1) * 256] = dot(
            normed, weight_ref[:, start : start + 256]
        ).astype(bf16)


def project(tokens, gain, weight, cosine, sine, qgain, kgain, own, block=256):
    rows, width = tokens.shape
    sizes = [(width, bf16), (width, bf16)]
    if own:
        sizes += [(width, bf16), (2 * width, f32), (width, bf16)]
    by_rows = lambda i: (i, 0)
    whole = lambda i: (0, 0)
    return pl.pallas_call(
        qkv_kernel,
        grid=(rows // block,),
        in_specs=[
            pl.BlockSpec((block, width), by_rows),
            pl.BlockSpec((1, width), whole),
            pl.BlockSpec((width, 3 * width), whole, pipeline_mode=pl.Buffered(1)),
            pl.BlockSpec((block, PAIR), by_rows),
            pl.BlockSpec((block, PAIR), by_rows),
            pl.BlockSpec((1, PAIR), whole),
            pl.BlockSpec((1, PAIR), whole),
        ],
        out_specs=[pl.BlockSpec((block, size), by_rows) for size, _ in sizes],
        out_shape=[jax.ShapeDtypeStruct((rows, size), kind) for size, kind in sizes],
        compiler_params=pltpu.CompilerParams(vmem_limit_bytes=VMEM_BYTES),
        cost_estimate=NO_COST,
    )(tokens, gain, weight, cosine, sine, qgain, kgain)


def merge_kernel(sources, parts, *refs):
    dq_refs = refs[:parts]
    dkv_refs = refs[parts : parts + sources]
    rawq_ref, rawk_ref, cos_ref, sin_ref, qgain_ref, kgain_ref, out_ref, gains_ref = refs[parts + sources :]
    width = dq_refs[0].shape[1]
    ones = half_ones(True)
    cosine, sine = cos_ref[...], sin_ref[...]

    @pl.when(pl.program_id(0) == 0)
    def _():
        gains_ref[...] = jnp.zeros_like(gains_ref)

    def read(part, at):
        found = [ref[:, at] for ref in dq_refs] if part == 0 else [ref[part - 1, :, at] for ref in dkv_refs]
        return sum(value.astype(f32) for value in found).astype(bf16)

    for part, (raw_ref, head_gain) in enumerate(((rawq_ref, qgain_ref[...]), (rawk_ref, kgain_ref[...]))):
        for tile in range(width // PAIR):
            at = slice(tile * PAIR, (tile + 1) * PAIR)
            grad = read(part, at).astype(f32)
            grad = grad * cosine - swap_halves(grad) * sine
            raw = raw_ref[:, at]
            unit = lax.rsqrt(head_sums(raw * raw, ones) * (1.0 / 64) + EPSILON)
            hat = raw * unit
            gains_ref[part : part + 1, at] += jnp.sum(grad * hat, axis=0, keepdims=True)
            weighted = grad * head_gain
            inner = head_sums(weighted * hat, ones) * (1.0 / 64)
            there = slice(part * width + tile * PAIR, part * width + (tile + 1) * PAIR)
            out_ref[:, there] = (unit * (weighted - hat * inner)).astype(bf16)
    out_ref[:, 2 * width :] = read(2, slice(0, width))


def merge_grads(chunk, dqs, dkvs, raw, cosine, sine, qgain, kgain, block=256):
    rows, width = dqs[0].shape
    by_rows = lambda i: (i, 0)
    whole = lambda i: (0, 0)
    return pl.pallas_call(
        functools.partial(merge_kernel, len(dkvs), len(dqs)),
        grid=(rows // block,),
        in_specs=[pl.BlockSpec((block, width), by_rows)] * len(dqs)
        + [pl.BlockSpec((2, block, width), lambda i: (0, i, 0))] * len(dkvs)
        + [
            pl.BlockSpec((block, width), lambda i: (i, chunk)),
            pl.BlockSpec((block, width), lambda i: (i, CHUNKS + chunk)),
            pl.BlockSpec((block, PAIR), by_rows),
            pl.BlockSpec((block, PAIR), by_rows),
            pl.BlockSpec((1, PAIR), whole),
            pl.BlockSpec((1, PAIR), whole),
        ],
        out_specs=[pl.BlockSpec((block, 3 * width), by_rows), pl.BlockSpec((8, width), whole)],
        out_shape=[
            jax.ShapeDtypeStruct((rows, 3 * width), bf16),
            jax.ShapeDtypeStruct((8, width), f32),
        ],
        compiler_params=pltpu.CompilerParams(vmem_limit_bytes=VMEM_BYTES),
        cost_estimate=NO_COST,
    )(*dqs, *dkvs, raw, raw, cosine, sine, qgain, kgain)


def forward_kernel(sources, query_rows, flags, q_ref, aq_ref, coef_ref, *refs):
    keyed = refs[: 3 * sources]
    out_ref, full_ref, query, total = refs[3 * sources :]
    rows = q_ref.shape[0]
    lane = lane_index()
    half = lane < 64
    mine = (half, jnp.logical_not(half))
    both = q_ref[...]
    extra = aq_ref[...]
    for h in range(2):
        query[h] = jnp.where(mine[h], both, extra * coef_ref[0, h : h + 1, :])
        total[h] = jnp.zeros_like(total[h])
    blocks = keyed[0].shape[0] // KEY_ROWS
    for j in range(sources):
        k_ref, v_ref, ak_ref = keyed[3 * j : 3 * j + 3]
        for b in range(blocks):

            @pl.when(flags[j * blocks + b] != 0)
            def _():
                at = slice(b * KEY_ROWS, (b + 1) * KEY_ROWS)
                keys, values, columns = k_ref[at, :], v_ref[at, :], ak_ref[at, :]
                ones = jnp.ones_like(values)
                keys2 = [jnp.where(mine[h], keys, columns) for h in range(2)]
                values2 = [jnp.where(mine[h], values, ones) for h in range(2)]
                for i in range(rows // query_rows):
                    part = slice(i * query_rows, (i + 1) * query_rows)
                    for h in range(2):
                        probs = jnp.exp(dot(query[h, part, :], keys2[h], NT)).astype(bf16)
                        total[h, part, :] += dot(probs, values2[h])

    outs = []
    for h in range(2):
        summed = total[h]
        outs.append(summed / pltpu.roll(summed, 64, 1))
        log_total = jnp.log(jnp.maximum(summed, 1e-30))
        high = log_total.astype(bf16)
        mid, low = split_two(log_total - high.astype(f32))
        base = lane - 64 if h == 0 else lane
        full_ref[:, h * PAIR : (h + 1) * PAIR] = jnp.where(
            base == 11, -high, jnp.where(base == 12, -mid, jnp.where(base == 13, -low, query[h]))
        )
    out_ref[...] = jnp.where(half, outs[0], outs[1]).astype(bf16)


def attend(flags, queries, query_columns, coefficients, keyed):
    rows, width = queries.shape
    pairs = width // PAIR
    key_rows = keyed[0][0].shape[0]
    sources = len(keyed)
    by_pair = lambda p, f: (0, p)
    whole = lambda p, f: (0, 0)
    in_specs = [
        pl.BlockSpec((rows, PAIR), by_pair),
        pl.BlockSpec((rows, PAIR), whole),
        pl.BlockSpec((1, 2, PAIR), lambda p, f: (p, 0, 0)),
    ]
    operands = [queries, query_columns, coefficients]
    for keys, values, columns in keyed:
        in_specs += [
            pl.BlockSpec((key_rows, PAIR), by_pair),
            pl.BlockSpec((key_rows, PAIR), by_pair),
            pl.BlockSpec((key_rows, PAIR), whole),
        ]
        operands += [keys, values, columns]
    return pl.pallas_call(
        functools.partial(forward_kernel, sources, min(512, rows)),
        grid_spec=pltpu.PrefetchScalarGridSpec(
            num_scalar_prefetch=1,
            grid=(pairs,),
            in_specs=in_specs,
            out_specs=[
                pl.BlockSpec((rows, PAIR), by_pair),
                pl.BlockSpec((rows, 2 * PAIR), by_pair),
            ],
            scratch_shapes=[
                pltpu.VMEM((2, rows, PAIR), bf16),
                pltpu.VMEM((2, rows, PAIR), f32),
            ],
        ),
        out_shape=[
            jax.ShapeDtypeStruct((rows, width), bf16),
            jax.ShapeDtypeStruct((rows, 2 * width), bf16),
        ],
        compiler_params=pltpu.CompilerParams(vmem_limit_bytes=VMEM_BYTES),
        cost_estimate=NO_COST,
    )(flags, *operands)


def backward_kernel(
    flags, full_ref, grad_ref, out_ref, aq_ref, k_ref, v_ref, ak_ref,
    dq_ref, dkv_ref, bias_ref, grads, dq_total,
):
    rows = grad_ref.shape[0]
    lane = lane_index()
    half = lane < 64
    mine = (half, jnp.logical_not(half))
    base = (lane - 64, lane)
    both = grad_ref[...]
    row_total = head_sums(both.astype(f32) * out_ref[...].astype(f32), half_ones(False))
    high, low = split_two(row_total)
    zero = jnp.zeros_like(high)
    for h in range(2):
        extra = jnp.where(base[h] == 0, -high, jnp.where(base[h] == 1, -low, zero))
        grads[h] = jnp.where(mine[h], both, extra)
        dq_total[h] = jnp.zeros_like(dq_total[h])
    for b in range(k_ref.shape[0] // KEY_ROWS):
        at = slice(b * KEY_ROWS, (b + 1) * KEY_ROWS)

        @pl.when(flags[b] != 0)
        def _():
            keys, values, columns = k_ref[at, :], v_ref[at, :], ak_ref[at, :]
            ones = jnp.ones_like(values)
            dks, dvs = [], []
            for h in range(2):
                keys2 = jnp.where(mine[h], keys, columns)
                pick = (base[h] >= 0) & (base[h] < 2)
                values2 = jnp.where(mine[h], values, jnp.where(pick, ones, jnp.zeros_like(ones)))
                full = full_ref[:, h * PAIR : (h + 1) * PAIR]
                probs = jnp.exp(dot(keys2, full, NT))
                score_low = (probs * dot(values2, grads[h], NT)).astype(bf16)
                dks.append(dot(score_low, full))
                dvs.append(dot(probs.astype(bf16), grads[h]))
                dq_total[h] += dot(keys2, score_low, TN)
            dkv_ref[0, at, :] = jnp.where(half, dks[0], dks[1]).astype(bf16)
            dkv_ref[1, at, :] = jnp.where(half, dvs[0], dvs[1]).astype(bf16)

        @pl.when(flags[b] == 0)
        def _():
            dkv_ref[:, at, :] = jnp.zeros((2, KEY_ROWS, PAIR), bf16)

    dq = [dq_total[h].T for h in range(2)]
    dq_ref[...] = jnp.where(half, dq[0], dq[1]) * 0.125
    variates = aq_ref[...].astype(f32)
    for h in range(2):
        pick = (base[h] >= 0) & (base[h] < 4)
        bias_ref[0, h : h + 1, :] = jnp.sum(
            jnp.where(pick, dq[h] * variates, 0.0), axis=0, keepdims=True
        )


def attend_back(chunk, flags, full, grad, out, query_columns, keys, values, key_columns):
    rows, width = grad.shape
    pairs = width // PAIR // CHUNKS
    width = width // CHUNKS
    key_rows = keys.shape[0]
    by_pair = lambda p, f: (0, p)
    from_pair = lambda p, f: (0, chunk * pairs + p)
    whole = lambda p, f: (0, 0)
    return pl.pallas_call(
        backward_kernel,
        grid_spec=pltpu.PrefetchScalarGridSpec(
            num_scalar_prefetch=1,
            grid=(pairs,),
            in_specs=[
                pl.BlockSpec((rows, 2 * PAIR), from_pair),
                pl.BlockSpec((rows, PAIR), from_pair),
                pl.BlockSpec((rows, PAIR), from_pair),
                pl.BlockSpec((rows, PAIR), whole),
                pl.BlockSpec((key_rows, PAIR), from_pair),
                pl.BlockSpec((key_rows, PAIR), from_pair),
                pl.BlockSpec((key_rows, PAIR), whole),
            ],
            out_specs=[
                pl.BlockSpec((rows, PAIR), by_pair),
                pl.BlockSpec((2, key_rows, PAIR), lambda p, f: (0, 0, p)),
                pl.BlockSpec((1, 2, PAIR), lambda p, f: (p, 0, 0)),
            ],
            scratch_shapes=[
                pltpu.VMEM((2, rows, PAIR), bf16),
                pltpu.VMEM((2, PAIR, rows), f32),
            ],
        ),
        out_shape=[
            jax.ShapeDtypeStruct((rows, width), f32),
            jax.ShapeDtypeStruct((2, key_rows, width), bf16),
            jax.ShapeDtypeStruct((pairs, 2, PAIR), f32),
        ],
        compiler_params=pltpu.CompilerParams(vmem_limit_bytes=VMEM_BYTES),
        cost_estimate=NO_COST,
    )(flags, full, grad, out, query_columns, keys, values, key_columns)


def slot_columns(segment, variates):
    column = jnp.arange(PAIR, dtype=jnp.int32)[None, :] % 64
    same_var = (column < 8) & (variates[:, None] == column % 4)
    in_seg = (column >= 8) & (column < 11)
    same_seg = segment[:, None] == column - 8
    three = (column >= 11) & (column < 14)
    query = jnp.where(in_seg & jnp.logical_not(same_seg), NEG_FILL, same_var.astype(f32))
    key = (same_var | (in_seg & same_seg) | three).astype(f32)
    return query.astype(bf16), key.astype(bf16)


def bias_columns(head_bias):
    delta = head_bias[:, 0] - head_bias[:, 1]
    high, low = split_two(delta)
    heads = delta.shape[0]
    row = jnp.concatenate(
        [
            jnp.broadcast_to(high[:, None], (heads, 4)),
            jnp.broadcast_to(low[:, None], (heads, 4)),
            jnp.ones((heads, 3), bf16),
            jnp.zeros((heads, 53), bf16),
        ],
        1,
    )
    return jnp.concatenate([row, row], 1).reshape(heads // 2, 2, PAIR)


def arrange_rows(places, spot, left_ref, turned, arranged):
    shard = left_ref.shape[1] // places
    turned[...] = left_ref[...].T
    for i in range(places):
        at = pl.multiple_of(spot[2 + i] * shard, shard)
        arranged[i * shard : (i + 1) * shard, :] = turned[pl.ds(at, shard), :]


def ffn_kernel(
    places, first, spot, nf_ref, seed_ref, start_ref, nfstart_ref, wg_ref, wu_ref, wd_ref,
    branch_ref, nfgrad_ref, down_far, down_cross, down_own, gate_far, gate_cross, gate_own,
    turned, arranged, branch,
):
    step = pl.program_id(0)
    rows, width = nf_ref.shape
    shard = width // places
    chunk = wg_ref.shape[1]

    @pl.when(step == 0)
    def _():
        arrange_rows(places, spot, nf_ref, turned, arranged)
        branch[...] = start_ref[...]
        nfgrad_ref[...] = jnp.zeros_like(nfgrad_ref) if first else nfstart_ref[...]

    wg, wu = wg_ref[...], wu_ref[...]
    wd = jnp.concatenate(
        [
            wd_ref[i * shard : (i + 1) * shard, k * width : (k + 1) * width]
            for i in range(2)
            for k in range(chunk // 2 // shard)
        ],
        axis=0,
    )
    hiddens, gates, ups = [], [], []
    part_rows = min(256, rows)
    for i in range(rows // part_rows):
        at = slice(i * part_rows, (i + 1) * part_rows)
        nf = nf_ref[at, :]
        g, u = dot(nf, wg), dot(nf, wu)
        hidden_grad = dot(seed_ref[at, :], wd, NT)
        sg = 1.0 / (1.0 + jnp.exp(-g))
        silu = g * sg
        hidden = (silu * u).astype(bf16)
        gate = (hidden_grad * u * sg * (1.0 + g * (1.0 - sg))).astype(bf16)
        up = (hidden_grad * silu).astype(bf16)
        branch[at, :] += dot(hidden, wd)
        nfgrad_ref[at, :] += dot(gate, wg, NT) + dot(up, wu, NT)
        hiddens.append(hidden)
        gates.append(gate)
        ups.append(up)
    hidden = jnp.concatenate(hiddens, axis=0)
    gate = jnp.concatenate(gates, axis=0)
    up = jnp.concatenate(ups, axis=0)
    down = dot(hidden, seed_ref[...], TN).astype(bf16)
    lower, upper = down[: chunk // 2, :], down[chunk // 2 :, :]
    on_upper = spot[0] == 1
    far = jnp.where(on_upper, lower, upper)
    near = jnp.where(on_upper, upper, lower)
    folds = [slice(k * shard, (k + 1) * shard) for k in range(chunk // 2 // shard)]
    for k, at in enumerate(folds):
        down_far[k] = far[at, :]

    @pl.when(step % 2 != spot[1])
    def _():
        for k, at in enumerate(folds):
            down_cross[k] = near[at, :]

    @pl.when(step % 2 == spot[1])
    def _():
        for k, at in enumerate(folds):
            down_own[k] = near[at, :]

    half = width // 2
    for part, grad in enumerate((gate, up)):
        gate_far[part, 0] = dot(arranged[:half, :], grad).astype(bf16)
        gate_cross[part, 0] = dot(arranged[half : half + half // 2, :], grad).astype(bf16)
        gate_own[part, 0] = dot(arranged[half + half // 2 :, :], grad).astype(bf16)

    @pl.when(step == pl.num_programs(0) - 1)
    def _():
        branch_ref[...] = branch[...].astype(branch_ref.dtype)


def feed_forward(spot, normed, seed, start, nfstart, weights):
    rows, width = normed.shape
    places = spot.shape[0] - 2
    groups = places // 4
    first = nfstart is None
    hidden = weights.shape[1] // 3
    chunk = 2 * hidden // places
    steps = places // 2
    whole = lambda t, o: (0, 0)
    once = pl.Buffered(1)
    shard = width // places
    folds = chunk // 2 // shard
    spans = hidden // width
    per_span = steps // spans
    by_cols = lambda t, o: (0, t // per_span, 0, t % per_span)
    return pl.pallas_call(
        functools.partial(ffn_kernel, places, first),
        grid_spec=pltpu.PrefetchScalarGridSpec(
            num_scalar_prefetch=1,
            grid=(steps,),
            in_specs=[
                pl.BlockSpec((rows, width), whole, pipeline_mode=once),
                pl.BlockSpec((rows, width), whole, pipeline_mode=once),
                pl.BlockSpec((rows, width), whole, pipeline_mode=once),
                pl.BlockSpec((8, 128) if first else (rows, width), whole, pipeline_mode=once),
                pl.BlockSpec((width, chunk), lambda t, o: (0, t)),
                pl.BlockSpec((width, chunk), lambda t, o: (0, steps + t)),
                pl.BlockSpec((2 * width // places, hidden), lambda t, o: (t, 2)),
            ],
            out_specs=[
                pl.BlockSpec((rows, width), whole),
                pl.BlockSpec((rows, width), whole),
                pl.BlockSpec(
                    (folds, shard, width),
                    lambda t, o: (0, jnp.where(t % 2 == o[1], groups, 0) + t // 2, 0),
                ),
                pl.BlockSpec((folds, shard, width), lambda t, o: (0, t // 2, 0)),
                pl.BlockSpec((folds, shard, width), lambda t, o: (0, t // 2, 0)),
                pl.BlockSpec((2, 1, width // 2, chunk), by_cols),
                pl.BlockSpec((2, 1, width // 4, chunk), by_cols),
                pl.BlockSpec((2, 1, width // 4, chunk), by_cols),
            ],
            scratch_shapes=[
                pltpu.VMEM((width, rows), bf16),
                pltpu.VMEM((width, rows), bf16),
                pltpu.VMEM((rows, width), f32),
            ],
        ),
        out_shape=[
            jax.ShapeDtypeStruct((rows, width), f32 if first else bf16),
            jax.ShapeDtypeStruct((rows, width), f32),
            jax.ShapeDtypeStruct((folds, width // 2, width), bf16),
            jax.ShapeDtypeStruct((folds, width // 4, width), bf16),
            jax.ShapeDtypeStruct((folds, width // 4, width), bf16),
            jax.ShapeDtypeStruct((2, spans, width // 2, width), bf16),
            jax.ShapeDtypeStruct((2, spans, width // 4, width), bf16),
            jax.ShapeDtypeStruct((2, spans, width // 4, width), bf16),
        ],
        compiler_params=pltpu.CompilerParams(vmem_limit_bytes=56 * 2**20),
        cost_estimate=NO_COST,
    )(spot, normed, seed, start, start if first else nfstart, weights, weights, weights)


def outer_kernel(places, spot, left_ref, right_ref, far_ref, cross_ref, own_ref, turned, arranged):
    width = left_ref.shape[1]

    @pl.when(pl.program_id(0) == 0)
    def _():
        arrange_rows(places, spot, left_ref, turned, arranged)

    right = right_ref[...]
    half = width // 2
    far_ref[0] = dot(arranged[:half, :], right).astype(bf16)
    cross_ref[0] = dot(arranged[half : half + half // 2, :], right).astype(bf16)
    own_ref[0] = dot(arranged[half + half // 2 :, :], right).astype(bf16)


def outer(spot, left, right, block):
    rows, width = left.shape
    columns = right.shape[1]
    places = spot.shape[0] - 2
    by_cols = lambda t, o: (0, t)
    one_block = lambda t, o: (t, 0, 0)
    return pl.pallas_call(
        functools.partial(outer_kernel, places),
        grid_spec=pltpu.PrefetchScalarGridSpec(
            num_scalar_prefetch=1,
            grid=(columns // block,),
            in_specs=[
                pl.BlockSpec((rows, width), lambda t, o: (0, 0)),
                pl.BlockSpec((rows, block), by_cols),
            ],
            out_specs=[
                pl.BlockSpec((1, width // 2, block), one_block),
                pl.BlockSpec((1, width // 4, block), one_block),
                pl.BlockSpec((1, width // 4, block), one_block),
            ],
            scratch_shapes=[pltpu.VMEM((width, rows), bf16), pltpu.VMEM((width, rows), bf16)],
        ),
        out_shape=[
            jax.ShapeDtypeStruct((columns // block, width // 2, block), bf16),
            jax.ShapeDtypeStruct((columns // block, width // 4, block), bf16),
            jax.ShapeDtypeStruct((columns // block, width // 4, block), bf16),
        ],
        compiler_params=pltpu.CompilerParams(vmem_limit_bytes=VMEM_BYTES),
        cost_estimate=NO_COST,
    )(spot, left, right)


def rms_forward(values, gain_vec):
    inv_rms = lax.rsqrt(jnp.mean(values * values, axis=-1, keepdims=True) + EPSILON)
    return (values * inv_rms * gain_vec, inv_rms)


def rms_backward(values, inv_rms, gain_vec, upstream):
    weighted = upstream * gain_vec
    inner_sum = jnp.mean(weighted * values, axis=-1, keepdims=True)
    value_grad = inv_rms * weighted - values * inv_rms * inv_rms * inv_rms * inner_sum
    return (value_grad, upstream * values * inv_rms)


def shift_by(values, count, step):
    return lax.ppermute(values, "seq", [(i, (i + step) % count) for i in range(count)])


def cross_core(values, places):
    return lax.ppermute(values, "dp", [(i, i ^ 1) for i in range(places)])


def cross_x(values, places):
    return lax.ppermute(values, "dp", [(i, i ^ 2) for i in range(places)])


def core_sum(pieces, places):
    crossed, terms = [], []
    for far, cross, own in pieces:
        quarter = own.shape[1]
        far = cross_core(far, places)
        crossed.append(cross + far[:, :quarter])
        terms.append([own, far[:, quarter:]])
    return jnp.concatenate(crossed, axis=0), terms


def add_received(terms, received):
    start, longer = 0, []
    for held in terms:
        count = held[0].shape[0]
        longer.append(held + [received[start : start + count]])
        start += count
    return longer


def total_of(terms):
    return jnp.concatenate([sum(term.astype(f32) for term in held) for held in terms], axis=0).astype(bf16)


def halve(terms, step, places):
    mine = lax.axis_index("dp") // 4 // 2**step % 2

    def cut(value, which):
        blocks, rows, columns = value.shape
        left = places // 4 // 2**step
        value = value.reshape(blocks, left // 2, 2, rows // left, columns)
        value = lax.dynamic_index_in_dim(value, which, 2, keepdims=False)
        return value.reshape(blocks, rows // 2, columns)

    sent = total_of([[cut(term, 1 - mine) for term in held] for held in terms])
    return sent, [[cut(term, mine) for term in held] for held in terms]


def cross_z(values, step, places):
    return lax.ppermute(values, "dp", [(i, i ^ (4 * 2**step)) for i in range(places)])


def sum_seq(values, count):
    if count == 2:
        return values.astype(f32) + shift_by(values, count, 1).astype(f32)
    return lax.psum(values.astype(f32), "seq")


def after(value, *before):
    return lax.optimization_barrier((value, before))[0]


def sum_small(values, places, seq_count):
    step = 1
    while step < places:
        values = values + lax.ppermute(values, "dp", [(i, i ^ step) for i in range(places)])
        step *= 2
    if seq_count == 2:
        return values + shift_by(values, 2, 1)
    return lax.psum(values, "seq")


def body(
    tokens, doc_lengths, variate_ids, time_ids, in_proj, out_proj, gate_up, down_proj,
    attn_gain, ffn_gain, query_gain, key_gain, head_bias, cotangent,
):
    seq_count = lax.axis_size("seq")
    seq_rank = lax.axis_index("seq")
    local_rows, width = tokens.shape
    pack_rows = local_rows * seq_count
    head_dim = query_gain.shape[0]
    places = lax.axis_size("dp")
    place = lax.axis_index("dp")
    core, across = place % 2, place // 2 % 2
    groups = places // 4
    spot = jnp.stack(
        [core, across]
        + [
            group * 4 + (across + 1 - near_x) % 2 * 2 + (core + 1 - near_core) % 2
            for near_core in range(2)
            for near_x in range(2)
            for group in range(groups)
        ]
    ).astype(jnp.int32)

    gains = jnp.stack([attn_gain, ffn_gain], axis=1)
    gather = lambda w: lax.all_gather(w, "dp", axis=0, tiled=True)
    in_chunks = in_proj.reshape(-1, 3, CHUNKS, width // CHUNKS).transpose(0, 2, 1, 3)
    in_chunks = in_chunks.reshape(in_proj.shape)
    first_shard = jnp.concatenate(
        [in_chunks, out_proj, jnp.pad(gains, ((0, 0), (0, PAIR - 2)))], axis=1
    )
    if places == 16 and seq_count == 2:
        wide, *there = gather_first(first_shard, tokens, time_ids.reshape(-1, PAIR), places)
        slots = [(tokens, time_ids), (there[0], there[1].reshape(-1))]
    else:
        wide = gather(first_shard)
        slots = [(tokens, time_ids)]
        for step in range(1, seq_count):
            slots.append(tuple(shift_by(array, seq_count, -step) for array in slots[0]))
    out_full = wide[:, 3 * width : 4 * width]
    attn_gain_f = wide[:, 4 * width].astype(f32)[None, :]
    ffn_gain_f = wide[:, 4 * width + 1].astype(f32)[None, :]
    shard = in_proj.shape[0]
    hidden_part = down_proj.shape[0] // 2
    columns = gate_up.reshape(shard, 2, places, 2, hidden_part)
    folds = down_proj.reshape(2, hidden_part // shard, shard, width)
    ffn_weights = []
    for part in range(2):
        piece = jnp.concatenate(
            [columns[:, 0, :, part].reshape(shard, -1), columns[:, 1, :, part].reshape(shard, -1)]
            + [folds[part, k] for k in range(hidden_part // shard)],
            axis=1,
        )
        ffn_weights.append(piece)
    ffn_weights[0] = gather(after(ffn_weights[0], wide))

    positions = jnp.arange(pack_rows, dtype=jnp.int32)
    first_end = doc_lengths[0, 0]
    second_end = first_end + doc_lengths[0, 1]
    segment = (positions >= first_end).astype(jnp.int32) + (positions >= second_end).astype(jnp.int32)
    query_columns, key_columns = slot_columns(segment, variate_ids[0])
    coefficients = bias_columns(head_bias)
    start = seq_rank * local_rows
    query_columns = lax.dynamic_slice_in_dim(query_columns, start, local_rows)
    local_segment = lax.dynamic_slice_in_dim(segment, start, local_rows)
    valid_rows = (local_segment < 2).astype(f32)
    source_columns, source_flags = [], []
    for step in range(seq_count):
        begin = ((seq_rank + step) % seq_count) * local_rows
        source_columns.append(lax.dynamic_slice_in_dim(key_columns, begin, local_rows))
        there = lax.dynamic_slice_in_dim(segment, begin, local_rows).reshape(-1, KEY_ROWS)
        source_flags.append(
            ((there[:, 0] <= local_segment[-1]) & (there[:, -1] >= local_segment[0])).astype(jnp.int32)
        )

    half_dim = head_dim // 2
    frequency = jnp.exp(jnp.arange(half_dim, dtype=f32) * (-math.log(ROPE_BASE) / half_dim))
    qgain = jnp.tile(query_gain, 2)[None, :]
    kgain = jnp.tile(key_gain, 2)[None, :]

    def rope_tables(times):
        angles = times.astype(f32)[:, None] * jnp.tile(frequency, 4)[None, :]
        sign = jnp.where(jnp.arange(PAIR) % head_dim < half_dim, -1.0, 1.0)
        return jnp.cos(angles), jnp.sin(angles) * sign[None, :]

    tables = [rope_tables(times) for _, times in slots]
    seed_grad = cotangent.astype(f32) * valid_rows[:, None]
    seed_low = seed_grad.astype(bf16)
    keyed = []
    for step, (there_tokens, _) in enumerate(slots):
        keys, values, *own = project(
            there_tokens, attn_gain_f, wide, *tables[step], qgain, kgain, step == 0
        )
        keyed.append((keys, values, source_columns[step]))
        if step == 0:
            cosine, sine = tables[0]
            queries, raw, normed_low = own
            ffn_weights[1] = gather(after(ffn_weights[1], queries))
    attended, full_query = attend(
        jnp.concatenate(source_flags), queries, query_columns, coefficients, keyed
    )

    inputs_f = tokens.astype(f32)
    residual = inputs_f + dot(attended, out_full)
    normed_ffn, ffn_scale = rms_forward(residual, ffn_gain_f)
    normed_ffn_low = normed_ffn.astype(bf16)
    def ffn_pieces(arrays):
        gates = [array.reshape(-1, *array.shape[2:]) for array in arrays[3:]]
        return [gates, arrays[:3]]

    branch, normed_ffn_grad, *pieces = feed_forward(
        spot, normed_ffn_low, seed_low, residual, None, ffn_weights[0]
    )
    crossed, first_terms = core_sum(ffn_pieces(pieces), places)
    layer_out, normed_ffn_grad, *pieces = feed_forward(
        spot, after(normed_ffn_low, crossed), seed_low, branch, normed_ffn_grad, ffn_weights[1]
    )
    across = cross_x(crossed, places)
    normed_ffn_grad = after(normed_ffn_grad, across)
    first_terms = add_received(first_terms, across)
    resid_norm_grad, ffn_gain_terms = rms_backward(residual, ffn_scale, ffn_gain_f, normed_ffn_grad)
    residual_grad = seed_grad + resid_norm_grad
    mixed_low = residual_grad.astype(bf16)
    attended_grad = dot(mixed_low, out_full, NT).astype(bf16)

    attended_grad = dot(mixed_low, out_full, NT).astype(bf16)
    crossed, second_terms = core_sum(
        ffn_pieces(pieces) + [outer(spot, attended, mixed_low, width)], places
    )
    steps = (places // 4).bit_length() - 1
    sent, first_terms = halve(first_terms, 0, places)
    attended_grad = after(attended_grad, crossed, sent)

    remote = list(range(1, seq_count))
    dqs = [[] for _ in range(CHUNKS)]
    dkvs = [[] for _ in range(CHUNKS)]
    biases = [0.0] * CHUNKS

    def back(chunk, sources, grad):
        for step in sources:
            dq, dkv, bias = attend_back(
                chunk, source_flags[step], full_query, grad, attended, query_columns, *keyed[step]
            )
            grad = after(grad, dkv)
            dqs[chunk].append(dq)
            dkvs[chunk].append(shift_by(dkv, seq_count, step) if step else dkv)
            biases[chunk] = biases[chunk] + bias
        return grad

    def merge(chunk):
        return merge_grads(chunk, dqs[chunk], dkvs[chunk], raw, cosine, sine, qgain, kgain)

    def chunk_weights(chunk):
        return wide[:, chunk * 3 * width // CHUNKS : (chunk + 1) * 3 * width // CHUNKS]

    def finish_line(terms, sent, first):
        for step in range(first, steps):
            terms = add_received(terms, cross_z(sent, step, places))
            if step + 1 < steps:
                sent, terms = halve(terms, step + 1, places)
        return total_of(terms)

    second_across = cross_x(crossed, places)
    first_received = cross_z(sent, 0, places)
    grad = back(0, remote, attended_grad)
    grad = back(1, remote, after(grad, first_received))
    first_terms = add_received(first_terms, first_received)
    sent, first_terms = halve(first_terms, 1, places)
    grad = after(grad, sent)
    first_received = cross_z(sent, 1, places)
    grad = back(0, [0], grad)

    second_across = after(second_across, grad)
    second_terms = add_received(second_terms, second_across)
    sent, second_terms = halve(second_terms, 0, places)
    second_received = cross_z(sent, 0, places)
    dqs[0][0] = after(dqs[0][0], grad, sent)
    merged_0, gains_0 = merge(0)
    crossed, in_terms_0 = core_sum([outer(spot, normed_low, merged_0, width // CHUNKS)], places)
    normed_grad_0 = dot(merged_0, chunk_weights(0), NT)
    grad = after(grad, crossed, normed_grad_0)
    in_across_0 = cross_x(crossed, places)
    grad = back(1, [0], grad)
    dqs[1][0] = after(dqs[1][0], grad, in_across_0, second_received, first_received)

    merged_1, gains_1 = merge(1)
    crossed, in_terms_1 = core_sum([outer(spot, normed_low, merged_1, width // CHUNKS)], places)
    in_terms_1 = add_received(in_terms_1, cross_x(crossed, places))
    normed_grad = normed_grad_0 + dot(after(merged_1, crossed), chunk_weights(1), NT)
    first_terms = add_received(first_terms, first_received)
    first_total = finish_line(*halve(first_terms, 2, places)[::-1], 2) if steps > 2 else total_of(first_terms)
    second_terms = add_received(second_terms, second_received)
    sent, second_terms = halve(second_terms, 1, places)
    second_total = finish_line(second_terms, sent, 1)
    sent, in_terms_0 = halve(add_received(in_terms_0, in_across_0), 0, places)
    in_total_0 = finish_line(in_terms_0, sent, 0)
    sent, in_terms_1 = halve(in_terms_1, 0, places)
    in_total_1 = finish_line(in_terms_1, sent, 0)
    first_sum = sum_seq(first_total, seq_count)
    second_sum = sum_seq(second_total, seq_count)
    in_sum = jnp.concatenate(
        [sum_seq(in_total_0, seq_count), sum_seq(in_total_1, seq_count)], axis=2
    )
    norm_scale = lax.rsqrt(jnp.mean(inputs_f * inputs_f, axis=-1, keepdims=True) + EPSILON)
    input_norm_grad, attn_gain_terms = rms_backward(inputs_f, norm_scale, attn_gain_f, normed_grad)
    input_grad = residual_grad + input_norm_grad

    same_bias = jnp.concatenate([jnp.sum(bias, axis=-1).reshape(-1) for bias in biases])
    heads = same_bias.shape[0]
    head_gains = sum(jnp.sum(part[:2].reshape(2, -1, head_dim), axis=1) for part in (gains_0, gains_1))
    small = sum_small(
        jnp.concatenate(
            [
                jnp.sum(attn_gain_terms, axis=0),
                jnp.sum(ffn_gain_terms, axis=0),
                head_gains[0],
                head_gains[1],
                same_bias,
            ]
        ),
        places,
        seq_count,
    )
    in_proj_grad = in_sum.transpose(1, 0, 2).reshape(in_proj.shape)
    spans = places * hidden_part // width
    gates = 2 * spans
    down_grad = jnp.concatenate(
        [part[gates : gates + hidden_part // shard].reshape(-1, width) for part in (first_sum, second_sum)]
    )
    gate_up_grad = jnp.stack(
        [
            part[:gates].reshape(2, spans, shard, -1, hidden_part).transpose(2, 0, 1, 3, 4)
            for part in (first_sum, second_sum)
        ],
        axis=4,
    ).reshape(gate_up.shape)
    gain_rows = attn_gain.shape[0]
    here = place * gain_rows
    tail = small[2 * width :]
    same_bias = tail[2 * head_dim : 2 * head_dim + heads]
    return (
        layer_out,
        input_grad,
        in_proj_grad,
        second_sum[-1],
        gate_up_grad,
        down_grad,
        lax.dynamic_slice_in_dim(small, here, gain_rows),
        lax.dynamic_slice_in_dim(small, width + here, gain_rows),
        tail[:head_dim],
        tail[head_dim : 2 * head_dim],
        jnp.stack([same_bias, -same_bias], axis=1),
    )


def solution(mesh):
    in_specs = (
        P(("dp", "seq"), None),
        P("dp", None),
        P("dp", None),
        P(("dp", "seq")),
        P("dp", None),
        P("dp", None),
        P("dp", None),
        P("dp", None),
        P("dp"),
        P("dp"),
        P(),
        P(),
        P(),
        P(("dp", "seq"), None),
    )
    out_specs = (
        P(("dp", "seq"), None),
        P(("dp", "seq"), None),
        P("dp", None),
        P("dp", None),
        P("dp", None),
        P("dp", None),
        P("dp"),
        P("dp"),
        P(),
        P(),
        P(),
    )
    return jax.shard_map(body, mesh=mesh, in_specs=in_specs, out_specs=out_specs, check_vma=False)
```

```python
import functools
import math

import jax
import jax.numpy as jnp
from jax import lax
from jax.experimental import pallas as pl
from jax.experimental.pallas import tpu as pltpu
from jax.sharding import PartitionSpec as P

EPSILON = 1e-06
ROPE_BASE = 10000.0
NEG_FILL = -1e30
PAIR = 128
CHUNKS = 2
KEY_ROWS = 256
VMEM_BYTES = 48 * 2**20
NO_COST = pl.CostEstimate(flops=1, bytes_accessed=1, transcendentals=0)
bf16 = jnp.bfloat16
f32 = jnp.float32
NN = (((1,), (0,)), ((), ()))
NT = (((1,), (1,)), ((), ()))
TN = (((0,), (0,)), ((), ()))


def dot(left, right, dims=NN):
    return lax.dot_general(left, right, dims, preferred_element_type=f32)


def split_two(values):
    high = values.astype(bf16)
    return high, (values - high.astype(f32)).astype(bf16)


def lane_index():
    return lax.broadcasted_iota(jnp.int32, (1, PAIR), 1)


def half_ones(same):
    rows = lax.broadcasted_iota(jnp.int32, (2 * PAIR, PAIR), 0) % PAIR
    cols = lax.broadcasted_iota(jnp.int32, (2 * PAIR, PAIR), 1)
    match = (rows < 64) == (cols < 64)
    return jnp.where(match if same else jnp.logical_not(match), 1.0, 0.0).astype(bf16)


def head_sums(values, ones):
    return dot(jnp.concatenate(split_two(values), axis=1), ones)


def swap_halves(values):
    first = lane_index() % 64 < 32
    return jnp.where(first, pltpu.roll(values, PAIR - 32, 1), pltpu.roll(values, 32, 1))


def gather_kernel(shard_ref, tokens_ref, times_ref, wide_ref, there_tokens_ref, there_times_ref, arrived, sent, keep):
    place, rank = lax.axis_index("dp"), lax.axis_index("seq")
    z, x, core = place // 4, place // 2 % 2, place % 2
    rows = shard_ref.shape[0]
    lines = 4

    def device(z, x, core, seq):
        return {"dp": z * 4 + x * 2 + core, "seq": seq}

    up, down = device(z + 1, x, core, rank), device(z - 1, x, core, rank)
    over, twin = device(z, 1 - x, core, rank), device(z, x, 1 - core, rank)
    other = device(z, x, core, 1 - rank)
    barrier = pltpu.get_barrier_semaphore()

    def greet(target):
        pl.semaphore_signal(barrier, inc=1, device_id=target, device_id_type=pl.DeviceIdType.MESH)

    for target in (over, twin, other):
        greet(target)
    pl.when(z < lines - 1)(lambda: greet(up))
    pl.when(z > 0)(lambda: greet(down))
    ends = (z == 0).astype(jnp.int32) + (z == lines - 1).astype(jnp.int32)
    pl.semaphore_wait(barrier, 5 - ends)

    def block(z, x, core):
        return z * 4 + x * 2 + core

    def rows_of(which):
        return wide_ref.at[pl.ds(pl.multiple_of(which * rows, rows), rows)]

    def copy(which, path, target, own=False):
        return pltpu.make_async_remote_copy(
            src_ref=shard_ref if own else rows_of(which),
            dst_ref=rows_of(which),
            send_sem=sent.at[path, which],
            recv_sem=arrived.at[which],
            device_id=target,
            device_id_type=pl.DeviceIdType.MESH,
        )

    def swap(source, target, index):
        return pltpu.make_async_remote_copy(
            src_ref=source,
            dst_ref=target,
            send_sem=keep.at[index],
            recv_sem=keep.at[index + 1],
            device_id=other,
            device_id_type=pl.DeviceIdType.MESH,
        )

    me = block(z, x, core)
    pl.when(z < lines - 1)(lambda: copy(me, 0, up, True).start())
    pl.when(z > 0)(lambda: copy(me, 3, down, True).start())
    copy(me, 1, over, True).start()
    copy(me, 2, twin, True).start()
    swaps = [swap(tokens_ref, there_tokens_ref, 0), swap(times_ref, there_times_ref, 2)]
    for each in swaps:
        each.start()
    here = pltpu.make_async_copy(shard_ref, rows_of(me), keep.at[4])
    here.start()

    def pass_over(which):
        copy(which, 2, twin).start()

    for step in range(1, lines):

        @pl.when(z >= step)
        def _():
            which = block(z - step, x, core)
            copy(which, 0, up).wait_recv()
            pl.when(z < lines - 1)(lambda: copy(which, 0, up).start())
            copy(which, 1, over).start()
            pass_over(which)

        @pl.when(z + step < lines)
        def _():
            which = block(z + step, x, core)
            copy(which, 3, down).wait_recv()
            pl.when(z > 0)(lambda: copy(which, 3, down).start())
            copy(which, 1, over).start()
            pass_over(which)

    for line in range(lines):
        which = block(line, 1 - x, core)
        copy(which, 1, over).wait_recv()
        pass_over(which)
    for line in range(lines):
        for side in range(2):
            copy(block(line, side, 1 - core), 2, twin).wait_recv()
    for line in range(lines):
        which = block(line, x, core)
        copy(which, 1, over).wait_send()
        copy(which, 2, twin).wait_send()
        copy(block(line, 1 - x, core), 2, twin).wait_send()
        pl.when((line <= z) & (z < lines - 1))(lambda: copy(which, 0, up).wait_send())
        pl.when((line >= z) & (z > 0))(lambda: copy(which, 3, down).wait_send())
    for each in swaps:
        each.wait()
    here.wait()


def gather_first(shard, tokens, times, places):
    anywhere = pl.BlockSpec(memory_space=pl.ANY)
    return pl.pallas_call(
        gather_kernel,
        in_specs=[anywhere] * 3,
        out_specs=[anywhere] * 3,
        out_shape=[
            jax.ShapeDtypeStruct((shard.shape[0] * places, shard.shape[1]), shard.dtype),
            jax.ShapeDtypeStruct(tokens.shape, tokens.dtype),
            jax.ShapeDtypeStruct(times.shape, times.dtype),
        ],
        scratch_shapes=[
            pltpu.SemaphoreType.DMA((places,)),
            pltpu.SemaphoreType.DMA((4, places)),
            pltpu.SemaphoreType.DMA((5,)),
        ],
        compiler_params=pltpu.CompilerParams(collective_id=0, has_side_effects=True),
        cost_estimate=NO_COST,
    )(shard, tokens, times)


def column_of(part, column, width):
    size = width // CHUNKS
    return (column // size * 3 + part) * size + column % size


def qkv_kernel(
    tokens_ref, gain_ref, weight_ref, cos_ref, sin_ref, qgain_ref, kgain_ref,
    k_ref, v_ref, *own_refs,
):
    width = tokens_ref.shape[1]
    values = tokens_ref[...].astype(f32)
    inv = lax.rsqrt(jnp.mean(values * values, axis=-1, keepdims=True) + EPSILON)
    normed = (values * inv * gain_ref[...]).astype(bf16)
    ones = half_ones(True)
    cosine, sine = cos_ref[...], sin_ref[...]
    turned = [(1, k_ref, kgain_ref[...], 1.0)]
    if own_refs:
        q_ref, raw_ref, normed_ref = own_refs
        normed_ref[...] = normed
        turned.append((0, q_ref, qgain_ref[...], 0.125))
    for part, out_ref, head_gain, scale in turned:
        for chunk in range(width // 256):
            start = column_of(part, chunk * 256, width)
            raw = dot(normed, weight_ref[:, start : start + 256])
            if own_refs:
                raw_ref[:, part * width + chunk * 256 : part * width + (chunk + 1) * 256] = raw
            for tile in range(2):
                u = raw[:, tile * PAIR : (tile + 1) * PAIR]
                unit = lax.rsqrt(head_sums(u * u, ones) * (1.0 / 64) + EPSILON)
                u = u * unit * head_gain
                u = u * cosine + swap_halves(u) * sine
                at = chunk * 256 + tile * PAIR
                out_ref[:, at : at + PAIR] = (u * scale).astype(bf16)
    for chunk in range(width // 256):
        start = column_of(2, chunk * 256, width)
        v_ref[:, chunk * 256 : (chunk + 1) * 256] = dot(
            normed, weight_ref[:, start : start + 256]
        ).astype(bf16)


def project(tokens, gain, weight, cosine, sine, qgain, kgain, own, block=256):
    rows, width = tokens.shape
    sizes = [(width, bf16), (width, bf16)]
    if own:
        sizes += [(width, bf16), (2 * width, f32), (width, bf16)]
    by_rows = lambda i: (i, 0)
    whole = lambda i: (0, 0)
    return pl.pallas_call(
        qkv_kernel,
        grid=(rows // block,),
        in_specs=[
            pl.BlockSpec((block, width), by_rows),
            pl.BlockSpec((1, width), whole),
            pl.BlockSpec((width, 3 * width), whole, pipeline_mode=pl.Buffered(1)),
            pl.BlockSpec((block, PAIR), by_rows),
            pl.BlockSpec((block, PAIR), by_rows),
            pl.BlockSpec((1, PAIR), whole),
            pl.BlockSpec((1, PAIR), whole),
        ],
        out_specs=[pl.BlockSpec((block, size), by_rows) for size, _ in sizes],
        out_shape=[jax.ShapeDtypeStruct((rows, size), kind) for size, kind in sizes],
        compiler_params=pltpu.CompilerParams(vmem_limit_bytes=VMEM_BYTES),
        cost_estimate=NO_COST,
    )(tokens, gain, weight, cosine, sine, qgain, kgain)


def merge_kernel(sources, parts, *refs):
    dq_refs = refs[:parts]
    dkv_refs = refs[parts : parts + sources]
    rawq_ref, rawk_ref, cos_ref, sin_ref, qgain_ref, kgain_ref, out_ref, gains_ref = refs[parts + sources :]
    width = dq_refs[0].shape[1]
    ones = half_ones(True)
    cosine, sine = cos_ref[...], sin_ref[...]

    @pl.when(pl.program_id(0) == 0)
    def _():
        gains_ref[...] = jnp.zeros_like(gains_ref)

    def read(part, at):
        found = [ref[:, at] for ref in dq_refs] if part == 0 else [ref[part - 1, :, at] for ref in dkv_refs]
        return sum(value.astype(f32) for value in found).astype(bf16)

    for part, (raw_ref, head_gain) in enumerate(((rawq_ref, qgain_ref[...]), (rawk_ref, kgain_ref[...]))):
        for tile in range(width // PAIR):
            at = slice(tile * PAIR, (tile + 1) * PAIR)
            grad = read(part, at).astype(f32)
            grad = grad * cosine - swap_halves(grad) * sine
            raw = raw_ref[:, at]
            unit = lax.rsqrt(head_sums(raw * raw, ones) * (1.0 / 64) + EPSILON)
            hat = raw * unit
            gains_ref[part : part + 1, at] += jnp.sum(grad * hat, axis=0, keepdims=True)
            weighted = grad * head_gain
            inner = head_sums(weighted * hat, ones) * (1.0 / 64)
            there = slice(part * width + tile * PAIR, part * width + (tile + 1) * PAIR)
            out_ref[:, there] = (unit * (weighted - hat * inner)).astype(bf16)
    out_ref[:, 2 * width :] = read(2, slice(0, width))


def merge_grads(chunk, dqs, dkvs, raw, cosine, sine, qgain, kgain, block=256):
    rows, width = dqs[0].shape
    by_rows = lambda i: (i, 0)
    whole = lambda i: (0, 0)
    return pl.pallas_call(
        functools.partial(merge_kernel, len(dkvs), len(dqs)),
        grid=(rows // block,),
        in_specs=[pl.BlockSpec((block, width), by_rows)] * len(dqs)
        + [pl.BlockSpec((2, block, width), lambda i: (0, i, 0))] * len(dkvs)
        + [
            pl.BlockSpec((block, width), lambda i: (i, chunk)),
            pl.BlockSpec((block, width), lambda i: (i, CHUNKS + chunk)),
            pl.BlockSpec((block, PAIR), by_rows),
            pl.BlockSpec((block, PAIR), by_rows),
            pl.BlockSpec((1, PAIR), whole),
            pl.BlockSpec((1, PAIR), whole),
        ],
        out_specs=[pl.BlockSpec((block, 3 * width), by_rows), pl.BlockSpec((8, width), whole)],
        out_shape=[
            jax.ShapeDtypeStruct((rows, 3 * width), bf16),
            jax.ShapeDtypeStruct((8, width), f32),
        ],
        compiler_params=pltpu.CompilerParams(vmem_limit_bytes=VMEM_BYTES),
        cost_estimate=NO_COST,
    )(*dqs, *dkvs, raw, raw, cosine, sine, qgain, kgain)


def forward_kernel(sources, query_rows, flags, q_ref, aq_ref, coef_ref, *refs):
    keyed = refs[: 3 * sources]
    out_ref, full_ref, query, total = refs[3 * sources :]
    rows = q_ref.shape[0]
    lane = lane_index()
    half = lane < 64
    mine = (half, jnp.logical_not(half))
    both = q_ref[...]
    extra = aq_ref[...]
    for h in range(2):
        query[h] = jnp.where(mine[h], both, extra * coef_ref[0, h : h + 1, :])
        total[h] = jnp.zeros_like(total[h])
    blocks = keyed[0].shape[0] // KEY_ROWS
    for j in range(sources):
        k_ref, v_ref, ak_ref = keyed[3 * j : 3 * j + 3]
        for b in range(blocks):

            @pl.when(flags[j * blocks + b] != 0)
            def _():
                at = slice(b * KEY_ROWS, (b + 1) * KEY_ROWS)
                keys, values, columns = k_ref[at, :], v_ref[at, :], ak_ref[at, :]
                ones = jnp.ones_like(values)
                keys2 = [jnp.where(mine[h], keys, columns) for h in range(2)]
                values2 = [jnp.where(mine[h], values, ones) for h in range(2)]
                for i in range(rows // query_rows):
                    part = slice(i * query_rows, (i + 1) * query_rows)
                    for h in range(2):
                        probs = jnp.exp(dot(query[h, part, :], keys2[h], NT)).astype(bf16)
                        total[h, part, :] += dot(probs, values2[h])

    outs = []
    for h in range(2):
        summed = total[h]
        outs.append(summed / pltpu.roll(summed, 64, 1))
        log_total = jnp.log(jnp.maximum(summed, 1e-30))
        high = log_total.astype(bf16)
        mid, low = split_two(log_total - high.astype(f32))
        base = lane - 64 if h == 0 else lane
        full_ref[:, h * PAIR : (h + 1) * PAIR] = jnp.where(
            base == 11, -high, jnp.where(base == 12, -mid, jnp.where(base == 13, -low, query[h]))
        )
    out_ref[...] = jnp.where(half, outs[0], outs[1]).astype(bf16)


def attend(flags, queries, query_columns, coefficients, keyed):
    rows, width = queries.shape
    pairs = width // PAIR
    key_rows = keyed[0][0].shape[0]
    sources = len(keyed)
    by_pair = lambda p, f: (0, p)
    whole = lambda p, f: (0, 0)
    in_specs = [
        pl.BlockSpec((rows, PAIR), by_pair),
        pl.BlockSpec((rows, PAIR), whole),
        pl.BlockSpec((1, 2, PAIR), lambda p, f: (p, 0, 0)),
    ]
    operands = [queries, query_columns, coefficients]
    for keys, values, columns in keyed:
        in_specs += [
            pl.BlockSpec((key_rows, PAIR), by_pair),
            pl.BlockSpec((key_rows, PAIR), by_pair),
            pl.BlockSpec((key_rows, PAIR), whole),
        ]
        operands += [keys, values, columns]
    return pl.pallas_call(
        functools.partial(forward_kernel, sources, min(512, rows)),
        grid_spec=pltpu.PrefetchScalarGridSpec(
            num_scalar_prefetch=1,
            grid=(pairs,),
            in_specs=in_specs,
            out_specs=[
                pl.BlockSpec((rows, PAIR), by_pair),
                pl.BlockSpec((rows, 2 * PAIR), by_pair),
            ],
            scratch_shapes=[
                pltpu.VMEM((2, rows, PAIR), bf16),
                pltpu.VMEM((2, rows, PAIR), f32),
            ],
        ),
        out_shape=[
            jax.ShapeDtypeStruct((rows, width), bf16),
            jax.ShapeDtypeStruct((rows, 2 * width), bf16),
        ],
        compiler_params=pltpu.CompilerParams(vmem_limit_bytes=VMEM_BYTES),
        cost_estimate=NO_COST,
    )(flags, *operands)


def backward_kernel(
    flags, full_ref, grad_ref, out_ref, aq_ref, k_ref, v_ref, ak_ref,
    dq_ref, dkv_ref, bias_ref, grads, dq_total,
):
    rows = grad_ref.shape[0]
    lane = lane_index()
    half = lane < 64
    mine = (half, jnp.logical_not(half))
    base = (lane - 64, lane)
    both = grad_ref[...]
    row_total = head_sums(both.astype(f32) * out_ref[...].astype(f32), half_ones(False))
    high, low = split_two(row_total)
    zero = jnp.zeros_like(high)
    for h in range(2):
        extra = jnp.where(base[h] == 0, -high, jnp.where(base[h] == 1, -low, zero))
        grads[h] = jnp.where(mine[h], both, extra)
        dq_total[h] = jnp.zeros_like(dq_total[h])
    for b in range(k_ref.shape[0] // KEY_ROWS):
        at = slice(b * KEY_ROWS, (b + 1) * KEY_ROWS)

        @pl.when(flags[b] != 0)
        def _():
            keys, values, columns = k_ref[at, :], v_ref[at, :], ak_ref[at, :]
            ones = jnp.ones_like(values)
            dks, dvs = [], []
            for h in range(2):
                keys2 = jnp.where(mine[h], keys, columns)
                pick = (base[h] >= 0) & (base[h] < 2)
                values2 = jnp.where(mine[h], values, jnp.where(pick, ones, jnp.zeros_like(ones)))
                full = full_ref[:, h * PAIR : (h + 1) * PAIR]
                probs = jnp.exp(dot(keys2, full, NT))
                score_low = (probs * dot(values2, grads[h], NT)).astype(bf16)
                dks.append(dot(score_low, full))
                dvs.append(dot(probs.astype(bf16), grads[h]))
                dq_total[h] += dot(keys2, score_low, TN)
            dkv_ref[0, at, :] = jnp.where(half, dks[0], dks[1]).astype(bf16)
            dkv_ref[1, at, :] = jnp.where(half, dvs[0], dvs[1]).astype(bf16)

        @pl.when(flags[b] == 0)
        def _():
            dkv_ref[:, at, :] = jnp.zeros((2, KEY_ROWS, PAIR), bf16)

    dq = [dq_total[h].T for h in range(2)]
    dq_ref[...] = jnp.where(half, dq[0], dq[1]) * 0.125
    variates = aq_ref[...].astype(f32)
    for h in range(2):
        pick = (base[h] >= 0) & (base[h] < 4)
        bias_ref[0, h : h + 1, :] = jnp.sum(
            jnp.where(pick, dq[h] * variates, 0.0), axis=0, keepdims=True
        )


def attend_back(chunk, flags, full, grad, out, query_columns, keys, values, key_columns):
    rows, width = grad.shape
    pairs = width // PAIR // CHUNKS
    width = width // CHUNKS
    key_rows = keys.shape[0]
    by_pair = lambda p, f: (0, p)
    from_pair = lambda p, f: (0, chunk * pairs + p)
    whole = lambda p, f: (0, 0)
    return pl.pallas_call(
        backward_kernel,
        grid_spec=pltpu.PrefetchScalarGridSpec(
            num_scalar_prefetch=1,
            grid=(pairs,),
            in_specs=[
                pl.BlockSpec((rows, 2 * PAIR), from_pair),
                pl.BlockSpec((rows, PAIR), from_pair),
                pl.BlockSpec((rows, PAIR), from_pair),
                pl.BlockSpec((rows, PAIR), whole),
                pl.BlockSpec((key_rows, PAIR), from_pair),
                pl.BlockSpec((key_rows, PAIR), from_pair),
                pl.BlockSpec((key_rows, PAIR), whole),
            ],
            out_specs=[
                pl.BlockSpec((rows, PAIR), by_pair),
                pl.BlockSpec((2, key_rows, PAIR), lambda p, f: (0, 0, p)),
                pl.BlockSpec((1, 2, PAIR), lambda p, f: (p, 0, 0)),
            ],
            scratch_shapes=[
                pltpu.VMEM((2, rows, PAIR), bf16),
                pltpu.VMEM((2, PAIR, rows), f32),
            ],
        ),
        out_shape=[
            jax.ShapeDtypeStruct((rows, width), f32),
            jax.ShapeDtypeStruct((2, key_rows, width), bf16),
            jax.ShapeDtypeStruct((pairs, 2, PAIR), f32),
        ],
        compiler_params=pltpu.CompilerParams(vmem_limit_bytes=VMEM_BYTES),
        cost_estimate=NO_COST,
    )(flags, full, grad, out, query_columns, keys, values, key_columns)


def slot_columns(segment, variates):
    column = jnp.arange(PAIR, dtype=jnp.int32)[None, :] % 64
    same_var = (column < 8) & (variates[:, None] == column % 4)
    in_seg = (column >= 8) & (column < 11)
    same_seg = segment[:, None] == column - 8
    three = (column >= 11) & (column < 14)
    query = jnp.where(in_seg & jnp.logical_not(same_seg), NEG_FILL, same_var.astype(f32))
    key = (same_var | (in_seg & same_seg) | three).astype(f32)
    return query.astype(bf16), key.astype(bf16)


def bias_columns(head_bias):
    delta = head_bias[:, 0] - head_bias[:, 1]
    high, low = split_two(delta)
    heads = delta.shape[0]
    row = jnp.concatenate(
        [
            jnp.broadcast_to(high[:, None], (heads, 4)),
            jnp.broadcast_to(low[:, None], (heads, 4)),
            jnp.ones((heads, 3), bf16),
            jnp.zeros((heads, 53), bf16),
        ],
        1,
    )
    return jnp.concatenate([row, row], 1).reshape(heads // 2, 2, PAIR)


def arrange_rows(places, spot, left_ref, turned, arranged):
    shard = left_ref.shape[1] // places
    turned[...] = left_ref[...].T
    for i in range(places):
        at = pl.multiple_of(spot[2 + i] * shard, shard)
        arranged[i * shard : (i + 1) * shard, :] = turned[pl.ds(at, shard), :]


def ffn_kernel(
    places, first, nf_ref, seed_ref, start_ref, nfstart_ref, wg_ref, wu_ref, wd_ref, *refs
):
    if first:
        branch_ref, nfgrad_ref, far_ref, cross_ref, own_ref, *refs = refs
    else:
        across_ref, branch_ref, nfgrad_ref, far_ref, cross_ref, own_ref, got_ref, *refs = refs
    turned, branch, columns_out, rows_out, sems, arrived, *x_sems = refs
    step = pl.program_id(0)
    steps = pl.num_programs(0)
    rows, width = nf_ref.shape
    shard = width // places
    chunk = wg_ref.shape[1]
    folds = chunk // 2 // shard

    place = lax.axis_index("dp")
    groups = places // 4

    twin = {"dp": place + 1 - place % 2 * 2}
    over = {"dp": place + 2 - place // 2 % 2 * 4}
    mesh_id = pl.DeviceIdType.MESH

    def carry():
        return pltpu.make_async_remote_copy(
            src_ref=across_ref, dst_ref=got_ref, send_sem=x_sems[0].at[0], recv_sem=x_sems[0].at[1],
            device_id=over, device_id_type=mesh_id,
        )

    @pl.when(step == 0)
    def _():
        barrier = pltpu.get_barrier_semaphore()
        for target in (twin,) if first else (twin, over):
            pl.semaphore_signal(barrier, inc=1, device_id=target, device_id_type=mesh_id)
        pl.semaphore_wait(barrier, 1 if first else 2)
        if not first:
            carry().start()
        turned[...] = nf_ref[...].T
        branch[...] = start_ref[...]
        nfgrad_ref[...] = jnp.zeros_like(nfgrad_ref) if first else nfstart_ref[...]

    def spot_of(line, x, core):
        near_core = (core == place % 2).astype(jnp.int32)
        near_x = (x == place // 2 % 2).astype(jnp.int32)
        return (near_core * 2 + near_x) * groups + line

    def to_twin(source, target, send_sem, recv_sem):
        return pltpu.make_async_remote_copy(
            src_ref=source, dst_ref=target, send_sem=send_sem, recv_sem=recv_sem,
            device_id=twin, device_id_type=mesh_id,
        )

    def column_copies(at):
        slot = lax.rem(at, 2)
        start = pl.multiple_of(at * chunk, chunk)
        made, begin = [], 0
        for k, ref in enumerate((far_ref, cross_ref, own_ref)):
            count = ref.shape[0]
            source = columns_out.at[slot, pl.ds(begin, count)]
            target = ref.at[:, pl.ds(0, 2), :, pl.ds(start, chunk)]
            if k == 0:
                made.append(to_twin(source, target, sems.at[slot, k], arrived.at[at, 0]))
            else:
                made.append(pltpu.make_async_copy(source, target, sems.at[slot, k]))
            begin += count
        return made

    def row_copies(at, ref, index, k):
        slot = lax.rem(at, 2)
        source, target = rows_out.at[slot, k], ref.at[index, 2]
        if k == 0:
            return to_twin(source, target, sems.at[slot, 3], arrived.at[at, 1])
        return pltpu.make_async_copy(source, target, sems.at[slot, 4])

    def sent(copy):
        copy.wait_send() if copy.is_remote else copy.wait()

    def each_copy(at, act):
        for copy in column_copies(at):
            act(copy)
        line, x = at // 2, lax.rem(at, 2)
        near = x == place // 2 % 2
        act(row_copies(at, far_ref, near.astype(jnp.int32) * groups + line, 0))
        pl.when(near)(lambda: act(row_copies(at, own_ref, line, 1)))
        pl.when(jnp.logical_not(near))(lambda: act(row_copies(at, cross_ref, line, 1)))

    @pl.when(step >= 2)
    def _():
        each_copy(step - 2, sent)

    slot = lax.rem(step, 2)
    wg, wu = wg_ref[...], wu_ref[...]
    wd = jnp.concatenate(
        [
            wd_ref[i * shard : (i + 1) * shard, k * width : (k + 1) * width]
            for i in range(2)
            for k in range(folds)
        ],
        axis=0,
    )
    hiddens, gates, ups = [], [], []
    part_rows = min(256, rows)
    for i in range(rows // part_rows):
        at = slice(i * part_rows, (i + 1) * part_rows)
        nf = nf_ref[at, :]
        g, u = dot(nf, wg), dot(nf, wu)
        hidden_grad = dot(seed_ref[at, :], wd, NT)
        sg = 1.0 / (1.0 + jnp.exp(-g))
        silu = g * sg
        hidden = (silu * u).astype(bf16)
        gate = (hidden_grad * u * sg * (1.0 + g * (1.0 - sg))).astype(bf16)
        up = (hidden_grad * silu).astype(bf16)
        branch[at, :] += dot(hidden, wd)
        nfgrad_ref[at, :] += dot(gate, wg, NT) + dot(up, wu, NT)
        hiddens.append(hidden)
        gates.append(gate)
        ups.append(up)
    hidden = jnp.concatenate(hiddens, axis=0)
    down = dot(hidden, seed_ref[...], TN).astype(bf16)
    on_upper = place % 2 == 1
    lower, upper = down[: chunk // 2, :], down[chunk // 2 :, :]
    for i, part in enumerate((jnp.where(on_upper, lower, upper), jnp.where(on_upper, upper, lower))):
        for k in range(folds):
            rows_out[slot, i, :, k * width : (k + 1) * width] = part[k * shard : (k + 1) * shard, :]
    for part, grad in enumerate((gates, ups)):
        columns = dot(turned[...], jnp.concatenate(grad, axis=0)).astype(bf16)
        for j in range(places):
            spot = spot_of(j // 4, j // 2 % 2, j % 2)
            columns_out[slot, spot, part] = columns[j * shard : (j + 1) * shard, :]
    each_copy(step, lambda copy: copy.start())

    @pl.when(step == steps - 1)
    def _():
        branch_ref[...] = branch[...].astype(branch_ref.dtype)
        each_copy(step - 1, sent)
        each_copy(step, sent)
        for at in range(places // 2):
            column_copies(at)[0].wait_recv()
            near = (at % 2 == place // 2 % 2).astype(jnp.int32)
            row_copies(at, far_ref, near * groups + at // 2, 0).wait_recv()
        if not first:
            carry().wait()


def feed_forward(places, normed, seed, start, nfstart, weights, across=None):
    rows, width = normed.shape
    first = nfstart is None
    hidden = weights.shape[1] // 3
    chunk = 2 * hidden // places
    steps = places // 2
    shard = width // places
    whole = lambda t: (0, 0)
    once = pl.Buffered(1)
    return pl.pallas_call(
        functools.partial(ffn_kernel, places, first),
        grid=(steps,),
        in_specs=[
            pl.BlockSpec((rows, width), whole, pipeline_mode=once),
            pl.BlockSpec((rows, width), whole, pipeline_mode=once),
            pl.BlockSpec((rows, width), whole, pipeline_mode=once),
            pl.BlockSpec((8, 128) if first else (rows, width), whole, pipeline_mode=once),
            pl.BlockSpec((width, chunk), lambda t: (0, t)),
            pl.BlockSpec((width, chunk), lambda t: (0, steps + t)),
            pl.BlockSpec((2 * shard, hidden), lambda t: (t, 2)),
        ]
        + [pl.BlockSpec(memory_space=pl.ANY)] * (not first),
        out_specs=[
            pl.BlockSpec((rows, width), whole),
            pl.BlockSpec((rows, width), whole),
        ]
        + [pl.BlockSpec(memory_space=pl.ANY)] * (3 if first else 4),
        scratch_shapes=[
            pltpu.VMEM((width, rows), bf16),
            pltpu.VMEM((rows, width), f32),
            pltpu.VMEM((2, places, 2, shard, chunk), bf16),
            pltpu.VMEM((2, 2, shard, hidden), bf16),
            pltpu.SemaphoreType.DMA((2, 5)),
            pltpu.SemaphoreType.DMA((steps, 2)),
        ]
        + [pltpu.SemaphoreType.DMA((2,))] * (not first),
        out_shape=[
            jax.ShapeDtypeStruct((rows, width), f32 if first else bf16),
            jax.ShapeDtypeStruct((rows, width), f32),
        ]
        + [jax.ShapeDtypeStruct((places // part, 3, shard, hidden), bf16) for part in ((2, 4, 4) if first else (2, 4, 4, 4))],
        compiler_params=pltpu.CompilerParams(
            vmem_limit_bytes=56 * 2**20, collective_id=1 if first else 2, has_side_effects=True
        ),
        cost_estimate=NO_COST,
    )(
        normed, seed, start, start if first else nfstart, weights, weights, weights,
        *(() if first else (across,)),
    )


def outer_kernel(places, spot, left_ref, right_ref, far_ref, cross_ref, own_ref, turned, arranged):
    width = left_ref.shape[1]

    @pl.when(pl.program_id(0) == 0)
    def _():
        arrange_rows(places, spot, left_ref, turned, arranged)

    right = right_ref[...]
    half = width // 2
    far_ref[0] = dot(arranged[:half, :], right).astype(bf16)
    cross_ref[0] = dot(arranged[half : half + half // 2, :], right).astype(bf16)
    own_ref[0] = dot(arranged[half + half // 2 :, :], right).astype(bf16)


def outer(spot, left, right, block):
    rows, width = left.shape
    columns = right.shape[1]
    places = spot.shape[0] - 2
    by_cols = lambda t, o: (0, t)
    one_block = lambda t, o: (t, 0, 0)
    return pl.pallas_call(
        functools.partial(outer_kernel, places),
        grid_spec=pltpu.PrefetchScalarGridSpec(
            num_scalar_prefetch=1,
            grid=(columns // block,),
            in_specs=[
                pl.BlockSpec((rows, width), lambda t, o: (0, 0)),
                pl.BlockSpec((rows, block), by_cols),
            ],
            out_specs=[
                pl.BlockSpec((1, width // 2, block), one_block),
                pl.BlockSpec((1, width // 4, block), one_block),
                pl.BlockSpec((1, width // 4, block), one_block),
            ],
            scratch_shapes=[pltpu.VMEM((width, rows), bf16), pltpu.VMEM((width, rows), bf16)],
        ),
        out_shape=[
            jax.ShapeDtypeStruct((columns // block, width // 2, block), bf16),
            jax.ShapeDtypeStruct((columns // block, width // 4, block), bf16),
            jax.ShapeDtypeStruct((columns // block, width // 4, block), bf16),
        ],
        compiler_params=pltpu.CompilerParams(vmem_limit_bytes=VMEM_BYTES),
        cost_estimate=NO_COST,
    )(spot, left, right)


def rms_forward(values, gain_vec):
    inv_rms = lax.rsqrt(jnp.mean(values * values, axis=-1, keepdims=True) + EPSILON)
    return (values * inv_rms * gain_vec, inv_rms)


def rms_backward(values, inv_rms, gain_vec, upstream):
    weighted = upstream * gain_vec
    inner_sum = jnp.mean(weighted * values, axis=-1, keepdims=True)
    value_grad = inv_rms * weighted - values * inv_rms * inv_rms * inv_rms * inner_sum
    return (value_grad, upstream * values * inv_rms)


def shift_by(values, count, step):
    return lax.ppermute(values, "seq", [(i, (i + step) % count) for i in range(count)])


def cross_core(values, places):
    return lax.ppermute(values, "dp", [(i, i ^ 1) for i in range(places)])


def cross_x(values, places):
    return lax.ppermute(values, "dp", [(i, i ^ 2) for i in range(places)])


def core_sum(pieces, places):
    crossed, terms = [], []
    for far, cross, own in pieces:
        quarter = own.shape[1]
        far = cross_core(far, places)
        crossed.append(cross + far[:, :quarter])
        terms.append([own, far[:, quarter:]])
    return jnp.concatenate(crossed, axis=0), terms


def add_received(terms, received):
    start, longer = 0, []
    for held in terms:
        count = held[0].shape[0]
        longer.append(held + [received[start : start + count]])
        start += count
    return longer


def total_of(terms):
    return jnp.concatenate([sum(term.astype(f32) for term in held) for held in terms], axis=0).astype(bf16)


def halve(terms, step, places):
    mine = lax.axis_index("dp") // 4 // 2**step % 2

    def cut(value, which):
        blocks, rows, columns = value.shape
        left = places // 4 // 2**step
        value = value.reshape(blocks, left // 2, 2, rows // left, columns)
        value = lax.dynamic_index_in_dim(value, which, 2, keepdims=False)
        return value.reshape(blocks, rows // 2, columns)

    sent = total_of([[cut(term, 1 - mine) for term in held] for held in terms])
    return sent, [[cut(term, mine) for term in held] for held in terms]


def cross_z(values, step, places):
    return lax.ppermute(values, "dp", [(i, i ^ (4 * 2**step)) for i in range(places)])


def sum_seq(values, count):
    if count == 2:
        return values.astype(f32) + shift_by(values, count, 1).astype(f32)
    return lax.psum(values.astype(f32), "seq")


def after(value, *before):
    return lax.optimization_barrier((value, before))[0]


def sum_small(values, places, seq_count):
    step = 1
    while step < places:
        values = values + lax.ppermute(values, "dp", [(i, i ^ step) for i in range(places)])
        step *= 2
    if seq_count == 2:
        return values + shift_by(values, 2, 1)
    return lax.psum(values, "seq")


def body(
    tokens, doc_lengths, variate_ids, time_ids, in_proj, out_proj, gate_up, down_proj,
    attn_gain, ffn_gain, query_gain, key_gain, head_bias, cotangent,
):
    seq_count = lax.axis_size("seq")
    seq_rank = lax.axis_index("seq")
    local_rows, width = tokens.shape
    pack_rows = local_rows * seq_count
    head_dim = query_gain.shape[0]
    places = lax.axis_size("dp")
    place = lax.axis_index("dp")
    core, across = place % 2, place // 2 % 2
    groups = places // 4
    spot = jnp.stack(
        [core, across]
        + [
            group * 4 + (across + 1 - near_x) % 2 * 2 + (core + 1 - near_core) % 2
            for near_core in range(2)
            for near_x in range(2)
            for group in range(groups)
        ]
    ).astype(jnp.int32)

    gains = jnp.stack([attn_gain, ffn_gain], axis=1)
    gather = lambda w: lax.all_gather(w, "dp", axis=0, tiled=True)
    in_chunks = in_proj.reshape(-1, 3, CHUNKS, width // CHUNKS).transpose(0, 2, 1, 3)
    in_chunks = in_chunks.reshape(in_proj.shape)
    first_shard = jnp.concatenate(
        [in_chunks, out_proj, jnp.pad(gains, ((0, 0), (0, PAIR - 2)))], axis=1
    )
    if places == 16 and seq_count == 2:
        wide, *there = gather_first(first_shard, tokens, time_ids.reshape(-1, PAIR), places)
        slots = [(tokens, time_ids), (there[0], there[1].reshape(-1))]
    else:
        wide = gather(first_shard)
        slots = [(tokens, time_ids)]
        for step in range(1, seq_count):
            slots.append(tuple(shift_by(array, seq_count, -step) for array in slots[0]))
    out_full = wide[:, 3 * width : 4 * width]
    attn_gain_f = wide[:, 4 * width].astype(f32)[None, :]
    ffn_gain_f = wide[:, 4 * width + 1].astype(f32)[None, :]
    shard = in_proj.shape[0]
    hidden_part = down_proj.shape[0] // 2
    columns = gate_up.reshape(shard, 2, places, 2, hidden_part)
    folds = down_proj.reshape(2, hidden_part // shard, shard, width)
    ffn_weights = []
    for part in range(2):
        piece = jnp.concatenate(
            [columns[:, 0, :, part].reshape(shard, -1), columns[:, 1, :, part].reshape(shard, -1)]
            + [folds[part, k] for k in range(hidden_part // shard)],
            axis=1,
        )
        ffn_weights.append(piece)
    ffn_weights[0] = gather(after(ffn_weights[0], wide))

    positions = jnp.arange(pack_rows, dtype=jnp.int32)
    first_end = doc_lengths[0, 0]
    second_end = first_end + doc_lengths[0, 1]
    segment = (positions >= first_end).astype(jnp.int32) + (positions >= second_end).astype(jnp.int32)
    query_columns, key_columns = slot_columns(segment, variate_ids[0])
    coefficients = bias_columns(head_bias)
    start = seq_rank * local_rows
    query_columns = lax.dynamic_slice_in_dim(query_columns, start, local_rows)
    local_segment = lax.dynamic_slice_in_dim(segment, start, local_rows)
    valid_rows = (local_segment < 2).astype(f32)
    source_columns, source_flags = [], []
    for step in range(seq_count):
        begin = ((seq_rank + step) % seq_count) * local_rows
        source_columns.append(lax.dynamic_slice_in_dim(key_columns, begin, local_rows))
        there = lax.dynamic_slice_in_dim(segment, begin, local_rows).reshape(-1, KEY_ROWS)
        source_flags.append(
            ((there[:, 0] <= local_segment[-1]) & (there[:, -1] >= local_segment[0])).astype(jnp.int32)
        )

    half_dim = head_dim // 2
    frequency = jnp.exp(jnp.arange(half_dim, dtype=f32) * (-math.log(ROPE_BASE) / half_dim))
    qgain = jnp.tile(query_gain, 2)[None, :]
    kgain = jnp.tile(key_gain, 2)[None, :]

    def rope_tables(times):
        angles = times.astype(f32)[:, None] * jnp.tile(frequency, 4)[None, :]
        sign = jnp.where(jnp.arange(PAIR) % head_dim < half_dim, -1.0, 1.0)
        return jnp.cos(angles), jnp.sin(angles) * sign[None, :]

    tables = [rope_tables(times) for _, times in slots]
    seed_grad = cotangent.astype(f32) * valid_rows[:, None]
    seed_low = seed_grad.astype(bf16)
    keyed = []
    for step, (there_tokens, _) in enumerate(slots):
        keys, values, *own = project(
            there_tokens, attn_gain_f, wide, *tables[step], qgain, kgain, step == 0
        )
        keyed.append((keys, values, source_columns[step]))
        if step == 0:
            cosine, sine = tables[0]
            queries, raw, normed_low = own
            ffn_weights[1] = gather(after(ffn_weights[1], queries))
    attended, full_query = attend(
        jnp.concatenate(source_flags), queries, query_columns, coefficients, keyed
    )

    inputs_f = tokens.astype(f32)
    residual = inputs_f + dot(attended, out_full)
    normed_ffn, ffn_scale = rms_forward(residual, ffn_gain_f)
    normed_ffn_low = normed_ffn.astype(bf16)
    def x_part(received, own, far):
        total = received.astype(f32) + own.astype(f32) + far[groups:].astype(f32)
        return total.astype(bf16)

    def scatter_line(parts):
        lines = [[line * 4 + k for line in range(groups)] for k in range(4)]
        return lax.psum_scatter(parts, "dp", scatter_dimension=0, axis_index_groups=lines, tiled=True)[0]

    branch, normed_ffn_grad, *grads = feed_forward(
        places, normed_ffn_low, seed_low, residual, None, ffn_weights[0]
    )
    far, cross, own = grads
    layer_out, normed_ffn_grad, *grads, received = feed_forward(
        places, normed_ffn_low, seed_low, branch, normed_ffn_grad, ffn_weights[1], cross + far[:groups]
    )
    first_total = scatter_line(x_part(received, own, far))
    far, cross, own = grads
    second_crossed = cross + far[:groups]
    resid_norm_grad, ffn_gain_terms = rms_backward(residual, ffn_scale, ffn_gain_f, normed_ffn_grad)
    residual_grad = seed_grad + resid_norm_grad
    mixed_low = residual_grad.astype(bf16)
    attended_grad = dot(mixed_low, out_full, NT).astype(bf16)

    attended_grad = dot(mixed_low, out_full, NT).astype(bf16)
    out_crossed, out_terms = core_sum([outer(spot, attended, mixed_low, width)], places)
    steps = (places // 4).bit_length() - 1
    attended_grad = after(attended_grad, out_crossed, second_crossed)
    second_across = cross_x(second_crossed, places)
    out_across = cross_x(out_crossed, places)

    remote = list(range(1, seq_count))
    dqs = [[] for _ in range(CHUNKS)]
    dkvs = [[] for _ in range(CHUNKS)]
    biases = [0.0] * CHUNKS

    def back(chunk, sources, grad):
        for step in sources:
            dq, dkv, bias = attend_back(
                chunk, source_flags[step], full_query, grad, attended, query_columns, *keyed[step]
            )
            grad = after(grad, dkv)
            dqs[chunk].append(dq)
            dkvs[chunk].append(shift_by(dkv, seq_count, step) if step else dkv)
            biases[chunk] = biases[chunk] + bias
        return grad

    def merge(chunk):
        return merge_grads(chunk, dqs[chunk], dkvs[chunk], raw, cosine, sine, qgain, kgain)

    def chunk_weights(chunk):
        return wide[:, chunk * 3 * width // CHUNKS : (chunk + 1) * 3 * width // CHUNKS]

    def finish_line(terms, sent, first):
        for step in range(first, steps):
            terms = add_received(terms, cross_z(sent, step, places))
            if step + 1 < steps:
                sent, terms = halve(terms, step + 1, places)
        return total_of(terms)

    def line_of(terms):
        total = total_of(terms)
        blocks, rows, columns = total.shape
        return total.reshape(blocks, groups, rows // groups, columns).transpose(1, 0, 2, 3)

    grad = back(0, remote, attended_grad)
    grad = back(1, remote, grad)
    grad = back(0, [0], grad)
    second_across = after(second_across, grad)
    second = x_part(second_across, own, far).reshape(groups, -1, second_across.shape[-1])
    out_total = line_of(add_received(out_terms, out_across))
    folds = second.shape[-1] // width
    out_total = out_total.reshape(groups, folds, -1, width).transpose(0, 2, 1, 3)
    out_total = out_total.reshape(groups, -1, folds * width)
    second = scatter_line(jnp.concatenate([second, out_total], axis=1))
    dqs[0][0] = after(dqs[0][0], grad)
    merged_0, gains_0 = merge(0)
    crossed, in_terms_0 = core_sum([outer(spot, normed_low, merged_0, width // CHUNKS)], places)
    normed_grad_0 = dot(merged_0, chunk_weights(0), NT)
    grad = after(grad, crossed, normed_grad_0)
    in_across_0 = cross_x(crossed, places)
    grad = back(1, [0], grad)
    dqs[1][0] = after(dqs[1][0], grad, in_across_0)
    in_total_0 = scatter_line(line_of(add_received(in_terms_0, in_across_0)))

    merged_1, gains_1 = merge(1)
    crossed, in_terms_1 = core_sum([outer(spot, normed_low, merged_1, width // CHUNKS)], places)
    in_terms_1 = add_received(in_terms_1, cross_x(crossed, places))
    normed_grad = normed_grad_0 + dot(after(merged_1, crossed), chunk_weights(1), NT)
    sent, in_terms_1 = halve(in_terms_1, 0, places)
    in_total_1 = finish_line(in_terms_1, sent, 0)
    second_total = second[: 3 * shard].reshape(3, shard, -1)
    out_total = second[3 * shard :].reshape(-1, folds, width).transpose(1, 0, 2).reshape(shard, width)
    out_proj_grad = sum_seq(out_total, seq_count)
    first_sum = sum_seq(first_total, seq_count)
    second_sum = sum_seq(second_total, seq_count)
    in_sum = jnp.concatenate(
        [sum_seq(in_total_0, seq_count), sum_seq(in_total_1, seq_count)], axis=2
    )
    norm_scale = lax.rsqrt(jnp.mean(inputs_f * inputs_f, axis=-1, keepdims=True) + EPSILON)
    input_norm_grad, attn_gain_terms = rms_backward(inputs_f, norm_scale, attn_gain_f, normed_grad)
    input_grad = residual_grad + input_norm_grad

    same_bias = jnp.concatenate([jnp.sum(bias, axis=-1).reshape(-1) for bias in biases])
    heads = same_bias.shape[0]
    head_gains = sum(jnp.sum(part[:2].reshape(2, -1, head_dim), axis=1) for part in (gains_0, gains_1))
    small = sum_small(
        jnp.concatenate(
            [
                jnp.sum(attn_gain_terms, axis=0),
                jnp.sum(ffn_gain_terms, axis=0),
                head_gains[0],
                head_gains[1],
                same_bias,
            ]
        ),
        places,
        seq_count,
    )
    in_proj_grad = in_sum.transpose(1, 0, 2).reshape(in_proj.shape)
    down_grad = jnp.concatenate(
        [
            part[2].reshape(shard, -1, width).transpose(1, 0, 2).reshape(hidden_part, width)
            for part in (first_sum, second_sum)
        ]
    )
    gate_up_grad = jnp.stack(
        [
            part[:2].reshape(2, shard, places, hidden_part).transpose(1, 0, 2, 3)
            for part in (first_sum, second_sum)
        ],
        axis=3,
    ).reshape(gate_up.shape)
    gain_rows = attn_gain.shape[0]
    here = place * gain_rows
    tail = small[2 * width :]
    same_bias = tail[2 * head_dim : 2 * head_dim + heads]
    return (
        layer_out,
        input_grad,
        in_proj_grad,
        out_proj_grad,
        gate_up_grad,
        down_grad,
        lax.dynamic_slice_in_dim(small, here, gain_rows),
        lax.dynamic_slice_in_dim(small, width + here, gain_rows),
        tail[:head_dim],
        tail[head_dim : 2 * head_dim],
        jnp.stack([same_bias, -same_bias], axis=1),
    )


def solution(mesh):
    in_specs = (
        P(("dp", "seq"), None),
        P("dp", None),
        P("dp", None),
        P(("dp", "seq")),
        P("dp", None),
        P("dp", None),
        P("dp", None),
        P("dp", None),
        P("dp"),
        P("dp"),
        P(),
        P(),
        P(),
        P(("dp", "seq"), None),
    )
    out_specs = (
        P(("dp", "seq"), None),
        P(("dp", "seq"), None),
        P("dp", None),
        P("dp", None),
        P("dp", None),
        P("dp", None),
        P("dp"),
        P("dp"),
        P(),
        P(),
        P(),
    )
    return jax.shard_map(body, mesh=mesh, in_specs=in_specs, out_specs=out_specs, check_vma=False)
```

```python
import functools
import math

import jax
import jax.numpy as jnp
from jax import lax
from jax.experimental import pallas as pl
from jax.experimental.pallas import tpu as pltpu
from jax.sharding import PartitionSpec as P

EPSILON = 1e-06
ROPE_BASE = 10000.0
NEG_FILL = -1e30
PAIR = 128
KEY_ROWS = 256
VMEM_BYTES = 48 * 2**20
NO_COST = pl.CostEstimate(flops=1, bytes_accessed=1, transcendentals=0)
bf16 = jnp.bfloat16
f32 = jnp.float32
NN = (((1,), (0,)), ((), ()))
NT = (((1,), (1,)), ((), ()))
TN = (((0,), (0,)), ((), ()))


def dot(left, right, dims=NN):
    return lax.dot_general(left, right, dims, preferred_element_type=f32)


def split_two(values):
    high = values.astype(bf16)
    return high, (values - high.astype(f32)).astype(bf16)


def lane_index():
    return lax.broadcasted_iota(jnp.int32, (1, PAIR), 1)


def half_ones(same):
    rows = lax.broadcasted_iota(jnp.int32, (2 * PAIR, PAIR), 0) % PAIR
    cols = lax.broadcasted_iota(jnp.int32, (2 * PAIR, PAIR), 1)
    match = (rows < 64) == (cols < 64)
    return jnp.where(match if same else jnp.logical_not(match), 1.0, 0.0).astype(bf16)


def head_sums(values, ones):
    return dot(jnp.concatenate(split_two(values), axis=1), ones)


def swap_halves(values):
    first = lane_index() % 64 < 32
    return jnp.where(first, pltpu.roll(values, PAIR - 32, 1), pltpu.roll(values, 32, 1))


def gather_kernel(shard_ref, tokens_ref, times_ref, wide_ref, there_tokens_ref, there_times_ref, arrived, sent, keep):
    place, rank = lax.axis_index("dp"), lax.axis_index("seq")
    z, x, core = place // 4, place // 2 % 2, place % 2
    rows = shard_ref.shape[0]
    lines = 4

    def device(z, x, core, seq):
        return {"dp": z * 4 + x * 2 + core, "seq": seq}

    up, down = device(z + 1, x, core, rank), device(z - 1, x, core, rank)
    over, twin = device(z, 1 - x, core, rank), device(z, x, 1 - core, rank)
    other = device(z, x, core, 1 - rank)
    barrier = pltpu.get_barrier_semaphore()

    def greet(target):
        pl.semaphore_signal(barrier, inc=1, device_id=target, device_id_type=pl.DeviceIdType.MESH)

    for target in (over, twin, other):
        greet(target)
    pl.when(z < lines - 1)(lambda: greet(up))
    pl.when(z > 0)(lambda: greet(down))
    ends = (z == 0).astype(jnp.int32) + (z == lines - 1).astype(jnp.int32)
    pl.semaphore_wait(barrier, 5 - ends)

    def block(z, x, core):
        return z * 4 + x * 2 + core

    def rows_of(which):
        return wide_ref.at[pl.ds(pl.multiple_of(which * rows, rows), rows)]

    def copy(which, path, target, own=False):
        return pltpu.make_async_remote_copy(
            src_ref=shard_ref if own else rows_of(which),
            dst_ref=rows_of(which),
            send_sem=sent.at[path, which],
            recv_sem=arrived.at[which],
            device_id=target,
            device_id_type=pl.DeviceIdType.MESH,
        )

    def swap(source, target, index):
        return pltpu.make_async_remote_copy(
            src_ref=source,
            dst_ref=target,
            send_sem=keep.at[index],
            recv_sem=keep.at[index + 1],
            device_id=other,
            device_id_type=pl.DeviceIdType.MESH,
        )

    me = block(z, x, core)
    pl.when(z < lines - 1)(lambda: copy(me, 0, up, True).start())
    pl.when(z > 0)(lambda: copy(me, 3, down, True).start())
    copy(me, 1, over, True).start()
    copy(me, 2, twin, True).start()
    swaps = [swap(tokens_ref, there_tokens_ref, 0), swap(times_ref, there_times_ref, 2)]
    for each in swaps:
        each.start()
    here = pltpu.make_async_copy(shard_ref, rows_of(me), keep.at[4])
    here.start()

    def pass_over(which):
        copy(which, 2, twin).start()

    for step in range(1, lines):

        @pl.when(z >= step)
        def _():
            which = block(z - step, x, core)
            copy(which, 0, up).wait_recv()
            pl.when(z < lines - 1)(lambda: copy(which, 0, up).start())
            copy(which, 1, over).start()
            pass_over(which)

        @pl.when(z + step < lines)
        def _():
            which = block(z + step, x, core)
            copy(which, 3, down).wait_recv()
            pl.when(z > 0)(lambda: copy(which, 3, down).start())
            copy(which, 1, over).start()
            pass_over(which)

    for line in range(lines):
        which = block(line, 1 - x, core)
        copy(which, 1, over).wait_recv()
        pass_over(which)
    for line in range(lines):
        for side in range(2):
            copy(block(line, side, 1 - core), 2, twin).wait_recv()
    for line in range(lines):
        which = block(line, x, core)
        copy(which, 1, over).wait_send()
        copy(which, 2, twin).wait_send()
        copy(block(line, 1 - x, core), 2, twin).wait_send()
        pl.when((line <= z) & (z < lines - 1))(lambda: copy(which, 0, up).wait_send())
        pl.when((line >= z) & (z > 0))(lambda: copy(which, 3, down).wait_send())
    for each in swaps:
        each.wait()
    here.wait()


def gather_first(shard, tokens, times, places):
    anywhere = pl.BlockSpec(memory_space=pl.ANY)
    return pl.pallas_call(
        gather_kernel,
        in_specs=[anywhere] * 3,
        out_specs=[anywhere] * 3,
        out_shape=[
            jax.ShapeDtypeStruct((shard.shape[0] * places, shard.shape[1]), shard.dtype),
            jax.ShapeDtypeStruct(tokens.shape, tokens.dtype),
            jax.ShapeDtypeStruct(times.shape, times.dtype),
        ],
        scratch_shapes=[
            pltpu.SemaphoreType.DMA((places,)),
            pltpu.SemaphoreType.DMA((4, places)),
            pltpu.SemaphoreType.DMA((5,)),
        ],
        compiler_params=pltpu.CompilerParams(collective_id=0, has_side_effects=True),
        cost_estimate=NO_COST,
    )(shard, tokens, times)


def qkv_kernel(
    tokens_ref, gain_ref, weight_ref, cos_ref, sin_ref, qgain_ref, kgain_ref,
    k_ref, v_ref, *own_refs,
):
    width = tokens_ref.shape[1]
    values = tokens_ref[...].astype(f32)
    inv = lax.rsqrt(jnp.mean(values * values, axis=-1, keepdims=True) + EPSILON)
    normed = (values * inv * gain_ref[...]).astype(bf16)
    ones = half_ones(True)
    cosine, sine = cos_ref[...], sin_ref[...]
    turned = [(1, k_ref, kgain_ref[...], 1.0)]
    if own_refs:
        q_ref, *raw_refs, normed_ref = own_refs
        normed_ref[...] = normed
        turned.append((0, q_ref, qgain_ref[...], 0.125))
    for part, out_ref, head_gain, scale in turned:
        for chunk in range(width // 256):
            start = part * width + chunk * 256
            raw = dot(normed, weight_ref[:, start : start + 256])
            if own_refs:
                raw_refs[part][:, chunk * 256 : (chunk + 1) * 256] = raw
            for tile in range(2):
                u = raw[:, tile * PAIR : (tile + 1) * PAIR]
                unit = lax.rsqrt(head_sums(u * u, ones) * (1.0 / 64) + EPSILON)
                u = u * unit * head_gain
                u = u * cosine + swap_halves(u) * sine
                at = chunk * 256 + tile * PAIR
                out_ref[:, at : at + PAIR] = (u * scale).astype(bf16)
    for chunk in range(width // 256):
        start = 2 * width + chunk * 256
        v_ref[:, chunk * 256 : (chunk + 1) * 256] = dot(
            normed, weight_ref[:, start : start + 256]
        ).astype(bf16)


def project(tokens, gain, weight, cosine, sine, qgain, kgain, own, block=256):
    rows, width = tokens.shape
    sizes = [(width, bf16), (width, bf16)]
    if own:
        sizes += [(width, bf16), (width, f32), (width, f32), (width, bf16)]
    by_rows = lambda i: (i, 0)
    whole = lambda i: (0, 0)
    return pl.pallas_call(
        qkv_kernel,
        grid=(rows // block,),
        in_specs=[
            pl.BlockSpec((block, width), by_rows),
            pl.BlockSpec((1, width), whole),
            pl.BlockSpec((width, 3 * width), whole, pipeline_mode=pl.Buffered(1)),
            pl.BlockSpec((block, PAIR), by_rows),
            pl.BlockSpec((block, PAIR), by_rows),
            pl.BlockSpec((1, PAIR), whole),
            pl.BlockSpec((1, PAIR), whole),
        ],
        out_specs=[pl.BlockSpec((block, size), by_rows) for size, _ in sizes],
        out_shape=[jax.ShapeDtypeStruct((rows, size), kind) for size, kind in sizes],
        compiler_params=pltpu.CompilerParams(vmem_limit_bytes=VMEM_BYTES),
        cost_estimate=NO_COST,
    )(tokens, gain, weight, cosine, sine, qgain, kgain)


def merge_kernel(sources, parts, *refs):
    dq_refs = refs[:parts]
    dkv_refs = refs[parts : parts + sources]
    rawq_ref, rawk_ref, cos_ref, sin_ref, qgain_ref, kgain_ref, out_ref, gains_ref = refs[parts + sources :]
    width = dq_refs[0].shape[1]
    ones = half_ones(True)
    cosine, sine = cos_ref[...], sin_ref[...]

    @pl.when(pl.program_id(0) == 0)
    def _():
        gains_ref[...] = jnp.zeros_like(gains_ref)

    def read(part, at):
        found = [ref[:, at] for ref in dq_refs] if part == 0 else [ref[part - 1, :, at] for ref in dkv_refs]
        return sum(value.astype(f32) for value in found).astype(bf16)

    for part, (raw_ref, head_gain) in enumerate(((rawq_ref, qgain_ref[...]), (rawk_ref, kgain_ref[...]))):
        for tile in range(width // PAIR):
            at = slice(tile * PAIR, (tile + 1) * PAIR)
            grad = read(part, at).astype(f32)
            grad = grad * cosine - swap_halves(grad) * sine
            raw = raw_ref[:, at]
            unit = lax.rsqrt(head_sums(raw * raw, ones) * (1.0 / 64) + EPSILON)
            hat = raw * unit
            gains_ref[part : part + 1, at] += jnp.sum(grad * hat, axis=0, keepdims=True)
            weighted = grad * head_gain
            inner = head_sums(weighted * hat, ones) * (1.0 / 64)
            there = slice(part * width + tile * PAIR, part * width + (tile + 1) * PAIR)
            out_ref[:, there] = (unit * (weighted - hat * inner)).astype(bf16)
    out_ref[:, 2 * width :] = read(2, slice(0, width))


def merge_grads(width, at, dqs, dkvs, raws, cosine, sine, qgain, kgain, block=256):
    rows = raws[0].shape[0]
    by_rows = lambda i: (i, 0)
    whole = lambda i: (0, 0)
    cut = lambda index: pl.BlockSpec((block, width), lambda i: (i, index))
    cut_two = lambda index: pl.BlockSpec((2, block, width), lambda i: (0, i, index))
    return pl.pallas_call(
        functools.partial(merge_kernel, len(dkvs), len(dqs)),
        grid=(rows // block,),
        in_specs=[cut(index) for _, index in dqs]
        + [cut_two(index) for _, index in dkvs]
        + [
            cut(at),
            cut(at),
            pl.BlockSpec((block, PAIR), by_rows),
            pl.BlockSpec((block, PAIR), by_rows),
            pl.BlockSpec((1, PAIR), whole),
            pl.BlockSpec((1, PAIR), whole),
        ],
        out_specs=[pl.BlockSpec((block, 3 * width), by_rows), pl.BlockSpec((8, width), whole)],
        out_shape=[
            jax.ShapeDtypeStruct((rows, 3 * width), bf16),
            jax.ShapeDtypeStruct((8, width), f32),
        ],
        compiler_params=pltpu.CompilerParams(vmem_limit_bytes=VMEM_BYTES),
        cost_estimate=NO_COST,
    )(*[array for array, _ in dqs], *[array for array, _ in dkvs], *raws, cosine, sine, qgain, kgain)


def forward_kernel(sources, query_rows, flags, q_ref, aq_ref, coef_ref, *refs):
    keyed = refs[: 3 * sources]
    out_ref, full_ref, query, total = refs[3 * sources :]
    rows = q_ref.shape[0]
    lane = lane_index()
    half = lane < 64
    mine = (half, jnp.logical_not(half))
    both = q_ref[...]
    extra = aq_ref[...]
    for h in range(2):
        query[h] = jnp.where(mine[h], both, extra * coef_ref[0, h : h + 1, :])
        total[h] = jnp.zeros_like(total[h])
    blocks = keyed[0].shape[0] // KEY_ROWS
    for j in range(sources):
        k_ref, v_ref, ak_ref = keyed[3 * j : 3 * j + 3]
        for b in range(blocks):

            @pl.when(flags[j * blocks + b] != 0)
            def _():
                at = slice(b * KEY_ROWS, (b + 1) * KEY_ROWS)
                keys, values, columns = k_ref[at, :], v_ref[at, :], ak_ref[at, :]
                ones = jnp.ones_like(values)
                keys2 = [jnp.where(mine[h], keys, columns) for h in range(2)]
                values2 = [jnp.where(mine[h], values, ones) for h in range(2)]
                for i in range(rows // query_rows):
                    part = slice(i * query_rows, (i + 1) * query_rows)
                    for h in range(2):
                        probs = jnp.exp(dot(query[h, part, :], keys2[h], NT)).astype(bf16)
                        total[h, part, :] += dot(probs, values2[h])

    outs = []
    for h in range(2):
        summed = total[h]
        outs.append(summed / pltpu.roll(summed, 64, 1))
        log_total = jnp.log(jnp.maximum(summed, 1e-30))
        high = log_total.astype(bf16)
        mid, low = split_two(log_total - high.astype(f32))
        base = lane - 64 if h == 0 else lane
        full_ref[:, h * PAIR : (h + 1) * PAIR] = jnp.where(
            base == 11, -high, jnp.where(base == 12, -mid, jnp.where(base == 13, -low, query[h]))
        )
    out_ref[...] = jnp.where(half, outs[0], outs[1]).astype(bf16)


def attend(flags, queries, query_columns, coefficients, keyed):
    rows, width = queries.shape
    pairs = width // PAIR
    key_rows = keyed[0][0].shape[0]
    sources = len(keyed)
    by_pair = lambda p, f: (0, p)
    whole = lambda p, f: (0, 0)
    in_specs = [
        pl.BlockSpec((rows, PAIR), by_pair),
        pl.BlockSpec((rows, PAIR), whole),
        pl.BlockSpec((1, 2, PAIR), lambda p, f: (p, 0, 0)),
    ]
    operands = [queries, query_columns, coefficients]
    for keys, values, columns in keyed:
        in_specs += [
            pl.BlockSpec((key_rows, PAIR), by_pair),
            pl.BlockSpec((key_rows, PAIR), by_pair),
            pl.BlockSpec((key_rows, PAIR), whole),
        ]
        operands += [keys, values, columns]
    return pl.pallas_call(
        functools.partial(forward_kernel, sources, min(512, rows)),
        grid_spec=pltpu.PrefetchScalarGridSpec(
            num_scalar_prefetch=1,
            grid=(pairs,),
            in_specs=in_specs,
            out_specs=[
                pl.BlockSpec((rows, PAIR), by_pair),
                pl.BlockSpec((rows, 2 * PAIR), by_pair),
            ],
            scratch_shapes=[
                pltpu.VMEM((2, rows, PAIR), bf16),
                pltpu.VMEM((2, rows, PAIR), f32),
            ],
        ),
        out_shape=[
            jax.ShapeDtypeStruct((rows, width), bf16),
            jax.ShapeDtypeStruct((rows, 2 * width), bf16),
        ],
        compiler_params=pltpu.CompilerParams(vmem_limit_bytes=VMEM_BYTES),
        cost_estimate=NO_COST,
    )(flags, *operands)


def backward_start(grad_ref, out_ref, grads, dq_total):
    lane = lane_index()
    half = lane < 64
    mine = (half, jnp.logical_not(half))
    base = (lane - 64, lane)
    both = grad_ref[...]
    row_total = head_sums(both.astype(f32) * out_ref[...].astype(f32), half_ones(False))
    high, low = split_two(row_total)
    zero = jnp.zeros_like(high)
    for h in range(2):
        extra = jnp.where(base[h] == 0, -high, jnp.where(base[h] == 1, -low, zero))
        grads[h] = jnp.where(mine[h], both, extra)
        dq_total[h] = jnp.zeros_like(dq_total[h])


def backward_block(full_ref, keys, values, columns, grads, dq_total):
    lane = lane_index()
    half = lane < 64
    mine = (half, jnp.logical_not(half))
    base = (lane - 64, lane)
    ones = jnp.ones_like(values)
    dks, dvs = [], []
    for h in range(2):
        keys2 = jnp.where(mine[h], keys, columns)
        pick = (base[h] >= 0) & (base[h] < 2)
        values2 = jnp.where(mine[h], values, jnp.where(pick, ones, jnp.zeros_like(ones)))
        full = full_ref[:, h * PAIR : (h + 1) * PAIR]
        probs = jnp.exp(dot(keys2, full, NT))
        score_low = (probs * dot(values2, grads[h], NT)).astype(bf16)
        dks.append(dot(score_low, full))
        dvs.append(dot(probs.astype(bf16), grads[h]))
        dq_total[h] += dot(keys2, score_low, TN)
    return (
        jnp.where(half, dks[0], dks[1]).astype(bf16),
        jnp.where(half, dvs[0], dvs[1]).astype(bf16),
    )


def backward_end(aq_ref, dq_ref, bias_ref, dq_total):
    lane = lane_index()
    base = (lane - 64, lane)
    dq = [dq_total[h].T for h in range(2)]
    dq_ref[...] = jnp.where(lane < 64, dq[0], dq[1]) * 0.125
    variates = aq_ref[...].astype(f32)
    for h in range(2):
        pick = (base[h] >= 0) & (base[h] < 4)
        bias_ref[0, h : h + 1, :] = jnp.sum(
            jnp.where(pick, dq[h] * variates, 0.0), axis=0, keepdims=True
        )


def backward_kernel(
    flags, full_ref, grad_ref, out_ref, aq_ref, k_ref, v_ref, ak_ref,
    dq_ref, dkv_ref, bias_ref, grads, dq_total,
):
    backward_start(grad_ref, out_ref, grads, dq_total)
    for b in range(k_ref.shape[0] // KEY_ROWS):
        at = slice(b * KEY_ROWS, (b + 1) * KEY_ROWS)

        @pl.when(flags[b] != 0)
        def _():
            dkv_ref[0, at, :], dkv_ref[1, at, :] = backward_block(
                full_ref, k_ref[at, :], v_ref[at, :], ak_ref[at, :], grads, dq_total
            )

        @pl.when(flags[b] == 0)
        def _():
            dkv_ref[:, at, :] = jnp.zeros((2, KEY_ROWS, PAIR), bf16)

    backward_end(aq_ref, dq_ref, bias_ref, dq_total)


def attend_back(first_pair, pairs, flags, full, grad, out, query_columns, keys, values, key_columns):
    rows = grad.shape[0]
    width = pairs * PAIR
    key_rows = keys.shape[0]
    by_pair = lambda p, f: (0, p)
    from_pair = lambda p, f: (0, first_pair + p)
    whole = lambda p, f: (0, 0)
    return pl.pallas_call(
        backward_kernel,
        grid_spec=pltpu.PrefetchScalarGridSpec(
            num_scalar_prefetch=1,
            grid=(pairs,),
            in_specs=[
                pl.BlockSpec((rows, 2 * PAIR), from_pair),
                pl.BlockSpec((rows, PAIR), from_pair),
                pl.BlockSpec((rows, PAIR), from_pair),
                pl.BlockSpec((rows, PAIR), whole),
                pl.BlockSpec((key_rows, PAIR), from_pair),
                pl.BlockSpec((key_rows, PAIR), from_pair),
                pl.BlockSpec((key_rows, PAIR), whole),
            ],
            out_specs=[
                pl.BlockSpec((rows, PAIR), by_pair),
                pl.BlockSpec((2, key_rows, PAIR), lambda p, f: (0, 0, p)),
                pl.BlockSpec((1, 2, PAIR), lambda p, f: (p, 0, 0)),
            ],
            scratch_shapes=[
                pltpu.VMEM((2, rows, PAIR), bf16),
                pltpu.VMEM((2, PAIR, rows), f32),
            ],
        ),
        out_shape=[
            jax.ShapeDtypeStruct((rows, width), f32),
            jax.ShapeDtypeStruct((2, key_rows, width), bf16),
            jax.ShapeDtypeStruct((pairs, 2, PAIR), f32),
        ],
        compiler_params=pltpu.CompilerParams(vmem_limit_bytes=VMEM_BYTES),
        cost_estimate=NO_COST,
    )(flags, full, grad, out, query_columns, keys, values, key_columns)


LINES = 4
STARTS = (0, 3, 7, 0)
ARRIVALS = (7, 10, 13, 4)


def line_device(place, line):
    return {"dp": line * 4 + place % 4}


def carry_kernel(
    pairs, full_ref, grad_ref, out_ref, aq_ref,
    far_k_ref, far_v_ref, far_ak_ref, near_k_ref, near_v_ref, near_ak_ref,
    across_ref, own_ref, far_ref, out_across_ref, out_own_ref, out_far_ref,
    dq_ref, bias_ref, got_ref, near_ref, line_ref, line_got_ref, across_got, out_got,
    grads, dq_total, stage, near_stage, terms, sums,
    send_sems, recv_sems, near_sems, across_sems, term_sems, line_send, line_recv, line_own,
):
    step = pl.program_id(0)
    place, rank = lax.axis_index("dp"), lax.axis_index("seq")
    line = place // 4
    other = {"seq": 1 - rank}
    over = {"dp": place + 2 - place // 2 % 2 * 4}
    mesh_id = pl.DeviceIdType.MESH

    def lanes(index):
        return pl.ds(pl.multiple_of(index * PAIR, PAIR), PAIR)

    def part_of(refs, part):
        return refs[1] if part == 3 else refs[0].at[:, part]

    def held(ref, part):
        return ref.at[:, :, pl.ds(0, out_own_ref.shape[2])] if part == 3 else ref

    def across(part):
        return pltpu.make_async_remote_copy(
            src_ref=part_of((across_ref, out_across_ref), part),
            dst_ref=part_of((across_got, out_got), part),
            send_sem=across_sems.at[part, 0], recv_sem=across_sems.at[part, 1],
            device_id=over, device_id_type=mesh_id,
        )

    def load(part, k):
        source = part_of(((own_ref, out_own_ref), (far_ref, out_far_ref), (across_got, out_got))[k], part)
        return pltpu.make_async_copy(source, held(terms.at[k], part), term_sems.at[k])

    def along(part, k):
        to = lax.rem(line + k, LINES)
        columns = pl.ds(0, out_own_ref.shape[2] if part == 3 else sums.shape[3])
        return pltpu.make_async_remote_copy(
            src_ref=sums.at[part, to, :, columns], dst_ref=line_got_ref.at[k - 1, part, :, columns],
            send_sem=line_send.at[part, k - 1], recv_sem=line_recv.at[part, k - 1],
            device_id=line_device(place, to), device_id_type=mesh_id,
        )

    def stay(part):
        columns = pl.ds(0, out_own_ref.shape[2] if part == 3 else sums.shape[3])
        return pltpu.make_async_copy(
            sums.at[part, line, :, columns], line_ref.at[part, :, columns], line_own.at[part]
        )

    def to_other(pair):
        return pltpu.make_async_remote_copy(
            src_ref=stage.at[pair], dst_ref=got_ref.at[:, :, lanes(pair)], send_sem=send_sems.at[pair],
            recv_sem=recv_sems.at[pair], device_id=other, device_id_type=mesh_id,
        )

    def to_near(pair):
        slot = lax.rem(pair, 2)
        return pltpu.make_async_copy(
            near_stage.at[slot], near_ref.at[:, :, lanes(pair)], near_sems.at[slot]
        )

    @pl.when(step == 0)
    def _():
        barrier = pltpu.get_barrier_semaphore()
        peers = [other, over] + [line_device(place, lax.rem(line + k, LINES)) for k in range(1, LINES)]
        for target in peers:
            pl.semaphore_signal(barrier, inc=1, device_id=target, device_id_type=mesh_id)
        pl.semaphore_wait(barrier, len(peers))

    for part in range(4):

        @pl.when(step == STARTS[part])
        def _():
            across(part).start()

        @pl.when(step == ARRIVALS[part] - 1)
        def _():
            load(part, 0).start()
            load(part, 1).start()

        @pl.when(step == ARRIVALS[part])
        def _():
            across(part).wait()
            load(part, 2).start()
            for k in range(3):
                load(part, k).wait()
            columns = out_own_ref.shape[2] if part == 3 else sums.shape[3]
            for i in range(LINES):
                sums[part, i, :, :columns] = sum(
                    terms[k, i, :, :columns].astype(f32) for k in range(3)
                ).astype(bf16)
            for k in range(1, LINES):
                along(part, k).start()
            stay(part).start()

    @pl.when(step >= pairs + 2)
    def _():
        to_near(step - pairs - 2).wait()

    backward_start(grad_ref, out_ref, grads, dq_total)
    is_far = step < pairs
    slot = lax.rem(step - jnp.where(is_far, 0, pairs), 2)
    for b in range(far_k_ref.shape[0] // KEY_ROWS):
        at = slice(b * KEY_ROWS, (b + 1) * KEY_ROWS)
        block = [
            jnp.where(is_far, far[at, :], near[at, :])
            for far, near in ((far_k_ref, near_k_ref), (far_v_ref, near_v_ref), (far_ak_ref, near_ak_ref))
        ]
        dk, dv = backward_block(full_ref, *block, grads, dq_total)

        @pl.when(is_far)
        def _():
            stage[step, 0, at, :] = dk
            stage[step, 1, at, :] = dv

        @pl.when(jnp.logical_not(is_far))
        def _():
            near_stage[slot, 0, at, :] = dk
            near_stage[slot, 1, at, :] = dv

    backward_end(aq_ref, dq_ref, bias_ref, dq_total)
    pl.when(is_far)(lambda: to_other(step).start())
    pl.when(jnp.logical_not(is_far))(lambda: to_near(step - pairs).start())

    @pl.when(step == pl.num_programs(0) - 1)
    def _():
        to_near(step - pairs - 1).wait()
        to_near(step - pairs).wait()
        for pair in range(pairs):
            to_other(pair).wait()
        for part in range(4):
            for k in range(1, LINES):
                along(part, k).wait()
            stay(part).wait()


def attend_back_carry(full, grad, out, query_columns, near, far, sums, out_sums):
    rows, width = grad.shape
    pairs = width // PAIR
    key_rows = near[0].shape[0]
    pair_of = lambda i: jnp.where(i < pairs, i, i - pairs)
    by_pair = lambda i: (0, pair_of(i))
    far_pair = lambda i: (0, jnp.minimum(i, pairs - 1))
    near_pair = lambda i: (0, jnp.maximum(i - pairs, 0))
    whole = lambda i: (0, 0)
    anywhere = pl.BlockSpec(memory_space=pl.ANY)
    shard, hidden = sums[0].shape[2:]

    def key_specs(pair):
        return [
            pl.BlockSpec((key_rows, PAIR), pair),
            pl.BlockSpec((key_rows, PAIR), pair),
            pl.BlockSpec((key_rows, PAIR), whole),
        ]

    return pl.pallas_call(
        functools.partial(carry_kernel, pairs),
        grid=(2 * pairs,),
        in_specs=[
            pl.BlockSpec((rows, 2 * PAIR), by_pair),
            pl.BlockSpec((rows, PAIR), by_pair),
            pl.BlockSpec((rows, PAIR), by_pair),
            pl.BlockSpec((rows, PAIR), whole),
        ]
        + key_specs(far_pair)
        + key_specs(near_pair)
        + [anywhere] * 6,
        out_specs=[
            pl.BlockSpec((rows, PAIR), lambda i: (0, i)),
            pl.BlockSpec((1, 2, PAIR), lambda i: (i, 0, 0)),
        ]
        + [anywhere] * 6,
        out_shape=[
            jax.ShapeDtypeStruct((rows, 2 * width), f32),
            jax.ShapeDtypeStruct((2 * pairs, 2, PAIR), f32),
            jax.ShapeDtypeStruct((2, key_rows, width), bf16),
            jax.ShapeDtypeStruct((2, key_rows, width), bf16),
            jax.ShapeDtypeStruct((4, shard, hidden), bf16),
            jax.ShapeDtypeStruct((LINES - 1, 4, shard, hidden), bf16),
            jax.ShapeDtypeStruct(sums[0].shape, bf16),
            jax.ShapeDtypeStruct(out_sums[0].shape, bf16),
        ],
        scratch_shapes=[
            pltpu.VMEM((2, rows, PAIR), bf16),
            pltpu.VMEM((2, PAIR, rows), f32),
            pltpu.VMEM((pairs, 2, key_rows, PAIR), bf16),
            pltpu.VMEM((2, 2, key_rows, PAIR), bf16),
            pltpu.VMEM((3, LINES, shard, hidden), bf16),
            pltpu.VMEM((4, LINES, shard, hidden), bf16),
            pltpu.SemaphoreType.DMA((pairs,)),
            pltpu.SemaphoreType.DMA((pairs,)),
            pltpu.SemaphoreType.DMA((2,)),
            pltpu.SemaphoreType.DMA((4, 2)),
            pltpu.SemaphoreType.DMA((3,)),
            pltpu.SemaphoreType.DMA((4, LINES - 1)),
            pltpu.SemaphoreType.DMA((4, LINES - 1)),
            pltpu.SemaphoreType.DMA((4,)),
        ],
        compiler_params=pltpu.CompilerParams(
            vmem_limit_bytes=VMEM_BYTES, collective_id=3, has_side_effects=True
        ),
        cost_estimate=NO_COST,
    )(full, grad, out, query_columns, *far, *near, *sums, *out_sums)


def slot_columns(segment, variates):
    column = jnp.arange(PAIR, dtype=jnp.int32)[None, :] % 64
    same_var = (column < 8) & (variates[:, None] == column % 4)
    in_seg = (column >= 8) & (column < 11)
    same_seg = segment[:, None] == column - 8
    three = (column >= 11) & (column < 14)
    query = jnp.where(in_seg & jnp.logical_not(same_seg), NEG_FILL, same_var.astype(f32))
    key = (same_var | (in_seg & same_seg) | three).astype(f32)
    return query.astype(bf16), key.astype(bf16)


def bias_columns(head_bias):
    delta = head_bias[:, 0] - head_bias[:, 1]
    high, low = split_two(delta)
    heads = delta.shape[0]
    row = jnp.concatenate(
        [
            jnp.broadcast_to(high[:, None], (heads, 4)),
            jnp.broadcast_to(low[:, None], (heads, 4)),
            jnp.ones((heads, 3), bf16),
            jnp.zeros((heads, 53), bf16),
        ],
        1,
    )
    return jnp.concatenate([row, row], 1).reshape(heads // 2, 2, PAIR)


def arrange_rows(places, spot, left_ref, turned, arranged):
    shard = left_ref.shape[1] // places
    turned[...] = left_ref[...].T
    for i in range(places):
        at = pl.multiple_of(spot[2 + i] * shard, shard)
        arranged[i * shard : (i + 1) * shard, :] = turned[pl.ds(at, shard), :]


def ffn_kernel(
    places, first, nf_ref, seed_ref, start_ref, nfstart_ref, wg_ref, wu_ref, wd_ref, *refs
):
    if first:
        branch_ref, nfgrad_ref, far_ref, cross_ref, own_ref, *refs = refs
    else:
        across_ref, branch_ref, nfgrad_ref, far_ref, cross_ref, own_ref, got_ref, *refs = refs
    turned, branch, columns_out, rows_out, sems, arrived, *x_sems = refs
    step = pl.program_id(0)
    steps = pl.num_programs(0)
    rows, width = nf_ref.shape
    shard = width // places
    chunk = wg_ref.shape[1]
    folds = chunk // 2 // shard

    place = lax.axis_index("dp")
    groups = places // 4

    twin = {"dp": place + 1 - place % 2 * 2}
    over = {"dp": place + 2 - place // 2 % 2 * 4}
    mesh_id = pl.DeviceIdType.MESH

    def carry():
        return pltpu.make_async_remote_copy(
            src_ref=across_ref, dst_ref=got_ref, send_sem=x_sems[0].at[0], recv_sem=x_sems[0].at[1],
            device_id=over, device_id_type=mesh_id,
        )

    @pl.when(step == 0)
    def _():
        barrier = pltpu.get_barrier_semaphore()
        for target in (twin,) if first else (twin, over):
            pl.semaphore_signal(barrier, inc=1, device_id=target, device_id_type=mesh_id)
        pl.semaphore_wait(barrier, 1 if first else 2)
        if not first:
            carry().start()
        turned[...] = nf_ref[...].T
        branch[...] = start_ref[...]
        nfgrad_ref[...] = jnp.zeros_like(nfgrad_ref) if first else nfstart_ref[...]

    def spot_of(line, x, core):
        near_core = (core == place % 2).astype(jnp.int32)
        near_x = (x == place // 2 % 2).astype(jnp.int32)
        return (near_core * 2 + near_x) * groups + line

    def to_twin(source, target, send_sem, recv_sem):
        return pltpu.make_async_remote_copy(
            src_ref=source, dst_ref=target, send_sem=send_sem, recv_sem=recv_sem,
            device_id=twin, device_id_type=mesh_id,
        )

    def column_copies(at):
        slot = lax.rem(at, 2)
        start = pl.multiple_of(at * chunk, chunk)
        made, begin = [], 0
        for k, ref in enumerate((far_ref, cross_ref, own_ref)):
            count = ref.shape[0]
            source = columns_out.at[slot, pl.ds(begin, count)]
            target = ref.at[:, pl.ds(0, 2), :, pl.ds(start, chunk)]
            if k == 0:
                made.append(to_twin(source, target, sems.at[slot, k], arrived.at[at, 0]))
            else:
                made.append(pltpu.make_async_copy(source, target, sems.at[slot, k]))
            begin += count
        return made

    def row_copies(at, ref, index, k):
        slot = lax.rem(at, 2)
        source, target = rows_out.at[slot, k], ref.at[index, 2]
        if k == 0:
            return to_twin(source, target, sems.at[slot, 3], arrived.at[at, 1])
        return pltpu.make_async_copy(source, target, sems.at[slot, 4])

    def sent(copy):
        copy.wait_send() if copy.is_remote else copy.wait()

    def each_copy(at, act):
        for copy in column_copies(at):
            act(copy)
        line, x = at // 2, lax.rem(at, 2)
        near = x == place // 2 % 2
        act(row_copies(at, far_ref, near.astype(jnp.int32) * groups + line, 0))
        pl.when(near)(lambda: act(row_copies(at, own_ref, line, 1)))
        pl.when(jnp.logical_not(near))(lambda: act(row_copies(at, cross_ref, line, 1)))

    @pl.when(step >= 2)
    def _():
        each_copy(step - 2, sent)

    slot = lax.rem(step, 2)
    wg, wu = wg_ref[...], wu_ref[...]
    wd = jnp.concatenate(
        [
            wd_ref[i * shard : (i + 1) * shard, k * width : (k + 1) * width]
            for i in range(2)
            for k in range(folds)
        ],
        axis=0,
    )
    hiddens, gates, ups = [], [], []
    part_rows = min(256, rows)
    for i in range(rows // part_rows):
        at = slice(i * part_rows, (i + 1) * part_rows)
        nf = nf_ref[at, :]
        g, u = dot(nf, wg), dot(nf, wu)
        hidden_grad = dot(seed_ref[at, :], wd, NT)
        sg = 1.0 / (1.0 + jnp.exp(-g))
        silu = g * sg
        hidden = (silu * u).astype(bf16)
        gate = (hidden_grad * u * sg * (1.0 + g * (1.0 - sg))).astype(bf16)
        up = (hidden_grad * silu).astype(bf16)
        branch[at, :] += dot(hidden, wd)
        nfgrad_ref[at, :] += dot(gate, wg, NT) + dot(up, wu, NT)
        hiddens.append(hidden)
        gates.append(gate)
        ups.append(up)
    hidden = jnp.concatenate(hiddens, axis=0)
    down = dot(hidden, seed_ref[...], TN).astype(bf16)
    on_upper = place % 2 == 1
    lower, upper = down[: chunk // 2, :], down[chunk // 2 :, :]
    for i, part in enumerate((jnp.where(on_upper, lower, upper), jnp.where(on_upper, upper, lower))):
        for k in range(folds):
            rows_out[slot, i, :, k * width : (k + 1) * width] = part[k * shard : (k + 1) * shard, :]
    for part, grad in enumerate((gates, ups)):
        columns = dot(turned[...], jnp.concatenate(grad, axis=0)).astype(bf16)
        for j in range(places):
            spot = spot_of(j // 4, j // 2 % 2, j % 2)
            columns_out[slot, spot, part] = columns[j * shard : (j + 1) * shard, :]
    each_copy(step, lambda copy: copy.start())

    @pl.when(step == steps - 1)
    def _():
        branch_ref[...] = branch[...].astype(branch_ref.dtype)
        each_copy(step - 1, sent)
        each_copy(step, sent)
        for at in range(places // 2):
            column_copies(at)[0].wait_recv()
            near = (at % 2 == place // 2 % 2).astype(jnp.int32)
            row_copies(at, far_ref, near * groups + at // 2, 0).wait_recv()
        if not first:
            carry().wait()


def feed_forward(places, normed, seed, start, nfstart, weights, across=None):
    rows, width = normed.shape
    first = nfstart is None
    hidden = weights.shape[1] // 3
    chunk = 2 * hidden // places
    steps = places // 2
    shard = width // places
    whole = lambda t: (0, 0)
    once = pl.Buffered(1)
    return pl.pallas_call(
        functools.partial(ffn_kernel, places, first),
        grid=(steps,),
        in_specs=[
            pl.BlockSpec((rows, width), whole, pipeline_mode=once),
            pl.BlockSpec((rows, width), whole, pipeline_mode=once),
            pl.BlockSpec((rows, width), whole, pipeline_mode=once),
            pl.BlockSpec((8, 128) if first else (rows, width), whole, pipeline_mode=once),
            pl.BlockSpec((width, chunk), lambda t: (0, t)),
            pl.BlockSpec((width, chunk), lambda t: (0, steps + t)),
            pl.BlockSpec((2 * shard, hidden), lambda t: (t, 2)),
        ]
        + [pl.BlockSpec(memory_space=pl.ANY)] * (not first),
        out_specs=[
            pl.BlockSpec((rows, width), whole),
            pl.BlockSpec((rows, width), whole),
        ]
        + [pl.BlockSpec(memory_space=pl.ANY)] * (3 if first else 4),
        scratch_shapes=[
            pltpu.VMEM((width, rows), bf16),
            pltpu.VMEM((rows, width), f32),
            pltpu.VMEM((2, places, 2, shard, chunk), bf16),
            pltpu.VMEM((2, 2, shard, hidden), bf16),
            pltpu.SemaphoreType.DMA((2, 5)),
            pltpu.SemaphoreType.DMA((steps, 2)),
        ]
        + [pltpu.SemaphoreType.DMA((2,))] * (not first),
        out_shape=[
            jax.ShapeDtypeStruct((rows, width), f32 if first else bf16),
            jax.ShapeDtypeStruct((rows, width), f32),
        ]
        + [jax.ShapeDtypeStruct((places // part, 3, shard, hidden), bf16) for part in ((2, 4, 4) if first else (2, 4, 4, 4))],
        compiler_params=pltpu.CompilerParams(
            vmem_limit_bytes=56 * 2**20, collective_id=1 if first else 2, has_side_effects=True
        ),
        cost_estimate=NO_COST,
    )(
        normed, seed, start, start if first else nfstart, weights, weights, weights,
        *(() if first else (across,)),
    )


def outer_kernel(places, spot, left_ref, right_ref, far_ref, cross_ref, own_ref, turned, arranged):
    width = left_ref.shape[1]

    @pl.when(pl.program_id(0) == 0)
    def _():
        arrange_rows(places, spot, left_ref, turned, arranged)

    right = right_ref[...]
    half = width // 2
    far_ref[0] = dot(arranged[:half, :], right).astype(bf16)
    cross_ref[0] = dot(arranged[half : half + half // 2, :], right).astype(bf16)
    own_ref[0] = dot(arranged[half + half // 2 :, :], right).astype(bf16)


def outer(spot, left, right, block):
    rows, width = left.shape
    columns = right.shape[1]
    places = spot.shape[0] - 2
    by_cols = lambda t, o: (0, t)
    one_block = lambda t, o: (t, 0, 0)
    return pl.pallas_call(
        functools.partial(outer_kernel, places),
        grid_spec=pltpu.PrefetchScalarGridSpec(
            num_scalar_prefetch=1,
            grid=(columns // block,),
            in_specs=[
                pl.BlockSpec((rows, width), lambda t, o: (0, 0)),
                pl.BlockSpec((rows, block), by_cols),
            ],
            out_specs=[
                pl.BlockSpec((1, width // 2, block), one_block),
                pl.BlockSpec((1, width // 4, block), one_block),
                pl.BlockSpec((1, width // 4, block), one_block),
            ],
            scratch_shapes=[pltpu.VMEM((width, rows), bf16), pltpu.VMEM((width, rows), bf16)],
        ),
        out_shape=[
            jax.ShapeDtypeStruct((columns // block, width // 2, block), bf16),
            jax.ShapeDtypeStruct((columns // block, width // 4, block), bf16),
            jax.ShapeDtypeStruct((columns // block, width // 4, block), bf16),
        ],
        compiler_params=pltpu.CompilerParams(vmem_limit_bytes=VMEM_BYTES),
        cost_estimate=NO_COST,
    )(spot, left, right)


def finish_kernel(
    far_ref, cross_ref, own_ref, line_ref, line_got_ref, first_ref, small_ref,
    merged_ref, weight_ref, tokens_ref, resid_ref, gain_ref,
    in_ref, first_out_ref, second_out_ref, small_out_ref, grad_ref,
    core_got, x_sent, x_got, z_sent, z_got, y_sent, y_got, first_got, second, second_got, small_sent, small_got,
    merged, weight, tokens, resid, grad,
    core_sems, x_sems, z_send, z_recv, y_sems, first_sems, second_sems, small_sems, load_sems, store_sem,
):
    place, rank = lax.axis_index("dp"), lax.axis_index("seq")
    line = place // 4
    mesh_id = pl.DeviceIdType.MESH
    twin = {"dp": place + 1 - place % 2 * 2}
    over = {"dp": place + 2 - place // 2 % 2 * 4}
    other = {"seq": 1 - rank}
    lines = [line_device(place, lax.rem(line + k, LINES)) for k in range(1, LINES)]
    low = line_device(place, line + 1 - line % 2 * 2)
    high = line_device(place, lax.rem(line + 2, LINES))
    blocks, quarter = cross_ref.shape[:2]
    shard = quarter // LINES

    def send(source, target, sems, to):
        return pltpu.make_async_remote_copy(
            src_ref=source, dst_ref=target, send_sem=sems[0], recv_sem=sems[1],
            device_id=to, device_id_type=mesh_id,
        )

    def pair_of(sems, *index):
        return sems.at[*index, 0], sems.at[*index, 1]

    to_core = [send(far_ref.at[b], core_got.at[b], pair_of(core_sems, b), twin) for b in range(blocks)]
    to_x = [send(x_sent.at[b], x_got.at[b], pair_of(x_sems, b), over) for b in range(blocks)]
    to_y = [send(y_sent.at[b], y_got.at[b], pair_of(y_sems, b), other) for b in range(blocks)]
    first_y = send(first_ref, first_got, pair_of(first_sems), other)
    second_y = send(second, second_got, pair_of(second_sems), other)
    rounds = [
        send(small_sent.at[k], small_got.at[k], pair_of(small_sems, k), to)
        for k, to in enumerate((twin, over, low, high, other))
    ]

    def to_z(b, k):
        return send(
            z_sent.at[b, lax.rem(line + k, LINES)], z_got.at[b, k - 1],
            (z_send.at[b, k - 1], z_recv.at[b, k - 1]), lines[k - 1],
        )

    loads = [
        pltpu.make_async_copy(source, target, load_sems.at[k])
        for k, (source, target) in enumerate(
            ((merged_ref, merged), (weight_ref.at[:, pl.ds(0, weight.shape[1])], weight),
             (tokens_ref, tokens), (resid_ref, resid))
        )
    ]
    store = pltpu.make_async_copy(grad, grad_ref, store_sem.at[0])

    barrier = pltpu.get_barrier_semaphore()
    peers = [twin, over, other] + lines
    for target in peers:
        pl.semaphore_signal(barrier, inc=1, device_id=target, device_id_type=mesh_id)
    pl.semaphore_wait(barrier, len(peers))
    for copy in to_core + [first_y] + loads:
        copy.start()
    second[...] = sum(
        part.astype(f32) for part in [line_ref[...]] + [line_got_ref[k] for k in range(LINES - 1)]
    ).astype(bf16)
    second_y.start()
    for b in range(blocks):
        to_core[b].wait()
        x_sent[b] = (cross_ref[b].astype(f32) + core_got[b, :quarter].astype(f32)).astype(bf16)
        to_x[b].start()

    for copy in loads:
        copy.wait()
    gain = gain_ref[...]
    rows = tokens.shape[0]
    step = min(256, rows)
    gain_grad = jnp.zeros_like(gain)
    for i in range(rows // step):
        at = slice(i * step, (i + 1) * step)
        normed_grad = dot(merged[at, :], weight[...], NT)
        values = tokens[at, :].astype(f32)
        inv = lax.rsqrt(jnp.mean(values * values, axis=-1, keepdims=True) + EPSILON)
        hat = values * inv
        weighted = normed_grad * gain
        inner = jnp.mean(weighted * hat, axis=-1, keepdims=True)
        grad[at, :] = resid[at, :] + inv * (weighted - hat * inner)
        gain_grad = gain_grad + jnp.sum(normed_grad * hat, axis=0, keepdims=True)
    store.start()
    small_sent[0] = small_ref[...]
    for k in range(gain.shape[1] // PAIR):
        small_sent[0, k : k + 1, :] = gain_grad[:, k * PAIR : (k + 1) * PAIR]
    rounds[0].start()

    def next_round(k):
        rounds[k].wait()
        total = small_sent[k] + small_got[k]
        if k + 1 < len(rounds):
            small_sent[k + 1] = total
            rounds[k + 1].start()
        else:
            small_out_ref[...] = total

    next_round(0)
    for b in range(blocks):
        to_x[b].wait()
        total = own_ref[b].astype(f32) + core_got[b, quarter:].astype(f32) + x_got[b].astype(f32)
        total = total.astype(bf16)
        for k in range(LINES):
            z_sent[b, k] = total[k * shard : (k + 1) * shard, :]
        for k in range(1, LINES):
            to_z(b, k).start()
    next_round(1)
    first_y.wait()
    first_out_ref[...] = first_ref[...].astype(f32) + first_got[...].astype(f32)
    second_y.wait()
    second_out_ref[...] = second[...].astype(f32) + second_got[...].astype(f32)
    for b in range(blocks):
        for k in range(1, LINES):
            to_z(b, k).wait()
        total = z_sent[b, line].astype(f32)
        for k in range(LINES - 1):
            total = total + z_got[b, k].astype(f32)
        y_sent[b] = total.astype(bf16)
        to_y[b].start()
    for k in range(2, len(rounds)):
        next_round(k)
    for b in range(blocks):
        to_y[b].wait()
        in_ref[b] = y_sent[b].astype(f32) + y_got[b].astype(f32)
    store.wait()


def finish(in_grads, line_sums, line_got, first, small, merged, weight, tokens, resid, gain):
    far, cross, own = in_grads
    blocks, quarter, columns = cross.shape
    shard = quarter // LINES
    rows, width = tokens.shape
    vmem = pl.BlockSpec(memory_space=pltpu.VMEM)
    anywhere = pl.BlockSpec(memory_space=pl.ANY)
    dma = pltpu.SemaphoreType.DMA
    return pl.pallas_call(
        finish_kernel,
        in_specs=[vmem] * 7 + [anywhere] * 4 + [vmem],
        out_specs=[vmem] * 4 + [anywhere],
        out_shape=[
            jax.ShapeDtypeStruct((blocks, shard, columns), f32),
            jax.ShapeDtypeStruct(first.shape, f32),
            jax.ShapeDtypeStruct(line_sums.shape, f32),
            jax.ShapeDtypeStruct(small.shape, f32),
            jax.ShapeDtypeStruct((rows, width), f32),
        ],
        scratch_shapes=[
            pltpu.VMEM(far.shape, bf16),
            pltpu.VMEM(cross.shape, bf16),
            pltpu.VMEM(cross.shape, bf16),
            pltpu.VMEM((blocks, LINES, shard, columns), bf16),
            pltpu.VMEM((blocks, LINES - 1, shard, columns), bf16),
            pltpu.VMEM((blocks, shard, columns), bf16),
            pltpu.VMEM((blocks, shard, columns), bf16),
            pltpu.VMEM(first.shape, bf16),
            pltpu.VMEM(line_sums.shape, bf16),
            pltpu.VMEM(line_sums.shape, bf16),
            pltpu.VMEM((5, *small.shape), f32),
            pltpu.VMEM((5, *small.shape), f32),
            pltpu.VMEM(merged.shape, bf16),
            pltpu.VMEM(merged.shape, bf16),
            pltpu.VMEM((rows, width), bf16),
            pltpu.VMEM((rows, width), f32),
            pltpu.VMEM((rows, width), f32),
            dma((blocks, 2)),
            dma((blocks, 2)),
            dma((blocks, LINES - 1)),
            dma((blocks, LINES - 1)),
            dma((blocks, 2)),
            dma((2,)),
            dma((2,)),
            dma((5, 2)),
            dma((4,)),
            dma((1,)),
        ],
        compiler_params=pltpu.CompilerParams(
            vmem_limit_bytes=56 * 2**20, collective_id=4, has_side_effects=True
        ),
        cost_estimate=NO_COST,
    )(far, cross, own, line_sums, line_got, first, small, merged, weight, tokens, resid, gain)


def rms_forward(values, gain_vec):
    inv_rms = lax.rsqrt(jnp.mean(values * values, axis=-1, keepdims=True) + EPSILON)
    return (values * inv_rms * gain_vec, inv_rms)


def rms_backward(values, inv_rms, gain_vec, upstream):
    weighted = upstream * gain_vec
    inner_sum = jnp.mean(weighted * values, axis=-1, keepdims=True)
    value_grad = inv_rms * weighted - values * inv_rms * inv_rms * inv_rms * inner_sum
    return (value_grad, upstream * values * inv_rms)


def shift_by(values, count, step):
    return lax.ppermute(values, "seq", [(i, (i + step) % count) for i in range(count)])


def cross_core(values, places):
    return lax.ppermute(values, "dp", [(i, i ^ 1) for i in range(places)])


def cross_x(values, places):
    return lax.ppermute(values, "dp", [(i, i ^ 2) for i in range(places)])


def core_sum(pieces, places):
    crossed, terms = [], []
    for far, cross, own in pieces:
        quarter = own.shape[1]
        far = cross_core(far, places)
        crossed.append(cross + far[:, :quarter])
        terms.append([own, far[:, quarter:]])
    return jnp.concatenate(crossed, axis=0), terms


def add_received(terms, received):
    start, longer = 0, []
    for held in terms:
        count = held[0].shape[0]
        longer.append(held + [received[start : start + count]])
        start += count
    return longer


def total_of(terms):
    return jnp.concatenate([sum(term.astype(f32) for term in held) for held in terms], axis=0).astype(bf16)


def sum_seq(values, count):
    if count == 2:
        return values.astype(f32) + shift_by(values, count, 1).astype(f32)
    return lax.psum(values.astype(f32), "seq")


def after(value, *before):
    return lax.optimization_barrier((value, before))[0]


def sum_small(values, places, seq_count):
    step = 1
    while step < places:
        values = values + lax.ppermute(values, "dp", [(i, i ^ step) for i in range(places)])
        step *= 2
    if seq_count == 2:
        return values + shift_by(values, 2, 1)
    return lax.psum(values, "seq")


def body(
    tokens, doc_lengths, variate_ids, time_ids, in_proj, out_proj, gate_up, down_proj,
    attn_gain, ffn_gain, query_gain, key_gain, head_bias, cotangent,
):
    seq_count = lax.axis_size("seq")
    seq_rank = lax.axis_index("seq")
    local_rows, width = tokens.shape
    pack_rows = local_rows * seq_count
    head_dim = query_gain.shape[0]
    places = lax.axis_size("dp")
    place = lax.axis_index("dp")
    core, across = place % 2, place // 2 % 2
    groups = places // 4
    spot = jnp.stack(
        [core, across]
        + [
            group * 4 + (across + 1 - near_x) % 2 * 2 + (core + 1 - near_core) % 2
            for near_core in range(2)
            for near_x in range(2)
            for group in range(groups)
        ]
    ).astype(jnp.int32)

    gains = jnp.stack([attn_gain, ffn_gain], axis=1)
    gather = lambda w: lax.all_gather(w, "dp", axis=0, tiled=True)
    first_shard = jnp.concatenate(
        [in_proj, out_proj, jnp.pad(gains, ((0, 0), (0, PAIR - 2)))], axis=1
    )
    fused = places == 16 and seq_count == 2
    if fused:
        wide, *there = gather_first(first_shard, tokens, time_ids.reshape(-1, PAIR), places)
        slots = [(tokens, time_ids), (there[0], there[1].reshape(-1))]
    else:
        wide = gather(first_shard)
        slots = [(tokens, time_ids)]
        for step in range(1, seq_count):
            slots.append(tuple(shift_by(array, seq_count, -step) for array in slots[0]))
    out_full = wide[:, 3 * width : 4 * width]
    attn_gain_f = wide[:, 4 * width].astype(f32)[None, :]
    ffn_gain_f = wide[:, 4 * width + 1].astype(f32)[None, :]
    shard = in_proj.shape[0]
    hidden_part = down_proj.shape[0] // 2
    columns = gate_up.reshape(shard, 2, places, 2, hidden_part)
    folds = down_proj.reshape(2, hidden_part // shard, shard, width)
    ffn_weights = []
    for part in range(2):
        piece = jnp.concatenate(
            [columns[:, 0, :, part].reshape(shard, -1), columns[:, 1, :, part].reshape(shard, -1)]
            + [folds[part, k] for k in range(hidden_part // shard)],
            axis=1,
        )
        ffn_weights.append(piece)
    ffn_weights[0] = gather(after(ffn_weights[0], wide))

    positions = jnp.arange(pack_rows, dtype=jnp.int32)
    first_end = doc_lengths[0, 0]
    second_end = first_end + doc_lengths[0, 1]
    segment = (positions >= first_end).astype(jnp.int32) + (positions >= second_end).astype(jnp.int32)
    query_columns, key_columns = slot_columns(segment, variate_ids[0])
    coefficients = bias_columns(head_bias)
    start = seq_rank * local_rows
    query_columns = lax.dynamic_slice_in_dim(query_columns, start, local_rows)
    local_segment = lax.dynamic_slice_in_dim(segment, start, local_rows)
    valid_rows = (local_segment < 2).astype(f32)
    source_columns, source_flags = [], []
    for step in range(seq_count):
        begin = ((seq_rank + step) % seq_count) * local_rows
        source_columns.append(lax.dynamic_slice_in_dim(key_columns, begin, local_rows))
        there = lax.dynamic_slice_in_dim(segment, begin, local_rows).reshape(-1, KEY_ROWS)
        source_flags.append(
            ((there[:, 0] <= local_segment[-1]) & (there[:, -1] >= local_segment[0])).astype(jnp.int32)
        )

    half_dim = head_dim // 2
    frequency = jnp.exp(jnp.arange(half_dim, dtype=f32) * (-math.log(ROPE_BASE) / half_dim))
    qgain = jnp.tile(query_gain, 2)[None, :]
    kgain = jnp.tile(key_gain, 2)[None, :]

    def rope_tables(times):
        angles = times.astype(f32)[:, None] * jnp.tile(frequency, 4)[None, :]
        sign = jnp.where(jnp.arange(PAIR) % head_dim < half_dim, -1.0, 1.0)
        return jnp.cos(angles), jnp.sin(angles) * sign[None, :]

    tables = [rope_tables(times) for _, times in slots]
    seed_grad = cotangent.astype(f32) * valid_rows[:, None]
    seed_low = seed_grad.astype(bf16)
    keyed = []
    for step, (there_tokens, _) in enumerate(slots):
        keys, values, *own = project(
            there_tokens, attn_gain_f, wide, *tables[step], qgain, kgain, step == 0
        )
        keyed.append((keys, values, source_columns[step]))
        if step == 0:
            cosine, sine = tables[0]
            queries, *raws, normed_low = own
            ffn_weights[1] = gather(after(ffn_weights[1], queries))
    attended, full_query = attend(
        jnp.concatenate(source_flags), queries, query_columns, coefficients, keyed
    )

    inputs_f = tokens.astype(f32)
    residual = inputs_f + dot(attended, out_full)
    normed_ffn, ffn_scale = rms_forward(residual, ffn_gain_f)
    normed_ffn_low = normed_ffn.astype(bf16)
    def x_part(received, own, far):
        total = received.astype(f32) + own.astype(f32) + far[groups:].astype(f32)
        return total.astype(bf16)

    def scatter_line(parts):
        lines = [[line * 4 + k for line in range(groups)] for k in range(4)]
        return lax.psum_scatter(parts, "dp", scatter_dimension=0, axis_index_groups=lines, tiled=True)[0]

    branch, normed_ffn_grad, *grads = feed_forward(
        places, normed_ffn_low, seed_low, residual, None, ffn_weights[0]
    )
    far, cross, own = grads
    layer_out, normed_ffn_grad, *grads, received = feed_forward(
        places, normed_ffn_low, seed_low, branch, normed_ffn_grad, ffn_weights[1], cross + far[:groups]
    )
    first_total = scatter_line(x_part(received, own, far))
    far, cross, own = grads
    second_crossed = cross + far[:groups]
    resid_norm_grad, ffn_gain_terms = rms_backward(residual, ffn_scale, ffn_gain_f, normed_ffn_grad)
    residual_grad = seed_grad + resid_norm_grad
    mixed_low = residual_grad.astype(bf16)
    attended_grad = dot(mixed_low, out_full, NT).astype(bf16)

    attended_grad = dot(mixed_low, out_full, NT).astype(bf16)
    out_grads = outer(spot, attended, mixed_low, width)
    folds = hidden_part // shard
    ffn_gain_sum = jnp.sum(ffn_gain_terms, axis=0)

    def merge(dqs, dkvs):
        merged, gains = merge_grads(width, 0, dqs, dkvs, raws, cosine, sine, qgain, kgain)
        return merged, jnp.sum(gains[:2].reshape(2, -1, head_dim), axis=1)

    def small_parts(bias, head_gains):
        same_bias = jnp.sum(bias, axis=-1).reshape(-1)
        tail = jnp.concatenate([head_gains[0], head_gains[1], same_bias])
        return jnp.concatenate([ffn_gain_sum, tail, jnp.zeros(-tail.shape[0] % 1024, f32)])

    if fused:
        (out_far,), out_cross, out_own = (cross_core(out_grads[0], places),), *out_grads[1:]
        by_line = lambda array: array.reshape(groups, -1, width)
        out_sums = [
            by_line(array) for array in (out_cross + out_far[:, : shard * groups], out_own, out_far[:, shard * groups :])
        ]
        dq_all, bias_all, received, own_kv, line_sums, line_got, *_ = attend_back_carry(
            full_query, attended_grad, attended, query_columns, keyed[0], keyed[1],
            (second_crossed, own, far[groups:]), out_sums,
        )
        merged_grad, head_gains = merge([(dq_all, 0), (dq_all, 1)], [(received, 0), (own_kv, 0)])
        in_grads = outer(spot, normed_low, merged_grad, width)
        half = bias_all.shape[0] // 2
        small = small_parts(bias_all[:half] + bias_all[half:], head_gains)
        small = jnp.concatenate([jnp.zeros(width, f32), small]).reshape(-1, PAIR)
        in_sum, first_sum, second_sum, small, input_grad = finish(
            in_grads, line_sums, line_got, first_total, small, merged_grad, wide, tokens,
            residual_grad, attn_gain_f,
        )
        small = small.reshape(-1)
        out_proj_grad = second_sum[3, :, :width]
    else:
        second = scatter_line(x_part(cross_x(second_crossed, places), own, far))
        dqs, dkvs, biases = [], [], 0.0
        for step in list(range(1, seq_count)) + [0]:
            dq, dkv, bias = attend_back(
                0, width // PAIR, source_flags[step], full_query, attended_grad, attended,
                query_columns, *keyed[step],
            )
            dqs.append((dq, 0))
            dkvs.append((shift_by(dkv, seq_count, step) if step else dkv, 0))
            biases = biases + bias
        merged_grad, head_gains = merge(dqs, dkvs)

        def sum_rows(pieces):
            crossed, terms = core_sum([pieces], places)
            total = total_of(add_received(terms, cross_x(crossed, places)))
            total = total.reshape(total.shape[0], groups, shard, -1).transpose(1, 0, 2, 3)
            return sum_seq(scatter_line(total), seq_count)

        in_sum = sum_rows(outer(spot, normed_low, merged_grad, width))
        out_proj_grad = sum_rows(out_grads)[0]
        first_sum = sum_seq(first_total, seq_count)
        second_sum = sum_seq(second, seq_count)
        normed_grad = dot(merged_grad, wide[:, : 3 * width], NT)
        norm_scale = lax.rsqrt(jnp.mean(inputs_f * inputs_f, axis=-1, keepdims=True) + EPSILON)
        input_norm_grad, attn_gain_terms = rms_backward(inputs_f, norm_scale, attn_gain_f, normed_grad)
        input_grad = residual_grad + input_norm_grad
        small = jnp.concatenate([jnp.sum(attn_gain_terms, axis=0), small_parts(biases, head_gains)])
        small = sum_small(small, places, seq_count)
    heads = head_bias.shape[0]
    in_proj_grad = in_sum.transpose(1, 0, 2).reshape(in_proj.shape)
    down_grad = jnp.concatenate(
        [
            part[2].reshape(shard, -1, width).transpose(1, 0, 2).reshape(hidden_part, width)
            for part in (first_sum, second_sum)
        ]
    )
    gate_up_grad = jnp.stack(
        [
            part[:2].reshape(2, shard, places, hidden_part).transpose(1, 0, 2, 3)
            for part in (first_sum, second_sum)
        ],
        axis=3,
    ).reshape(gate_up.shape)
    gain_rows = attn_gain.shape[0]
    here = place * gain_rows
    tail = small[2 * width :]
    same_bias = tail[2 * head_dim : 2 * head_dim + heads]
    return (
        layer_out,
        input_grad,
        in_proj_grad,
        out_proj_grad,
        gate_up_grad,
        down_grad,
        lax.dynamic_slice_in_dim(small, here, gain_rows),
        lax.dynamic_slice_in_dim(small, width + here, gain_rows),
        tail[:head_dim],
        tail[head_dim : 2 * head_dim],
        jnp.stack([same_bias, -same_bias], axis=1),
    )


def solution(mesh):
    in_specs = (
        P(("dp", "seq"), None),
        P("dp", None),
        P("dp", None),
        P(("dp", "seq")),
        P("dp", None),
        P("dp", None),
        P("dp", None),
        P("dp", None),
        P("dp"),
        P("dp"),
        P(),
        P(),
        P(),
        P(("dp", "seq"), None),
    )
    out_specs = (
        P(("dp", "seq"), None),
        P(("dp", "seq"), None),
        P("dp", None),
        P("dp", None),
        P("dp", None),
        P("dp", None),
        P("dp"),
        P("dp"),
        P(),
        P(),
        P(),
    )
    return jax.shard_map(body, mesh=mesh, in_specs=in_specs, out_specs=out_specs, check_vma=False)
```

```python
import functools
import math

import jax
import jax.numpy as jnp
from jax import lax
from jax.experimental import pallas as pl
from jax.experimental.pallas import tpu as pltpu
from jax.sharding import PartitionSpec as P

EPSILON = 1e-06
ROPE_BASE = 10000.0
NEG_FILL = -1e30
PAIR = 128
KEY_ROWS = 256
VMEM_BYTES = 48 * 2**20
NO_COST = pl.CostEstimate(flops=1, bytes_accessed=1, transcendentals=0)
bf16 = jnp.bfloat16
f32 = jnp.float32
NN = (((1,), (0,)), ((), ()))
NT = (((1,), (1,)), ((), ()))
TN = (((0,), (0,)), ((), ()))


def dot(left, right, dims=NN):
    return lax.dot_general(left, right, dims, preferred_element_type=f32)


def split_two(values):
    high = values.astype(bf16)
    return high, (values - high.astype(f32)).astype(bf16)


def lane_index():
    return lax.broadcasted_iota(jnp.int32, (1, PAIR), 1)


def half_ones(same):
    rows = lax.broadcasted_iota(jnp.int32, (2 * PAIR, PAIR), 0) % PAIR
    cols = lax.broadcasted_iota(jnp.int32, (2 * PAIR, PAIR), 1)
    match = (rows < 64) == (cols < 64)
    return jnp.where(match if same else jnp.logical_not(match), 1.0, 0.0).astype(bf16)


def head_sums(values, ones):
    return dot(jnp.concatenate(split_two(values), axis=1), ones)


def swap_halves(values):
    first = lane_index() % 64 < 32
    return jnp.where(first, pltpu.roll(values, PAIR - 32, 1), pltpu.roll(values, 32, 1))


LINES = 4


def line_device(place, line):
    return {"dp": line * 4 + place % 4}


class Spread:
    def __init__(self, shard_ref, whole_ref, arrived, sent, kept):
        self.shard_ref, self.whole_ref = shard_ref, whole_ref
        self.arrived, self.sent, self.kept = arrived, sent, kept
        self.place = place = lax.axis_index("dp")
        self.z, self.x, self.core = place // 4, place // 2 % 2, place % 2
        self.lines = whole_ref.shape[0] // shard_ref.shape[0] // 4
        self.ends = (self.z == 0).astype(jnp.int32) + (self.z == self.lines - 1).astype(jnp.int32)
        self.up, self.down = {"dp": place + 4}, {"dp": place - 4}
        self.over = {"dp": place + 2 - self.x * 4}
        self.twin = {"dp": place + 1 - self.core * 2}
        self.not_last, self.not_first = self.z < self.lines - 1, self.z > 0

    def greet(self, barrier):
        def one(target):
            pl.semaphore_signal(barrier, inc=1, device_id=target, device_id_type=pl.DeviceIdType.MESH)

        pl.when(self.not_last)(lambda: one(self.up))
        pl.when(self.not_first)(lambda: one(self.down))

    def block(self, z, x, core):
        return z * 4 + x * 2 + core

    def rows_of(self, which):
        rows = self.shard_ref.shape[0]
        return self.whole_ref.at[pl.ds(pl.multiple_of(which * rows, rows), rows)]

    def copy(self, which, path, own=False):
        return pltpu.make_async_remote_copy(
            src_ref=self.shard_ref if own else self.rows_of(which),
            dst_ref=self.rows_of(which),
            send_sem=self.sent.at[path, which],
            recv_sem=self.arrived.at[which],
            device_id=(self.up, self.over, self.twin, self.down)[path],
            device_id_type=pl.DeviceIdType.MESH,
        )

    def stay(self):
        me = self.block(self.z, self.x, self.core)
        return pltpu.make_async_copy(self.shard_ref, self.rows_of(me), self.kept.at[0])

    def begin(self):
        me = self.block(self.z, self.x, self.core)
        pl.when(self.not_last)(lambda: self.copy(me, 0, True).start())
        pl.when(self.not_first)(lambda: self.copy(me, 3, True).start())
        self.copy(me, 1, True).start()
        self.copy(me, 2, True).start()
        self.stay().start()

    def along(self, step):
        def take(which, path, more):
            self.copy(which, path).wait_recv()
            pl.when(more)(lambda: self.copy(which, path).start())
            self.copy(which, 1).start()
            self.copy(which, 2).start()

        pl.when(self.z >= step)(
            lambda: take(self.block(self.z - step, self.x, self.core), 0, self.not_last)
        )
        pl.when(self.z + step < self.lines)(
            lambda: take(self.block(self.z + step, self.x, self.core), 3, self.not_first)
        )

    def to_twin(self):
        for line in range(self.lines):
            which = self.block(line, 1 - self.x, self.core)
            self.copy(which, 1).wait_recv()
            self.copy(which, 2).start()

    def end(self):
        for line in range(self.lines):
            for side in range(2):
                self.copy(self.block(line, side, 1 - self.core), 2).wait_recv()
        for line in range(self.lines):
            which = self.block(line, self.x, self.core)
            self.copy(which, 1).wait_send()
            self.copy(which, 2).wait_send()
            self.copy(self.block(line, 1 - self.x, self.core), 2).wait_send()
            pl.when((line <= self.z) & self.not_last)(lambda: self.copy(which, 0).wait_send())
            pl.when((line >= self.z) & self.not_first)(lambda: self.copy(which, 3).wait_send())
        self.stay().wait()


def gather_kernel(
    shard_ref, tokens_ref, times_ref, wide_ref, there_tokens_ref, there_times_ref, arrived, sent, kept, swapped
):
    other = {"seq": 1 - lax.axis_index("seq")}
    spread = Spread(shard_ref, wide_ref, arrived, sent, kept)
    barrier = pltpu.get_barrier_semaphore()
    for target in (spread.over, spread.twin, other):
        pl.semaphore_signal(barrier, inc=1, device_id=target, device_id_type=pl.DeviceIdType.MESH)
    spread.greet(barrier)
    pl.semaphore_wait(barrier, 5 - spread.ends)

    def swap(source, target, index):
        return pltpu.make_async_remote_copy(
            src_ref=source,
            dst_ref=target,
            send_sem=swapped.at[index],
            recv_sem=swapped.at[index + 1],
            device_id=other,
            device_id_type=pl.DeviceIdType.MESH,
        )

    swaps = [swap(tokens_ref, there_tokens_ref, 0), swap(times_ref, there_times_ref, 2)]
    spread.begin()
    for each in swaps:
        each.start()
    for step in range(1, spread.lines):
        spread.along(step)
    spread.to_twin()
    spread.end()
    for each in swaps:
        each.wait()


def gather_first(shard, tokens, times, places):
    anywhere = pl.BlockSpec(memory_space=pl.ANY)
    return pl.pallas_call(
        gather_kernel,
        in_specs=[anywhere] * 3,
        out_specs=[anywhere] * 3,
        out_shape=[
            jax.ShapeDtypeStruct((shard.shape[0] * places, shard.shape[1]), shard.dtype),
            jax.ShapeDtypeStruct(tokens.shape, tokens.dtype),
            jax.ShapeDtypeStruct(times.shape, times.dtype),
        ],
        scratch_shapes=[
            pltpu.SemaphoreType.DMA((places,)),
            pltpu.SemaphoreType.DMA((4, places)),
            pltpu.SemaphoreType.DMA((1,)),
            pltpu.SemaphoreType.DMA((4,)),
        ],
        compiler_params=pltpu.CompilerParams(collective_id=0, has_side_effects=True),
        cost_estimate=NO_COST,
    )(shard, tokens, times)


def qkv_kernel(
    tokens_ref, gain_ref, weight_ref, cos_ref, sin_ref, qgain_ref, kgain_ref,
    k_ref, v_ref, *own_refs,
):
    width = tokens_ref.shape[1]
    values = tokens_ref[...].astype(f32)
    inv = lax.rsqrt(jnp.mean(values * values, axis=-1, keepdims=True) + EPSILON)
    normed = (values * inv * gain_ref[...]).astype(bf16)
    ones = half_ones(True)
    cosine, sine = cos_ref[...], sin_ref[...]
    turned = [(1, k_ref, kgain_ref[...], 1.0)]
    if own_refs:
        q_ref, *raw_refs, normed_ref = own_refs
        normed_ref[...] = normed
        turned.append((0, q_ref, qgain_ref[...], 0.125))
    for part, out_ref, head_gain, scale in turned:
        for chunk in range(width // 256):
            start = part * width + chunk * 256
            raw = dot(normed, weight_ref[:, start : start + 256])
            if own_refs:
                raw_refs[part][:, chunk * 256 : (chunk + 1) * 256] = raw
            for tile in range(2):
                u = raw[:, tile * PAIR : (tile + 1) * PAIR]
                unit = lax.rsqrt(head_sums(u * u, ones) * (1.0 / 64) + EPSILON)
                u = u * unit * head_gain
                u = u * cosine + swap_halves(u) * sine
                at = chunk * 256 + tile * PAIR
                out_ref[:, at : at + PAIR] = (u * scale).astype(bf16)
    for chunk in range(width // 256):
        start = 2 * width + chunk * 256
        v_ref[:, chunk * 256 : (chunk + 1) * 256] = dot(
            normed, weight_ref[:, start : start + 256]
        ).astype(bf16)


def project(tokens, gain, weight, cosine, sine, qgain, kgain, own, block=256):
    rows, width = tokens.shape
    sizes = [(width, bf16), (width, bf16)]
    if own:
        sizes += [(width, bf16), (width, f32), (width, f32), (width, bf16)]
    by_rows = lambda i: (i, 0)
    whole = lambda i: (0, 0)
    return pl.pallas_call(
        qkv_kernel,
        grid=(rows // block,),
        in_specs=[
            pl.BlockSpec((block, width), by_rows),
            pl.BlockSpec((1, width), whole),
            pl.BlockSpec((width, 3 * width), whole, pipeline_mode=pl.Buffered(1)),
            pl.BlockSpec((block, PAIR), by_rows),
            pl.BlockSpec((block, PAIR), by_rows),
            pl.BlockSpec((1, PAIR), whole),
            pl.BlockSpec((1, PAIR), whole),
        ],
        out_specs=[pl.BlockSpec((block, size), by_rows) for size, _ in sizes],
        out_shape=[jax.ShapeDtypeStruct((rows, size), kind) for size, kind in sizes],
        compiler_params=pltpu.CompilerParams(vmem_limit_bytes=VMEM_BYTES),
        cost_estimate=NO_COST,
    )(tokens, gain, weight, cosine, sine, qgain, kgain)


def merge_kernel(sources, parts, *refs):
    dq_refs = refs[:parts]
    dkv_refs = refs[parts : parts + sources]
    rawq_ref, rawk_ref, cos_ref, sin_ref, qgain_ref, kgain_ref, out_ref, gains_ref = refs[parts + sources :]
    width = dq_refs[0].shape[1]
    ones = half_ones(True)
    cosine, sine = cos_ref[...], sin_ref[...]

    @pl.when(pl.program_id(0) == 0)
    def _():
        gains_ref[...] = jnp.zeros_like(gains_ref)

    def read(part, at):
        found = [ref[:, at] for ref in dq_refs] if part == 0 else [ref[part - 1, :, at] for ref in dkv_refs]
        return sum(value.astype(f32) for value in found).astype(bf16)

    for part, (raw_ref, head_gain) in enumerate(((rawq_ref, qgain_ref[...]), (rawk_ref, kgain_ref[...]))):
        for tile in range(width // PAIR):
            at = slice(tile * PAIR, (tile + 1) * PAIR)
            grad = read(part, at).astype(f32)
            grad = grad * cosine - swap_halves(grad) * sine
            raw = raw_ref[:, at]
            unit = lax.rsqrt(head_sums(raw * raw, ones) * (1.0 / 64) + EPSILON)
            hat = raw * unit
            gains_ref[part : part + 1, at] += jnp.sum(grad * hat, axis=0, keepdims=True)
            weighted = grad * head_gain
            inner = head_sums(weighted * hat, ones) * (1.0 / 64)
            there = slice(part * width + tile * PAIR, part * width + (tile + 1) * PAIR)
            out_ref[:, there] = (unit * (weighted - hat * inner)).astype(bf16)
    out_ref[:, 2 * width :] = read(2, slice(0, width))


def merge_grads(width, at, dqs, dkvs, raws, cosine, sine, qgain, kgain, block=256):
    rows = raws[0].shape[0]
    by_rows = lambda i: (i, 0)
    whole = lambda i: (0, 0)
    cut = lambda index: pl.BlockSpec((block, width), lambda i: (i, index))
    cut_two = lambda index: pl.BlockSpec((2, block, width), lambda i: (0, i, index))
    return pl.pallas_call(
        functools.partial(merge_kernel, len(dkvs), len(dqs)),
        grid=(rows // block,),
        in_specs=[cut(index) for _, index in dqs]
        + [cut_two(index) for _, index in dkvs]
        + [
            cut(at),
            cut(at),
            pl.BlockSpec((block, PAIR), by_rows),
            pl.BlockSpec((block, PAIR), by_rows),
            pl.BlockSpec((1, PAIR), whole),
            pl.BlockSpec((1, PAIR), whole),
        ],
        out_specs=[pl.BlockSpec((block, 3 * width), by_rows), pl.BlockSpec((8, width), whole)],
        out_shape=[
            jax.ShapeDtypeStruct((rows, 3 * width), bf16),
            jax.ShapeDtypeStruct((8, width), f32),
        ],
        compiler_params=pltpu.CompilerParams(vmem_limit_bytes=VMEM_BYTES),
        cost_estimate=NO_COST,
    )(*[array for array, _ in dqs], *[array for array, _ in dkvs], *raws, cosine, sine, qgain, kgain)


def forward_kernel(sources, query_rows, flags, q_ref, aq_ref, coef_ref, *refs):
    keyed = refs[: 3 * sources]
    out_ref, full_ref, query, total = refs[3 * sources :]
    rows = q_ref.shape[0]
    lane = lane_index()
    half = lane < 64
    mine = (half, jnp.logical_not(half))
    both = q_ref[...]
    extra = aq_ref[...]
    for h in range(2):
        query[h] = jnp.where(mine[h], both, extra * coef_ref[0, h : h + 1, :])
        total[h] = jnp.zeros_like(total[h])
    blocks = keyed[0].shape[0] // KEY_ROWS
    for j in range(sources):
        k_ref, v_ref, ak_ref = keyed[3 * j : 3 * j + 3]
        for b in range(blocks):

            @pl.when(flags[j * blocks + b] != 0)
            def _():
                at = slice(b * KEY_ROWS, (b + 1) * KEY_ROWS)
                keys, values, columns = k_ref[at, :], v_ref[at, :], ak_ref[at, :]
                ones = jnp.ones_like(values)
                keys2 = [jnp.where(mine[h], keys, columns) for h in range(2)]
                values2 = [jnp.where(mine[h], values, ones) for h in range(2)]
                for i in range(rows // query_rows):
                    part = slice(i * query_rows, (i + 1) * query_rows)
                    for h in range(2):
                        probs = jnp.exp(dot(query[h, part, :], keys2[h], NT)).astype(bf16)
                        total[h, part, :] += dot(probs, values2[h])

    outs = []
    for h in range(2):
        summed = total[h]
        outs.append(summed / pltpu.roll(summed, 64, 1))
        log_total = jnp.log(jnp.maximum(summed, 1e-30))
        high = log_total.astype(bf16)
        mid, low = split_two(log_total - high.astype(f32))
        base = lane - 64 if h == 0 else lane
        full_ref[:, h * PAIR : (h + 1) * PAIR] = jnp.where(
            base == 11, -high, jnp.where(base == 12, -mid, jnp.where(base == 13, -low, query[h]))
        )
    out_ref[...] = jnp.where(half, outs[0], outs[1]).astype(bf16)


def attend(flags, queries, query_columns, coefficients, keyed):
    rows, width = queries.shape
    pairs = width // PAIR
    key_rows = keyed[0][0].shape[0]
    sources = len(keyed)
    by_pair = lambda p, f: (0, p)
    whole = lambda p, f: (0, 0)
    in_specs = [
        pl.BlockSpec((rows, PAIR), by_pair),
        pl.BlockSpec((rows, PAIR), whole),
        pl.BlockSpec((1, 2, PAIR), lambda p, f: (p, 0, 0)),
    ]
    operands = [queries, query_columns, coefficients]
    for keys, values, columns in keyed:
        in_specs += [
            pl.BlockSpec((key_rows, PAIR), by_pair),
            pl.BlockSpec((key_rows, PAIR), by_pair),
            pl.BlockSpec((key_rows, PAIR), whole),
        ]
        operands += [keys, values, columns]
    return pl.pallas_call(
        functools.partial(forward_kernel, sources, min(512, rows)),
        grid_spec=pltpu.PrefetchScalarGridSpec(
            num_scalar_prefetch=1,
            grid=(pairs,),
            in_specs=in_specs,
            out_specs=[
                pl.BlockSpec((rows, PAIR), by_pair),
                pl.BlockSpec((rows, 2 * PAIR), by_pair),
            ],
            scratch_shapes=[
                pltpu.VMEM((2, rows, PAIR), bf16),
                pltpu.VMEM((2, rows, PAIR), f32),
            ],
        ),
        out_shape=[
            jax.ShapeDtypeStruct((rows, width), bf16),
            jax.ShapeDtypeStruct((rows, 2 * width), bf16),
        ],
        compiler_params=pltpu.CompilerParams(vmem_limit_bytes=VMEM_BYTES),
        cost_estimate=NO_COST,
    )(flags, *operands)


def backward_start(grad_ref, out_ref, grads, dq_total):
    lane = lane_index()
    half = lane < 64
    mine = (half, jnp.logical_not(half))
    base = (lane - 64, lane)
    both = grad_ref[...]
    row_total = head_sums(both.astype(f32) * out_ref[...].astype(f32), half_ones(False))
    high, low = split_two(row_total)
    zero = jnp.zeros_like(high)
    for h in range(2):
        extra = jnp.where(base[h] == 0, -high, jnp.where(base[h] == 1, -low, zero))
        grads[h] = jnp.where(mine[h], both, extra)
        dq_total[h] = jnp.zeros_like(dq_total[h])


def backward_block(full_ref, keys, values, columns, grads, dq_total):
    lane = lane_index()
    half = lane < 64
    mine = (half, jnp.logical_not(half))
    base = (lane - 64, lane)
    ones = jnp.ones_like(values)
    dks, dvs = [], []
    for h in range(2):
        keys2 = jnp.where(mine[h], keys, columns)
        pick = (base[h] >= 0) & (base[h] < 2)
        values2 = jnp.where(mine[h], values, jnp.where(pick, ones, jnp.zeros_like(ones)))
        full = full_ref[:, h * PAIR : (h + 1) * PAIR]
        probs = jnp.exp(dot(keys2, full, NT))
        score_low = (probs * dot(values2, grads[h], NT)).astype(bf16)
        dks.append(dot(score_low, full))
        dvs.append(dot(probs.astype(bf16), grads[h]))
        dq_total[h] += dot(keys2, score_low, TN)
    return (
        jnp.where(half, dks[0], dks[1]).astype(bf16),
        jnp.where(half, dvs[0], dvs[1]).astype(bf16),
    )


def backward_end(aq_ref, dq_ref, bias_ref, dq_total):
    lane = lane_index()
    base = (lane - 64, lane)
    dq = [dq_total[h].T for h in range(2)]
    dq_ref[...] = (jnp.where(lane < 64, dq[0], dq[1]) * 0.125).astype(dq_ref.dtype)
    variates = aq_ref[...].astype(f32)
    for h in range(2):
        pick = (base[h] >= 0) & (base[h] < 4)
        bias_ref[0, h : h + 1, :] = jnp.sum(
            jnp.where(pick, dq[h] * variates, 0.0), axis=0, keepdims=True
        )


def backward_kernel(
    flags, full_ref, grad_ref, out_ref, aq_ref, k_ref, v_ref, ak_ref,
    dq_ref, dkv_ref, bias_ref, grads, dq_total,
):
    backward_start(grad_ref, out_ref, grads, dq_total)
    for b in range(k_ref.shape[0] // KEY_ROWS):
        at = slice(b * KEY_ROWS, (b + 1) * KEY_ROWS)

        @pl.when(flags[b] != 0)
        def _():
            dkv_ref[0, at, :], dkv_ref[1, at, :] = backward_block(
                full_ref, k_ref[at, :], v_ref[at, :], ak_ref[at, :], grads, dq_total
            )

        @pl.when(flags[b] == 0)
        def _():
            dkv_ref[:, at, :] = jnp.zeros((2, KEY_ROWS, PAIR), bf16)

    backward_end(aq_ref, dq_ref, bias_ref, dq_total)


def attend_back(first_pair, pairs, flags, full, grad, out, query_columns, keys, values, key_columns):
    rows = grad.shape[0]
    width = pairs * PAIR
    key_rows = keys.shape[0]
    by_pair = lambda p, f: (0, p)
    from_pair = lambda p, f: (0, first_pair + p)
    whole = lambda p, f: (0, 0)
    return pl.pallas_call(
        backward_kernel,
        grid_spec=pltpu.PrefetchScalarGridSpec(
            num_scalar_prefetch=1,
            grid=(pairs,),
            in_specs=[
                pl.BlockSpec((rows, 2 * PAIR), from_pair),
                pl.BlockSpec((rows, PAIR), from_pair),
                pl.BlockSpec((rows, PAIR), from_pair),
                pl.BlockSpec((rows, PAIR), whole),
                pl.BlockSpec((key_rows, PAIR), from_pair),
                pl.BlockSpec((key_rows, PAIR), from_pair),
                pl.BlockSpec((key_rows, PAIR), whole),
            ],
            out_specs=[
                pl.BlockSpec((rows, PAIR), by_pair),
                pl.BlockSpec((2, key_rows, PAIR), lambda p, f: (0, 0, p)),
                pl.BlockSpec((1, 2, PAIR), lambda p, f: (p, 0, 0)),
            ],
            scratch_shapes=[
                pltpu.VMEM((2, rows, PAIR), bf16),
                pltpu.VMEM((2, PAIR, rows), f32),
            ],
        ),
        out_shape=[
            jax.ShapeDtypeStruct((rows, width), f32),
            jax.ShapeDtypeStruct((2, key_rows, width), bf16),
            jax.ShapeDtypeStruct((pairs, 2, PAIR), f32),
        ],
        compiler_params=pltpu.CompilerParams(vmem_limit_bytes=VMEM_BYTES),
        cost_estimate=NO_COST,
    )(flags, full, grad, out, query_columns, keys, values, key_columns)


STARTS = (0, 7, 19, 33, 47)
ARRIVALS = (10, 23, 37, 50, 62)


def carry_kernel(
    pairs, full_ref, grad_ref, out_ref, aq_ref,
    far_k_ref, far_v_ref, far_ak_ref, near_k_ref, near_v_ref, near_ak_ref,
    early_across_ref, early_own_ref, early_far_ref, across_ref, own_ref, far_ref,
    out_across_ref, out_own_ref, out_far_ref,
    dq_ref, bias_ref, got_ref, near_ref, line_ref, line_got_ref, late_ref, early_got, across_got, out_got,
    grads, dq_total, stage, terms, sums,
    send_sems, recv_sems, near_sems, across_sems, term_sems, line_send, line_recv, line_own,
):
    step = pl.program_id(0)
    place, rank = lax.axis_index("dp"), lax.axis_index("seq")
    line = place // 4
    other = {"seq": 1 - rank}
    over = {"dp": place + 2 - place // 2 % 2 * 4}
    mesh_id = pl.DeviceIdType.MESH

    def lanes(index):
        return pl.ds(pl.multiple_of(index * PAIR, PAIR), PAIR)

    last = len(STARTS) - 1

    def part_of(refs, part):
        if part == last:
            return refs[0]
        return refs[2] if part == 0 else refs[1].at[:, part - 1]

    def width_of(part):
        return out_own_ref.shape[2] if part == 0 else sums.shape[3]

    def across(part):
        return pltpu.make_async_remote_copy(
            src_ref=part_of((early_across_ref, across_ref, out_across_ref), part),
            dst_ref=part_of((early_got, across_got, out_got), part),
            send_sem=across_sems.at[part, 0], recv_sem=across_sems.at[part, 1],
            device_id=over, device_id_type=mesh_id,
        )

    def load(part, k):
        if k == 0:
            source = part_of((early_own_ref.at[:, 2], own_ref, out_own_ref), part)
        elif k == 1:
            near = pl.ds(LINES, LINES)
            source = part_of((early_far_ref.at[near, 2], far_ref.at[near], out_far_ref), part)
        else:
            source = part_of((early_got, across_got, out_got), part)
        return pltpu.make_async_copy(
            source, terms.at[k, :, :, pl.ds(0, width_of(part))], term_sems.at[k]
        )

    def along(part, k):
        to = lax.rem(line + k, LINES)
        columns = pl.ds(0, width_of(part))
        return pltpu.make_async_remote_copy(
            src_ref=sums.at[part, to, :, columns], dst_ref=line_got_ref.at[k - 1, part, :, columns],
            send_sem=line_send.at[part, k - 1], recv_sem=line_recv.at[part, k - 1],
            device_id=line_device(place, to), device_id_type=mesh_id,
        )

    def stay(part):
        if part == last:
            return pltpu.make_async_copy(sums.at[part], late_ref, line_own.at[part])
        columns = pl.ds(0, width_of(part))
        return pltpu.make_async_copy(
            sums.at[part, line, :, columns], line_ref.at[part, :, columns], line_own.at[part]
        )

    def to_other(pair):
        return pltpu.make_async_remote_copy(
            src_ref=stage.at[pair], dst_ref=got_ref.at[:, :, lanes(pair)], send_sem=send_sems.at[pair],
            recv_sem=recv_sems.at[pair], device_id=other, device_id_type=mesh_id,
        )

    def to_near(pair):
        return pltpu.make_async_copy(
            stage.at[pairs + pair], near_ref.at[:, :, lanes(pair)], near_sems.at[pair]
        )

    @pl.when(step == 0)
    def _():
        barrier = pltpu.get_barrier_semaphore()
        peers = [other, over] + [line_device(place, lax.rem(line + k, LINES)) for k in range(1, LINES)]
        for target in peers:
            pl.semaphore_signal(barrier, inc=1, device_id=target, device_id_type=mesh_id)
        pl.semaphore_wait(barrier, len(peers))

    def arrive(part):
        across(part).wait()
        load(part, 2).start()
        for k in range(3):
            load(part, k).wait()
        columns = width_of(part)
        for i in range(LINES):
            sums[part, i, :, :columns] = sum(
                terms[k, i, :, :columns].astype(f32) for k in range(3)
            ).astype(bf16)
        if part < last:
            for k in range(1, LINES):
                along(part, k).start()
        stay(part).start()

    def go_on(quarter):
        for part in range(last + 1):

            before = ARRIVALS[part] - 3
            if STARTS[part] % 4 == quarter:

                @pl.when(step == STARTS[part] // 4)
                def _():
                    across(part).start()

            if before % 4 == quarter:

                @pl.when(step == before // 4)
                def _():
                    load(part, 0).start()
                    load(part, 1).start()

            if ARRIVALS[part] % 4 == quarter:
                pl.when(step == ARRIVALS[part] // 4)(functools.partial(arrive, part))

    backward_start(grad_ref, out_ref, grads, dq_total)
    is_far = step < pairs
    for b in range(far_k_ref.shape[0] // KEY_ROWS):
        at = slice(b * KEY_ROWS, (b + 1) * KEY_ROWS)
        go_on(b)
        block = [
            jnp.where(is_far, far[at, :], near[at, :])
            for far, near in ((far_k_ref, near_k_ref), (far_v_ref, near_v_ref), (far_ak_ref, near_ak_ref))
        ]
        stage[step, 0, at, :], stage[step, 1, at, :] = backward_block(
            full_ref, *block, grads, dq_total
        )

    backward_end(aq_ref, dq_ref, bias_ref, dq_total)
    pl.when(is_far)(lambda: to_other(step).start())
    pl.when(jnp.logical_not(is_far))(lambda: to_near(step - pairs).start())

    @pl.when(step == pl.num_programs(0) - 1)
    def _():
        for pair in range(pairs):
            to_near(pair).wait()
            to_other(pair).wait()
        for part in range(last + 1):
            if part < last:
                for k in range(1, LINES):
                    along(part, k).wait()
            stay(part).wait()


def attend_back_carry(full, grad, out, query_columns, near, far, early, sums, out_sums):
    rows, width = grad.shape
    pairs = width // PAIR
    key_rows = near[0].shape[0]
    pair_of = lambda i: jnp.where(i < pairs, i, i - pairs)
    by_pair = lambda i: (0, pair_of(i))
    far_pair = lambda i: (0, jnp.minimum(i, pairs - 1))
    near_pair = lambda i: (0, jnp.maximum(i - pairs, 0))
    whole = lambda i: (0, 0)
    anywhere = pl.BlockSpec(memory_space=pl.ANY)
    shard, hidden = sums[0].shape[2:]
    parts = len(STARTS)

    def key_specs(pair):
        return [
            pl.BlockSpec((key_rows, PAIR), pair),
            pl.BlockSpec((key_rows, PAIR), pair),
            pl.BlockSpec((key_rows, PAIR), whole),
        ]

    return pl.pallas_call(
        functools.partial(carry_kernel, pairs),
        grid=(2 * pairs,),
        in_specs=[
            pl.BlockSpec((rows, 2 * PAIR), by_pair),
            pl.BlockSpec((rows, PAIR), by_pair),
            pl.BlockSpec((rows, PAIR), by_pair),
            pl.BlockSpec((rows, PAIR), whole),
        ]
        + key_specs(far_pair)
        + key_specs(near_pair)
        + [anywhere] * 9,
        out_specs=[
            pl.BlockSpec((rows, PAIR), lambda i: (0, i)),
            pl.BlockSpec((1, 2, PAIR), lambda i: (i, 0, 0)),
        ]
        + [anywhere] * 8,
        out_shape=[
            jax.ShapeDtypeStruct((rows, 2 * width), bf16),
            jax.ShapeDtypeStruct((2 * pairs, 2, PAIR), f32),
            jax.ShapeDtypeStruct((2, key_rows, width), bf16),
            jax.ShapeDtypeStruct((2, key_rows, width), bf16),
            jax.ShapeDtypeStruct((parts - 1, shard, hidden), bf16),
            jax.ShapeDtypeStruct((LINES - 1, parts - 1, shard, hidden), bf16),
            jax.ShapeDtypeStruct((LINES, shard, hidden), bf16),
            jax.ShapeDtypeStruct(early[0].shape, bf16),
            jax.ShapeDtypeStruct(sums[0].shape, bf16),
            jax.ShapeDtypeStruct(out_sums[0].shape, bf16),
        ],
        scratch_shapes=[
            pltpu.VMEM((2, rows, PAIR), bf16),
            pltpu.VMEM((2, PAIR, rows), f32),
            pltpu.VMEM((2 * pairs, 2, key_rows, PAIR), bf16),
            pltpu.VMEM((3, LINES, shard, hidden), bf16),
            pltpu.VMEM((parts, LINES, shard, hidden), bf16),
            pltpu.SemaphoreType.DMA((pairs,)),
            pltpu.SemaphoreType.DMA((pairs,)),
            pltpu.SemaphoreType.DMA((pairs,)),
            pltpu.SemaphoreType.DMA((parts, 2)),
            pltpu.SemaphoreType.DMA((3,)),
            pltpu.SemaphoreType.DMA((parts - 1, LINES - 1)),
            pltpu.SemaphoreType.DMA((parts - 1, LINES - 1)),
            pltpu.SemaphoreType.DMA((parts,)),
        ],
        compiler_params=pltpu.CompilerParams(
            vmem_limit_bytes=VMEM_BYTES, collective_id=3, has_side_effects=True
        ),
        cost_estimate=NO_COST,
    )(full, grad, out, query_columns, *far, *near, *early, *sums, *out_sums)


def slot_columns(segment, variates):
    column = jnp.arange(PAIR, dtype=jnp.int32)[None, :] % 64
    same_var = (column < 8) & (variates[:, None] == column % 4)
    in_seg = (column >= 8) & (column < 11)
    same_seg = segment[:, None] == column - 8
    three = (column >= 11) & (column < 14)
    query = jnp.where(in_seg & jnp.logical_not(same_seg), NEG_FILL, same_var.astype(f32))
    key = (same_var | (in_seg & same_seg) | three).astype(f32)
    return query.astype(bf16), key.astype(bf16)


def bias_columns(head_bias):
    delta = head_bias[:, 0] - head_bias[:, 1]
    high, low = split_two(delta)
    heads = delta.shape[0]
    row = jnp.concatenate(
        [
            jnp.broadcast_to(high[:, None], (heads, 4)),
            jnp.broadcast_to(low[:, None], (heads, 4)),
            jnp.ones((heads, 3), bf16),
            jnp.zeros((heads, 53), bf16),
        ],
        1,
    )
    return jnp.concatenate([row, row], 1).reshape(heads // 2, 2, PAIR)


def arrange_rows(places, spot, left_ref, turned, arranged):
    shard = left_ref.shape[1] // places
    turned[...] = left_ref[...].T
    for i in range(places):
        at = pl.multiple_of(spot[2 + i] * shard, shard)
        arranged[i * shard : (i + 1) * shard, :] = turned[pl.ds(at, shard), :]


def ffn_kernel(
    places, first, nf_ref, seed_ref, start_ref, nfstart_ref, wg_ref, wu_ref, wd_ref, *refs
):
    if first:
        branch_ref, nfgrad_ref, far_ref, cross_ref, own_ref, *refs = refs
    else:
        resid_ref, gain_ref, across_ref, branch_ref, nfgrad_ref, *refs = refs
        low_ref, gain_grad_ref, far_ref, cross_ref, own_ref, got_ref, *refs = refs
    turned, branch, columns_out, rows_out, sems, arrived, *x_sems = refs
    step = pl.program_id(0)
    steps = pl.num_programs(0)
    rows, width = nf_ref.shape
    shard = width // places
    chunk = wg_ref.shape[1]
    folds = chunk // 2 // shard

    place = lax.axis_index("dp")
    groups = places // 4

    twin = {"dp": place + 1 - place % 2 * 2}
    over = {"dp": place + 2 - place // 2 % 2 * 4}
    mesh_id = pl.DeviceIdType.MESH

    def carry():
        return pltpu.make_async_remote_copy(
            src_ref=across_ref, dst_ref=got_ref, send_sem=x_sems[0].at[0], recv_sem=x_sems[0].at[1],
            device_id=over, device_id_type=mesh_id,
        )

    @pl.when(step == 0)
    def _():
        barrier = pltpu.get_barrier_semaphore()
        for target in (twin,) if first else (twin, over):
            pl.semaphore_signal(barrier, inc=1, device_id=target, device_id_type=mesh_id)
        pl.semaphore_wait(barrier, 1 if first else 2)
        if not first:
            carry().start()
        turned[...] = nf_ref[...].T
        branch[...] = start_ref[...]
        nfgrad_ref[...] = jnp.zeros_like(nfgrad_ref) if first else nfstart_ref[...]

    def spot_of(line, x, core):
        near_core = (core == place % 2).astype(jnp.int32)
        near_x = (x == place // 2 % 2).astype(jnp.int32)
        return (near_core * 2 + near_x) * groups + line

    def to_twin(source, target, send_sem, recv_sem):
        return pltpu.make_async_remote_copy(
            src_ref=source, dst_ref=target, send_sem=send_sem, recv_sem=recv_sem,
            device_id=twin, device_id_type=mesh_id,
        )

    def column_copies(at):
        slot = lax.rem(at, 2)
        start = pl.multiple_of(at * chunk, chunk)
        made, begin = [], 0
        for k, ref in enumerate((far_ref, cross_ref, own_ref)):
            count = ref.shape[0]
            source = columns_out.at[slot, pl.ds(begin, count)]
            target = ref.at[:, pl.ds(0, 2), :, pl.ds(start, chunk)]
            if k == 0:
                made.append(to_twin(source, target, sems.at[slot, k], arrived.at[at, 0]))
            else:
                made.append(pltpu.make_async_copy(source, target, sems.at[slot, k]))
            begin += count
        return made

    def row_copies(at, ref, index, k):
        slot = lax.rem(at, 2)
        source, target = rows_out.at[slot, k], ref.at[index, 2]
        if k == 0:
            return to_twin(source, target, sems.at[slot, 3], arrived.at[at, 1])
        return pltpu.make_async_copy(source, target, sems.at[slot, 4])

    def sent(copy):
        copy.wait_send() if copy.is_remote else copy.wait()

    def each_copy(at, act):
        for copy in column_copies(at):
            act(copy)
        line, x = at // 2, lax.rem(at, 2)
        near = x == place // 2 % 2
        act(row_copies(at, far_ref, near.astype(jnp.int32) * groups + line, 0))
        pl.when(near)(lambda: act(row_copies(at, own_ref, line, 1)))
        pl.when(jnp.logical_not(near))(lambda: act(row_copies(at, cross_ref, line, 1)))

    @pl.when(step >= 2)
    def _():
        each_copy(step - 2, sent)

    slot = lax.rem(step, 2)
    wg, wu = wg_ref[...], wu_ref[...]
    wd = jnp.concatenate(
        [
            wd_ref[i * shard : (i + 1) * shard, k * width : (k + 1) * width]
            for i in range(2)
            for k in range(folds)
        ],
        axis=0,
    )
    hiddens, gates, ups = [], [], []
    part_rows = min(512, rows)
    for i in range(rows // part_rows):
        at = slice(i * part_rows, (i + 1) * part_rows)
        nf = nf_ref[at, :]
        g, u = dot(nf, wg), dot(nf, wu)
        hidden_grad = dot(seed_ref[at, :], wd, NT)
        sg = 1.0 / (1.0 + jnp.exp(-g))
        silu = g * sg
        hidden = (silu * u).astype(bf16)
        gate = (hidden_grad * u * sg * (1.0 + g * (1.0 - sg))).astype(bf16)
        up = (hidden_grad * silu).astype(bf16)
        branch[at, :] += dot(hidden, wd)
        nfgrad_ref[at, :] += dot(gate, wg, NT) + dot(up, wu, NT)
        hiddens.append(hidden)
        gates.append(gate)
        ups.append(up)
    hidden = jnp.concatenate(hiddens, axis=0)
    down = dot(hidden, seed_ref[...], TN).astype(bf16)
    on_upper = place % 2 == 1
    lower, upper = down[: chunk // 2, :], down[chunk // 2 :, :]
    for i, part in enumerate((jnp.where(on_upper, lower, upper), jnp.where(on_upper, upper, lower))):
        for k in range(folds):
            rows_out[slot, i, :, k * width : (k + 1) * width] = part[k * shard : (k + 1) * shard, :]
    for part, grad in enumerate((gates, ups)):
        columns = dot(turned[...], jnp.concatenate(grad, axis=0)).astype(bf16)
        for j in range(places):
            spot = spot_of(j // 4, j // 2 % 2, j % 2)
            columns_out[slot, spot, part] = columns[j * shard : (j + 1) * shard, :]
    each_copy(step, lambda copy: copy.start())

    def through_norm():
        gain = gain_ref[...]
        gain_grad = jnp.zeros_like(gain)
        part_rows = min(256, rows)
        for i in range(rows // part_rows):
            at = slice(i * part_rows, (i + 1) * part_rows)
            values, upstream = resid_ref[at, :], nfgrad_ref[at, :]
            inv = lax.rsqrt(jnp.mean(values * values, axis=-1, keepdims=True) + EPSILON)
            hat = values * inv
            weighted = upstream * gain
            inner = jnp.mean(weighted * hat, axis=-1, keepdims=True)
            gain_grad = gain_grad + jnp.sum(upstream * hat, axis=0, keepdims=True)
            total = seed_ref[at, :].astype(f32) + inv * (weighted - hat * inner)
            nfgrad_ref[at, :] = total
            low_ref[at, :] = total.astype(bf16)
        gain_grad_ref[...] = gain_grad

    @pl.when(step == steps - 1)
    def _():
        branch_ref[...] = branch[...].astype(branch_ref.dtype)
        each_copy(step - 1, sent)
        each_copy(step, sent)
        for at in range(places // 2):
            column_copies(at)[0].wait_recv()
            near = (at % 2 == place // 2 % 2).astype(jnp.int32)
            row_copies(at, far_ref, near * groups + at // 2, 0).wait_recv()
        if not first:
            through_norm()
            carry().wait()


def feed_forward(places, normed, seed, start, nfstart, weights, resid=None, gain=None, across=None):
    rows, width = normed.shape
    first = nfstart is None
    hidden = weights.shape[1] // 3
    chunk = 2 * hidden // places
    steps = places // 2
    shard = width // places
    whole = lambda t: (0, 0)
    once = pl.Buffered(1)
    return pl.pallas_call(
        functools.partial(ffn_kernel, places, first),
        grid=(steps,),
        in_specs=[
            pl.BlockSpec((rows, width), whole, pipeline_mode=once),
            pl.BlockSpec((rows, width), whole, pipeline_mode=once),
            pl.BlockSpec((rows, width), whole, pipeline_mode=once),
            pl.BlockSpec((8, 128) if first else (rows, width), whole, pipeline_mode=once),
            pl.BlockSpec((width, chunk), lambda t: (0, t)),
            pl.BlockSpec((width, chunk), lambda t: (0, steps + t)),
            pl.BlockSpec((2 * shard, hidden), lambda t: (t, 2)),
        ]
        + (
            []
            if first
            else [
                pl.BlockSpec((rows, width), whole, pipeline_mode=once),
                pl.BlockSpec((1, width), whole),
                pl.BlockSpec(memory_space=pl.ANY),
            ]
        ),
        out_specs=[
            pl.BlockSpec((rows, width), whole),
            pl.BlockSpec((rows, width), whole),
        ]
        + ([] if first else [pl.BlockSpec((rows, width), whole), pl.BlockSpec((1, width), whole)])
        + [pl.BlockSpec(memory_space=pl.ANY)] * (3 if first else 4),
        scratch_shapes=[
            pltpu.VMEM((width, rows), bf16),
            pltpu.VMEM((rows, width), f32),
            pltpu.VMEM((2, places, 2, shard, chunk), bf16),
            pltpu.VMEM((2, 2, shard, hidden), bf16),
            pltpu.SemaphoreType.DMA((2, 5)),
            pltpu.SemaphoreType.DMA((steps, 2)),
        ]
        + [pltpu.SemaphoreType.DMA((2,))] * (not first),
        out_shape=[
            jax.ShapeDtypeStruct((rows, width), f32 if first else bf16),
            jax.ShapeDtypeStruct((rows, width), f32),
        ]
        + (
            []
            if first
            else [jax.ShapeDtypeStruct((rows, width), bf16), jax.ShapeDtypeStruct((1, width), f32)]
        )
        + [jax.ShapeDtypeStruct((places // part, 3, shard, hidden), bf16) for part in (2, 4, 4)]
        + ([] if first else [jax.ShapeDtypeStruct(across.shape, bf16)]),
        compiler_params=pltpu.CompilerParams(
            vmem_limit_bytes=56 * 2**20, collective_id=1 if first else 2, has_side_effects=True
        ),
        cost_estimate=NO_COST,
    )(
        normed, seed, start, start if first else nfstart, weights, weights, weights,
        *(() if first else (resid, gain, across)),
    )


def outer_kernel(places, spot, left_ref, right_ref, far_ref, cross_ref, own_ref, turned, arranged):
    width = left_ref.shape[1]

    @pl.when(pl.program_id(0) == 0)
    def _():
        arrange_rows(places, spot, left_ref, turned, arranged)

    right = right_ref[...]
    half = width // 2
    far_ref[0] = dot(arranged[:half, :], right).astype(bf16)
    cross_ref[0] = dot(arranged[half : half + half // 2, :], right).astype(bf16)
    own_ref[0] = dot(arranged[half + half // 2 :, :], right).astype(bf16)


def outer(spot, left, right, block):
    rows, width = left.shape
    columns = right.shape[1]
    places = spot.shape[0] - 2
    by_cols = lambda t, o: (0, t)
    one_block = lambda t, o: (t, 0, 0)
    return pl.pallas_call(
        functools.partial(outer_kernel, places),
        grid_spec=pltpu.PrefetchScalarGridSpec(
            num_scalar_prefetch=1,
            grid=(columns // block,),
            in_specs=[
                pl.BlockSpec((rows, width), lambda t, o: (0, 0)),
                pl.BlockSpec((rows, block), by_cols),
            ],
            out_specs=[
                pl.BlockSpec((1, width // 2, block), one_block),
                pl.BlockSpec((1, width // 4, block), one_block),
                pl.BlockSpec((1, width // 4, block), one_block),
            ],
            scratch_shapes=[pltpu.VMEM((width, rows), bf16), pltpu.VMEM((width, rows), bf16)],
        ),
        out_shape=[
            jax.ShapeDtypeStruct((columns // block, width // 2, block), bf16),
            jax.ShapeDtypeStruct((columns // block, width // 4, block), bf16),
            jax.ShapeDtypeStruct((columns // block, width // 4, block), bf16),
        ],
        compiler_params=pltpu.CompilerParams(vmem_limit_bytes=VMEM_BYTES),
        cost_estimate=NO_COST,
    )(spot, left, right)


def finish_kernel(
    line_ref, line_got_ref, late_ref, first_ref, ffn_ref, bias_ref, cos_ref, sin_ref, qgain_ref, kgain_ref, gain_ref,
    normed_ref, dq_ref, got_kv_ref, own_kv_ref, rawq_ref, rawk_ref, weight_ref, tokens_ref, resid_ref,
    in_ref, out_ref, gate_up_ref, down_ref, small_out_ref, grad_ref,
    merged, low_a, low_b, low_c, low_d, wide_a, wide_b, sums,
    arranged, far, own, core_got, x_sent, x_got, z_sent, z_got, y_sent, y_got,
    first_got, second, second_got, late_got, late, late_there, small_sent, small_got,
    core_sems, x_sems, z_send, z_recv, y_sems, first_sems, second_sems, late_send, late_recv, late_sems, small_sems,
    load_sems, store_sem,
):
    place, rank = lax.axis_index("dp"), lax.axis_index("seq")
    line = place // 4
    mesh_id = pl.DeviceIdType.MESH
    twin = {"dp": place + 1 - place % 2 * 2}
    over = {"dp": place + 2 - place // 2 % 2 * 4}
    other = {"seq": 1 - rank}
    lines = [line_device(place, lax.rem(line + k, LINES)) for k in range(1, LINES)]
    low = line_device(place, line + 1 - line % 2 * 2)
    high = line_device(place, lax.rem(line + 2, LINES))
    blocks, quarter, columns = x_sent.shape
    rows = merged.shape[0]
    step = min(256, rows)
    shard = quarter // LINES
    places = 4 * LINES

    def send(source, target, sems, to):
        return pltpu.make_async_remote_copy(
            src_ref=source, dst_ref=target, send_sem=sems[0], recv_sem=sems[1],
            device_id=to, device_id_type=mesh_id,
        )

    def pair_of(sems, *index):
        return sems.at[*index, 0], sems.at[*index, 1]

    to_core = [send(far.at[b], core_got.at[b], pair_of(core_sems, b), twin) for b in range(blocks)]
    to_x = [send(x_sent.at[b], x_got.at[b], pair_of(x_sems, b), over) for b in range(blocks)]
    to_y = [send(y_sent.at[b], y_got.at[b], pair_of(y_sems, b), other) for b in range(blocks)]
    first_y = send(first_ref, first_got, pair_of(first_sems), other)
    second_y = send(second, second_got, pair_of(second_sems), other)
    late_y = send(late, late_there, pair_of(late_sems), other)

    def late_z(k):
        return send(
            late_ref.at[lax.rem(line + k, LINES)], late_got.at[k - 1],
            (late_send.at[k - 1], late_recv.at[k - 1]), lines[k - 1],
        )

    rounds = [
        send(small_sent.at[k], small_got.at[k], pair_of(small_sems, k), to)
        for k, to in enumerate((twin, over, low, high, other))
    ]

    def to_z(b, k):
        return send(
            z_sent.at[b, lax.rem(line + k, LINES)], z_got.at[b, k - 1],
            (z_send.at[b, k - 1], z_recv.at[b, k - 1]), lines[k - 1],
        )

    def cut(ref, index):
        return ref.at[:, pl.ds(index * columns, columns)]

    def load(k):
        source, target = (
            (normed_ref, low_a), (own_kv_ref.at[1], low_b), (got_kv_ref.at[1], low_c),
            (rawk_ref, wide_a), (own_kv_ref.at[0], low_d), (rawq_ref, wide_b),
            (got_kv_ref.at[0], low_a), (cut(dq_ref, 0), low_b), (cut(dq_ref, 1), low_c),
            (tokens_ref, low_d), (resid_ref, wide_a),
            (cut(weight_ref, 0), low_b), (cut(weight_ref, 1), low_c), (cut(weight_ref, 2), low_a),
        )[k]
        return pltpu.make_async_copy(source, target, load_sems.at[k])

    def start(*which):
        for k in which:
            load(k).start()

    def ready(*which):
        for k in which:
            load(k).wait()

    store = pltpu.make_async_copy(wide_b, grad_ref, store_sem.at[0])

    barrier = pltpu.get_barrier_semaphore()
    peers = [twin, over, other] + lines
    for target in peers:
        pl.semaphore_signal(barrier, inc=1, device_id=target, device_id_type=mesh_id)
    pl.semaphore_wait(barrier, len(peers))
    start(0, 1, 2, 4, 3, 5)
    for copy in [first_y] + [late_z(k) for k in range(1, LINES)]:
        copy.start()
    ready(0)
    turned = low_a[...].T
    for i in range(places):
        near_core = (i % 2 == place % 2).astype(jnp.int32)
        near_x = (i // 2 % 2 == place // 2 % 2).astype(jnp.int32)
        at = pl.multiple_of(((near_core * 2 + near_x) * LINES + i // 4) * shard, shard)
        arranged[pl.ds(at, shard), :] = turned[i * shard : (i + 1) * shard, :]
    start(6)

    def product(begin, count, b):
        return dot(arranged[begin : begin + count, :], merged[:, b * columns : (b + 1) * columns])

    def send_block(b):
        far[b] = product(0, 2 * quarter, b).astype(bf16)
        to_core[b].start()
        cross = product(2 * quarter, quarter, b)
        own[b] = product(3 * quarter, quarter, b).astype(bf16)
        to_core[b].wait()
        x_sent[b] = (cross + core_got[b, :quarter].astype(f32)).astype(bf16)
        to_x[b].start()

    def pass_on(b):
        to_x[b].wait()
        total = own[b].astype(f32) + core_got[b, quarter:].astype(f32) + x_got[b].astype(f32)
        total = total.astype(bf16)
        for k in range(LINES):
            z_sent[b, k] = total[k * shard : (k + 1) * shard, :]
        for k in range(1, LINES):
            to_z(b, k).start()

    ones = half_ones(True)

    def turn_back(b, left, right, raw_ref, head_gain):
        sums[b : b + 1, :] = jnp.zeros((1, PAIR), f32)

        def some_rows(i, carry):
            at = pl.ds(pl.multiple_of(i * step, step), step)
            cosine, sine = cos_ref[at, :], sin_ref[at, :]
            for tile in range(columns // PAIR):
                lanes = slice(tile * PAIR, (tile + 1) * PAIR)
                grad = left[at, lanes].astype(f32) + right[at, lanes].astype(f32)
                grad = grad.astype(bf16).astype(f32)
                grad = grad * cosine - swap_halves(grad) * sine
                raw = raw_ref[at, lanes]
                unit = lax.rsqrt(head_sums(raw * raw, ones) * (1.0 / 64) + EPSILON)
                hat = raw * unit
                sums[b : b + 1, :] += jnp.sum(grad * hat, axis=0, keepdims=True)
                weighted = grad * head_gain
                inner = head_sums(weighted * hat, ones) * (1.0 / 64)
                there = slice(b * columns + tile * PAIR, b * columns + (tile + 1) * PAIR)
                merged[at, there] = (unit * (weighted - hat * inner)).astype(bf16)
            return carry

        lax.fori_loop(0, rows // step, some_rows, 0)

    ready(1, 2)

    def add_rows(i, carry):
        at = pl.ds(pl.multiple_of(i * step, step), step)
        merged[at, 2 * columns :] = (low_b[at, :].astype(f32) + low_c[at, :].astype(f32)).astype(bf16)
        return carry

    lax.fori_loop(0, rows // step, add_rows, 0)
    start(7, 8)
    send_block(2)
    ready(3, 4, 6)
    turn_back(1, low_d, low_a, wide_a, kgain_ref[...])
    start(9, 10, 13)
    send_block(1)
    for i in range(line_ref.shape[0]):
        second[i] = sum(
            part.astype(f32) for part in [line_ref[i]] + [line_got_ref[k, i] for k in range(LINES - 1)]
        ).astype(bf16)
    second_y.start()
    ready(5, 7, 8)
    turn_back(0, low_b, low_c, wide_b, qgain_ref[...])
    start(11, 12)
    pass_on(2)
    send_block(0)
    pass_on(1)

    ready(9, 10, 11, 12, 13)
    gain = gain_ref[...]
    gain_grad = jnp.zeros_like(gain)
    for i in range(rows // step):
        at = slice(i * step, (i + 1) * step)
        normed_grad = sum(
            dot(merged[at, b * columns : (b + 1) * columns], part[...], NT)
            for b, part in enumerate((low_b, low_c, low_a))
        )
        values = low_d[at, :].astype(f32)
        inv = lax.rsqrt(jnp.mean(values * values, axis=-1, keepdims=True) + EPSILON)
        hat = values * inv
        weighted = normed_grad * gain
        inner = jnp.mean(weighted * hat, axis=-1, keepdims=True)
        wide_b[at, :] = wide_a[at, :] + inv * (weighted - hat * inner)
        gain_grad = gain_grad + jnp.sum(normed_grad * hat, axis=0, keepdims=True)
    store.start()
    tiles = columns // PAIR
    for k in range(tiles):
        small_sent[0, k : k + 1, :] = gain_grad[:, k * PAIR : (k + 1) * PAIR]
    small_sent[0, tiles : 2 * tiles, :] = ffn_ref[...]
    small_sent[0, 2 * tiles : 2 * tiles + 8, :] = sums[...]
    for pair in range(tiles):
        at = 2 * tiles + 8 + 2 * pair
        small_sent[0, at : at + 2, :] = bias_ref[pair] + bias_ref[tiles + pair]
    rounds[0].start()

    def next_round(k):
        rounds[k].wait()
        total = small_sent[k] + small_got[k]
        if k + 1 < len(rounds):
            small_sent[k + 1] = total
            rounds[k + 1].start()
        else:
            small_out_ref[...] = total

    def to_last(b):
        for k in range(1, LINES):
            to_z(b, k).wait()
        total = z_sent[b, line].astype(f32)
        for k in range(LINES - 1):
            total = total + z_got[b, k].astype(f32)
        y_sent[b] = total.astype(bf16)
        to_y[b].start()

    for k in range(1, LINES):
        late_z(k).wait()
    late[...] = sum(
        part.astype(f32) for part in [late_ref[line]] + [late_got[k] for k in range(LINES - 1)]
    ).astype(bf16)
    late_y.start()
    next_round(0)
    pass_on(0)
    next_round(1)
    to_last(2)
    to_last(1)
    next_round(2)
    first_y.wait()
    second_y.wait()
    part_columns = second.shape[2] // places
    hidden = second.shape[2] * 2
    for part in range(2):
        halves = [
            first_ref[part].astype(f32) + first_got[part].astype(f32),
            second[1 + part].astype(f32) + second_got[1 + part].astype(f32),
        ]
        for j in range(places):
            for h in range(2):
                at = part * hidden + (2 * j + h) * part_columns
                gate_up_ref[:, at : at + part_columns] = halves[h][:, j * part_columns : (j + 1) * part_columns]
    next_round(3)
    to_last(0)
    out_ref[...] = second[0, :, :columns].astype(f32) + second_got[0, :, :columns].astype(f32)
    late_y.wait()
    for h in range(2):
        if h == 0:
            total = late[...].astype(f32) + late_there[...].astype(f32)
        else:
            total = second[3].astype(f32) + second_got[3].astype(f32)
        for k in range(total.shape[1] // columns):
            at = h * down_ref.shape[0] // 2 + k * shard
            down_ref[at : at + shard, :] = total[:, k * columns : (k + 1) * columns]
    next_round(4)
    for b in (2, 1, 0):
        to_y[b].wait()
        in_ref[:, b * columns : (b + 1) * columns] = y_sent[b].astype(f32) + y_got[b].astype(f32)
    store.wait()


def finish(
    places, line_sums, line_got, late, first, ffn_gain, bias, cosine, sine, qgain, kgain, gain,
    normed, dq, got_kv, own_kv, raws, weight, tokens, resid,
):
    rows, width = tokens.shape
    blocks = 3
    quarter, shard, columns = width // 4, width // places, width
    hidden = line_sums.shape[2]
    small = (4 * width // PAIR + 8, PAIR)
    vmem = pl.BlockSpec(memory_space=pltpu.VMEM)
    anywhere = pl.BlockSpec(memory_space=pl.ANY)
    dma = pltpu.SemaphoreType.DMA
    return pl.pallas_call(
        finish_kernel,
        in_specs=[vmem] * 11 + [anywhere] * 9,
        out_specs=[vmem] * 5 + [anywhere],
        out_shape=[
            jax.ShapeDtypeStruct((shard, blocks * columns), f32),
            jax.ShapeDtypeStruct((shard, columns), f32),
            jax.ShapeDtypeStruct((shard, 4 * hidden), f32),
            jax.ShapeDtypeStruct((2 * hidden // places, columns), f32),
            jax.ShapeDtypeStruct(small, f32),
            jax.ShapeDtypeStruct((rows, width), f32),
        ],
        scratch_shapes=[
            pltpu.VMEM((rows, blocks * columns), bf16),
            pltpu.VMEM((rows, columns), bf16),
            pltpu.VMEM((rows, columns), bf16),
            pltpu.VMEM((rows, columns), bf16),
            pltpu.VMEM((rows, columns), bf16),
            pltpu.VMEM((rows, columns), f32),
            pltpu.VMEM((rows, columns), f32),
            pltpu.VMEM((8, PAIR), f32),
            pltpu.VMEM((width, rows), bf16),
            pltpu.VMEM((blocks, 2 * quarter, columns), bf16),
            pltpu.VMEM((blocks, quarter, columns), bf16),
            pltpu.VMEM((blocks, 2 * quarter, columns), bf16),
            pltpu.VMEM((blocks, quarter, columns), bf16),
            pltpu.VMEM((blocks, quarter, columns), bf16),
            pltpu.VMEM((blocks, LINES, shard, columns), bf16),
            pltpu.VMEM((blocks, LINES - 1, shard, columns), bf16),
            pltpu.VMEM((blocks, shard, columns), bf16),
            pltpu.VMEM((blocks, shard, columns), bf16),
            pltpu.VMEM(first.shape, bf16),
            pltpu.VMEM(line_sums.shape, bf16),
            pltpu.VMEM(line_sums.shape, bf16),
            pltpu.VMEM((LINES - 1, *late.shape[1:]), bf16),
            pltpu.VMEM(late.shape[1:], bf16),
            pltpu.VMEM(late.shape[1:], bf16),
            pltpu.VMEM((5, *small), f32),
            pltpu.VMEM((5, *small), f32),
            dma((blocks, 2)),
            dma((blocks, 2)),
            dma((blocks, LINES - 1)),
            dma((blocks, LINES - 1)),
            dma((blocks, 2)),
            dma((2,)),
            dma((2,)),
            dma((LINES - 1,)),
            dma((LINES - 1,)),
            dma((2,)),
            dma((5, 2)),
            dma((14,)),
            dma((1,)),
        ],
        compiler_params=pltpu.CompilerParams(
            vmem_limit_bytes=60 * 2**20, collective_id=4, has_side_effects=True
        ),
        cost_estimate=NO_COST,
    )(
        line_sums, line_got, late, first, ffn_gain, bias, cosine, sine, qgain, kgain, gain,
        normed, dq, got_kv, own_kv, *raws, weight, tokens, resid,
    )


def rms_forward(values, gain_vec):
    inv_rms = lax.rsqrt(jnp.mean(values * values, axis=-1, keepdims=True) + EPSILON)
    return (values * inv_rms * gain_vec, inv_rms)


def rms_backward(values, inv_rms, gain_vec, upstream):
    weighted = upstream * gain_vec
    inner_sum = jnp.mean(weighted * values, axis=-1, keepdims=True)
    value_grad = inv_rms * weighted - values * inv_rms * inv_rms * inv_rms * inner_sum
    return (value_grad, upstream * values * inv_rms)


def shift_by(values, count, step):
    return lax.ppermute(values, "seq", [(i, (i + step) % count) for i in range(count)])


def cross_core(values, places):
    return lax.ppermute(values, "dp", [(i, i ^ 1) for i in range(places)])


def cross_x(values, places):
    return lax.ppermute(values, "dp", [(i, i ^ 2) for i in range(places)])


def core_sum(pieces, places):
    crossed, terms = [], []
    for far, cross, own in pieces:
        quarter = own.shape[1]
        far = cross_core(far, places)
        crossed.append(cross + far[:, :quarter])
        terms.append([own, far[:, quarter:]])
    return jnp.concatenate(crossed, axis=0), terms


def add_received(terms, received):
    start, longer = 0, []
    for held in terms:
        count = held[0].shape[0]
        longer.append(held + [received[start : start + count]])
        start += count
    return longer


def total_of(terms):
    return jnp.concatenate([sum(term.astype(f32) for term in held) for held in terms], axis=0).astype(bf16)


def sum_seq(values, count):
    if count == 2:
        return values.astype(f32) + shift_by(values, count, 1).astype(f32)
    return lax.psum(values.astype(f32), "seq")


def after(value, *before):
    return lax.optimization_barrier((value, before))[0]


def sum_small(values, places, seq_count):
    step = 1
    while step < places:
        values = values + lax.ppermute(values, "dp", [(i, i ^ step) for i in range(places)])
        step *= 2
    if seq_count == 2:
        return values + shift_by(values, 2, 1)
    return lax.psum(values, "seq")


def body(
    tokens, doc_lengths, variate_ids, time_ids, in_proj, out_proj, gate_up, down_proj,
    attn_gain, ffn_gain, query_gain, key_gain, head_bias, cotangent,
):
    seq_count = lax.axis_size("seq")
    seq_rank = lax.axis_index("seq")
    local_rows, width = tokens.shape
    pack_rows = local_rows * seq_count
    head_dim = query_gain.shape[0]
    places = lax.axis_size("dp")
    place = lax.axis_index("dp")
    core, across = place % 2, place // 2 % 2
    groups = places // 4
    spot = jnp.stack(
        [core, across]
        + [
            group * 4 + (across + 1 - near_x) % 2 * 2 + (core + 1 - near_core) % 2
            for near_core in range(2)
            for near_x in range(2)
            for group in range(groups)
        ]
    ).astype(jnp.int32)

    fused = places == 16 and seq_count == 2
    gains = jnp.stack([attn_gain, ffn_gain], axis=1)
    gather = lambda w: lax.all_gather(w, "dp", axis=0, tiled=True)
    first_shard = jnp.concatenate([in_proj, out_proj, jnp.pad(gains, ((0, 0), (0, PAIR - 2)))], axis=1)
    if fused:
        wide, *there = gather_first(first_shard, tokens, time_ids.reshape(-1, PAIR), places)
        slots = [(tokens, time_ids), (there[0], there[1].reshape(-1))]
    else:
        wide = gather(first_shard)
        slots = [(tokens, time_ids)]
        for step in range(1, seq_count):
            slots.append(tuple(shift_by(array, seq_count, -step) for array in slots[0]))
    out_full = wide[:, 3 * width : 4 * width]
    attn_gain_f = wide[:, 4 * width].astype(f32)[None, :]
    ffn_gain_f = wide[:, 4 * width + 1].astype(f32)[None, :]
    shard = in_proj.shape[0]
    hidden_part = down_proj.shape[0] // 2
    folds = hidden_part // shard

    columns = gate_up.reshape(shard, 2, places, 2, hidden_part)
    fold_rows = down_proj.reshape(2, folds, shard, width)
    ffn_weights = [
        jnp.concatenate(
            [columns[:, 0, :, part].reshape(shard, -1), columns[:, 1, :, part].reshape(shard, -1)]
            + [fold_rows[part, k] for k in range(folds)],
            axis=1,
        )
        for part in range(2)
    ]
    ffn_weights[0] = gather(after(ffn_weights[0], wide))

    positions = jnp.arange(pack_rows, dtype=jnp.int32)
    first_end = doc_lengths[0, 0]
    second_end = first_end + doc_lengths[0, 1]
    segment = (positions >= first_end).astype(jnp.int32) + (positions >= second_end).astype(jnp.int32)
    query_columns, key_columns = slot_columns(segment, variate_ids[0])
    coefficients = bias_columns(head_bias)
    start = seq_rank * local_rows
    query_columns = lax.dynamic_slice_in_dim(query_columns, start, local_rows)
    local_segment = lax.dynamic_slice_in_dim(segment, start, local_rows)
    valid_rows = (local_segment < 2).astype(f32)
    source_columns, source_flags = [], []
    for step in range(seq_count):
        begin = ((seq_rank + step) % seq_count) * local_rows
        source_columns.append(lax.dynamic_slice_in_dim(key_columns, begin, local_rows))
        there = lax.dynamic_slice_in_dim(segment, begin, local_rows).reshape(-1, KEY_ROWS)
        source_flags.append(
            ((there[:, 0] <= local_segment[-1]) & (there[:, -1] >= local_segment[0])).astype(jnp.int32)
        )

    half_dim = head_dim // 2
    frequency = jnp.exp(jnp.arange(half_dim, dtype=f32) * (-math.log(ROPE_BASE) / half_dim))
    qgain = jnp.tile(query_gain, 2)[None, :]
    kgain = jnp.tile(key_gain, 2)[None, :]

    def rope_tables(times):
        angles = times.astype(f32)[:, None] * jnp.tile(frequency, 4)[None, :]
        sign = jnp.where(jnp.arange(PAIR) % head_dim < half_dim, -1.0, 1.0)
        return jnp.cos(angles), jnp.sin(angles) * sign[None, :]

    tables = [rope_tables(times) for _, times in slots]
    seed_grad = cotangent.astype(f32) * valid_rows[:, None]
    seed_low = seed_grad.astype(bf16)
    keyed = []
    for step, (there_tokens, _) in enumerate(slots):
        keys, values, *own = project(
            there_tokens, attn_gain_f, wide, *tables[step], qgain, kgain, step == 0
        )
        keyed.append((keys, values, source_columns[step]))
        if step == 0:
            cosine, sine = tables[0]
            queries, *raws, normed_low = own
            ffn_weights[1] = gather(after(ffn_weights[1], queries))
    attended, full_query = attend(
        jnp.concatenate(source_flags), queries, query_columns, coefficients, keyed
    )

    inputs_f = tokens.astype(f32)
    residual = inputs_f + dot(attended, out_full)
    normed_ffn, _ = rms_forward(residual, ffn_gain_f)
    normed_ffn_low = normed_ffn.astype(bf16)
    def scatter_line(parts):
        lines = [[line * 4 + k for line in range(groups)] for k in range(4)]
        return lax.psum_scatter(parts, "dp", scatter_dimension=0, axis_index_groups=lines, tiled=True)[0]

    def total3(first, *others):
        return sum((other.astype(f32) for other in others), first.astype(f32)).astype(bf16)

    branch, normed_ffn_grad, early_far, early_cross, early_own = feed_forward(
        places, normed_ffn_low, seed_low, residual, None, ffn_weights[0]
    )
    crossed = early_cross[:, :2] + early_far[:groups, :2]
    early_crossed = early_cross[:, 2] + early_far[:groups, 2]
    layer_out, residual_grad, mixed_low, ffn_gain_sum, far, cross, own, received = feed_forward(
        places, after(normed_ffn_low, early_crossed), seed_low, branch, normed_ffn_grad,
        ffn_weights[1], residual, ffn_gain_f, crossed,
    )
    first_total = scatter_line(total3(received, early_own[:, :2], early_far[groups:, :2]))
    second_crossed = cross + far[:groups]
    attended_grad = dot(mixed_low, out_full, NT).astype(bf16)

    attended_grad = dot(mixed_low, out_full, NT).astype(bf16)
    out_grads = outer(spot, attended, mixed_low, width)

    def merge(dqs, dkvs):
        merged, gains = merge_grads(width, 0, dqs, dkvs, raws, cosine, sine, qgain, kgain)
        return merged, jnp.sum(gains[:2].reshape(2, -1, head_dim), axis=1)

    def small_parts(bias, head_gains):
        same_bias = jnp.sum(bias, axis=-1).reshape(-1)
        tail = jnp.concatenate([head_gains[0], head_gains[1], same_bias])
        return jnp.concatenate([ffn_gain_sum[0], tail, jnp.zeros(-tail.shape[0] % 1024, f32)])

    if fused:
        (out_far,), out_cross, out_own = (cross_core(out_grads[0], places),), *out_grads[1:]
        by_line = lambda array: array.reshape(groups, -1, width)
        out_sums = [
            by_line(array) for array in (out_cross + out_far[:, : shard * groups], out_own, out_far[:, shard * groups :])
        ]
        dq_all, bias_all, received, own_kv, line_sums, line_got, late, *_ = attend_back_carry(
            full_query, attended_grad, attended, query_columns, keyed[0], keyed[1],
            (early_crossed, early_own, early_far), (second_crossed, own, far), out_sums,
        )
        in_proj_grad, out_proj_grad, gate_up_grad, down_grad, small, input_grad = finish(
            places, line_sums, line_got, late, first_total, ffn_gain_sum.reshape(-1, PAIR), bias_all,
            cosine, sine, qgain, kgain, attn_gain_f, normed_low, dq_all, received, own_kv, raws,
            wide, tokens, residual_grad,
        )
        rows_done = 2 * width // PAIR
        head_gains = jnp.sum(small[rows_done : rows_done + 2].reshape(2, 2, head_dim), axis=1)
        same_bias = jnp.sum(small[rows_done + 8 :], axis=1)
        small = jnp.concatenate([small[:rows_done].reshape(-1), head_gains.reshape(-1), same_bias])
    else:
        second = scatter_line(total3(cross_x(second_crossed, places), own, far[groups:]))
        early_down = total3(cross_x(early_crossed, places), early_own[:, 2], early_far[groups:, 2])
        early_down = scatter_line(early_down)
        dqs, dkvs, biases = [], [], 0.0
        for step in list(range(1, seq_count)) + [0]:
            dq, dkv, bias = attend_back(
                0, width // PAIR, source_flags[step], full_query, attended_grad, attended,
                query_columns, *keyed[step],
            )
            dqs.append((dq, 0))
            dkvs.append((shift_by(dkv, seq_count, step) if step else dkv, 0))
            biases = biases + bias
        merged_grad, head_gains = merge(dqs, dkvs)

        def sum_rows(pieces):
            crossed, terms = core_sum([pieces], places)
            total = total_of(add_received(terms, cross_x(crossed, places)))
            total = total.reshape(total.shape[0], groups, shard, -1).transpose(1, 0, 2, 3)
            return sum_seq(scatter_line(total), seq_count)

        in_sum = sum_rows(outer(spot, normed_low, merged_grad, width))
        out_proj_grad = sum_rows(out_grads)[0]
        in_proj_grad = in_sum.transpose(1, 0, 2).reshape(in_proj.shape)
        first_gates = sum_seq(first_total, seq_count)
        second_sum = sum_seq(second, seq_count)
        downs = [sum_seq(early_down, seq_count), second_sum[2]]
        down_grad = jnp.concatenate(
            [part.reshape(shard, -1, width).transpose(1, 0, 2).reshape(hidden_part, width) for part in downs]
        )
        gate_up_grad = jnp.stack(
            [
                part.reshape(2, shard, places, hidden_part).transpose(1, 0, 2, 3)
                for part in (first_gates, second_sum[:2])
            ],
            axis=3,
        ).reshape(gate_up.shape)
        normed_grad = dot(merged_grad, wide[:, : 3 * width], NT)
        norm_scale = lax.rsqrt(jnp.mean(inputs_f * inputs_f, axis=-1, keepdims=True) + EPSILON)
        input_norm_grad, attn_gain_terms = rms_backward(inputs_f, norm_scale, attn_gain_f, normed_grad)
        input_grad = residual_grad + input_norm_grad
        small = jnp.concatenate([jnp.sum(attn_gain_terms, axis=0), small_parts(biases, head_gains)])
        small = sum_small(small, places, seq_count)
    heads = head_bias.shape[0]
    gain_rows = attn_gain.shape[0]
    here = place * gain_rows
    tail = small[2 * width :]
    same_bias = tail[2 * head_dim : 2 * head_dim + heads]
    return (
        layer_out,
        input_grad,
        in_proj_grad,
        out_proj_grad,
        gate_up_grad,
        down_grad,
        lax.dynamic_slice_in_dim(small, here, gain_rows),
        lax.dynamic_slice_in_dim(small, width + here, gain_rows),
        tail[:head_dim],
        tail[head_dim : 2 * head_dim],
        jnp.stack([same_bias, -same_bias], axis=1),
    )


def solution(mesh):
    in_specs = (
        P(("dp", "seq"), None),
        P("dp", None),
        P("dp", None),
        P(("dp", "seq")),
        P("dp", None),
        P("dp", None),
        P("dp", None),
        P("dp", None),
        P("dp"),
        P("dp"),
        P(),
        P(),
        P(),
        P(("dp", "seq"), None),
    )
    out_specs = (
        P(("dp", "seq"), None),
        P(("dp", "seq"), None),
        P("dp", None),
        P("dp", None),
        P("dp", None),
        P("dp", None),
        P("dp"),
        P("dp"),
        P(),
        P(),
        P(),
    )
    return jax.shard_map(body, mesh=mesh, in_specs=in_specs, out_specs=out_specs, check_vma=False)
```

```python
import functools
import math

import jax
import jax.numpy as jnp
from jax import lax
from jax.experimental import pallas as pl
from jax.experimental.pallas import tpu as pltpu
from jax.sharding import PartitionSpec as P

EPSILON = 1e-06
ROPE_BASE = 10000.0
NEG_FILL = -1e30
PAIR = 128
KEY_ROWS = 256
VMEM_BYTES = 48 * 2**20
NO_COST = pl.CostEstimate(flops=1, bytes_accessed=1, transcendentals=0)
bf16 = jnp.bfloat16
f32 = jnp.float32
NN = (((1,), (0,)), ((), ()))
NT = (((1,), (1,)), ((), ()))
TN = (((0,), (0,)), ((), ()))


def dot(left, right, dims=NN):
    return lax.dot_general(left, right, dims, preferred_element_type=f32)


def split_two(values):
    high = values.astype(bf16)
    return high, (values - high.astype(f32)).astype(bf16)


def lane_index():
    return lax.broadcasted_iota(jnp.int32, (1, PAIR), 1)


def half_ones(same):
    rows = lax.broadcasted_iota(jnp.int32, (2 * PAIR, PAIR), 0) % PAIR
    cols = lax.broadcasted_iota(jnp.int32, (2 * PAIR, PAIR), 1)
    match = (rows < 64) == (cols < 64)
    return jnp.where(match if same else jnp.logical_not(match), 1.0, 0.0).astype(bf16)


def head_sums(values, ones):
    return dot(jnp.concatenate(split_two(values), axis=1), ones)


def swap_halves(values):
    first = lane_index() % 64 < 32
    return jnp.where(first, pltpu.roll(values, PAIR - 32, 1), pltpu.roll(values, 32, 1))


LINES = 4


def line_device(place, line):
    return {"dp": line * 4 + place % 4}


class Spread:
    def __init__(self, shard_ref, whole_ref, arrived, sent, kept):
        self.shard_ref, self.whole_ref = shard_ref, whole_ref
        self.arrived, self.sent, self.kept = arrived, sent, kept
        self.place = place = lax.axis_index("dp")
        self.z, self.x, self.core = place // 4, place // 2 % 2, place % 2
        self.lines = whole_ref.shape[0] // shard_ref.shape[0] // 4
        self.ends = (self.z == 0).astype(jnp.int32) + (self.z == self.lines - 1).astype(jnp.int32)
        self.up, self.down = {"dp": place + 4}, {"dp": place - 4}
        self.over = {"dp": place + 2 - self.x * 4}
        self.twin = {"dp": place + 1 - self.core * 2}
        self.not_last, self.not_first = self.z < self.lines - 1, self.z > 0

    def greet(self, barrier):
        def one(target):
            pl.semaphore_signal(barrier, inc=1, device_id=target, device_id_type=pl.DeviceIdType.MESH)

        pl.when(self.not_last)(lambda: one(self.up))
        pl.when(self.not_first)(lambda: one(self.down))

    def block(self, z, x, core):
        return z * 4 + x * 2 + core

    def rows_of(self, which):
        rows = self.shard_ref.shape[0]
        return self.whole_ref.at[pl.ds(pl.multiple_of(which * rows, rows), rows)]

    def copy(self, which, path, own=False):
        return pltpu.make_async_remote_copy(
            src_ref=self.shard_ref if own else self.rows_of(which),
            dst_ref=self.rows_of(which),
            send_sem=self.sent.at[path, which],
            recv_sem=self.arrived.at[which],
            device_id=(self.up, self.over, self.twin, self.down)[path],
            device_id_type=pl.DeviceIdType.MESH,
        )

    def stay(self):
        me = self.block(self.z, self.x, self.core)
        return pltpu.make_async_copy(self.shard_ref, self.rows_of(me), self.kept.at[0])

    def begin(self):
        me = self.block(self.z, self.x, self.core)
        pl.when(self.not_last)(lambda: self.copy(me, 0, True).start())
        pl.when(self.not_first)(lambda: self.copy(me, 3, True).start())
        self.copy(me, 1, True).start()
        self.copy(me, 2, True).start()
        self.stay().start()

    def along(self, step):
        def take(which, path, more):
            self.copy(which, path).wait_recv()
            pl.when(more)(lambda: self.copy(which, path).start())
            self.copy(which, 1).start()
            self.copy(which, 2).start()

        pl.when(self.z >= step)(
            lambda: take(self.block(self.z - step, self.x, self.core), 0, self.not_last)
        )
        pl.when(self.z + step < self.lines)(
            lambda: take(self.block(self.z + step, self.x, self.core), 3, self.not_first)
        )

    def to_twin(self):
        for line in range(self.lines):
            which = self.block(line, 1 - self.x, self.core)
            self.copy(which, 1).wait_recv()
            self.copy(which, 2).start()

    def end(self):
        for line in range(self.lines):
            for side in range(2):
                self.copy(self.block(line, side, 1 - self.core), 2).wait_recv()
        for line in range(self.lines):
            which = self.block(line, self.x, self.core)
            self.copy(which, 1).wait_send()
            self.copy(which, 2).wait_send()
            self.copy(self.block(line, 1 - self.x, self.core), 2).wait_send()
            pl.when((line <= self.z) & self.not_last)(lambda: self.copy(which, 0).wait_send())
            pl.when((line >= self.z) & self.not_first)(lambda: self.copy(which, 3).wait_send())
        self.stay().wait()


def gather_kernel(
    shard_ref, tokens_ref, times_ref, wide_ref, there_tokens_ref, there_times_ref, arrived, sent, kept, swapped
):
    other = {"seq": 1 - lax.axis_index("seq")}
    spread = Spread(shard_ref, wide_ref, arrived, sent, kept)
    barrier = pltpu.get_barrier_semaphore()
    for target in (spread.over, spread.twin, other):
        pl.semaphore_signal(barrier, inc=1, device_id=target, device_id_type=pl.DeviceIdType.MESH)
    spread.greet(barrier)
    pl.semaphore_wait(barrier, 5 - spread.ends)

    def swap(source, target, index):
        return pltpu.make_async_remote_copy(
            src_ref=source,
            dst_ref=target,
            send_sem=swapped.at[index],
            recv_sem=swapped.at[index + 1],
            device_id=other,
            device_id_type=pl.DeviceIdType.MESH,
        )

    swaps = [swap(tokens_ref, there_tokens_ref, 0), swap(times_ref, there_times_ref, 2)]
    spread.begin()
    for each in swaps:
        each.start()
    for step in range(1, spread.lines):
        spread.along(step)
    spread.to_twin()
    spread.end()
    for each in swaps:
        each.wait()


def gather_first(shard, tokens, times, places):
    anywhere = pl.BlockSpec(memory_space=pl.ANY)
    return pl.pallas_call(
        gather_kernel,
        in_specs=[anywhere] * 3,
        out_specs=[anywhere] * 3,
        out_shape=[
            jax.ShapeDtypeStruct((shard.shape[0] * places, shard.shape[1]), shard.dtype),
            jax.ShapeDtypeStruct(tokens.shape, tokens.dtype),
            jax.ShapeDtypeStruct(times.shape, times.dtype),
        ],
        scratch_shapes=[
            pltpu.SemaphoreType.DMA((places,)),
            pltpu.SemaphoreType.DMA((4, places)),
            pltpu.SemaphoreType.DMA((1,)),
            pltpu.SemaphoreType.DMA((4,)),
        ],
        compiler_params=pltpu.CompilerParams(collective_id=0, has_side_effects=True),
        cost_estimate=NO_COST,
    )(shard, tokens, times)


def qkv_kernel(
    tokens_ref, gain_ref, weight_ref, cos_ref, sin_ref, qgain_ref, kgain_ref,
    k_ref, v_ref, *own_refs,
):
    width = tokens_ref.shape[1]
    values = tokens_ref[...].astype(f32)
    inv = lax.rsqrt(jnp.mean(values * values, axis=-1, keepdims=True) + EPSILON)
    normed = (values * inv * gain_ref[...]).astype(bf16)
    ones = half_ones(True)
    cosine, sine = cos_ref[...], sin_ref[...]
    turned = [(1, k_ref, kgain_ref[...], 1.0)]
    if own_refs:
        q_ref, *raw_refs, normed_ref = own_refs
        normed_ref[...] = normed.T
        turned.append((0, q_ref, qgain_ref[...], 0.125))
    for part, out_ref, head_gain, scale in turned:
        for chunk in range(width // 256):
            start = part * width + chunk * 256
            raw = dot(normed, weight_ref[:, start : start + 256])
            if own_refs:
                raw_refs[part][:, chunk * 256 : (chunk + 1) * 256] = raw
            for tile in range(2):
                u = raw[:, tile * PAIR : (tile + 1) * PAIR]
                unit = lax.rsqrt(head_sums(u * u, ones) * (1.0 / 64) + EPSILON)
                u = u * unit * head_gain
                u = u * cosine + swap_halves(u) * sine
                at = chunk * 256 + tile * PAIR
                out_ref[:, at : at + PAIR] = (u * scale).astype(bf16)
    for chunk in range(width // 256):
        start = 2 * width + chunk * 256
        v_ref[:, chunk * 256 : (chunk + 1) * 256] = dot(
            normed, weight_ref[:, start : start + 256]
        ).astype(bf16)


def project(tokens, gain, weight, cosine, sine, qgain, kgain, own, block=256):
    rows, width = tokens.shape
    sizes = [(width, bf16), (width, bf16)]
    if own:
        sizes += [(width, bf16), (width, f32), (width, f32)]
    by_rows = lambda i: (i, 0)
    whole = lambda i: (0, 0)
    return pl.pallas_call(
        qkv_kernel,
        grid=(rows // block,),
        in_specs=[
            pl.BlockSpec((block, width), by_rows),
            pl.BlockSpec((1, width), whole),
            pl.BlockSpec((width, 3 * width), whole, pipeline_mode=pl.Buffered(1)),
            pl.BlockSpec((block, PAIR), by_rows),
            pl.BlockSpec((block, PAIR), by_rows),
            pl.BlockSpec((1, PAIR), whole),
            pl.BlockSpec((1, PAIR), whole),
        ],
        out_specs=[pl.BlockSpec((block, size), by_rows) for size, _ in sizes]
        + [pl.BlockSpec((width, block), lambda i: (0, i))] * own,
        out_shape=[jax.ShapeDtypeStruct((rows, size), kind) for size, kind in sizes]
        + [jax.ShapeDtypeStruct((width, rows), bf16)] * own,
        compiler_params=pltpu.CompilerParams(vmem_limit_bytes=VMEM_BYTES),
        cost_estimate=NO_COST,
    )(tokens, gain, weight, cosine, sine, qgain, kgain)


def merge_kernel(sources, parts, *refs):
    dq_refs = refs[:parts]
    dkv_refs = refs[parts : parts + sources]
    rawq_ref, rawk_ref, cos_ref, sin_ref, qgain_ref, kgain_ref, out_ref, gains_ref = refs[parts + sources :]
    width = dq_refs[0].shape[1]
    ones = half_ones(True)
    cosine, sine = cos_ref[...], sin_ref[...]

    @pl.when(pl.program_id(0) == 0)
    def _():
        gains_ref[...] = jnp.zeros_like(gains_ref)

    def read(part, at):
        found = [ref[:, at] for ref in dq_refs] if part == 0 else [ref[part - 1, :, at] for ref in dkv_refs]
        return sum(value.astype(f32) for value in found).astype(bf16)

    for part, (raw_ref, head_gain) in enumerate(((rawq_ref, qgain_ref[...]), (rawk_ref, kgain_ref[...]))):
        for tile in range(width // PAIR):
            at = slice(tile * PAIR, (tile + 1) * PAIR)
            grad = read(part, at).astype(f32)
            grad = grad * cosine - swap_halves(grad) * sine
            raw = raw_ref[:, at]
            unit = lax.rsqrt(head_sums(raw * raw, ones) * (1.0 / 64) + EPSILON)
            hat = raw * unit
            gains_ref[part : part + 1, at] += jnp.sum(grad * hat, axis=0, keepdims=True)
            weighted = grad * head_gain
            inner = head_sums(weighted * hat, ones) * (1.0 / 64)
            there = slice(part * width + tile * PAIR, part * width + (tile + 1) * PAIR)
            out_ref[:, there] = (unit * (weighted - hat * inner)).astype(bf16)
    out_ref[:, 2 * width :] = read(2, slice(0, width))


def merge_grads(width, at, dqs, dkvs, raws, cosine, sine, qgain, kgain, block=256):
    rows = raws[0].shape[0]
    by_rows = lambda i: (i, 0)
    whole = lambda i: (0, 0)
    cut = lambda index: pl.BlockSpec((block, width), lambda i: (i, index))
    cut_two = lambda index: pl.BlockSpec((2, block, width), lambda i: (0, i, index))
    return pl.pallas_call(
        functools.partial(merge_kernel, len(dkvs), len(dqs)),
        grid=(rows // block,),
        in_specs=[cut(index) for _, index in dqs]
        + [cut_two(index) for _, index in dkvs]
        + [
            cut(at),
            cut(at),
            pl.BlockSpec((block, PAIR), by_rows),
            pl.BlockSpec((block, PAIR), by_rows),
            pl.BlockSpec((1, PAIR), whole),
            pl.BlockSpec((1, PAIR), whole),
        ],
        out_specs=[pl.BlockSpec((block, 3 * width), by_rows), pl.BlockSpec((8, width), whole)],
        out_shape=[
            jax.ShapeDtypeStruct((rows, 3 * width), bf16),
            jax.ShapeDtypeStruct((8, width), f32),
        ],
        compiler_params=pltpu.CompilerParams(vmem_limit_bytes=VMEM_BYTES),
        cost_estimate=NO_COST,
    )(*[array for array, _ in dqs], *[array for array, _ in dkvs], *raws, cosine, sine, qgain, kgain)


def forward_kernel(sources, query_rows, flags, q_ref, aq_ref, coef_ref, *refs):
    keyed = refs[: 3 * sources]
    out_ref, full_ref, query, total = refs[3 * sources :]
    rows = q_ref.shape[0]
    lane = lane_index()
    half = lane < 64
    mine = (half, jnp.logical_not(half))
    both = q_ref[...]
    extra = aq_ref[...]
    for h in range(2):
        query[h] = jnp.where(mine[h], both, extra * coef_ref[0, h : h + 1, :])
        total[h] = jnp.zeros_like(total[h])
    blocks = keyed[0].shape[0] // KEY_ROWS
    for j in range(sources):
        k_ref, v_ref, ak_ref = keyed[3 * j : 3 * j + 3]
        for b in range(blocks):

            @pl.when(flags[j * blocks + b] != 0)
            def _():
                at = slice(b * KEY_ROWS, (b + 1) * KEY_ROWS)
                keys, values, columns = k_ref[at, :], v_ref[at, :], ak_ref[at, :]
                ones = jnp.ones_like(values)
                keys2 = [jnp.where(mine[h], keys, columns) for h in range(2)]
                values2 = [jnp.where(mine[h], values, ones) for h in range(2)]
                for i in range(rows // query_rows):
                    part = slice(i * query_rows, (i + 1) * query_rows)
                    for h in range(2):
                        probs = jnp.exp(dot(query[h, part, :], keys2[h], NT)).astype(bf16)
                        total[h, part, :] += dot(probs, values2[h])

    outs = []
    for h in range(2):
        summed = total[h]
        outs.append(summed / pltpu.roll(summed, 64, 1))
        log_total = jnp.log(jnp.maximum(summed, 1e-30))
        high = log_total.astype(bf16)
        mid, low = split_two(log_total - high.astype(f32))
        base = lane - 64 if h == 0 else lane
        full_ref[:, h * PAIR : (h + 1) * PAIR] = jnp.where(
            base == 11, -high, jnp.where(base == 12, -mid, jnp.where(base == 13, -low, query[h]))
        )
    out_ref[...] = jnp.where(half, outs[0], outs[1]).astype(bf16)


def attend(flags, queries, query_columns, coefficients, keyed):
    rows, width = queries.shape
    pairs = width // PAIR
    key_rows = keyed[0][0].shape[0]
    sources = len(keyed)
    by_pair = lambda p, f: (0, p)
    whole = lambda p, f: (0, 0)
    in_specs = [
        pl.BlockSpec((rows, PAIR), by_pair),
        pl.BlockSpec((rows, PAIR), whole),
        pl.BlockSpec((1, 2, PAIR), lambda p, f: (p, 0, 0)),
    ]
    operands = [queries, query_columns, coefficients]
    for keys, values, columns in keyed:
        in_specs += [
            pl.BlockSpec((key_rows, PAIR), by_pair),
            pl.BlockSpec((key_rows, PAIR), by_pair),
            pl.BlockSpec((key_rows, PAIR), whole),
        ]
        operands += [keys, values, columns]
    return pl.pallas_call(
        functools.partial(forward_kernel, sources, min(512, rows)),
        grid_spec=pltpu.PrefetchScalarGridSpec(
            num_scalar_prefetch=1,
            grid=(pairs,),
            in_specs=in_specs,
            out_specs=[
                pl.BlockSpec((rows, PAIR), by_pair),
                pl.BlockSpec((rows, 2 * PAIR), by_pair),
            ],
            scratch_shapes=[
                pltpu.VMEM((2, rows, PAIR), bf16),
                pltpu.VMEM((2, rows, PAIR), f32),
            ],
        ),
        out_shape=[
            jax.ShapeDtypeStruct((rows, width), bf16),
            jax.ShapeDtypeStruct((rows, 2 * width), bf16),
        ],
        compiler_params=pltpu.CompilerParams(vmem_limit_bytes=VMEM_BYTES),
        cost_estimate=NO_COST,
    )(flags, *operands)


def backward_start(grad_ref, out_ref, grads, dq_total):
    lane = lane_index()
    half = lane < 64
    mine = (half, jnp.logical_not(half))
    base = (lane - 64, lane)
    both = grad_ref[...]
    row_total = head_sums(both.astype(f32) * out_ref[...].astype(f32), half_ones(False))
    high, low = split_two(row_total)
    zero = jnp.zeros_like(high)
    for h in range(2):
        extra = jnp.where(base[h] == 0, -high, jnp.where(base[h] == 1, -low, zero))
        grads[h] = jnp.where(mine[h], both, extra)
        dq_total[h] = jnp.zeros_like(dq_total[h])


def backward_block(full_ref, keys, values, columns, grads, dq_total):
    lane = lane_index()
    half = lane < 64
    mine = (half, jnp.logical_not(half))
    base = (lane - 64, lane)
    ones = jnp.ones_like(values)
    dks, dvs = [], []
    for h in range(2):
        keys2 = jnp.where(mine[h], keys, columns)
        pick = (base[h] >= 0) & (base[h] < 2)
        values2 = jnp.where(mine[h], values, jnp.where(pick, ones, jnp.zeros_like(ones)))
        full = full_ref[:, h * PAIR : (h + 1) * PAIR]
        probs = jnp.exp(dot(keys2, full, NT))
        score_low = (probs * dot(values2, grads[h], NT)).astype(bf16)
        dks.append(dot(score_low, full))
        dvs.append(dot(probs.astype(bf16), grads[h]))
        dq_total[h] += dot(keys2, score_low, TN)
    return (
        jnp.where(half, dks[0], dks[1]).astype(bf16),
        jnp.where(half, dvs[0], dvs[1]).astype(bf16),
    )


def backward_end(aq_ref, dq_ref, bias_ref, dq_total):
    lane = lane_index()
    base = (lane - 64, lane)
    dq = [dq_total[h].T for h in range(2)]
    dq_ref[...] = (jnp.where(lane < 64, dq[0], dq[1]) * 0.125).astype(dq_ref.dtype)
    variates = aq_ref[...].astype(f32)
    for h in range(2):
        pick = (base[h] >= 0) & (base[h] < 4)
        bias_ref[0, h : h + 1, :] = jnp.sum(
            jnp.where(pick, dq[h] * variates, 0.0), axis=0, keepdims=True
        )


def backward_kernel(
    flags, full_ref, grad_ref, out_ref, aq_ref, k_ref, v_ref, ak_ref,
    dq_ref, dkv_ref, bias_ref, grads, dq_total,
):
    backward_start(grad_ref, out_ref, grads, dq_total)
    for b in range(k_ref.shape[0] // KEY_ROWS):
        at = slice(b * KEY_ROWS, (b + 1) * KEY_ROWS)

        @pl.when(flags[b] != 0)
        def _():
            dkv_ref[0, at, :], dkv_ref[1, at, :] = backward_block(
                full_ref, k_ref[at, :], v_ref[at, :], ak_ref[at, :], grads, dq_total
            )

        @pl.when(flags[b] == 0)
        def _():
            dkv_ref[:, at, :] = jnp.zeros((2, KEY_ROWS, PAIR), bf16)

    backward_end(aq_ref, dq_ref, bias_ref, dq_total)


def attend_back(first_pair, pairs, flags, full, grad, out, query_columns, keys, values, key_columns):
    rows = grad.shape[0]
    width = pairs * PAIR
    key_rows = keys.shape[0]
    by_pair = lambda p, f: (0, p)
    from_pair = lambda p, f: (0, first_pair + p)
    whole = lambda p, f: (0, 0)
    return pl.pallas_call(
        backward_kernel,
        grid_spec=pltpu.PrefetchScalarGridSpec(
            num_scalar_prefetch=1,
            grid=(pairs,),
            in_specs=[
                pl.BlockSpec((rows, 2 * PAIR), from_pair),
                pl.BlockSpec((rows, PAIR), from_pair),
                pl.BlockSpec((rows, PAIR), from_pair),
                pl.BlockSpec((rows, PAIR), whole),
                pl.BlockSpec((key_rows, PAIR), from_pair),
                pl.BlockSpec((key_rows, PAIR), from_pair),
                pl.BlockSpec((key_rows, PAIR), whole),
            ],
            out_specs=[
                pl.BlockSpec((rows, PAIR), by_pair),
                pl.BlockSpec((2, key_rows, PAIR), lambda p, f: (0, 0, p)),
                pl.BlockSpec((1, 2, PAIR), lambda p, f: (p, 0, 0)),
            ],
            scratch_shapes=[
                pltpu.VMEM((2, rows, PAIR), bf16),
                pltpu.VMEM((2, PAIR, rows), f32),
            ],
        ),
        out_shape=[
            jax.ShapeDtypeStruct((rows, width), f32),
            jax.ShapeDtypeStruct((2, key_rows, width), bf16),
            jax.ShapeDtypeStruct((pairs, 2, PAIR), f32),
        ],
        compiler_params=pltpu.CompilerParams(vmem_limit_bytes=VMEM_BYTES),
        cost_estimate=NO_COST,
    )(flags, full, grad, out, query_columns, keys, values, key_columns)


STARTS = (0, 7, 19, 33, 47)
ARRIVALS = (10, 23, 37, 50, 62)


def carry_kernel(
    pairs, full_ref, grad_ref, out_ref, aq_ref,
    far_k_ref, far_v_ref, far_ak_ref, near_k_ref, near_v_ref, near_ak_ref,
    early_across_ref, early_own_ref, early_far_ref, across_ref, own_ref, far_ref,
    out_across_ref, out_own_ref, out_far_ref,
    dq_ref, bias_ref, got_ref, near_ref, line_ref, line_got_ref, late_ref, early_got, across_got, out_got,
    grads, dq_total, stage, terms, sums,
    send_sems, recv_sems, near_sems, across_sems, term_sems, line_send, line_recv, line_own,
):
    step = pl.program_id(0)
    place, rank = lax.axis_index("dp"), lax.axis_index("seq")
    line = place // 4
    other = {"seq": 1 - rank}
    over = {"dp": place + 2 - place // 2 % 2 * 4}
    mesh_id = pl.DeviceIdType.MESH

    def lanes(index):
        return pl.ds(pl.multiple_of(index * PAIR, PAIR), PAIR)

    last = len(STARTS) - 1

    def part_of(refs, part):
        if part == last:
            return refs[0]
        return refs[2] if part == 0 else refs[1].at[:, part - 1]

    def width_of(part):
        return out_own_ref.shape[2] if part == 0 else sums.shape[3]

    def across(part):
        return pltpu.make_async_remote_copy(
            src_ref=part_of((early_across_ref, across_ref, out_across_ref), part),
            dst_ref=part_of((early_got, across_got, out_got), part),
            send_sem=across_sems.at[part, 0], recv_sem=across_sems.at[part, 1],
            device_id=over, device_id_type=mesh_id,
        )

    def load(part, k):
        if k == 0:
            source = part_of((early_own_ref.at[:, 2], own_ref, out_own_ref), part)
        elif k == 1:
            near = pl.ds(LINES, LINES)
            source = part_of((early_far_ref.at[near, 2], far_ref.at[near], out_far_ref), part)
        else:
            source = part_of((early_got, across_got, out_got), part)
        return pltpu.make_async_copy(
            source, terms.at[k, :, :, pl.ds(0, width_of(part))], term_sems.at[k]
        )

    def along(part, k):
        to = lax.rem(line + k, LINES)
        columns = pl.ds(0, width_of(part))
        return pltpu.make_async_remote_copy(
            src_ref=sums.at[part, to, :, columns], dst_ref=line_got_ref.at[k - 1, part, :, columns],
            send_sem=line_send.at[part, k - 1], recv_sem=line_recv.at[part, k - 1],
            device_id=line_device(place, to), device_id_type=mesh_id,
        )

    def stay(part):
        if part == last:
            return pltpu.make_async_copy(sums.at[part], late_ref, line_own.at[part])
        columns = pl.ds(0, width_of(part))
        return pltpu.make_async_copy(
            sums.at[part, line, :, columns], line_ref.at[part, :, columns], line_own.at[part]
        )

    def to_other(pair):
        return pltpu.make_async_remote_copy(
            src_ref=stage.at[pair], dst_ref=got_ref.at[:, :, lanes(pair)], send_sem=send_sems.at[pair],
            recv_sem=recv_sems.at[pair], device_id=other, device_id_type=mesh_id,
        )

    def to_near(pair):
        return pltpu.make_async_copy(
            stage.at[pairs + pair], near_ref.at[:, :, lanes(pair)], near_sems.at[pair]
        )

    @pl.when(step == 0)
    def _():
        barrier = pltpu.get_barrier_semaphore()
        peers = [other, over] + [line_device(place, lax.rem(line + k, LINES)) for k in range(1, LINES)]
        for target in peers:
            pl.semaphore_signal(barrier, inc=1, device_id=target, device_id_type=mesh_id)
        pl.semaphore_wait(barrier, len(peers))

    def arrive(part):
        across(part).wait()
        load(part, 2).start()
        for k in range(3):
            load(part, k).wait()
        columns = width_of(part)
        for i in range(LINES):
            sums[part, i, :, :columns] = sum(
                terms[k, i, :, :columns].astype(f32) for k in range(3)
            ).astype(bf16)
        if part < last:
            for k in range(1, LINES):
                along(part, k).start()
        stay(part).start()

    def go_on(quarter):
        for part in range(last + 1):

            before = ARRIVALS[part] - 3
            if STARTS[part] % 4 == quarter:

                @pl.when(step == STARTS[part] // 4)
                def _():
                    across(part).start()

            if before % 4 == quarter:

                @pl.when(step == before // 4)
                def _():
                    load(part, 0).start()
                    load(part, 1).start()

            if ARRIVALS[part] % 4 == quarter:
                pl.when(step == ARRIVALS[part] // 4)(functools.partial(arrive, part))

    backward_start(grad_ref, out_ref, grads, dq_total)
    is_far = step < pairs
    key_rows = min(512, far_k_ref.shape[0])
    key_blocks = far_k_ref.shape[0] // key_rows
    for b in range(key_blocks):
        at = slice(b * key_rows, (b + 1) * key_rows)
        for quarter in range(4 * b // key_blocks, 4 * (b + 1) // key_blocks):
            go_on(quarter)
        block = [
            jnp.where(is_far, far[at, :], near[at, :])
            for far, near in ((far_k_ref, near_k_ref), (far_v_ref, near_v_ref), (far_ak_ref, near_ak_ref))
        ]
        stage[step, 0, at, :], stage[step, 1, at, :] = backward_block(
            full_ref, *block, grads, dq_total
        )

    backward_end(aq_ref, dq_ref, bias_ref, dq_total)
    pl.when(is_far)(lambda: to_other(step).start())
    pl.when(jnp.logical_not(is_far))(lambda: to_near(step - pairs).start())

    @pl.when(step == pl.num_programs(0) - 1)
    def _():
        for pair in range(pairs):
            to_near(pair).wait()
            to_other(pair).wait()
        for part in range(last + 1):
            if part < last:
                for k in range(1, LINES):
                    along(part, k).wait()
            stay(part).wait()


def attend_back_carry(full, grad, out, query_columns, near, far, early, sums, out_sums):
    rows, width = grad.shape
    pairs = width // PAIR
    key_rows = near[0].shape[0]
    pair_of = lambda i: jnp.where(i < pairs, i, i - pairs)
    by_pair = lambda i: (0, pair_of(i))
    far_pair = lambda i: (0, jnp.minimum(i, pairs - 1))
    near_pair = lambda i: (0, jnp.maximum(i - pairs, 0))
    whole = lambda i: (0, 0)
    anywhere = pl.BlockSpec(memory_space=pl.ANY)
    shard, hidden = sums[0].shape[2:]
    parts = len(STARTS)

    def key_specs(pair):
        return [
            pl.BlockSpec((key_rows, PAIR), pair),
            pl.BlockSpec((key_rows, PAIR), pair),
            pl.BlockSpec((key_rows, PAIR), whole),
        ]

    return pl.pallas_call(
        functools.partial(carry_kernel, pairs),
        grid=(2 * pairs,),
        in_specs=[
            pl.BlockSpec((rows, 2 * PAIR), by_pair),
            pl.BlockSpec((rows, PAIR), by_pair),
            pl.BlockSpec((rows, PAIR), by_pair),
            pl.BlockSpec((rows, PAIR), whole),
        ]
        + key_specs(far_pair)
        + key_specs(near_pair)
        + [anywhere] * 9,
        out_specs=[
            pl.BlockSpec((rows, PAIR), lambda i: (0, i)),
            pl.BlockSpec((1, 2, PAIR), lambda i: (i, 0, 0)),
        ]
        + [anywhere] * 8,
        out_shape=[
            jax.ShapeDtypeStruct((rows, 2 * width), bf16),
            jax.ShapeDtypeStruct((2 * pairs, 2, PAIR), f32),
            jax.ShapeDtypeStruct((2, key_rows, width), bf16),
            jax.ShapeDtypeStruct((2, key_rows, width), bf16),
            jax.ShapeDtypeStruct((parts - 1, shard, hidden), bf16),
            jax.ShapeDtypeStruct((LINES - 1, parts - 1, shard, hidden), bf16),
            jax.ShapeDtypeStruct((LINES, shard, hidden), bf16),
            jax.ShapeDtypeStruct(early[0].shape, bf16),
            jax.ShapeDtypeStruct(sums[0].shape, bf16),
            jax.ShapeDtypeStruct(out_sums[0].shape, bf16),
        ],
        scratch_shapes=[
            pltpu.VMEM((2, rows, PAIR), bf16),
            pltpu.VMEM((2, PAIR, rows), f32),
            pltpu.VMEM((2 * pairs, 2, key_rows, PAIR), bf16),
            pltpu.VMEM((3, LINES, shard, hidden), bf16),
            pltpu.VMEM((parts, LINES, shard, hidden), bf16),
            pltpu.SemaphoreType.DMA((pairs,)),
            pltpu.SemaphoreType.DMA((pairs,)),
            pltpu.SemaphoreType.DMA((pairs,)),
            pltpu.SemaphoreType.DMA((parts, 2)),
            pltpu.SemaphoreType.DMA((3,)),
            pltpu.SemaphoreType.DMA((parts - 1, LINES - 1)),
            pltpu.SemaphoreType.DMA((parts - 1, LINES - 1)),
            pltpu.SemaphoreType.DMA((parts,)),
        ],
        compiler_params=pltpu.CompilerParams(
            vmem_limit_bytes=VMEM_BYTES, collective_id=3, has_side_effects=True
        ),
        cost_estimate=NO_COST,
    )(full, grad, out, query_columns, *far, *near, *early, *sums, *out_sums)


def slot_columns(segment, variates):
    column = jnp.arange(PAIR, dtype=jnp.int32)[None, :] % 64
    same_var = (column < 8) & (variates[:, None] == column % 4)
    in_seg = (column >= 8) & (column < 11)
    same_seg = segment[:, None] == column - 8
    three = (column >= 11) & (column < 14)
    query = jnp.where(in_seg & jnp.logical_not(same_seg), NEG_FILL, same_var.astype(f32))
    key = (same_var | (in_seg & same_seg) | three).astype(f32)
    return query.astype(bf16), key.astype(bf16)


def bias_columns(head_bias):
    delta = head_bias[:, 0] - head_bias[:, 1]
    high, low = split_two(delta)
    heads = delta.shape[0]
    row = jnp.concatenate(
        [
            jnp.broadcast_to(high[:, None], (heads, 4)),
            jnp.broadcast_to(low[:, None], (heads, 4)),
            jnp.ones((heads, 3), bf16),
            jnp.zeros((heads, 53), bf16),
        ],
        1,
    )
    return jnp.concatenate([row, row], 1).reshape(heads // 2, 2, PAIR)


def arrange_rows(places, spot, left_ref, turned, arranged):
    shard = left_ref.shape[1] // places
    turned[...] = left_ref[...].T
    for i in range(places):
        at = pl.multiple_of(spot[2 + i] * shard, shard)
        arranged[i * shard : (i + 1) * shard, :] = turned[pl.ds(at, shard), :]


def ffn_kernel(
    places, first, nf_ref, seed_ref, start_ref, nfstart_ref, wg_ref, wu_ref, wd_ref, *refs
):
    if first:
        branch_ref, nfgrad_ref, far_ref, cross_ref, own_ref, *refs = refs
    else:
        resid_ref, gain_ref, across_ref, branch_ref, nfgrad_ref, *refs = refs
        low_ref, gain_grad_ref, far_ref, cross_ref, own_ref, got_ref, *refs = refs
    turned, branch, columns_out, rows_out, sems, arrived, *x_sems = refs
    step = pl.program_id(0)
    steps = pl.num_programs(0)
    rows, width = nf_ref.shape
    shard = width // places
    chunk = wg_ref.shape[1]
    folds = chunk // 2 // shard

    place = lax.axis_index("dp")
    groups = places // 4

    twin = {"dp": place + 1 - place % 2 * 2}
    over = {"dp": place + 2 - place // 2 % 2 * 4}
    mesh_id = pl.DeviceIdType.MESH

    def carry():
        return pltpu.make_async_remote_copy(
            src_ref=across_ref, dst_ref=got_ref, send_sem=x_sems[0].at[0], recv_sem=x_sems[0].at[1],
            device_id=over, device_id_type=mesh_id,
        )

    @pl.when(step == 0)
    def _():
        barrier = pltpu.get_barrier_semaphore()
        for target in (twin,) if first else (twin, over):
            pl.semaphore_signal(barrier, inc=1, device_id=target, device_id_type=mesh_id)
        pl.semaphore_wait(barrier, 1 if first else 2)
        if not first:
            carry().start()
        turned[...] = nf_ref[...].T
        branch[...] = start_ref[...]
        nfgrad_ref[...] = jnp.zeros_like(nfgrad_ref) if first else nfstart_ref[...]

    def spot_of(line, x, core):
        near_core = (core == place % 2).astype(jnp.int32)
        near_x = (x == place // 2 % 2).astype(jnp.int32)
        return (near_core * 2 + near_x) * groups + line

    def to_twin(source, target, send_sem, recv_sem):
        return pltpu.make_async_remote_copy(
            src_ref=source, dst_ref=target, send_sem=send_sem, recv_sem=recv_sem,
            device_id=twin, device_id_type=mesh_id,
        )

    def column_copies(at):
        slot = lax.rem(at, 2)
        start = pl.multiple_of(at * chunk, chunk)
        made, begin = [], 0
        for k, ref in enumerate((far_ref, cross_ref, own_ref)):
            count = ref.shape[0]
            source = columns_out.at[slot, pl.ds(begin, count)]
            target = ref.at[:, pl.ds(0, 2), :, pl.ds(start, chunk)]
            if k == 0:
                made.append(to_twin(source, target, sems.at[slot, k], arrived.at[at, 0]))
            else:
                made.append(pltpu.make_async_copy(source, target, sems.at[slot, k]))
            begin += count
        return made

    def row_copies(at, ref, index, k):
        slot = lax.rem(at, 2)
        source, target = rows_out.at[slot, k], ref.at[index, 2]
        if k == 0:
            return to_twin(source, target, sems.at[slot, 3], arrived.at[at, 1])
        return pltpu.make_async_copy(source, target, sems.at[slot, 4])

    def sent(copy):
        copy.wait_send() if copy.is_remote else copy.wait()

    def each_copy(at, act):
        for copy in column_copies(at):
            act(copy)
        line, x = at // 2, lax.rem(at, 2)
        near = x == place // 2 % 2
        act(row_copies(at, far_ref, near.astype(jnp.int32) * groups + line, 0))
        pl.when(near)(lambda: act(row_copies(at, own_ref, line, 1)))
        pl.when(jnp.logical_not(near))(lambda: act(row_copies(at, cross_ref, line, 1)))

    @pl.when(step >= 2)
    def _():
        each_copy(step - 2, sent)

    slot = lax.rem(step, 2)
    wg, wu = wg_ref[...], wu_ref[...]
    wd = jnp.concatenate(
        [
            wd_ref[i * shard : (i + 1) * shard, k * width : (k + 1) * width]
            for i in range(2)
            for k in range(folds)
        ],
        axis=0,
    )
    hiddens, gates, ups = [], [], []
    part_rows = min(512, rows)
    for i in range(rows // part_rows):
        at = slice(i * part_rows, (i + 1) * part_rows)
        nf = nf_ref[at, :]
        g, u = dot(nf, wg), dot(nf, wu)
        hidden_grad = dot(seed_ref[at, :], wd, NT)
        sg = 1.0 / (1.0 + jnp.exp(-g))
        silu = g * sg
        hidden = (silu * u).astype(bf16)
        gate = (hidden_grad * u * sg * (1.0 + g * (1.0 - sg))).astype(bf16)
        up = (hidden_grad * silu).astype(bf16)
        branch[at, :] += dot(hidden, wd)
        nfgrad_ref[at, :] += dot(gate, wg, NT) + dot(up, wu, NT)
        hiddens.append(hidden)
        gates.append(gate)
        ups.append(up)
    hidden = jnp.concatenate(hiddens, axis=0)
    down = dot(hidden, seed_ref[...], TN).astype(bf16)
    on_upper = place % 2 == 1
    lower, upper = down[: chunk // 2, :], down[chunk // 2 :, :]
    for i, part in enumerate((jnp.where(on_upper, lower, upper), jnp.where(on_upper, upper, lower))):
        for k in range(folds):
            rows_out[slot, i, :, k * width : (k + 1) * width] = part[k * shard : (k + 1) * shard, :]
    for part, grad in enumerate((gates, ups)):
        columns = dot(turned[...], jnp.concatenate(grad, axis=0)).astype(bf16)
        for j in range(places):
            spot = spot_of(j // 4, j // 2 % 2, j % 2)
            columns_out[slot, spot, part] = columns[j * shard : (j + 1) * shard, :]
    each_copy(step, lambda copy: copy.start())

    def through_norm():
        gain = gain_ref[...]
        gain_grad = jnp.zeros_like(gain)
        part_rows = min(256, rows)
        for i in range(rows // part_rows):
            at = slice(i * part_rows, (i + 1) * part_rows)
            values, upstream = resid_ref[at, :], nfgrad_ref[at, :]
            inv = lax.rsqrt(jnp.mean(values * values, axis=-1, keepdims=True) + EPSILON)
            hat = values * inv
            weighted = upstream * gain
            inner = jnp.mean(weighted * hat, axis=-1, keepdims=True)
            gain_grad = gain_grad + jnp.sum(upstream * hat, axis=0, keepdims=True)
            total = seed_ref[at, :].astype(f32) + inv * (weighted - hat * inner)
            nfgrad_ref[at, :] = total
            low_ref[at, :] = total.astype(bf16)
        gain_grad_ref[...] = gain_grad

    @pl.when(step == steps - 1)
    def _():
        branch_ref[...] = branch[...].astype(branch_ref.dtype)
        each_copy(step - 1, sent)
        each_copy(step, sent)
        for at in range(places // 2):
            column_copies(at)[0].wait_recv()
            near = (at % 2 == place // 2 % 2).astype(jnp.int32)
            row_copies(at, far_ref, near * groups + at // 2, 0).wait_recv()
        if not first:
            through_norm()
            carry().wait()


def feed_forward(places, normed, seed, start, nfstart, weights, resid=None, gain=None, across=None):
    rows, width = normed.shape
    first = nfstart is None
    hidden = weights.shape[1] // 3
    chunk = 2 * hidden // places
    steps = places // 2
    shard = width // places
    whole = lambda t: (0, 0)
    once = pl.Buffered(1)
    return pl.pallas_call(
        functools.partial(ffn_kernel, places, first),
        grid=(steps,),
        in_specs=[
            pl.BlockSpec((rows, width), whole, pipeline_mode=once),
            pl.BlockSpec((rows, width), whole, pipeline_mode=once),
            pl.BlockSpec((rows, width), whole, pipeline_mode=once),
            pl.BlockSpec((8, 128) if first else (rows, width), whole, pipeline_mode=once),
            pl.BlockSpec((width, chunk), lambda t: (0, t)),
            pl.BlockSpec((width, chunk), lambda t: (0, steps + t)),
            pl.BlockSpec((2 * shard, hidden), lambda t: (t, 2)),
        ]
        + (
            []
            if first
            else [
                pl.BlockSpec((rows, width), whole, pipeline_mode=once),
                pl.BlockSpec((1, width), whole),
                pl.BlockSpec(memory_space=pl.ANY),
            ]
        ),
        out_specs=[
            pl.BlockSpec((rows, width), whole),
            pl.BlockSpec((rows, width), whole),
        ]
        + ([] if first else [pl.BlockSpec((rows, width), whole), pl.BlockSpec((1, width), whole)])
        + [pl.BlockSpec(memory_space=pl.ANY)] * (3 if first else 4),
        scratch_shapes=[
            pltpu.VMEM((width, rows), bf16),
            pltpu.VMEM((rows, width), f32),
            pltpu.VMEM((2, places, 2, shard, chunk), bf16),
            pltpu.VMEM((2, 2, shard, hidden), bf16),
            pltpu.SemaphoreType.DMA((2, 5)),
            pltpu.SemaphoreType.DMA((steps, 2)),
        ]
        + [pltpu.SemaphoreType.DMA((2,))] * (not first),
        out_shape=[
            jax.ShapeDtypeStruct((rows, width), f32 if first else bf16),
            jax.ShapeDtypeStruct((rows, width), f32),
        ]
        + (
            []
            if first
            else [jax.ShapeDtypeStruct((rows, width), bf16), jax.ShapeDtypeStruct((1, width), f32)]
        )
        + [jax.ShapeDtypeStruct((places // part, 3, shard, hidden), bf16) for part in (2, 4, 4)]
        + ([] if first else [jax.ShapeDtypeStruct(across.shape, bf16)]),
        compiler_params=pltpu.CompilerParams(
            vmem_limit_bytes=56 * 2**20, collective_id=1 if first else 2, has_side_effects=True
        ),
        cost_estimate=NO_COST,
    )(
        normed, seed, start, start if first else nfstart, weights, weights, weights,
        *(() if first else (resid, gain, across)),
    )


def outer_kernel(places, spot, left_ref, right_ref, far_ref, cross_ref, own_ref, turned, arranged):
    width = left_ref.shape[1]

    @pl.when(pl.program_id(0) == 0)
    def _():
        arrange_rows(places, spot, left_ref, turned, arranged)

    right = right_ref[...]
    half = width // 2
    far_ref[0] = dot(arranged[:half, :], right).astype(bf16)
    cross_ref[0] = dot(arranged[half : half + half // 2, :], right).astype(bf16)
    own_ref[0] = dot(arranged[half + half // 2 :, :], right).astype(bf16)


def outer(spot, left, right, block):
    rows, width = left.shape
    columns = right.shape[1]
    places = spot.shape[0] - 2
    by_cols = lambda t, o: (0, t)
    one_block = lambda t, o: (t, 0, 0)
    return pl.pallas_call(
        functools.partial(outer_kernel, places),
        grid_spec=pltpu.PrefetchScalarGridSpec(
            num_scalar_prefetch=1,
            grid=(columns // block,),
            in_specs=[
                pl.BlockSpec((rows, width), lambda t, o: (0, 0)),
                pl.BlockSpec((rows, block), by_cols),
            ],
            out_specs=[
                pl.BlockSpec((1, width // 2, block), one_block),
                pl.BlockSpec((1, width // 4, block), one_block),
                pl.BlockSpec((1, width // 4, block), one_block),
            ],
            scratch_shapes=[pltpu.VMEM((width, rows), bf16), pltpu.VMEM((width, rows), bf16)],
        ),
        out_shape=[
            jax.ShapeDtypeStruct((columns // block, width // 2, block), bf16),
            jax.ShapeDtypeStruct((columns // block, width // 4, block), bf16),
            jax.ShapeDtypeStruct((columns // block, width // 4, block), bf16),
        ],
        compiler_params=pltpu.CompilerParams(vmem_limit_bytes=VMEM_BYTES),
        cost_estimate=NO_COST,
    )(spot, left, right)


def finish_kernel(
    line_ref, late_ref, first_ref, ffn_ref, bias_ref, cos_ref, sin_ref, qgain_ref, kgain_ref, gain_ref,
    line_got_ref, normed_ref, dq_ref, got_kv_ref, own_kv_ref, rawq_ref, rawk_ref, weight_ref, tokens_ref, resid_ref,
    in_ref, out_ref, gate_up_ref, down_ref, small_out_ref, grad_ref,
    merged, low_a, low_b, low_c, low_d, wide_a, wide_b, sums,
    line_there, arranged, far, own, core_got, x_sent, x_got, z_sent, z_got, y_sent, y_got,
    first_got, second, second_got, late_got, late, late_there, small_sent, small_got,
    core_sems, x_sems, z_send, z_recv, y_sems, first_sems, second_sems, late_send, late_recv, late_sems, small_sems,
    load_sems, row_sems, store_sem,
):
    place, rank = lax.axis_index("dp"), lax.axis_index("seq")
    line = place // 4
    mesh_id = pl.DeviceIdType.MESH
    twin = {"dp": place + 1 - place % 2 * 2}
    over = {"dp": place + 2 - place // 2 % 2 * 4}
    other = {"seq": 1 - rank}
    lines = [line_device(place, lax.rem(line + k, LINES)) for k in range(1, LINES)]
    low = line_device(place, line + 1 - line % 2 * 2)
    high = line_device(place, lax.rem(line + 2, LINES))
    blocks, quarter, columns = x_sent.shape
    rows, width = merged.shape[0], low_a.shape[1]
    step = min(256, rows)
    shard = quarter // LINES
    places = 4 * LINES

    def send(source, target, sems, to):
        return pltpu.make_async_remote_copy(
            src_ref=source, dst_ref=target, send_sem=sems[0], recv_sem=sems[1],
            device_id=to, device_id_type=mesh_id,
        )

    def pair_of(sems, *index):
        return sems.at[*index, 0], sems.at[*index, 1]

    to_core = [send(far.at[b], core_got.at[b], pair_of(core_sems, b), twin) for b in range(blocks)]
    to_x = [send(x_sent.at[b], x_got.at[b], pair_of(x_sems, b), over) for b in range(blocks)]
    to_y = [send(y_sent.at[b], y_got.at[b], pair_of(y_sems, b), other) for b in range(blocks)]
    first_y = send(first_ref, first_got, pair_of(first_sems), other)
    second_y = send(second, second_got, pair_of(second_sems), other)
    late_y = send(late, late_there, pair_of(late_sems), other)

    def late_z(k):
        return send(
            late_ref.at[lax.rem(line + k, LINES)], late_got.at[k - 1],
            (late_send.at[k - 1], late_recv.at[k - 1]), lines[k - 1],
        )

    rounds = [
        send(small_sent.at[k], small_got.at[k], pair_of(small_sems, k), to)
        for k, to in enumerate((twin, over, low, high, other))
    ]

    def to_z(b, k):
        return send(
            z_sent.at[b, lax.rem(line + k, LINES)], z_got.at[b, k - 1],
            (z_send.at[b, k - 1], z_recv.at[b, k - 1]), lines[k - 1],
        )

    def cut(ref, index):
        return ref.at[:, pl.ds(index * width, width)]

    def load(k):
        source, target = (
            (line_got_ref, line_there), (own_kv_ref.at[1], low_b), (got_kv_ref.at[1], low_c),
            (rawk_ref, wide_a), (own_kv_ref.at[0], low_d), (rawq_ref, wide_b),
            (got_kv_ref.at[0], low_a), (cut(dq_ref, 0), low_b), (cut(dq_ref, 1), low_c),
            (tokens_ref, low_d), (resid_ref, wide_a),
            (cut(weight_ref, 0), low_b), (cut(weight_ref, 1), low_c), (cut(weight_ref, 2), low_a),
        )[k]
        return pltpu.make_async_copy(source, target, load_sems.at[k])

    def start(*which):
        for k in which:
            load(k).start()

    def ready(*which):
        for k in which:
            load(k).wait()

    store = pltpu.make_async_copy(wide_b, grad_ref, store_sem.at[0])

    barrier = pltpu.get_barrier_semaphore()
    peers = [twin, over, other] + lines
    for target in peers:
        pl.semaphore_signal(barrier, inc=1, device_id=target, device_id_type=mesh_id)
    pl.semaphore_wait(barrier, len(peers))
    def arrange(i):
        near_core = (i % 2 == place % 2).astype(jnp.int32)
        near_x = (i // 2 % 2 == place // 2 % 2).astype(jnp.int32)
        at = pl.multiple_of(((near_core * 2 + near_x) * LINES + i // 4) * shard, shard)
        return pltpu.make_async_copy(
            normed_ref.at[pl.ds(i * shard, shard)], arranged.at[pl.ds(at, shard)], row_sems.at[i]
        )

    start(1, 2)
    for i in range(places):
        arrange(i).start()
    for copy in [first_y] + [late_z(k) for k in range(1, LINES)]:
        copy.start()
    start(4, 3, 6, 0, 5)

    def product(begin, count, b):
        return dot(arranged[begin : begin + count, :], merged[:, b * columns : (b + 1) * columns])

    def send_block(b):
        far[b] = product(0, 2 * quarter, b).astype(bf16)
        to_core[b].start()
        cross = product(2 * quarter, quarter, b)
        own[b] = product(3 * quarter, quarter, b).astype(bf16)
        to_core[b].wait()
        x_sent[b] = (cross + core_got[b, :quarter].astype(f32)).astype(bf16)
        to_x[b].start()

    def pass_on(b):
        to_x[b].wait()
        total = own[b].astype(f32) + core_got[b, quarter:].astype(f32) + x_got[b].astype(f32)
        total = total.astype(bf16)
        for k in range(LINES):
            z_sent[b, k] = total[k * shard : (k + 1) * shard, :]
        for k in range(1, LINES):
            to_z(b, k).start()

    ones = half_ones(True)

    def turn_back(b, left, right, raw_ref, head_gain):
        sums[b : b + 1, :] = jnp.zeros((1, PAIR), f32)

        def some_rows(i, carry):
            at = pl.ds(pl.multiple_of(i * step, step), step)
            cosine, sine = cos_ref[at, :], sin_ref[at, :]
            for tile in range(width // PAIR):
                lanes = slice(tile * PAIR, (tile + 1) * PAIR)
                grad = left[at, lanes].astype(f32) + right[at, lanes].astype(f32)
                grad = grad.astype(bf16).astype(f32)
                grad = grad * cosine - swap_halves(grad) * sine
                raw = raw_ref[at, lanes]
                unit = lax.rsqrt(head_sums(raw * raw, ones) * (1.0 / 64) + EPSILON)
                hat = raw * unit
                sums[b : b + 1, :] += jnp.sum(grad * hat, axis=0, keepdims=True)
                weighted = grad * head_gain
                inner = head_sums(weighted * hat, ones) * (1.0 / 64)
                there = slice(b * width + tile * PAIR, b * width + (tile + 1) * PAIR)
                merged[at, there] = (unit * (weighted - hat * inner)).astype(bf16)
            return carry

        lax.fori_loop(0, rows // step, some_rows, 0)

    ready(1, 2)

    def add_rows(i, carry):
        at = pl.ds(pl.multiple_of(i * step, step), step)
        merged[at, 2 * width :] = (low_b[at, :].astype(f32) + low_c[at, :].astype(f32)).astype(bf16)
        return carry

    lax.fori_loop(0, rows // step, add_rows, 0)
    start(7, 8)
    for i in range(places):
        arrange(i).wait()
    send_block(4)
    send_block(5)
    ready(3, 4, 6)
    turn_back(1, low_d, low_a, wide_a, kgain_ref[...])
    start(9, 10, 13)
    send_block(2)
    send_block(3)
    ready(0)
    for i in range(line_ref.shape[0]):
        second[i] = sum(
            part.astype(f32) for part in [line_ref[i]] + [line_there[k, i] for k in range(LINES - 1)]
        ).astype(bf16)
    second_y.start()
    pass_on(4)
    ready(5, 7, 8)
    turn_back(0, low_b, low_c, wide_b, qgain_ref[...])
    start(11, 12)
    pass_on(5)
    send_block(0)
    send_block(1)
    pass_on(2)
    pass_on(3)

    ready(9, 10, 11, 12, 13)
    gain = gain_ref[...]
    gain_grad = jnp.zeros_like(gain)
    for i in range(rows // step):
        at = slice(i * step, (i + 1) * step)
        normed_grad = sum(
            dot(merged[at, b * width : (b + 1) * width], part[...], NT)
            for b, part in enumerate((low_b, low_c, low_a))
        )
        values = low_d[at, :].astype(f32)
        inv = lax.rsqrt(jnp.mean(values * values, axis=-1, keepdims=True) + EPSILON)
        hat = values * inv
        weighted = normed_grad * gain
        inner = jnp.mean(weighted * hat, axis=-1, keepdims=True)
        wide_b[at, :] = wide_a[at, :] + inv * (weighted - hat * inner)
        gain_grad = gain_grad + jnp.sum(normed_grad * hat, axis=0, keepdims=True)
    store.start()
    tiles = width // PAIR
    for k in range(tiles):
        small_sent[0, k : k + 1, :] = gain_grad[:, k * PAIR : (k + 1) * PAIR]
    small_sent[0, tiles : 2 * tiles, :] = ffn_ref[...]
    small_sent[0, 2 * tiles : 2 * tiles + 8, :] = sums[...]
    for pair in range(tiles):
        at = 2 * tiles + 8 + 2 * pair
        small_sent[0, at : at + 2, :] = bias_ref[pair] + bias_ref[tiles + pair]
    rounds[0].start()

    def next_round(k):
        rounds[k].wait()
        total = small_sent[k] + small_got[k]
        if k + 1 < len(rounds):
            small_sent[k + 1] = total
            rounds[k + 1].start()
        else:
            small_out_ref[...] = total

    def to_last(b):
        for k in range(1, LINES):
            to_z(b, k).wait()
        total = z_sent[b, line].astype(f32)
        for k in range(LINES - 1):
            total = total + z_got[b, k].astype(f32)
        y_sent[b] = total.astype(bf16)
        to_y[b].start()

    for k in range(1, LINES):
        late_z(k).wait()
    late[...] = sum(
        part.astype(f32) for part in [late_ref[line]] + [late_got[k] for k in range(LINES - 1)]
    ).astype(bf16)
    late_y.start()
    next_round(0)
    pass_on(0)
    pass_on(1)
    next_round(1)
    for b in (4, 5, 2, 3):
        to_last(b)
    next_round(2)
    first_y.wait()
    second_y.wait()
    part_columns = second.shape[2] // places
    hidden = second.shape[2] * 2
    for part in range(2):
        halves = [
            first_ref[part].astype(f32) + first_got[part].astype(f32),
            second[1 + part].astype(f32) + second_got[1 + part].astype(f32),
        ]
        for j in range(places):
            for h in range(2):
                at = part * hidden + (2 * j + h) * part_columns
                gate_up_ref[:, at : at + part_columns] = halves[h][:, j * part_columns : (j + 1) * part_columns]
    next_round(3)
    to_last(0)
    to_last(1)
    out_ref[...] = second[0, :, :width].astype(f32) + second_got[0, :, :width].astype(f32)
    late_y.wait()
    for h in range(2):
        if h == 0:
            total = late[...].astype(f32) + late_there[...].astype(f32)
        else:
            total = second[3].astype(f32) + second_got[3].astype(f32)
        for k in range(total.shape[1] // width):
            at = h * down_ref.shape[0] // 2 + k * shard
            down_ref[at : at + shard, :] = total[:, k * width : (k + 1) * width]
    next_round(4)
    for b in (4, 5, 2, 3, 0, 1):
        to_y[b].wait()
        in_ref[:, b * columns : (b + 1) * columns] = y_sent[b].astype(f32) + y_got[b].astype(f32)
    store.wait()


def finish(
    places, line_sums, line_got, late, first, ffn_gain, bias, cosine, sine, qgain, kgain, gain,
    normed, dq, got_kv, own_kv, raws, weight, tokens, resid,
):
    rows, width = tokens.shape
    blocks, columns = 6, width // 2
    quarter, shard = width // 4, width // places
    hidden = line_sums.shape[2]
    small = (4 * width // PAIR + 8, PAIR)
    vmem = pl.BlockSpec(memory_space=pltpu.VMEM)
    anywhere = pl.BlockSpec(memory_space=pl.ANY)
    dma = pltpu.SemaphoreType.DMA
    return pl.pallas_call(
        finish_kernel,
        in_specs=[vmem] * 10 + [anywhere] * 10,
        out_specs=[vmem] * 5 + [anywhere],
        out_shape=[
            jax.ShapeDtypeStruct((shard, blocks * columns), f32),
            jax.ShapeDtypeStruct((shard, width), f32),
            jax.ShapeDtypeStruct((shard, 4 * hidden), f32),
            jax.ShapeDtypeStruct((2 * hidden // places, width), f32),
            jax.ShapeDtypeStruct(small, f32),
            jax.ShapeDtypeStruct((rows, width), f32),
        ],
        scratch_shapes=[
            pltpu.VMEM((rows, blocks * columns), bf16),
            pltpu.VMEM((rows, width), bf16),
            pltpu.VMEM((rows, width), bf16),
            pltpu.VMEM((rows, width), bf16),
            pltpu.VMEM((rows, width), bf16),
            pltpu.VMEM((rows, width), f32),
            pltpu.VMEM((rows, width), f32),
            pltpu.VMEM((8, PAIR), f32),
            pltpu.VMEM(line_got.shape, bf16),
            pltpu.VMEM((width, rows), bf16),
            pltpu.VMEM((blocks, 2 * quarter, columns), bf16),
            pltpu.VMEM((blocks, quarter, columns), bf16),
            pltpu.VMEM((blocks, 2 * quarter, columns), bf16),
            pltpu.VMEM((blocks, quarter, columns), bf16),
            pltpu.VMEM((blocks, quarter, columns), bf16),
            pltpu.VMEM((blocks, LINES, shard, columns), bf16),
            pltpu.VMEM((blocks, LINES - 1, shard, columns), bf16),
            pltpu.VMEM((blocks, shard, columns), bf16),
            pltpu.VMEM((blocks, shard, columns), bf16),
            pltpu.VMEM(first.shape, bf16),
            pltpu.VMEM(line_sums.shape, bf16),
            pltpu.VMEM(line_sums.shape, bf16),
            pltpu.VMEM((LINES - 1, *late.shape[1:]), bf16),
            pltpu.VMEM(late.shape[1:], bf16),
            pltpu.VMEM(late.shape[1:], bf16),
            pltpu.VMEM((5, *small), f32),
            pltpu.VMEM((5, *small), f32),
            dma((blocks, 2)),
            dma((blocks, 2)),
            dma((blocks, LINES - 1)),
            dma((blocks, LINES - 1)),
            dma((blocks, 2)),
            dma((2,)),
            dma((2,)),
            dma((LINES - 1,)),
            dma((LINES - 1,)),
            dma((2,)),
            dma((5, 2)),
            dma((14,)),
            dma((places,)),
            dma((1,)),
        ],
        compiler_params=pltpu.CompilerParams(
            vmem_limit_bytes=60 * 2**20, collective_id=4, has_side_effects=True
        ),
        cost_estimate=NO_COST,
    )(
        line_sums, late, first, ffn_gain, bias, cosine, sine, qgain, kgain, gain,
        line_got, normed, dq, got_kv, own_kv, *raws, weight, tokens, resid,
    )


def rms_forward(values, gain_vec):
    inv_rms = lax.rsqrt(jnp.mean(values * values, axis=-1, keepdims=True) + EPSILON)
    return (values * inv_rms * gain_vec, inv_rms)


def rms_backward(values, inv_rms, gain_vec, upstream):
    weighted = upstream * gain_vec
    inner_sum = jnp.mean(weighted * values, axis=-1, keepdims=True)
    value_grad = inv_rms * weighted - values * inv_rms * inv_rms * inv_rms * inner_sum
    return (value_grad, upstream * values * inv_rms)


def shift_by(values, count, step):
    return lax.ppermute(values, "seq", [(i, (i + step) % count) for i in range(count)])


def cross_core(values, places):
    return lax.ppermute(values, "dp", [(i, i ^ 1) for i in range(places)])


def cross_x(values, places):
    return lax.ppermute(values, "dp", [(i, i ^ 2) for i in range(places)])


def core_sum(pieces, places):
    crossed, terms = [], []
    for far, cross, own in pieces:
        quarter = own.shape[1]
        far = cross_core(far, places)
        crossed.append(cross + far[:, :quarter])
        terms.append([own, far[:, quarter:]])
    return jnp.concatenate(crossed, axis=0), terms


def add_received(terms, received):
    start, longer = 0, []
    for held in terms:
        count = held[0].shape[0]
        longer.append(held + [received[start : start + count]])
        start += count
    return longer


def total_of(terms):
    return jnp.concatenate([sum(term.astype(f32) for term in held) for held in terms], axis=0).astype(bf16)


def sum_seq(values, count):
    if count == 2:
        return values.astype(f32) + shift_by(values, count, 1).astype(f32)
    return lax.psum(values.astype(f32), "seq")


def after(value, *before):
    return lax.optimization_barrier((value, before))[0]


def sum_small(values, places, seq_count):
    step = 1
    while step < places:
        values = values + lax.ppermute(values, "dp", [(i, i ^ step) for i in range(places)])
        step *= 2
    if seq_count == 2:
        return values + shift_by(values, 2, 1)
    return lax.psum(values, "seq")


def body(
    tokens, doc_lengths, variate_ids, time_ids, in_proj, out_proj, gate_up, down_proj,
    attn_gain, ffn_gain, query_gain, key_gain, head_bias, cotangent,
):
    seq_count = lax.axis_size("seq")
    seq_rank = lax.axis_index("seq")
    local_rows, width = tokens.shape
    pack_rows = local_rows * seq_count
    head_dim = query_gain.shape[0]
    places = lax.axis_size("dp")
    place = lax.axis_index("dp")
    core, across = place % 2, place // 2 % 2
    groups = places // 4
    spot = jnp.stack(
        [core, across]
        + [
            group * 4 + (across + 1 - near_x) % 2 * 2 + (core + 1 - near_core) % 2
            for near_core in range(2)
            for near_x in range(2)
            for group in range(groups)
        ]
    ).astype(jnp.int32)

    fused = places == 16 and seq_count == 2
    gains = jnp.stack([attn_gain, ffn_gain], axis=1)
    gather = lambda w: lax.all_gather(w, "dp", axis=0, tiled=True)
    first_shard = jnp.concatenate([in_proj, out_proj, jnp.pad(gains, ((0, 0), (0, PAIR - 2)))], axis=1)
    if fused:
        wide, *there = gather_first(first_shard, tokens, time_ids.reshape(-1, PAIR), places)
        slots = [(tokens, time_ids), (there[0], there[1].reshape(-1))]
    else:
        wide = gather(first_shard)
        slots = [(tokens, time_ids)]
        for step in range(1, seq_count):
            slots.append(tuple(shift_by(array, seq_count, -step) for array in slots[0]))
    out_full = wide[:, 3 * width : 4 * width]
    attn_gain_f = wide[:, 4 * width].astype(f32)[None, :]
    ffn_gain_f = wide[:, 4 * width + 1].astype(f32)[None, :]
    shard = in_proj.shape[0]
    hidden_part = down_proj.shape[0] // 2
    folds = hidden_part // shard

    def weights_part(part, gate_up, down_proj):
        columns = gate_up.reshape(shard, 2, places, 2, hidden_part)
        fold_rows = down_proj.reshape(2, folds, shard, width)
        return jnp.concatenate(
            [columns[:, 0, :, part].reshape(shard, -1), columns[:, 1, :, part].reshape(shard, -1)]
            + [fold_rows[part, k] for k in range(folds)],
            axis=1,
        )

    ffn_weights = [
        gather(after(weights_part(0, gate_up, down_proj), wide)),
        weights_part(1, *after((gate_up, down_proj), wide)),
    ]

    positions = jnp.arange(pack_rows, dtype=jnp.int32)
    first_end = doc_lengths[0, 0]
    second_end = first_end + doc_lengths[0, 1]
    segment = (positions >= first_end).astype(jnp.int32) + (positions >= second_end).astype(jnp.int32)
    query_columns, key_columns = slot_columns(segment, variate_ids[0])
    coefficients = bias_columns(head_bias)
    start = seq_rank * local_rows
    query_columns = lax.dynamic_slice_in_dim(query_columns, start, local_rows)
    local_segment = lax.dynamic_slice_in_dim(segment, start, local_rows)
    valid_rows = (local_segment < 2).astype(f32)
    source_columns, source_flags = [], []
    for step in range(seq_count):
        begin = ((seq_rank + step) % seq_count) * local_rows
        source_columns.append(lax.dynamic_slice_in_dim(key_columns, begin, local_rows))
        there = lax.dynamic_slice_in_dim(segment, begin, local_rows).reshape(-1, KEY_ROWS)
        source_flags.append(
            ((there[:, 0] <= local_segment[-1]) & (there[:, -1] >= local_segment[0])).astype(jnp.int32)
        )

    half_dim = head_dim // 2
    frequency = jnp.exp(jnp.arange(half_dim, dtype=f32) * (-math.log(ROPE_BASE) / half_dim))
    qgain = jnp.tile(query_gain, 2)[None, :]
    kgain = jnp.tile(key_gain, 2)[None, :]

    def rope_tables(times):
        angles = times.astype(f32)[:, None] * jnp.tile(frequency, 4)[None, :]
        sign = jnp.where(jnp.arange(PAIR) % head_dim < half_dim, -1.0, 1.0)
        return jnp.cos(angles), jnp.sin(angles) * sign[None, :]

    tables = [rope_tables(times) for _, times in slots]
    seed_grad = cotangent.astype(f32) * valid_rows[:, None]
    seed_low = seed_grad.astype(bf16)
    keyed = []
    for step, (there_tokens, _) in enumerate(slots):
        keys, values, *own = project(
            there_tokens, attn_gain_f, wide, *tables[step], qgain, kgain, step == 0
        )
        keyed.append((keys, values, source_columns[step]))
        if step == 0:
            cosine, sine = tables[0]
            queries, *raws, normed_low = own
            ffn_weights[1] = gather(after(ffn_weights[1], queries))
    attended, full_query = attend(
        jnp.concatenate(source_flags), queries, query_columns, coefficients, keyed
    )

    inputs_f = tokens.astype(f32)
    residual = inputs_f + dot(attended, out_full)
    normed_ffn, _ = rms_forward(residual, ffn_gain_f)
    normed_ffn_low = normed_ffn.astype(bf16)
    def scatter_line(parts):
        lines = [[line * 4 + k for line in range(groups)] for k in range(4)]
        return lax.psum_scatter(parts, "dp", scatter_dimension=0, axis_index_groups=lines, tiled=True)[0]

    def total3(first, *others):
        return sum((other.astype(f32) for other in others), first.astype(f32)).astype(bf16)

    branch, normed_ffn_grad, early_far, early_cross, early_own = feed_forward(
        places, normed_ffn_low, seed_low, residual, None, ffn_weights[0]
    )
    crossed = early_cross[:, :2] + early_far[:groups, :2]
    early_crossed = early_cross[:, 2] + early_far[:groups, 2]
    layer_out, residual_grad, mixed_low, ffn_gain_sum, far, cross, own, received = feed_forward(
        places, after(normed_ffn_low, early_crossed), seed_low, branch, normed_ffn_grad,
        ffn_weights[1], residual, ffn_gain_f, crossed,
    )
    first_total = scatter_line(total3(received, early_own[:, :2], early_far[groups:, :2]))
    second_crossed = cross + far[:groups]
    attended_grad = dot(mixed_low, out_full, NT).astype(bf16)

    attended_grad = dot(mixed_low, out_full, NT).astype(bf16)
    out_grads = outer(spot, attended, mixed_low, width)

    def merge(dqs, dkvs):
        merged, gains = merge_grads(width, 0, dqs, dkvs, raws, cosine, sine, qgain, kgain)
        return merged, jnp.sum(gains[:2].reshape(2, -1, head_dim), axis=1)

    def small_parts(bias, head_gains):
        same_bias = jnp.sum(bias, axis=-1).reshape(-1)
        tail = jnp.concatenate([head_gains[0], head_gains[1], same_bias])
        return jnp.concatenate([ffn_gain_sum[0], tail, jnp.zeros(-tail.shape[0] % 1024, f32)])

    if fused:
        (out_far,), out_cross, out_own = (cross_core(out_grads[0], places),), *out_grads[1:]
        by_line = lambda array: array.reshape(groups, -1, width)
        out_sums = [
            by_line(array) for array in (out_cross + out_far[:, : shard * groups], out_own, out_far[:, shard * groups :])
        ]
        dq_all, bias_all, received, own_kv, line_sums, line_got, late, *_ = attend_back_carry(
            full_query, attended_grad, attended, query_columns, keyed[0], keyed[1],
            (early_crossed, early_own, early_far), (second_crossed, own, far), out_sums,
        )
        in_proj_grad, out_proj_grad, gate_up_grad, down_grad, small, input_grad = finish(
            places, line_sums, line_got, late, first_total, ffn_gain_sum.reshape(-1, PAIR), bias_all,
            cosine, sine, qgain, kgain, attn_gain_f, normed_low, dq_all, received, own_kv, raws,
            wide, tokens, residual_grad,
        )
        rows_done = 2 * width // PAIR
        head_gains = jnp.sum(small[rows_done : rows_done + 2].reshape(2, 2, head_dim), axis=1)
        same_bias = jnp.sum(small[rows_done + 8 :], axis=1)
        small = jnp.concatenate([small[:rows_done].reshape(-1), head_gains.reshape(-1), same_bias])
    else:
        second = scatter_line(total3(cross_x(second_crossed, places), own, far[groups:]))
        early_down = total3(cross_x(early_crossed, places), early_own[:, 2], early_far[groups:, 2])
        early_down = scatter_line(early_down)
        dqs, dkvs, biases = [], [], 0.0
        for step in list(range(1, seq_count)) + [0]:
            dq, dkv, bias = attend_back(
                0, width // PAIR, source_flags[step], full_query, attended_grad, attended,
                query_columns, *keyed[step],
            )
            dqs.append((dq, 0))
            dkvs.append((shift_by(dkv, seq_count, step) if step else dkv, 0))
            biases = biases + bias
        merged_grad, head_gains = merge(dqs, dkvs)

        def sum_rows(pieces):
            crossed, terms = core_sum([pieces], places)
            total = total_of(add_received(terms, cross_x(crossed, places)))
            total = total.reshape(total.shape[0], groups, shard, -1).transpose(1, 0, 2, 3)
            return sum_seq(scatter_line(total), seq_count)

        in_sum = sum_rows(outer(spot, normed_low.T, merged_grad, width))
        out_proj_grad = sum_rows(out_grads)[0]
        in_proj_grad = in_sum.transpose(1, 0, 2).reshape(in_proj.shape)
        first_gates = sum_seq(first_total, seq_count)
        second_sum = sum_seq(second, seq_count)
        downs = [sum_seq(early_down, seq_count), second_sum[2]]
        down_grad = jnp.concatenate(
            [part.reshape(shard, -1, width).transpose(1, 0, 2).reshape(hidden_part, width) for part in downs]
        )
        gate_up_grad = jnp.stack(
            [
                part.reshape(2, shard, places, hidden_part).transpose(1, 0, 2, 3)
                for part in (first_gates, second_sum[:2])
            ],
            axis=3,
        ).reshape(gate_up.shape)
        normed_grad = dot(merged_grad, wide[:, : 3 * width], NT)
        norm_scale = lax.rsqrt(jnp.mean(inputs_f * inputs_f, axis=-1, keepdims=True) + EPSILON)
        input_norm_grad, attn_gain_terms = rms_backward(inputs_f, norm_scale, attn_gain_f, normed_grad)
        input_grad = residual_grad + input_norm_grad
        small = jnp.concatenate([jnp.sum(attn_gain_terms, axis=0), small_parts(biases, head_gains)])
        small = sum_small(small, places, seq_count)
    heads = head_bias.shape[0]
    gain_rows = attn_gain.shape[0]
    here = place * gain_rows
    tail = small[2 * width :]
    same_bias = tail[2 * head_dim : 2 * head_dim + heads]
    return (
        layer_out,
        input_grad,
        in_proj_grad,
        out_proj_grad,
        gate_up_grad,
        down_grad,
        lax.dynamic_slice_in_dim(small, here, gain_rows),
        lax.dynamic_slice_in_dim(small, width + here, gain_rows),
        tail[:head_dim],
        tail[head_dim : 2 * head_dim],
        jnp.stack([same_bias, -same_bias], axis=1),
    )


def solution(mesh):
    in_specs = (
        P(("dp", "seq"), None),
        P("dp", None),
        P("dp", None),
        P(("dp", "seq")),
        P("dp", None),
        P("dp", None),
        P("dp", None),
        P("dp", None),
        P("dp"),
        P("dp"),
        P(),
        P(),
        P(),
        P(("dp", "seq"), None),
    )
    out_specs = (
        P(("dp", "seq"), None),
        P(("dp", "seq"), None),
        P("dp", None),
        P("dp", None),
        P("dp", None),
        P("dp", None),
        P("dp"),
        P("dp"),
        P(),
        P(),
        P(),
    )
    return jax.shard_map(body, mesh=mesh, in_specs=in_specs, out_specs=out_specs, check_vma=False)
```

```python
import functools
import math

import jax
import jax.numpy as jnp
from jax import lax
from jax.experimental import pallas as pl
from jax.experimental.pallas import tpu as pltpu
from jax.sharding import PartitionSpec as P

EPSILON = 1e-06
ROPE_BASE = 10000.0
NEG_FILL = -1e30
PAIR = 128
KEY_ROWS = 256
VMEM_BYTES = 48 * 2**20
NO_COST = pl.CostEstimate(flops=1, bytes_accessed=1, transcendentals=0)
bf16 = jnp.bfloat16
f32 = jnp.float32
NN = (((1,), (0,)), ((), ()))
NT = (((1,), (1,)), ((), ()))
TN = (((0,), (0,)), ((), ()))


def dot(left, right, dims=NN):
    return lax.dot_general(left, right, dims, preferred_element_type=f32)


def split_two(values):
    high = values.astype(bf16)
    return high, (values - high.astype(f32)).astype(bf16)


def lane_index():
    return lax.broadcasted_iota(jnp.int32, (1, PAIR), 1)


def half_ones(same):
    rows = lax.broadcasted_iota(jnp.int32, (2 * PAIR, PAIR), 0) % PAIR
    cols = lax.broadcasted_iota(jnp.int32, (2 * PAIR, PAIR), 1)
    match = (rows < 64) == (cols < 64)
    return jnp.where(match if same else jnp.logical_not(match), 1.0, 0.0).astype(bf16)


def head_sums(values, ones):
    return dot(jnp.concatenate(split_two(values), axis=1), ones)


def swap_halves(values):
    first = lane_index() % 64 < 32
    return jnp.where(first, pltpu.roll(values, PAIR - 32, 1), pltpu.roll(values, 32, 1))


LINES = 4


def line_device(place, line):
    return {"dp": line * 4 + place % 4}


class Spread:
    def __init__(self, shard_ref, whole_ref, arrived, sent, kept):
        self.shard_ref, self.whole_ref = shard_ref, whole_ref
        self.arrived, self.sent, self.kept = arrived, sent, kept
        self.place = place = lax.axis_index("dp")
        self.z, self.x, self.core = place // 4, place // 2 % 2, place % 2
        self.lines = whole_ref.shape[0] // shard_ref.shape[0] // 4
        self.ends = (self.z == 0).astype(jnp.int32) + (self.z == self.lines - 1).astype(jnp.int32)
        self.up, self.down = {"dp": place + 4}, {"dp": place - 4}
        self.over = {"dp": place + 2 - self.x * 4}
        self.twin = {"dp": place + 1 - self.core * 2}
        self.not_last, self.not_first = self.z < self.lines - 1, self.z > 0

    def greet(self, barrier):
        def one(target):
            pl.semaphore_signal(barrier, inc=1, device_id=target, device_id_type=pl.DeviceIdType.MESH)

        pl.when(self.not_last)(lambda: one(self.up))
        pl.when(self.not_first)(lambda: one(self.down))

    def block(self, z, x, core):
        return z * 4 + x * 2 + core

    def rows_of(self, which):
        rows = self.shard_ref.shape[0]
        return self.whole_ref.at[pl.ds(pl.multiple_of(which * rows, rows), rows)]

    def copy(self, which, path, own=False):
        return pltpu.make_async_remote_copy(
            src_ref=self.shard_ref if own else self.rows_of(which),
            dst_ref=self.rows_of(which),
            send_sem=self.sent.at[path, which],
            recv_sem=self.arrived.at[which],
            device_id=(self.up, self.over, self.twin, self.down)[path],
            device_id_type=pl.DeviceIdType.MESH,
        )

    def stay(self):
        me = self.block(self.z, self.x, self.core)
        return pltpu.make_async_copy(self.shard_ref, self.rows_of(me), self.kept.at[0])

    def begin(self):
        me = self.block(self.z, self.x, self.core)
        pl.when(self.not_last)(lambda: self.copy(me, 0, True).start())
        pl.when(self.not_first)(lambda: self.copy(me, 3, True).start())
        self.copy(me, 1, True).start()
        self.copy(me, 2, True).start()
        self.stay().start()

    def along(self, step):
        def take(which, path, more):
            self.copy(which, path).wait_recv()
            pl.when(more)(lambda: self.copy(which, path).start())
            self.copy(which, 1).start()
            self.copy(which, 2).start()

        pl.when(self.z >= step)(
            lambda: take(self.block(self.z - step, self.x, self.core), 0, self.not_last)
        )
        pl.when(self.z + step < self.lines)(
            lambda: take(self.block(self.z + step, self.x, self.core), 3, self.not_first)
        )

    def to_twin(self):
        for line in range(self.lines):
            which = self.block(line, 1 - self.x, self.core)
            self.copy(which, 1).wait_recv()
            self.copy(which, 2).start()

    def end(self):
        for line in range(self.lines):
            for side in range(2):
                self.copy(self.block(line, side, 1 - self.core), 2).wait_recv()
        for line in range(self.lines):
            which = self.block(line, self.x, self.core)
            self.copy(which, 1).wait_send()
            self.copy(which, 2).wait_send()
            self.copy(self.block(line, 1 - self.x, self.core), 2).wait_send()
            pl.when((line <= self.z) & self.not_last)(lambda: self.copy(which, 0).wait_send())
            pl.when((line >= self.z) & self.not_first)(lambda: self.copy(which, 3).wait_send())
        self.stay().wait()


def gather_kernel(
    shard_ref, tokens_ref, times_ref, wide_ref, there_tokens_ref, there_times_ref, arrived, sent, kept, swapped
):
    other = {"seq": 1 - lax.axis_index("seq")}
    spread = Spread(shard_ref, wide_ref, arrived, sent, kept)
    barrier = pltpu.get_barrier_semaphore()
    for target in (spread.over, spread.twin, other):
        pl.semaphore_signal(barrier, inc=1, device_id=target, device_id_type=pl.DeviceIdType.MESH)
    spread.greet(barrier)
    pl.semaphore_wait(barrier, 5 - spread.ends)

    def swap(source, target, index):
        return pltpu.make_async_remote_copy(
            src_ref=source,
            dst_ref=target,
            send_sem=swapped.at[index],
            recv_sem=swapped.at[index + 1],
            device_id=other,
            device_id_type=pl.DeviceIdType.MESH,
        )

    swaps = [swap(tokens_ref, there_tokens_ref, 0), swap(times_ref, there_times_ref, 2)]
    spread.begin()
    for each in swaps:
        each.start()
    for step in range(1, spread.lines):
        spread.along(step)
    spread.to_twin()
    spread.end()
    for each in swaps:
        each.wait()


def gather_first(shard, tokens, times, places):
    anywhere = pl.BlockSpec(memory_space=pl.ANY)
    return pl.pallas_call(
        gather_kernel,
        in_specs=[anywhere] * 3,
        out_specs=[anywhere] * 3,
        out_shape=[
            jax.ShapeDtypeStruct((shard.shape[0] * places, shard.shape[1]), shard.dtype),
            jax.ShapeDtypeStruct(tokens.shape, tokens.dtype),
            jax.ShapeDtypeStruct(times.shape, times.dtype),
        ],
        scratch_shapes=[
            pltpu.SemaphoreType.DMA((places,)),
            pltpu.SemaphoreType.DMA((4, places)),
            pltpu.SemaphoreType.DMA((1,)),
            pltpu.SemaphoreType.DMA((4,)),
        ],
        compiler_params=pltpu.CompilerParams(collective_id=0, has_side_effects=True),
        cost_estimate=NO_COST,
    )(shard, tokens, times)


def qkv_kernel(
    tokens_ref, gain_ref, weight_ref, cos_ref, sin_ref, qgain_ref, kgain_ref,
    k_ref, v_ref, *own_refs,
):
    width = tokens_ref.shape[1]
    values = tokens_ref[...].astype(f32)
    inv = lax.rsqrt(jnp.mean(values * values, axis=-1, keepdims=True) + EPSILON)
    normed = (values * inv * gain_ref[...]).astype(bf16)
    ones = half_ones(True)
    cosine, sine = cos_ref[...], sin_ref[...]
    turned = [(1, k_ref, kgain_ref[...], 1.0)]
    if own_refs:
        q_ref, *raw_refs, normed_ref = own_refs
        normed_ref[...] = normed.T
        turned.append((0, q_ref, qgain_ref[...], 0.125))
    for part, out_ref, head_gain, scale in turned:
        for chunk in range(width // 256):
            start = part * width + chunk * 256
            raw = dot(normed, weight_ref[:, start : start + 256])
            if own_refs:
                raw_refs[part][:, chunk * 256 : (chunk + 1) * 256] = raw
            for tile in range(2):
                u = raw[:, tile * PAIR : (tile + 1) * PAIR]
                unit = lax.rsqrt(head_sums(u * u, ones) * (1.0 / 64) + EPSILON)
                u = u * unit * head_gain
                u = u * cosine + swap_halves(u) * sine
                at = chunk * 256 + tile * PAIR
                out_ref[:, at : at + PAIR] = (u * scale).astype(bf16)
    for chunk in range(width // 256):
        start = 2 * width + chunk * 256
        v_ref[:, chunk * 256 : (chunk + 1) * 256] = dot(
            normed, weight_ref[:, start : start + 256]
        ).astype(bf16)


def project(tokens, gain, weight, cosine, sine, qgain, kgain, own, block=256):
    rows, width = tokens.shape
    sizes = [(width, bf16), (width, bf16)]
    if own:
        sizes += [(width, bf16), (width, f32), (width, f32)]
    by_rows = lambda i: (i, 0)
    whole = lambda i: (0, 0)
    return pl.pallas_call(
        qkv_kernel,
        grid=(rows // block,),
        in_specs=[
            pl.BlockSpec((block, width), by_rows),
            pl.BlockSpec((1, width), whole),
            pl.BlockSpec((width, 3 * width), whole, pipeline_mode=pl.Buffered(1)),
            pl.BlockSpec((block, PAIR), by_rows),
            pl.BlockSpec((block, PAIR), by_rows),
            pl.BlockSpec((1, PAIR), whole),
            pl.BlockSpec((1, PAIR), whole),
        ],
        out_specs=[pl.BlockSpec((block, size), by_rows) for size, _ in sizes]
        + [pl.BlockSpec((width, block), lambda i: (0, i))] * own,
        out_shape=[jax.ShapeDtypeStruct((rows, size), kind) for size, kind in sizes]
        + [jax.ShapeDtypeStruct((width, rows), bf16)] * own,
        compiler_params=pltpu.CompilerParams(vmem_limit_bytes=VMEM_BYTES),
        cost_estimate=NO_COST,
    )(tokens, gain, weight, cosine, sine, qgain, kgain)


def merge_kernel(sources, parts, *refs):
    dq_refs = refs[:parts]
    dkv_refs = refs[parts : parts + sources]
    rawq_ref, rawk_ref, cos_ref, sin_ref, qgain_ref, kgain_ref, out_ref, gains_ref = refs[parts + sources :]
    width = dq_refs[0].shape[1]
    ones = half_ones(True)
    cosine, sine = cos_ref[...], sin_ref[...]

    @pl.when(pl.program_id(0) == 0)
    def _():
        gains_ref[...] = jnp.zeros_like(gains_ref)

    def read(part, at):
        found = [ref[:, at] for ref in dq_refs] if part == 0 else [ref[part - 1, :, at] for ref in dkv_refs]
        return sum(value.astype(f32) for value in found).astype(bf16)

    for part, (raw_ref, head_gain) in enumerate(((rawq_ref, qgain_ref[...]), (rawk_ref, kgain_ref[...]))):
        for tile in range(width // PAIR):
            at = slice(tile * PAIR, (tile + 1) * PAIR)
            grad = read(part, at).astype(f32)
            grad = grad * cosine - swap_halves(grad) * sine
            raw = raw_ref[:, at]
            unit = lax.rsqrt(head_sums(raw * raw, ones) * (1.0 / 64) + EPSILON)
            hat = raw * unit
            gains_ref[part : part + 1, at] += jnp.sum(grad * hat, axis=0, keepdims=True)
            weighted = grad * head_gain
            inner = head_sums(weighted * hat, ones) * (1.0 / 64)
            there = slice(part * width + tile * PAIR, part * width + (tile + 1) * PAIR)
            out_ref[:, there] = (unit * (weighted - hat * inner)).astype(bf16)
    out_ref[:, 2 * width :] = read(2, slice(0, width))


def merge_grads(width, at, dqs, dkvs, raws, cosine, sine, qgain, kgain, block=256):
    rows = raws[0].shape[0]
    by_rows = lambda i: (i, 0)
    whole = lambda i: (0, 0)
    cut = lambda index: pl.BlockSpec((block, width), lambda i: (i, index))
    cut_two = lambda index: pl.BlockSpec((2, block, width), lambda i: (0, i, index))
    return pl.pallas_call(
        functools.partial(merge_kernel, len(dkvs), len(dqs)),
        grid=(rows // block,),
        in_specs=[cut(index) for _, index in dqs]
        + [cut_two(index) for _, index in dkvs]
        + [
            cut(at),
            cut(at),
            pl.BlockSpec((block, PAIR), by_rows),
            pl.BlockSpec((block, PAIR), by_rows),
            pl.BlockSpec((1, PAIR), whole),
            pl.BlockSpec((1, PAIR), whole),
        ],
        out_specs=[pl.BlockSpec((block, 3 * width), by_rows), pl.BlockSpec((8, width), whole)],
        out_shape=[
            jax.ShapeDtypeStruct((rows, 3 * width), bf16),
            jax.ShapeDtypeStruct((8, width), f32),
        ],
        compiler_params=pltpu.CompilerParams(vmem_limit_bytes=VMEM_BYTES),
        cost_estimate=NO_COST,
    )(*[array for array, _ in dqs], *[array for array, _ in dkvs], *raws, cosine, sine, qgain, kgain)


def forward_kernel(sources, query_rows, flags, q_ref, aq_ref, coef_ref, *refs):
    keyed = refs[: 3 * sources]
    out_ref, full_ref, query, total = refs[3 * sources :]
    rows = q_ref.shape[0]
    lane = lane_index()
    half = lane < 64
    mine = (half, jnp.logical_not(half))
    both = q_ref[...]
    extra = aq_ref[...]
    for h in range(2):
        query[h] = jnp.where(mine[h], both, extra * coef_ref[0, h : h + 1, :])
        total[h] = jnp.zeros_like(total[h])
    blocks = keyed[0].shape[0] // KEY_ROWS
    for j in range(sources):
        k_ref, v_ref, ak_ref = keyed[3 * j : 3 * j + 3]
        for b in range(blocks):

            @pl.when(flags[j * blocks + b] != 0)
            def _():
                at = slice(b * KEY_ROWS, (b + 1) * KEY_ROWS)
                keys, values, columns = k_ref[at, :], v_ref[at, :], ak_ref[at, :]
                ones = jnp.ones_like(values)
                keys2 = [jnp.where(mine[h], keys, columns) for h in range(2)]
                values2 = [jnp.where(mine[h], values, ones) for h in range(2)]
                for i in range(rows // query_rows):
                    part = slice(i * query_rows, (i + 1) * query_rows)
                    for h in range(2):
                        probs = jnp.exp(dot(query[h, part, :], keys2[h], NT)).astype(bf16)
                        total[h, part, :] += dot(probs, values2[h])

    outs = []
    for h in range(2):
        summed = total[h]
        outs.append(summed / pltpu.roll(summed, 64, 1))
        log_total = jnp.log(jnp.maximum(summed, 1e-30))
        high = log_total.astype(bf16)
        mid, low = split_two(log_total - high.astype(f32))
        base = lane - 64 if h == 0 else lane
        full_ref[:, h * PAIR : (h + 1) * PAIR] = jnp.where(
            base == 11, -high, jnp.where(base == 12, -mid, jnp.where(base == 13, -low, query[h]))
        )
    out_ref[...] = jnp.where(half, outs[0], outs[1]).astype(bf16)


def attend(flags, queries, query_columns, coefficients, keyed):
    rows, width = queries.shape
    pairs = width // PAIR
    key_rows = keyed[0][0].shape[0]
    sources = len(keyed)
    by_pair = lambda p, f: (0, p)
    whole = lambda p, f: (0, 0)
    in_specs = [
        pl.BlockSpec((rows, PAIR), by_pair),
        pl.BlockSpec((rows, PAIR), whole),
        pl.BlockSpec((1, 2, PAIR), lambda p, f: (p, 0, 0)),
    ]
    operands = [queries, query_columns, coefficients]
    for keys, values, columns in keyed:
        in_specs += [
            pl.BlockSpec((key_rows, PAIR), by_pair),
            pl.BlockSpec((key_rows, PAIR), by_pair),
            pl.BlockSpec((key_rows, PAIR), whole),
        ]
        operands += [keys, values, columns]
    return pl.pallas_call(
        functools.partial(forward_kernel, sources, min(512, rows)),
        grid_spec=pltpu.PrefetchScalarGridSpec(
            num_scalar_prefetch=1,
            grid=(pairs,),
            in_specs=in_specs,
            out_specs=[
                pl.BlockSpec((rows, PAIR), by_pair),
                pl.BlockSpec((rows, 2 * PAIR), by_pair),
            ],
            scratch_shapes=[
                pltpu.VMEM((2, rows, PAIR), bf16),
                pltpu.VMEM((2, rows, PAIR), f32),
            ],
        ),
        out_shape=[
            jax.ShapeDtypeStruct((rows, width), bf16),
            jax.ShapeDtypeStruct((rows, 2 * width), bf16),
        ],
        compiler_params=pltpu.CompilerParams(vmem_limit_bytes=VMEM_BYTES),
        cost_estimate=NO_COST,
    )(flags, *operands)


def backward_start(grad_ref, out_ref, grads, dq_total):
    lane = lane_index()
    half = lane < 64
    mine = (half, jnp.logical_not(half))
    base = (lane - 64, lane)
    both = grad_ref[...]
    row_total = head_sums(both.astype(f32) * out_ref[...].astype(f32), half_ones(False))
    high, low = split_two(row_total)
    zero = jnp.zeros_like(high)
    for h in range(2):
        extra = jnp.where(base[h] == 0, -high, jnp.where(base[h] == 1, -low, zero))
        grads[h] = jnp.where(mine[h], both, extra)
        dq_total[h] = jnp.zeros_like(dq_total[h])


def backward_block(full_ref, keys, values, columns, grads, dq_total):
    lane = lane_index()
    half = lane < 64
    mine = (half, jnp.logical_not(half))
    base = (lane - 64, lane)
    ones = jnp.ones_like(values)
    dks, dvs = [], []
    for h in range(2):
        keys2 = jnp.where(mine[h], keys, columns)
        pick = (base[h] >= 0) & (base[h] < 2)
        values2 = jnp.where(mine[h], values, jnp.where(pick, ones, jnp.zeros_like(ones)))
        full = full_ref[:, h * PAIR : (h + 1) * PAIR]
        probs = jnp.exp(dot(keys2, full, NT))
        score_low = (probs * dot(values2, grads[h], NT)).astype(bf16)
        dks.append(dot(score_low, full))
        dvs.append(dot(probs.astype(bf16), grads[h]))
        dq_total[h] += dot(keys2, score_low, TN)
    return (
        jnp.where(half, dks[0], dks[1]).astype(bf16),
        jnp.where(half, dvs[0], dvs[1]).astype(bf16),
    )


def backward_end(aq_ref, dq_ref, bias_ref, dq_total):
    lane = lane_index()
    base = (lane - 64, lane)
    dq = [dq_total[h].T for h in range(2)]
    dq_ref[...] = (jnp.where(lane < 64, dq[0], dq[1]) * 0.125).astype(dq_ref.dtype)
    variates = aq_ref[...].astype(f32)
    for h in range(2):
        pick = (base[h] >= 0) & (base[h] < 4)
        bias_ref[0, h : h + 1, :] = jnp.sum(
            jnp.where(pick, dq[h] * variates, 0.0), axis=0, keepdims=True
        )


def backward_kernel(
    flags, full_ref, grad_ref, out_ref, aq_ref, k_ref, v_ref, ak_ref,
    dq_ref, dkv_ref, bias_ref, grads, dq_total,
):
    backward_start(grad_ref, out_ref, grads, dq_total)
    for b in range(k_ref.shape[0] // KEY_ROWS):
        at = slice(b * KEY_ROWS, (b + 1) * KEY_ROWS)

        @pl.when(flags[b] != 0)
        def _():
            dkv_ref[0, at, :], dkv_ref[1, at, :] = backward_block(
                full_ref, k_ref[at, :], v_ref[at, :], ak_ref[at, :], grads, dq_total
            )

        @pl.when(flags[b] == 0)
        def _():
            dkv_ref[:, at, :] = jnp.zeros((2, KEY_ROWS, PAIR), bf16)

    backward_end(aq_ref, dq_ref, bias_ref, dq_total)


def attend_back(first_pair, pairs, flags, full, grad, out, query_columns, keys, values, key_columns):
    rows = grad.shape[0]
    width = pairs * PAIR
    key_rows = keys.shape[0]
    by_pair = lambda p, f: (0, p)
    from_pair = lambda p, f: (0, first_pair + p)
    whole = lambda p, f: (0, 0)
    return pl.pallas_call(
        backward_kernel,
        grid_spec=pltpu.PrefetchScalarGridSpec(
            num_scalar_prefetch=1,
            grid=(pairs,),
            in_specs=[
                pl.BlockSpec((rows, 2 * PAIR), from_pair),
                pl.BlockSpec((rows, PAIR), from_pair),
                pl.BlockSpec((rows, PAIR), from_pair),
                pl.BlockSpec((rows, PAIR), whole),
                pl.BlockSpec((key_rows, PAIR), from_pair),
                pl.BlockSpec((key_rows, PAIR), from_pair),
                pl.BlockSpec((key_rows, PAIR), whole),
            ],
            out_specs=[
                pl.BlockSpec((rows, PAIR), by_pair),
                pl.BlockSpec((2, key_rows, PAIR), lambda p, f: (0, 0, p)),
                pl.BlockSpec((1, 2, PAIR), lambda p, f: (p, 0, 0)),
            ],
            scratch_shapes=[
                pltpu.VMEM((2, rows, PAIR), bf16),
                pltpu.VMEM((2, PAIR, rows), f32),
            ],
        ),
        out_shape=[
            jax.ShapeDtypeStruct((rows, width), f32),
            jax.ShapeDtypeStruct((2, key_rows, width), bf16),
            jax.ShapeDtypeStruct((pairs, 2, PAIR), f32),
        ],
        compiler_params=pltpu.CompilerParams(vmem_limit_bytes=VMEM_BYTES),
        cost_estimate=NO_COST,
    )(flags, full, grad, out, query_columns, keys, values, key_columns)


STARTS = (0, 7, 19, 33, 47)
ARRIVALS = (10, 23, 37, 50, 64)


def carry_kernel(
    pairs, full_ref, grad_ref, out_ref, aq_ref,
    far_k_ref, far_v_ref, far_ak_ref, near_k_ref, near_v_ref, near_ak_ref,
    early_across_ref, early_own_ref, early_far_ref, across_ref, own_ref, far_ref,
    out_across_ref, out_own_ref, out_far_ref,
    dq_ref, bias_ref, got_ref, near_ref, line_ref, line_got_ref, late_ref, early_got, across_got, out_got,
    grads, dq_total, stage, terms, sums,
    send_sems, recv_sems, near_sems, across_sems, term_sems, line_send, line_recv, line_own,
):
    step = pl.program_id(0)
    place, rank = lax.axis_index("dp"), lax.axis_index("seq")
    line = place // 4
    other = {"seq": 1 - rank}
    over = {"dp": place + 2 - place // 2 % 2 * 4}
    mesh_id = pl.DeviceIdType.MESH

    def lanes(index):
        return pl.ds(pl.multiple_of(index * PAIR, PAIR), PAIR)

    last = len(STARTS) - 1

    def part_of(refs, part):
        if part == last:
            return refs[0]
        return refs[2] if part == 0 else refs[1].at[:, part - 1]

    def width_of(part):
        return out_own_ref.shape[2] if part == 0 else sums.shape[3]

    def across(part):
        return pltpu.make_async_remote_copy(
            src_ref=part_of((early_across_ref, across_ref, out_across_ref), part),
            dst_ref=part_of((early_got, across_got, out_got), part),
            send_sem=across_sems.at[part, 0], recv_sem=across_sems.at[part, 1],
            device_id=over, device_id_type=mesh_id,
        )

    def load(part, k):
        if k == 0:
            source = part_of((early_own_ref.at[:, 2], own_ref, out_own_ref), part)
        elif k == 1:
            near = pl.ds(LINES, LINES)
            source = part_of((early_far_ref.at[near, 2], far_ref.at[near], out_far_ref), part)
        else:
            source = part_of((early_got, across_got, out_got), part)
        return pltpu.make_async_copy(
            source, terms.at[k, :, :, pl.ds(0, width_of(part))], term_sems.at[k]
        )

    def along(part, k):
        to = lax.rem(line + k, LINES)
        columns = pl.ds(0, width_of(part))
        return pltpu.make_async_remote_copy(
            src_ref=sums.at[part, to, :, columns], dst_ref=line_got_ref.at[k - 1, part, :, columns],
            send_sem=line_send.at[part, k - 1], recv_sem=line_recv.at[part, k - 1],
            device_id=line_device(place, to), device_id_type=mesh_id,
        )

    def stay(part):
        if part == last:
            return pltpu.make_async_copy(sums.at[part], late_ref, line_own.at[part])
        columns = pl.ds(0, width_of(part))
        return pltpu.make_async_copy(
            sums.at[part, line, :, columns], line_ref.at[part, :, columns], line_own.at[part]
        )

    def to_other(pair):
        return pltpu.make_async_remote_copy(
            src_ref=stage.at[pair], dst_ref=got_ref.at[:, :, lanes(pair)], send_sem=send_sems.at[pair],
            recv_sem=recv_sems.at[pair], device_id=other, device_id_type=mesh_id,
        )

    def to_near(pair):
        return pltpu.make_async_copy(
            stage.at[pairs + pair], near_ref.at[:, :, lanes(pair)], near_sems.at[pair]
        )

    @pl.when(step == 0)
    def _():
        barrier = pltpu.get_barrier_semaphore()
        peers = [other, over] + [line_device(place, lax.rem(line + k, LINES)) for k in range(1, LINES)]
        for target in peers:
            pl.semaphore_signal(barrier, inc=1, device_id=target, device_id_type=mesh_id)
        pl.semaphore_wait(barrier, len(peers))

    def arrive(part):
        across(part).wait()
        load(part, 2).start()
        for k in range(3):
            load(part, k).wait()
        columns = width_of(part)
        for i in range(LINES):
            sums[part, i, :, :columns] = sum(
                terms[k, i, :, :columns].astype(f32) for k in range(3)
            ).astype(bf16)
        if part < last:
            for k in range(1, LINES):
                along(part, k).start()
        stay(part).start()

    def go_on(quarter):
        for part in range(last + 1):

            before = ARRIVALS[part] - 3
            if STARTS[part] % 4 == quarter:

                @pl.when(step == STARTS[part] // 4)
                def _():
                    across(part).start()

            if before % 4 == quarter:

                @pl.when(step == before // 4)
                def _():
                    load(part, 0).start()
                    load(part, 1).start()

            if part < last and ARRIVALS[part] % 4 == quarter:
                pl.when(step == ARRIVALS[part] // 4)(functools.partial(arrive, part))

    backward_start(grad_ref, out_ref, grads, dq_total)
    is_far = step < pairs
    key_rows = min(512, far_k_ref.shape[0])
    key_blocks = far_k_ref.shape[0] // key_rows
    for b in range(key_blocks):
        at = slice(b * key_rows, (b + 1) * key_rows)
        for quarter in range(4 * b // key_blocks, 4 * (b + 1) // key_blocks):
            go_on(quarter)
        block = [
            jnp.where(is_far, far[at, :], near[at, :])
            for far, near in ((far_k_ref, near_k_ref), (far_v_ref, near_v_ref), (far_ak_ref, near_ak_ref))
        ]
        stage[step, 0, at, :], stage[step, 1, at, :] = backward_block(
            full_ref, *block, grads, dq_total
        )

    backward_end(aq_ref, dq_ref, bias_ref, dq_total)
    pl.when(is_far)(lambda: to_other(step).start())
    pl.when(jnp.logical_not(is_far))(lambda: to_near(step - pairs).start())

    @pl.when(step == pl.num_programs(0) - 1)
    def _():
        arrive(last)
        for pair in range(pairs):
            to_near(pair).wait()
            to_other(pair).wait()
        for part in range(last + 1):
            if part < last:
                for k in range(1, LINES):
                    along(part, k).wait()
            stay(part).wait()


def attend_back_carry(full, grad, out, query_columns, near, far, early, sums, out_sums):
    rows, width = grad.shape
    pairs = width // PAIR
    key_rows = near[0].shape[0]
    pair_of = lambda i: jnp.where(i < pairs, i, i - pairs)
    by_pair = lambda i: (0, pair_of(i))
    far_pair = lambda i: (0, jnp.minimum(i, pairs - 1))
    near_pair = lambda i: (0, jnp.maximum(i - pairs, 0))
    whole = lambda i: (0, 0)
    anywhere = pl.BlockSpec(memory_space=pl.ANY)
    shard, hidden = sums[0].shape[2:]
    parts = len(STARTS)

    def key_specs(pair):
        return [
            pl.BlockSpec((key_rows, PAIR), pair),
            pl.BlockSpec((key_rows, PAIR), pair),
            pl.BlockSpec((key_rows, PAIR), whole),
        ]

    return pl.pallas_call(
        functools.partial(carry_kernel, pairs),
        grid=(2 * pairs,),
        in_specs=[
            pl.BlockSpec((rows, 2 * PAIR), by_pair),
            pl.BlockSpec((rows, PAIR), by_pair),
            pl.BlockSpec((rows, PAIR), by_pair),
            pl.BlockSpec((rows, PAIR), whole),
        ]
        + key_specs(far_pair)
        + key_specs(near_pair)
        + [anywhere] * 9,
        out_specs=[
            pl.BlockSpec((rows, PAIR), lambda i: (0, i)),
            pl.BlockSpec((1, 2, PAIR), lambda i: (i, 0, 0)),
        ]
        + [anywhere] * 8,
        out_shape=[
            jax.ShapeDtypeStruct((rows, 2 * width), bf16),
            jax.ShapeDtypeStruct((2 * pairs, 2, PAIR), f32),
            jax.ShapeDtypeStruct((2, key_rows, width), bf16),
            jax.ShapeDtypeStruct((2, key_rows, width), bf16),
            jax.ShapeDtypeStruct((parts - 1, shard, hidden), bf16),
            jax.ShapeDtypeStruct((LINES - 1, parts - 1, shard, hidden), bf16),
            jax.ShapeDtypeStruct((LINES, shard, hidden), bf16),
            jax.ShapeDtypeStruct(early[0].shape, bf16),
            jax.ShapeDtypeStruct(sums[0].shape, bf16),
            jax.ShapeDtypeStruct(out_sums[0].shape, bf16),
        ],
        scratch_shapes=[
            pltpu.VMEM((2, rows, PAIR), bf16),
            pltpu.VMEM((2, PAIR, rows), f32),
            pltpu.VMEM((2 * pairs, 2, key_rows, PAIR), bf16),
            pltpu.VMEM((3, LINES, shard, hidden), bf16),
            pltpu.VMEM((parts, LINES, shard, hidden), bf16),
            pltpu.SemaphoreType.DMA((pairs,)),
            pltpu.SemaphoreType.DMA((pairs,)),
            pltpu.SemaphoreType.DMA((pairs,)),
            pltpu.SemaphoreType.DMA((parts, 2)),
            pltpu.SemaphoreType.DMA((3,)),
            pltpu.SemaphoreType.DMA((parts - 1, LINES - 1)),
            pltpu.SemaphoreType.DMA((parts - 1, LINES - 1)),
            pltpu.SemaphoreType.DMA((parts,)),
        ],
        compiler_params=pltpu.CompilerParams(
            vmem_limit_bytes=VMEM_BYTES, collective_id=3, has_side_effects=True
        ),
        cost_estimate=NO_COST,
    )(full, grad, out, query_columns, *far, *near, *early, *sums, *out_sums)


def slot_columns(segment, variates):
    column = jnp.arange(PAIR, dtype=jnp.int32)[None, :] % 64
    same_var = (column < 8) & (variates[:, None] == column % 4)
    in_seg = (column >= 8) & (column < 11)
    same_seg = segment[:, None] == column - 8
    three = (column >= 11) & (column < 14)
    query = jnp.where(in_seg & jnp.logical_not(same_seg), NEG_FILL, same_var.astype(f32))
    key = (same_var | (in_seg & same_seg) | three).astype(f32)
    return query.astype(bf16), key.astype(bf16)


def bias_columns(head_bias):
    delta = head_bias[:, 0] - head_bias[:, 1]
    high, low = split_two(delta)
    heads = delta.shape[0]
    row = jnp.concatenate(
        [
            jnp.broadcast_to(high[:, None], (heads, 4)),
            jnp.broadcast_to(low[:, None], (heads, 4)),
            jnp.ones((heads, 3), bf16),
            jnp.zeros((heads, 53), bf16),
        ],
        1,
    )
    return jnp.concatenate([row, row], 1).reshape(heads // 2, 2, PAIR)


def arrange_rows(places, spot, left_ref, turned, arranged):
    shard = left_ref.shape[1] // places
    turned[...] = left_ref[...].T
    for i in range(places):
        at = pl.multiple_of(spot[2 + i] * shard, shard)
        arranged[i * shard : (i + 1) * shard, :] = turned[pl.ds(at, shard), :]


def ffn_kernel(
    places, first, nf_ref, seed_ref, start_ref, nfstart_ref, wg_ref, wu_ref, wd_ref, *refs
):
    if first:
        branch_ref, nfgrad_ref, far_ref, cross_ref, own_ref, *refs = refs
    else:
        resid_ref, gain_ref, across_ref, branch_ref, nfgrad_ref, *refs = refs
        low_ref, gain_grad_ref, far_ref, cross_ref, own_ref, got_ref, *refs = refs
    turned, branch, columns_out, rows_out, sems, arrived, *x_sems = refs
    step = pl.program_id(0)
    steps = pl.num_programs(0)
    rows, width = nf_ref.shape
    shard = width // places
    chunk = wg_ref.shape[1]
    folds = chunk // 2 // shard

    place = lax.axis_index("dp")
    groups = places // 4

    twin = {"dp": place + 1 - place % 2 * 2}
    over = {"dp": place + 2 - place // 2 % 2 * 4}
    mesh_id = pl.DeviceIdType.MESH

    def carry():
        return pltpu.make_async_remote_copy(
            src_ref=across_ref, dst_ref=got_ref, send_sem=x_sems[0].at[0], recv_sem=x_sems[0].at[1],
            device_id=over, device_id_type=mesh_id,
        )

    @pl.when(step == 0)
    def _():
        barrier = pltpu.get_barrier_semaphore()
        for target in (twin,) if first else (twin, over):
            pl.semaphore_signal(barrier, inc=1, device_id=target, device_id_type=mesh_id)
        pl.semaphore_wait(barrier, 1 if first else 2)
        if not first:
            carry().start()
        turned[...] = nf_ref[...].T
        branch[...] = start_ref[...]
        nfgrad_ref[...] = jnp.zeros_like(nfgrad_ref) if first else nfstart_ref[...]

    def spot_of(line, x, core):
        near_core = (core == place % 2).astype(jnp.int32)
        near_x = (x == place // 2 % 2).astype(jnp.int32)
        return (near_core * 2 + near_x) * groups + line

    def to_twin(source, target, send_sem, recv_sem):
        return pltpu.make_async_remote_copy(
            src_ref=source, dst_ref=target, send_sem=send_sem, recv_sem=recv_sem,
            device_id=twin, device_id_type=mesh_id,
        )

    def column_copies(at):
        slot = lax.rem(at, 2)
        start = pl.multiple_of(at * chunk, chunk)
        made, begin = [], 0
        for k, ref in enumerate((far_ref, cross_ref, own_ref)):
            count = ref.shape[0]
            source = columns_out.at[slot, pl.ds(begin, count)]
            target = ref.at[:, pl.ds(0, 2), :, pl.ds(start, chunk)]
            if k == 0:
                made.append(to_twin(source, target, sems.at[slot, k], arrived.at[at, 0]))
            else:
                made.append(pltpu.make_async_copy(source, target, sems.at[slot, k]))
            begin += count
        return made

    def row_copies(at, ref, index, k):
        slot = lax.rem(at, 2)
        source, target = rows_out.at[slot, k], ref.at[index, 2]
        if k == 0:
            return to_twin(source, target, sems.at[slot, 3], arrived.at[at, 1])
        return pltpu.make_async_copy(source, target, sems.at[slot, 4])

    def sent(copy):
        copy.wait_send() if copy.is_remote else copy.wait()

    def each_copy(at, act):
        for copy in column_copies(at):
            act(copy)
        line, x = at // 2, lax.rem(at, 2)
        near = x == place // 2 % 2
        act(row_copies(at, far_ref, near.astype(jnp.int32) * groups + line, 0))
        pl.when(near)(lambda: act(row_copies(at, own_ref, line, 1)))
        pl.when(jnp.logical_not(near))(lambda: act(row_copies(at, cross_ref, line, 1)))

    @pl.when(step >= 2)
    def _():
        each_copy(step - 2, sent)

    slot = lax.rem(step, 2)
    wg, wu = wg_ref[...], wu_ref[...]
    wd = jnp.concatenate(
        [
            wd_ref[i * shard : (i + 1) * shard, k * width : (k + 1) * width]
            for i in range(2)
            for k in range(folds)
        ],
        axis=0,
    )
    hiddens, gates, ups = [], [], []
    part_rows = min(512, rows)
    for i in range(rows // part_rows):
        at = slice(i * part_rows, (i + 1) * part_rows)
        nf = nf_ref[at, :]
        g, u = dot(nf, wg), dot(nf, wu)
        hidden_grad = dot(seed_ref[at, :], wd, NT)
        sg = 1.0 / (1.0 + jnp.exp(-g))
        silu = g * sg
        hidden = (silu * u).astype(bf16)
        slope = hidden_grad * sg
        gate = (slope * u * (1.0 + (g - silu))).astype(bf16)
        up = (slope * g).astype(bf16)
        branch[at, :] += dot(hidden, wd)
        nfgrad_ref[at, :] += dot(gate, wg, NT) + dot(up, wu, NT)
        hiddens.append(hidden)
        gates.append(gate)
        ups.append(up)
    hidden = jnp.concatenate(hiddens, axis=0)
    down = dot(hidden, seed_ref[...], TN).astype(bf16)
    on_upper = place % 2 == 1
    lower, upper = down[: chunk // 2, :], down[chunk // 2 :, :]
    for i, part in enumerate((jnp.where(on_upper, lower, upper), jnp.where(on_upper, upper, lower))):
        for k in range(folds):
            rows_out[slot, i, :, k * width : (k + 1) * width] = part[k * shard : (k + 1) * shard, :]
    for part, grad in enumerate((gates, ups)):
        columns = dot(turned[...], jnp.concatenate(grad, axis=0)).astype(bf16)
        for j in range(places):
            spot = spot_of(j // 4, j // 2 % 2, j % 2)
            columns_out[slot, spot, part] = columns[j * shard : (j + 1) * shard, :]
    each_copy(step, lambda copy: copy.start())

    def through_norm():
        gain = gain_ref[...]
        gain_grad = jnp.zeros_like(gain)
        part_rows = min(256, rows)
        for i in range(rows // part_rows):
            at = slice(i * part_rows, (i + 1) * part_rows)
            values, upstream = resid_ref[at, :], nfgrad_ref[at, :]
            inv = lax.rsqrt(jnp.mean(values * values, axis=-1, keepdims=True) + EPSILON)
            hat = values * inv
            weighted = upstream * gain
            inner = jnp.mean(weighted * hat, axis=-1, keepdims=True)
            gain_grad = gain_grad + jnp.sum(upstream * hat, axis=0, keepdims=True)
            total = seed_ref[at, :].astype(f32) + inv * (weighted - hat * inner)
            nfgrad_ref[at, :] = total
            low_ref[at, :] = total.astype(bf16)
        gain_grad_ref[...] = gain_grad

    @pl.when(step == steps - 1)
    def _():
        branch_ref[...] = branch[...].astype(branch_ref.dtype)
        each_copy(step - 1, sent)
        each_copy(step, sent)
        for at in range(places // 2):
            column_copies(at)[0].wait_recv()
            near = (at % 2 == place // 2 % 2).astype(jnp.int32)
            row_copies(at, far_ref, near * groups + at // 2, 0).wait_recv()
        if not first:
            through_norm()
            carry().wait()


def feed_forward(places, normed, seed, start, nfstart, weights, resid=None, gain=None, across=None):
    rows, width = normed.shape
    first = nfstart is None
    hidden = weights.shape[1] // 3
    chunk = 2 * hidden // places
    steps = places // 2
    shard = width // places
    whole = lambda t: (0, 0)
    once = pl.Buffered(1)
    return pl.pallas_call(
        functools.partial(ffn_kernel, places, first),
        grid=(steps,),
        in_specs=[
            pl.BlockSpec((rows, width), whole, pipeline_mode=once),
            pl.BlockSpec((rows, width), whole, pipeline_mode=once),
            pl.BlockSpec((rows, width), whole, pipeline_mode=once),
            pl.BlockSpec((8, 128) if first else (rows, width), whole, pipeline_mode=once),
            pl.BlockSpec((width, chunk), lambda t: (0, t)),
            pl.BlockSpec((width, chunk), lambda t: (0, steps + t)),
            pl.BlockSpec((2 * shard, hidden), lambda t: (t, 2)),
        ]
        + (
            []
            if first
            else [
                pl.BlockSpec((rows, width), whole, pipeline_mode=once),
                pl.BlockSpec((1, width), whole),
                pl.BlockSpec(memory_space=pl.ANY),
            ]
        ),
        out_specs=[
            pl.BlockSpec((rows, width), whole),
            pl.BlockSpec((rows, width), whole),
        ]
        + ([] if first else [pl.BlockSpec((rows, width), whole), pl.BlockSpec((1, width), whole)])
        + [pl.BlockSpec(memory_space=pl.ANY)] * (3 if first else 4),
        scratch_shapes=[
            pltpu.VMEM((width, rows), bf16),
            pltpu.VMEM((rows, width), f32),
            pltpu.VMEM((2, places, 2, shard, chunk), bf16),
            pltpu.VMEM((2, 2, shard, hidden), bf16),
            pltpu.SemaphoreType.DMA((2, 5)),
            pltpu.SemaphoreType.DMA((steps, 2)),
        ]
        + [pltpu.SemaphoreType.DMA((2,))] * (not first),
        out_shape=[
            jax.ShapeDtypeStruct((rows, width), f32 if first else bf16),
            jax.ShapeDtypeStruct((rows, width), f32),
        ]
        + (
            []
            if first
            else [jax.ShapeDtypeStruct((rows, width), bf16), jax.ShapeDtypeStruct((1, width), f32)]
        )
        + [jax.ShapeDtypeStruct((places // part, 3, shard, hidden), bf16) for part in (2, 4, 4)]
        + ([] if first else [jax.ShapeDtypeStruct(across.shape, bf16)]),
        compiler_params=pltpu.CompilerParams(
            vmem_limit_bytes=56 * 2**20, collective_id=1 if first else 2, has_side_effects=True
        ),
        cost_estimate=NO_COST,
    )(
        normed, seed, start, start if first else nfstart, weights, weights, weights,
        *(() if first else (resid, gain, across)),
    )


def outer_kernel(places, spot, left_ref, right_ref, far_ref, cross_ref, own_ref, turned, arranged):
    width = left_ref.shape[1]

    @pl.when(pl.program_id(0) == 0)
    def _():
        arrange_rows(places, spot, left_ref, turned, arranged)

    right = right_ref[...]
    half = width // 2
    far_ref[0] = dot(arranged[:half, :], right).astype(bf16)
    cross_ref[0] = dot(arranged[half : half + half // 2, :], right).astype(bf16)
    own_ref[0] = dot(arranged[half + half // 2 :, :], right).astype(bf16)


def outer(spot, left, right, block):
    rows, width = left.shape
    columns = right.shape[1]
    places = spot.shape[0] - 2
    by_cols = lambda t, o: (0, t)
    one_block = lambda t, o: (t, 0, 0)
    return pl.pallas_call(
        functools.partial(outer_kernel, places),
        grid_spec=pltpu.PrefetchScalarGridSpec(
            num_scalar_prefetch=1,
            grid=(columns // block,),
            in_specs=[
                pl.BlockSpec((rows, width), lambda t, o: (0, 0)),
                pl.BlockSpec((rows, block), by_cols),
            ],
            out_specs=[
                pl.BlockSpec((1, width // 2, block), one_block),
                pl.BlockSpec((1, width // 4, block), one_block),
                pl.BlockSpec((1, width // 4, block), one_block),
            ],
            scratch_shapes=[pltpu.VMEM((width, rows), bf16), pltpu.VMEM((width, rows), bf16)],
        ),
        out_shape=[
            jax.ShapeDtypeStruct((columns // block, width // 2, block), bf16),
            jax.ShapeDtypeStruct((columns // block, width // 4, block), bf16),
            jax.ShapeDtypeStruct((columns // block, width // 4, block), bf16),
        ],
        compiler_params=pltpu.CompilerParams(vmem_limit_bytes=VMEM_BYTES),
        cost_estimate=NO_COST,
    )(spot, left, right)


def finish_kernel(
    line_ref, late_ref, first_ref, ffn_ref, bias_ref, cos_ref, sin_ref, qgain_ref, kgain_ref, gain_ref,
    line_got_ref, normed_ref, dq_ref, got_kv_ref, own_kv_ref, rawq_ref, rawk_ref, weight_ref, tokens_ref, resid_ref,
    in_ref, out_ref, gate_up_ref, down_ref, small_out_ref, grad_ref,
    merged, low_a, low_b, low_c, low_d, wide_a, wide_b, sums,
    line_there, arranged, far, own, core_got, x_sent, x_got, z_sent, z_got, y_sent, y_got,
    first_got, second, second_got, late_got, late, late_there, small_sent, small_got,
    core_sems, x_sems, z_send, z_recv, y_sems, first_sems, second_sems, late_send, late_recv, late_sems, small_sems,
    load_sems, row_sems, store_sem,
):
    place, rank = lax.axis_index("dp"), lax.axis_index("seq")
    line = place // 4
    mesh_id = pl.DeviceIdType.MESH
    twin = {"dp": place + 1 - place % 2 * 2}
    over = {"dp": place + 2 - place // 2 % 2 * 4}
    other = {"seq": 1 - rank}
    lines = [line_device(place, lax.rem(line + k, LINES)) for k in range(1, LINES)]
    low = line_device(place, line + 1 - line % 2 * 2)
    high = line_device(place, lax.rem(line + 2, LINES))
    blocks, quarter, columns = x_sent.shape
    rows, width = merged.shape[0], low_a.shape[1]
    step = min(256, rows)
    shard = quarter // LINES
    places = 4 * LINES

    def send(source, target, sems, to):
        return pltpu.make_async_remote_copy(
            src_ref=source, dst_ref=target, send_sem=sems[0], recv_sem=sems[1],
            device_id=to, device_id_type=mesh_id,
        )

    def pair_of(sems, *index):
        return sems.at[*index, 0], sems.at[*index, 1]

    to_core = [send(far.at[b], core_got.at[b], pair_of(core_sems, b), twin) for b in range(blocks)]
    to_x = [send(x_sent.at[b], x_got.at[b], pair_of(x_sems, b), over) for b in range(blocks)]
    to_y = [send(y_sent.at[b], y_got.at[b], pair_of(y_sems, b), other) for b in range(blocks)]
    first_y = send(first_ref, first_got, pair_of(first_sems), other)
    second_y = send(second, second_got, pair_of(second_sems), other)
    late_y = send(late, late_there, pair_of(late_sems), other)

    def late_z(k):
        return send(
            late_ref.at[lax.rem(line + k, LINES)], late_got.at[k - 1],
            (late_send.at[k - 1], late_recv.at[k - 1]), lines[k - 1],
        )

    rounds = [
        send(small_sent.at[k], small_got.at[k], pair_of(small_sems, k), to)
        for k, to in enumerate((twin, over, low, high, other))
    ]

    def to_z(b, k):
        return send(
            z_sent.at[b, lax.rem(line + k, LINES)], z_got.at[b, k - 1],
            (z_send.at[b, k - 1], z_recv.at[b, k - 1]), lines[k - 1],
        )

    def cut(ref, index):
        return ref.at[:, pl.ds(index * width, width)]

    def load(k):
        source, target = (
            (line_got_ref, line_there), (own_kv_ref.at[1], low_b), (got_kv_ref.at[1], low_c),
            (rawk_ref, wide_a), (own_kv_ref.at[0], low_d), (rawq_ref, wide_b),
            (got_kv_ref.at[0], low_a), (cut(dq_ref, 0), low_b), (cut(dq_ref, 1), low_c),
            (tokens_ref, low_d), (resid_ref, wide_a),
            (cut(weight_ref, 0), low_b), (cut(weight_ref, 1), low_c), (cut(weight_ref, 2), low_a),
        )[k]
        return pltpu.make_async_copy(source, target, load_sems.at[k])

    def start(*which):
        for k in which:
            load(k).start()

    def ready(*which):
        for k in which:
            load(k).wait()

    store = pltpu.make_async_copy(wide_b, grad_ref, store_sem.at[0])

    barrier = pltpu.get_barrier_semaphore()
    peers = [twin, over, other] + lines
    for target in peers:
        pl.semaphore_signal(barrier, inc=1, device_id=target, device_id_type=mesh_id)
    pl.semaphore_wait(barrier, len(peers))
    def arrange(i):
        near_core = (i % 2 == place % 2).astype(jnp.int32)
        near_x = (i // 2 % 2 == place // 2 % 2).astype(jnp.int32)
        at = pl.multiple_of(((near_core * 2 + near_x) * LINES + i // 4) * shard, shard)
        return pltpu.make_async_copy(
            normed_ref.at[pl.ds(i * shard, shard)], arranged.at[pl.ds(at, shard)], row_sems.at[i]
        )

    start(1, 2)
    for i in range(places):
        arrange(i).start()
    for copy in [first_y] + [late_z(k) for k in range(1, LINES)]:
        copy.start()
    start(4, 3, 6, 0, 5)

    def product(begin, count, b):
        return dot(arranged[begin : begin + count, :], merged[:, b * columns : (b + 1) * columns])

    def send_block(b):
        far[b] = product(0, 2 * quarter, b).astype(bf16)
        to_core[b].start()
        cross = product(2 * quarter, quarter, b)
        own[b] = product(3 * quarter, quarter, b).astype(bf16)
        to_core[b].wait()
        x_sent[b] = (cross + core_got[b, :quarter].astype(f32)).astype(bf16)
        to_x[b].start()

    def pass_on(b):
        to_x[b].wait()
        total = own[b].astype(f32) + core_got[b, quarter:].astype(f32) + x_got[b].astype(f32)
        total = total.astype(bf16)
        for k in range(LINES):
            z_sent[b, k] = total[k * shard : (k + 1) * shard, :]
        for k in range(1, LINES):
            to_z(b, k).start()

    ones = half_ones(True)

    def turn_back(b, left, right, raw_ref, head_gain):
        sums[b : b + 1, :] = jnp.zeros((1, PAIR), f32)

        def some_rows(i, carry):
            at = pl.ds(pl.multiple_of(i * step, step), step)
            cosine, sine = cos_ref[at, :], sin_ref[at, :]
            for tile in range(width // PAIR):
                lanes = slice(tile * PAIR, (tile + 1) * PAIR)
                grad = left[at, lanes].astype(f32) + right[at, lanes].astype(f32)
                grad = grad.astype(bf16).astype(f32)
                grad = grad * cosine - swap_halves(grad) * sine
                raw = raw_ref[at, lanes]
                unit = lax.rsqrt(head_sums(raw * raw, ones) * (1.0 / 64) + EPSILON)
                hat = raw * unit
                sums[b : b + 1, :] += jnp.sum(grad * hat, axis=0, keepdims=True)
                weighted = grad * head_gain
                inner = head_sums(weighted * hat, ones) * (1.0 / 64)
                there = slice(b * width + tile * PAIR, b * width + (tile + 1) * PAIR)
                merged[at, there] = (unit * (weighted - hat * inner)).astype(bf16)
            return carry

        lax.fori_loop(0, rows // step, some_rows, 0)

    ready(1, 2)

    def add_rows(i, carry):
        at = pl.ds(pl.multiple_of(i * step, step), step)
        merged[at, 2 * width :] = (low_b[at, :].astype(f32) + low_c[at, :].astype(f32)).astype(bf16)
        return carry

    lax.fori_loop(0, rows // step, add_rows, 0)
    start(7, 8)
    for i in range(places):
        arrange(i).wait()
    send_block(4)
    send_block(5)
    ready(3, 4, 6)
    turn_back(1, low_d, low_a, wide_a, kgain_ref[...])
    start(9, 10, 13)
    send_block(2)
    send_block(3)
    ready(0)
    for i in range(line_ref.shape[0]):
        second[i] = sum(
            part.astype(f32) for part in [line_ref[i]] + [line_there[k, i] for k in range(LINES - 1)]
        ).astype(bf16)
    second_y.start()
    pass_on(4)
    ready(5, 7, 8)
    turn_back(0, low_b, low_c, wide_b, qgain_ref[...])
    start(11, 12)
    pass_on(5)
    send_block(0)
    send_block(1)
    pass_on(2)
    pass_on(3)

    ready(9, 10, 11, 12, 13)
    gain = gain_ref[...]
    gain_grad = jnp.zeros_like(gain)
    for i in range(rows // step):
        at = slice(i * step, (i + 1) * step)
        normed_grad = sum(
            dot(merged[at, b * width : (b + 1) * width], part[...], NT)
            for b, part in enumerate((low_b, low_c, low_a))
        )
        values = low_d[at, :].astype(f32)
        inv = lax.rsqrt(jnp.mean(values * values, axis=-1, keepdims=True) + EPSILON)
        hat = values * inv
        weighted = normed_grad * gain
        inner = jnp.mean(weighted * hat, axis=-1, keepdims=True)
        wide_b[at, :] = wide_a[at, :] + inv * (weighted - hat * inner)
        gain_grad = gain_grad + jnp.sum(normed_grad * hat, axis=0, keepdims=True)
    store.start()
    tiles = width // PAIR
    for k in range(tiles):
        small_sent[0, k : k + 1, :] = gain_grad[:, k * PAIR : (k + 1) * PAIR]
    small_sent[0, tiles : 2 * tiles, :] = ffn_ref[...]
    small_sent[0, 2 * tiles : 2 * tiles + 8, :] = sums[...]
    for pair in range(tiles):
        at = 2 * tiles + 8 + 2 * pair
        small_sent[0, at : at + 2, :] = bias_ref[pair] + bias_ref[tiles + pair]
    rounds[0].start()

    def next_round(k):
        rounds[k].wait()
        total = small_sent[k] + small_got[k]
        if k + 1 < len(rounds):
            small_sent[k + 1] = total
            rounds[k + 1].start()
        else:
            small_out_ref[...] = total

    def to_last(b):
        for k in range(1, LINES):
            to_z(b, k).wait()
        total = z_sent[b, line].astype(f32)
        for k in range(LINES - 1):
            total = total + z_got[b, k].astype(f32)
        y_sent[b] = total.astype(bf16)
        to_y[b].start()

    for k in range(1, LINES):
        late_z(k).wait()
    late[...] = sum(
        part.astype(f32) for part in [late_ref[line]] + [late_got[k] for k in range(LINES - 1)]
    ).astype(bf16)
    late_y.start()
    next_round(0)
    pass_on(0)
    pass_on(1)
    next_round(1)
    for b in (4, 5, 2, 3):
        to_last(b)
    next_round(2)
    first_y.wait()
    second_y.wait()
    part_columns = second.shape[2] // places
    hidden = second.shape[2] * 2
    for part in range(2):
        halves = [
            first_ref[part].astype(f32) + first_got[part].astype(f32),
            second[1 + part].astype(f32) + second_got[1 + part].astype(f32),
        ]
        for j in range(places):
            for h in range(2):
                at = part * hidden + (2 * j + h) * part_columns
                gate_up_ref[:, at : at + part_columns] = halves[h][:, j * part_columns : (j + 1) * part_columns]
    next_round(3)
    to_last(0)
    to_last(1)
    out_ref[...] = second[0, :, :width].astype(f32) + second_got[0, :, :width].astype(f32)
    late_y.wait()
    for h in range(2):
        if h == 0:
            total = late[...].astype(f32) + late_there[...].astype(f32)
        else:
            total = second[3].astype(f32) + second_got[3].astype(f32)
        for k in range(total.shape[1] // width):
            at = h * down_ref.shape[0] // 2 + k * shard
            down_ref[at : at + shard, :] = total[:, k * width : (k + 1) * width]
    next_round(4)
    for b in (4, 5, 2, 3, 0, 1):
        to_y[b].wait()
        in_ref[:, b * columns : (b + 1) * columns] = y_sent[b].astype(f32) + y_got[b].astype(f32)
    store.wait()


def finish(
    places, line_sums, line_got, late, first, ffn_gain, bias, cosine, sine, qgain, kgain, gain,
    normed, dq, got_kv, own_kv, raws, weight, tokens, resid,
):
    rows, width = tokens.shape
    blocks, columns = 6, width // 2
    quarter, shard = width // 4, width // places
    hidden = line_sums.shape[2]
    small = (4 * width // PAIR + 8, PAIR)
    vmem = pl.BlockSpec(memory_space=pltpu.VMEM)
    anywhere = pl.BlockSpec(memory_space=pl.ANY)
    dma = pltpu.SemaphoreType.DMA
    return pl.pallas_call(
        finish_kernel,
        in_specs=[vmem] * 10 + [anywhere] * 10,
        out_specs=[vmem] * 5 + [anywhere],
        out_shape=[
            jax.ShapeDtypeStruct((shard, blocks * columns), f32),
            jax.ShapeDtypeStruct((shard, width), f32),
            jax.ShapeDtypeStruct((shard, 4 * hidden), f32),
            jax.ShapeDtypeStruct((2 * hidden // places, width), f32),
            jax.ShapeDtypeStruct(small, f32),
            jax.ShapeDtypeStruct((rows, width), f32),
        ],
        scratch_shapes=[
            pltpu.VMEM((rows, blocks * columns), bf16),
            pltpu.VMEM((rows, width), bf16),
            pltpu.VMEM((rows, width), bf16),
            pltpu.VMEM((rows, width), bf16),
            pltpu.VMEM((rows, width), bf16),
            pltpu.VMEM((rows, width), f32),
            pltpu.VMEM((rows, width), f32),
            pltpu.VMEM((8, PAIR), f32),
            pltpu.VMEM(line_got.shape, bf16),
            pltpu.VMEM((width, rows), bf16),
            pltpu.VMEM((blocks, 2 * quarter, columns), bf16),
            pltpu.VMEM((blocks, quarter, columns), bf16),
            pltpu.VMEM((blocks, 2 * quarter, columns), bf16),
            pltpu.VMEM((blocks, quarter, columns), bf16),
            pltpu.VMEM((blocks, quarter, columns), bf16),
            pltpu.VMEM((blocks, LINES, shard, columns), bf16),
            pltpu.VMEM((blocks, LINES - 1, shard, columns), bf16),
            pltpu.VMEM((blocks, shard, columns), bf16),
            pltpu.VMEM((blocks, shard, columns), bf16),
            pltpu.VMEM(first.shape, bf16),
            pltpu.VMEM(line_sums.shape, bf16),
            pltpu.VMEM(line_sums.shape, bf16),
            pltpu.VMEM((LINES - 1, *late.shape[1:]), bf16),
            pltpu.VMEM(late.shape[1:], bf16),
            pltpu.VMEM(late.shape[1:], bf16),
            pltpu.VMEM((5, *small), f32),
            pltpu.VMEM((5, *small), f32),
            dma((blocks, 2)),
            dma((blocks, 2)),
            dma((blocks, LINES - 1)),
            dma((blocks, LINES - 1)),
            dma((blocks, 2)),
            dma((2,)),
            dma((2,)),
            dma((LINES - 1,)),
            dma((LINES - 1,)),
            dma((2,)),
            dma((5, 2)),
            dma((14,)),
            dma((places,)),
            dma((1,)),
        ],
        compiler_params=pltpu.CompilerParams(
            vmem_limit_bytes=60 * 2**20, collective_id=4, has_side_effects=True
        ),
        cost_estimate=NO_COST,
    )(
        line_sums, late, first, ffn_gain, bias, cosine, sine, qgain, kgain, gain,
        line_got, normed, dq, got_kv, own_kv, *raws, weight, tokens, resid,
    )


def rms_forward(values, gain_vec):
    inv_rms = lax.rsqrt(jnp.mean(values * values, axis=-1, keepdims=True) + EPSILON)
    return (values * inv_rms * gain_vec, inv_rms)


def rms_backward(values, inv_rms, gain_vec, upstream):
    weighted = upstream * gain_vec
    inner_sum = jnp.mean(weighted * values, axis=-1, keepdims=True)
    value_grad = inv_rms * weighted - values * inv_rms * inv_rms * inv_rms * inner_sum
    return (value_grad, upstream * values * inv_rms)


def shift_by(values, count, step):
    return lax.ppermute(values, "seq", [(i, (i + step) % count) for i in range(count)])


def cross_core(values, places):
    return lax.ppermute(values, "dp", [(i, i ^ 1) for i in range(places)])


def cross_x(values, places):
    return lax.ppermute(values, "dp", [(i, i ^ 2) for i in range(places)])


def core_sum(pieces, places):
    crossed, terms = [], []
    for far, cross, own in pieces:
        quarter = own.shape[1]
        far = cross_core(far, places)
        crossed.append(cross + far[:, :quarter])
        terms.append([own, far[:, quarter:]])
    return jnp.concatenate(crossed, axis=0), terms


def add_received(terms, received):
    start, longer = 0, []
    for held in terms:
        count = held[0].shape[0]
        longer.append(held + [received[start : start + count]])
        start += count
    return longer


def total_of(terms):
    return jnp.concatenate([sum(term.astype(f32) for term in held) for held in terms], axis=0).astype(bf16)


def sum_seq(values, count):
    if count == 2:
        return values.astype(f32) + shift_by(values, count, 1).astype(f32)
    return lax.psum(values.astype(f32), "seq")


def after(value, *before):
    return lax.optimization_barrier((value, before))[0]


def sum_small(values, places, seq_count):
    step = 1
    while step < places:
        values = values + lax.ppermute(values, "dp", [(i, i ^ step) for i in range(places)])
        step *= 2
    if seq_count == 2:
        return values + shift_by(values, 2, 1)
    return lax.psum(values, "seq")


def body(
    tokens, doc_lengths, variate_ids, time_ids, in_proj, out_proj, gate_up, down_proj,
    attn_gain, ffn_gain, query_gain, key_gain, head_bias, cotangent,
):
    seq_count = lax.axis_size("seq")
    seq_rank = lax.axis_index("seq")
    local_rows, width = tokens.shape
    pack_rows = local_rows * seq_count
    head_dim = query_gain.shape[0]
    places = lax.axis_size("dp")
    place = lax.axis_index("dp")
    core, across = place % 2, place // 2 % 2
    groups = places // 4
    spot = jnp.stack(
        [core, across]
        + [
            group * 4 + (across + 1 - near_x) % 2 * 2 + (core + 1 - near_core) % 2
            for near_core in range(2)
            for near_x in range(2)
            for group in range(groups)
        ]
    ).astype(jnp.int32)

    fused = places == 16 and seq_count == 2
    gains = jnp.stack([attn_gain, ffn_gain], axis=1)
    gather = lambda w: lax.all_gather(w, "dp", axis=0, tiled=True)
    first_shard = jnp.concatenate([in_proj, out_proj, jnp.pad(gains, ((0, 0), (0, PAIR - 2)))], axis=1)
    if fused:
        wide, *there = gather_first(first_shard, tokens, time_ids.reshape(-1, PAIR), places)
        slots = [(tokens, time_ids), (there[0], there[1].reshape(-1))]
    else:
        wide = gather(first_shard)
        slots = [(tokens, time_ids)]
        for step in range(1, seq_count):
            slots.append(tuple(shift_by(array, seq_count, -step) for array in slots[0]))
    out_full = wide[:, 3 * width : 4 * width]
    attn_gain_f = wide[:, 4 * width].astype(f32)[None, :]
    ffn_gain_f = wide[:, 4 * width + 1].astype(f32)[None, :]
    shard = in_proj.shape[0]
    hidden_part = down_proj.shape[0] // 2
    folds = hidden_part // shard

    def weights_part(part, gate_up, down_proj):
        columns = gate_up.reshape(shard, 2, places, 2, hidden_part)
        fold_rows = down_proj.reshape(2, folds, shard, width)
        return jnp.concatenate(
            [columns[:, 0, :, part].reshape(shard, -1), columns[:, 1, :, part].reshape(shard, -1)]
            + [fold_rows[part, k] for k in range(folds)],
            axis=1,
        )

    ffn_weights = [
        gather(after(weights_part(0, gate_up, down_proj), wide)),
        weights_part(1, *after((gate_up, down_proj), wide)),
    ]

    positions = jnp.arange(pack_rows, dtype=jnp.int32)
    first_end = doc_lengths[0, 0]
    second_end = first_end + doc_lengths[0, 1]
    segment = (positions >= first_end).astype(jnp.int32) + (positions >= second_end).astype(jnp.int32)
    query_columns, key_columns = slot_columns(segment, variate_ids[0])
    coefficients = bias_columns(head_bias)
    start = seq_rank * local_rows
    query_columns = lax.dynamic_slice_in_dim(query_columns, start, local_rows)
    local_segment = lax.dynamic_slice_in_dim(segment, start, local_rows)
    valid_rows = (local_segment < 2).astype(f32)
    source_columns, source_flags = [], []
    for step in range(seq_count):
        begin = ((seq_rank + step) % seq_count) * local_rows
        source_columns.append(lax.dynamic_slice_in_dim(key_columns, begin, local_rows))
        there = lax.dynamic_slice_in_dim(segment, begin, local_rows).reshape(-1, KEY_ROWS)
        source_flags.append(
            ((there[:, 0] <= local_segment[-1]) & (there[:, -1] >= local_segment[0])).astype(jnp.int32)
        )

    half_dim = head_dim // 2
    frequency = jnp.exp(jnp.arange(half_dim, dtype=f32) * (-math.log(ROPE_BASE) / half_dim))
    qgain = jnp.tile(query_gain, 2)[None, :]
    kgain = jnp.tile(key_gain, 2)[None, :]

    def rope_tables(times):
        angles = times.astype(f32)[:, None] * jnp.tile(frequency, 4)[None, :]
        sign = jnp.where(jnp.arange(PAIR) % head_dim < half_dim, -1.0, 1.0)
        return jnp.cos(angles), jnp.sin(angles) * sign[None, :]

    tables = [rope_tables(times) for _, times in slots]
    seed_grad = cotangent.astype(f32) * valid_rows[:, None]
    seed_low = seed_grad.astype(bf16)
    keyed = []
    for step, (there_tokens, _) in enumerate(slots):
        keys, values, *own = project(
            there_tokens, attn_gain_f, wide, *tables[step], qgain, kgain, step == 0
        )
        keyed.append((keys, values, source_columns[step]))
        if step == 0:
            cosine, sine = tables[0]
            queries, *raws, normed_low = own
            ffn_weights[1] = gather(after(ffn_weights[1], queries))
    attended, full_query = attend(
        jnp.concatenate(source_flags), queries, query_columns, coefficients, keyed
    )

    inputs_f = tokens.astype(f32)
    residual = inputs_f + dot(attended, out_full)
    normed_ffn, _ = rms_forward(residual, ffn_gain_f)
    normed_ffn_low = normed_ffn.astype(bf16)
    def scatter_line(parts):
        lines = [[line * 4 + k for line in range(groups)] for k in range(4)]
        return lax.psum_scatter(parts, "dp", scatter_dimension=0, axis_index_groups=lines, tiled=True)[0]

    def total3(first, *others):
        return sum((other.astype(f32) for other in others), first.astype(f32)).astype(bf16)

    branch, normed_ffn_grad, early_far, early_cross, early_own = feed_forward(
        places, normed_ffn_low, seed_low, residual, None, ffn_weights[0]
    )
    crossed = early_cross[:, :2] + early_far[:groups, :2]
    early_crossed = early_cross[:, 2] + early_far[:groups, 2]
    layer_out, residual_grad, mixed_low, ffn_gain_sum, far, cross, own, received = feed_forward(
        places, after(normed_ffn_low, early_crossed), seed_low, branch, normed_ffn_grad,
        ffn_weights[1], residual, ffn_gain_f, crossed,
    )
    first_total = scatter_line(total3(received, early_own[:, :2], early_far[groups:, :2]))
    second_crossed = cross + far[:groups]
    attended_grad = dot(mixed_low, out_full, NT).astype(bf16)

    attended_grad = dot(mixed_low, out_full, NT).astype(bf16)
    out_grads = outer(spot, attended, mixed_low, width)

    def merge(dqs, dkvs):
        merged, gains = merge_grads(width, 0, dqs, dkvs, raws, cosine, sine, qgain, kgain)
        return merged, jnp.sum(gains[:2].reshape(2, -1, head_dim), axis=1)

    def small_parts(bias, head_gains):
        same_bias = jnp.sum(bias, axis=-1).reshape(-1)
        tail = jnp.concatenate([head_gains[0], head_gains[1], same_bias])
        return jnp.concatenate([ffn_gain_sum[0], tail, jnp.zeros(-tail.shape[0] % 1024, f32)])

    if fused:
        (out_far,), out_cross, out_own = (cross_core(out_grads[0], places),), *out_grads[1:]
        by_line = lambda array: array.reshape(groups, -1, width)
        out_sums = [
            by_line(array) for array in (out_cross + out_far[:, : shard * groups], out_own, out_far[:, shard * groups :])
        ]
        dq_all, bias_all, received, own_kv, line_sums, line_got, late, *_ = attend_back_carry(
            full_query, attended_grad, attended, query_columns, keyed[0], keyed[1],
            (early_crossed, early_own, early_far), (second_crossed, own, far), out_sums,
        )
        in_proj_grad, out_proj_grad, gate_up_grad, down_grad, small, input_grad = finish(
            places, line_sums, line_got, late, first_total, ffn_gain_sum.reshape(-1, PAIR), bias_all,
            cosine, sine, qgain, kgain, attn_gain_f, normed_low, dq_all, received, own_kv, raws,
            wide, tokens, residual_grad,
        )
        rows_done = 2 * width // PAIR
        head_gains = jnp.sum(small[rows_done : rows_done + 2].reshape(2, 2, head_dim), axis=1)
        same_bias = jnp.sum(small[rows_done + 8 :], axis=1)
        small = jnp.concatenate([small[:rows_done].reshape(-1), head_gains.reshape(-1), same_bias])
    else:
        second = scatter_line(total3(cross_x(second_crossed, places), own, far[groups:]))
        early_down = total3(cross_x(early_crossed, places), early_own[:, 2], early_far[groups:, 2])
        early_down = scatter_line(early_down)
        dqs, dkvs, biases = [], [], 0.0
        for step in list(range(1, seq_count)) + [0]:
            dq, dkv, bias = attend_back(
                0, width // PAIR, source_flags[step], full_query, attended_grad, attended,
                query_columns, *keyed[step],
            )
            dqs.append((dq, 0))
            dkvs.append((shift_by(dkv, seq_count, step) if step else dkv, 0))
            biases = biases + bias
        merged_grad, head_gains = merge(dqs, dkvs)

        def sum_rows(pieces):
            crossed, terms = core_sum([pieces], places)
            total = total_of(add_received(terms, cross_x(crossed, places)))
            total = total.reshape(total.shape[0], groups, shard, -1).transpose(1, 0, 2, 3)
            return sum_seq(scatter_line(total), seq_count)

        in_sum = sum_rows(outer(spot, normed_low.T, merged_grad, width))
        out_proj_grad = sum_rows(out_grads)[0]
        in_proj_grad = in_sum.transpose(1, 0, 2).reshape(in_proj.shape)
        first_gates = sum_seq(first_total, seq_count)
        second_sum = sum_seq(second, seq_count)
        downs = [sum_seq(early_down, seq_count), second_sum[2]]
        down_grad = jnp.concatenate(
            [part.reshape(shard, -1, width).transpose(1, 0, 2).reshape(hidden_part, width) for part in downs]
        )
        gate_up_grad = jnp.stack(
            [
                part.reshape(2, shard, places, hidden_part).transpose(1, 0, 2, 3)
                for part in (first_gates, second_sum[:2])
            ],
            axis=3,
        ).reshape(gate_up.shape)
        normed_grad = dot(merged_grad, wide[:, : 3 * width], NT)
        norm_scale = lax.rsqrt(jnp.mean(inputs_f * inputs_f, axis=-1, keepdims=True) + EPSILON)
        input_norm_grad, attn_gain_terms = rms_backward(inputs_f, norm_scale, attn_gain_f, normed_grad)
        input_grad = residual_grad + input_norm_grad
        small = jnp.concatenate([jnp.sum(attn_gain_terms, axis=0), small_parts(biases, head_gains)])
        small = sum_small(small, places, seq_count)
    heads = head_bias.shape[0]
    gain_rows = attn_gain.shape[0]
    here = place * gain_rows
    tail = small[2 * width :]
    same_bias = tail[2 * head_dim : 2 * head_dim + heads]
    return (
        layer_out,
        input_grad,
        in_proj_grad,
        out_proj_grad,
        gate_up_grad,
        down_grad,
        lax.dynamic_slice_in_dim(small, here, gain_rows),
        lax.dynamic_slice_in_dim(small, width + here, gain_rows),
        tail[:head_dim],
        tail[head_dim : 2 * head_dim],
        jnp.stack([same_bias, -same_bias], axis=1),
    )


def solution(mesh):
    in_specs = (
        P(("dp", "seq"), None),
        P("dp", None),
        P("dp", None),
        P(("dp", "seq")),
        P("dp", None),
        P("dp", None),
        P("dp", None),
        P("dp", None),
        P("dp"),
        P("dp"),
        P(),
        P(),
        P(),
        P(("dp", "seq"), None),
    )
    out_specs = (
        P(("dp", "seq"), None),
        P(("dp", "seq"), None),
        P("dp", None),
        P("dp", None),
        P("dp", None),
        P("dp", None),
        P("dp"),
        P("dp"),
        P(),
        P(),
        P(),
    )
    return jax.shard_map(body, mesh=mesh, in_specs=in_specs, out_specs=out_specs, check_vma=False)
```
